256 devices in a mesh: gx: 4 (over y), gy: 8 (over x, core), gz: 8 (over z).
Axes of the slice: x: 4, y: 4, z: 8, core: 2. Of those that a mesh axis runs over, the one named last changes fastest.
Arguments:
- x_field: float32 [64, 16, 64, 1024], P(None, 'gx', 'gy', 'gz'), may hold values from -1.2 to 1.2
- right_side: float32 [64, 16, 64, 1024], P(None, 'gx', 'gy', 'gz'), may hold values from -8 to 8, as said below
- diag_shift: float32 [16, 64, 1024], P('gx', 'gy', 'gz'), may hold values from 0.2 to 3
- velocity: float32 [3, 16, 64, 1024], P(None, 'gx', 'gy', 'gz'), may hold values from -0.6 to 0.6
- earlier_blocks: float32 [8, 64, 16, 64, 1024], P(None, None, 'gx', 'gy', 'gz'), may hold values from -1 to 1, as said below
- sep_cells: int32 [8, 1024], P('gz', ('gx', 'gy')), may hold values from 0 to 4095
- low_inv: bfloat16 [8, 1024, 1024], P('gz', ('gx', 'gy')), may hold values from -0.1875 to 0.1875
- low_off: bfloat16 [8, 1024, 1024], P('gz', ('gx', 'gy')), may hold values from -0.15625 to 0.15625
- up_off: bfloat16 [8, 1024, 1024], P('gz', ('gx', 'gy')), may hold values from -0.15625 to 0.15625
Outputs:
- residual: float32 [64, 16, 64, 1024], P(None, 'gx', 'gy', 'gz')
- new_block: float32 [64, 16, 64, 1024], P(None, 'gx', 'gy', 'gz')
- projection: float32 [512, 64], replicated
- chol_scaled: float32 [64, 64], replicated
The draws below stay inside these ranges and needn't reach their ends.
Inputs may be any that keep to these rules, and one draw needn't show every extreme that they name: `sep_cells`: every entry indexes a cell of its device's brick; cells may repeat. `right_side`: entries of order one. `earlier_blocks`: entries of order one over the square root of 1048576.
All inputs are finite; a program needn't handle non-finite values.
Results may differ from the reference program's by a relative error of at most 0.015.
Values may be sent and summed in bfloat16 or wider, within the bound.
A program may use at most 128 MiB of HBM per device.

```python
import math
import jax
import jax.numpy as jnp
from jax import lax

RHS_COUNT = 64
PRIOR_BLOCKS = 8
CX = 4
CY = 8
CZ = 128
SEP_DEV = 32
SEG = 1024
NX = 16
NY = 64
NZ = 1024
NCELLS = 1048576
N_GY = 8
N_GZ = 8


def shared_field(key):
    return jax.random.truncated_normal(key, -3.0, 3.0, (NX, NY, NZ), jnp.float32)


def draw_right_side(key, part):
    common = shared_field(key)
    key = jax.random.fold_in(key, 11)
    noise_key, weight_key = jax.random.split(key)
    shape = (RHS_COUNT, NX, NY, NZ)
    noise = jax.random.truncated_normal(noise_key, -4.0, 4.0, shape, jnp.float32)
    weights = jax.random.uniform(weight_key, (RHS_COUNT,), jnp.float32, 0.8, 1.6)
    values = noise + weights[:, None, None, None] * common[None]
    return jnp.clip(values, -8.0, 8.0)


def draw_earlier_blocks(key, part):
    common = shared_field(key)
    key = jax.random.fold_in(key, 23)
    noise_key, coef_key = jax.random.split(key)
    row_count = PRIOR_BLOCKS * RHS_COUNT
    shape = (row_count, NX, NY, NZ)
    noise = jax.random.truncated_normal(noise_key, -4.0, 4.0, shape, jnp.float32)
    share = 0.6
    coefs = jax.random.uniform(coef_key, (row_count,), jnp.float32, -1.0, 1.0)
    strength = jnp.sqrt(jnp.float32(3.0 * share / row_count))
    values = noise + (strength * coefs)[:, None, None, None] * common[None]
    values = values * jnp.float32(NCELLS) ** (-0.5)
    return values.reshape(PRIOR_BLOCKS, RHS_COUNT, NX, NY, NZ)


def with_ends(entries, stream_key, least, largest):
    spot = [jax.random.randint(jax.random.fold_in(stream_key, axis), (), 0, length) for axis, length in enumerate(entries.shape)]
    widest = entries.shape.index(max(entries.shape))
    beside = spot[:widest] + [(spot[widest] + 1) % entries.shape[widest]] + spot[widest + 1:]
    return entries.at[tuple(spot)].set(least).at[tuple(beside)].set(largest)


def steps_of(own_key, dims, pieces, smallest, largest):
    gain, own = 1.0, jax.random.fold_in(own_key, 6)
    for position, blocks in pieces:
        draws = jnp.exp(jax.random.uniform(jax.random.fold_in(own, position), (blocks,), jnp.float32, smallest / len(pieces), largest / len(pieces)))
        gain = gain * jnp.repeat(draws, dims[position] // blocks).reshape([-1 if axis == position else 1 for axis in range(len(dims))])
    return gain


def gaussian(own_key, extent, width, reach, pieces=(), kind=jnp.bfloat16):
    loudness = steps_of(own_key, extent, pieces, -0.22, 0.18) if pieces else 1.0
    values = jax.random.normal(own_key, extent, jnp.float32) * width * loudness
    return jnp.minimum(jnp.maximum(values, -reach), reach).astype(kind)


def setup_inputs(seed: int = 0) -> dict:
    arg_keys = jax.random.split(jax.random.key(seed), 10)
    return {
        "x_field": gaussian(arg_keys[0], (RHS_COUNT, NX, NY, NZ), 0.2, 1.2, ((1, 4), (2, 8), (3, 8)), jnp.float32),
        "right_side": draw_right_side(jax.random.fold_in(arg_keys[9], 71), 0),
        "diag_shift": jnp.clip(jnp.exp(math.log(3.0) - 2.7080502 * jax.random.uniform(arg_keys[2], (NX, NY, NZ), jnp.float32) ** steps_of(arg_keys[2], (NX, NY, NZ), ((0, 4), (1, 8), (2, 8)), -0.2, 0.2)), 0.2, 3.0),
        "velocity": jnp.clip(jax.random.uniform(arg_keys[3], (3, NX, NY, NZ), jnp.float32, -0.6, 0.6) * steps_of(arg_keys[3], (3, NX, NY, NZ), ((1, 4), (2, 8), (3, 8)), -0.4, 0.0), -0.6, 0.6),
        "earlier_blocks": draw_earlier_blocks(jax.random.fold_in(arg_keys[9], 71), 0),
        "sep_cells": with_ends(jax.random.randint(arg_keys[5], (N_GZ, SEG), 0, CX * CY * CZ), jax.random.fold_in(arg_keys[5], 1), 0, (CX * CY * CZ) - 1).astype(jnp.int32),
        "low_inv": gaussian(arg_keys[6], (N_GZ, SEG, SEG), SEG ** -0.5, 0.1875, ((0, 8), (1, 32))),
        "low_off": gaussian(arg_keys[7], (N_GZ, SEG, SEG), (SEG * 3 // 2) ** -0.5, 0.15625, ((0, 8), (1, 32))),
        "up_off": gaussian(arg_keys[8], (N_GZ, SEG, SEG), (SEG * 3 // 2) ** -0.5, 0.15625, ((0, 8), (1, 32))),
    }


def operate(field, diag_shift, velocity):
    padded = jnp.pad(field, ((0, 0), (1, 1), (1, 1), (1, 1)))
    result = (6.0 + diag_shift) * field
    result = result - (1.0 + velocity[0]) * padded[:, :-2, 1:-1, 1:-1] - (1.0 - velocity[0]) * padded[:, 2:, 1:-1, 1:-1]
    result = result - (1.0 + velocity[1]) * padded[:, 1:-1, :-2, 1:-1] - (1.0 - velocity[1]) * padded[:, 1:-1, 2:, 1:-1]
    result = result - (1.0 + velocity[2]) * padded[:, 1:-1, 1:-1, :-2] - (1.0 - velocity[2]) * padded[:, 1:-1, 1:-1, 2:]
    return result

def reference(x_field, right_side, diag_shift, velocity, earlier_blocks, sep_cells, low_inv, low_off, up_off):
    residual = right_side - operate(x_field, diag_shift, velocity)
    rows = jnp.arange(SEG, dtype=jnp.int32)
    group = rows // SEP_DEV
    brick_x = group // N_GY
    brick_y = group % N_GY
    seg_ids = jnp.arange(N_GZ, dtype=jnp.int32)[:, None]
    local_x = sep_cells // (CY * CZ)
    local_y = sep_cells // CZ % CY
    local_z = sep_cells % CZ
    glob_x = brick_x[None, :] * CX + local_x
    glob_y = brick_y[None, :] * CY + local_y
    glob_z = seg_ids * CZ + local_z
    flat_index = ((glob_x * NY + glob_y) * NZ + glob_z).astype(jnp.int32).reshape(-1)
    res_flat = residual.reshape(RHS_COUNT, -1)
    seps = jnp.transpose(res_flat[:, flat_index].reshape(RHS_COUNT, N_GZ, SEG), (1, 2, 0)).astype(jnp.bfloat16)
    base = [jnp.dot(low_inv[i].astype(jnp.float32), seps[i].astype(jnp.float32), preferred_element_type=jnp.float32) for i in range(N_GZ)]
    forward = [base[0]]
    for i in range(1, N_GZ):
        forward.append(base[i] - jnp.dot(low_off[i].astype(jnp.float32), forward[i - 1].astype(jnp.bfloat16).astype(jnp.float32), preferred_element_type=jnp.float32))
    solved = [None] * N_GZ
    solved[N_GZ - 1] = forward[N_GZ - 1]
    for i in range(N_GZ - 2, -1, -1):
        solved[i] = forward[i] - jnp.dot(up_off[i].astype(jnp.float32), solved[i + 1].astype(jnp.bfloat16).astype(jnp.float32), preferred_element_type=jnp.float32)
    sol_all = jnp.stack(solved)
    sol_rows = jnp.transpose(sol_all, (2, 0, 1)).reshape(RHS_COUNT, -1)
    separator_update = res_flat / (6.0 + diag_shift).reshape(1, -1)
    separator_update = separator_update.at[:, flat_index].add(sol_rows)
    basis_matrix = earlier_blocks.reshape(PRIOR_BLOCKS * RHS_COUNT, -1)
    projection = jnp.dot(basis_matrix, separator_update.T, precision=lax.Precision.HIGHEST)
    orthogonalize = separator_update - jnp.dot(projection.T, basis_matrix, precision=lax.Precision.HIGHEST)
    gram = jnp.dot(orthogonalize, orthogonalize.T, precision=lax.Precision.HIGHEST)
    factor = jnp.linalg.cholesky(gram)
    norm_scale = jnp.sqrt(jnp.float32(NCELLS))
    solved_block = lax.linalg.triangular_solve(factor, orthogonalize, left_side=True, lower=True)
    new_block = (solved_block * norm_scale).reshape(RHS_COUNT, NX, NY, NZ)
    return (residual, new_block, projection, factor / norm_scale)
```

```python
import functools
import math

import jax
import jax.numpy as jnp
from jax import lax
from jax.experimental import pallas as pl
from jax.experimental.pallas import tpu as pltpu
from jax.sharding import PartitionSpec as P

bf16, f32 = jnp.bfloat16, jnp.float32
RHS, CX, CY, CZ, SEP = 64, 4, 8, 128, 32
SLABS = CX * CY
PAIRS = SLABS // 2
ROWS = RHS * SLABS
LANES = 128


def nt(a, b):
    return lax.dot_general(a, b, (((1,), (1,)), ((), ())), preferred_element_type=f32)


def nn(a, b):
    return jnp.dot(a, b, preferred_element_type=f32)


def split(v):
    hi = v.astype(bf16)
    return hi, (v - hi.astype(f32)).astype(bf16)


def iota(shape, dim):
    return lax.broadcasted_iota(jnp.int32, shape, dim)


def flag(cond):
    return jnp.where(cond, jnp.float32(1.0), jnp.float32(0.0))


def cholesky_and_inverse(gram):
    n = RHS
    lane8 = iota((8, LANES), 1)
    row8 = iota((8, LANES), 0)
    blocks, low, inverse = [], [], []
    for k in range(n // 8):
        eye = (lane8 - n == row8 + 8 * k).astype(f32)
        blocks.append(jnp.where(lane8 < n, gram[8 * k : 8 * k + 8, :], eye))
        low.append(jnp.zeros((8, LANES), f32))
        inverse.append(jnp.zeros((8, LANES), f32))
    for j in range(n):
        kj, r = divmod(j, 8)
        row = jnp.broadcast_to(blocks[kj][r : r + 1, :], (8, LANES))
        pivot = jnp.broadcast_to(row[:, j : j + 1], (8, LANES))
        root = lax.rsqrt(pivot)
        scaled = row * root
        inverse[kj] = jnp.where(row8 == r, scaled, inverse[kj])
        for k in range(kj, n // 8):
            col = jnp.broadcast_to(blocks[k][:, j : j + 1], (8, LANES)) * root
            if k == kj:
                col = jnp.where(row8 >= r, col, 0.0)
                below = jnp.where(row8 > r, col, 0.0)
            else:
                below = col
            low[k] = jnp.where(lane8 == j, col, low[k])
            blocks[k] = blocks[k] - below * scaled
    return jnp.concatenate(low, axis=0), jnp.concatenate(inverse, axis=0)


def kernel(
    na, nb, nz, early,
    x_h, r_h, d_h, v_h, e_h, c_h, li_h, lo_h, up_h,
    res_o, new_o, proj_o, chol_o,
    x_v, r_v, d_v, v_v, e_v, c_v, m_v,
    xsb, hx, hy, hz, zsend, oh, gath,
    w0, wh, wl, vh, vl, pacc, vsh, vsl,
    sep_loc, sep_hop, sep_all, base, state, stateb, fw_in, bw_in, ret,
    psend, pin1, psum1, pin2, pin3, pin4, pin5, pt_hl,
    orth, g_loc, gin1, gin2, gin3, gin4, chol_v,
    loc_sem, send_sem, recv_sem,
):
    a, b, z = lax.axis_index("gx"), lax.axis_index("gy"), lax.axis_index("gz")
    size = {"gx": na, "gy": nb, "gz": nz}
    pos = {"gx": a, "gy": b, "gz": z}
    group = RHS // na
    wide = SEP * na
    depth = nb * wide
    count = [0]
    sent = []

    def place(axis, index):
        at = dict(pos)
        at[axis] = index
        return (at["gx"], at["gy"], at["gz"])

    def send(src, dst, where, keep=True):
        n = count[0]
        count[0] += 1
        copy = pltpu.make_async_remote_copy(
            src_ref=src, dst_ref=dst, send_sem=send_sem.at[n], recv_sem=recv_sem.at[n],
            device_id=where, device_id_type=pl.DeviceIdType.MESH,
        )
        copy.start()
        if keep:
            sent.append(copy)
        return copy

    def share(axis, src_of, dst):
        n = size[axis]
        copies = []
        for d in range(1, n):
            to = lax.rem(pos[axis] + d, n)
            copies.append(send(src_of(to), dst, place(axis, to)))
        return copies

    def arrive(copies):
        for copy in copies:
            copy.wait_recv()

    barrier = pltpu.get_barrier_semaphore()
    partners = 0
    for axis in ("gx", "gy", "gz"):
        for d in range(1, size[axis]):
            pl.semaphore_signal(
                barrier, inc=1, device_id=place(axis, lax.rem(pos[axis] + d, size[axis])),
                device_id_type=pl.DeviceIdType.MESH,
            )
            partners += 1

    def fetch(n, src, dst):
        copy = pltpu.make_async_copy(src, dst, loc_sem.at[n])
        copy.start()
        return copy

    get_x = fetch(0, x_h, x_v)
    get_m = [fetch(1 + i, h, m_v.at[i]) for i, h in enumerate((li_h, lo_h, up_h))]
    get_c = fetch(4, c_h, c_v)
    get_d = fetch(5, d_h, d_v)
    get_v = fetch(6, v_h, v_v)
    get_r = fetch(7, r_h, r_v)
    get_e = fetch(8, e_h, e_v)

    def slab(ref, s, n=RHS):
        return ref[pl.ds(s, n, stride=SLABS), :]

    get_x.wait()
    for s in range(SLABS):
        xsb[s // CY, (s % CY) * RHS : (s % CY + 1) * RHS, :] = slab(x_v, s).astype(bf16)
    q32, l32 = iota((32, LANES), 0), iota((32, LANES), 1)
    edge = jnp.zeros((32, LANES), f32)
    for p in range(PAIRS):
        pick = ((q32 == p) & (l32 == CZ - 1)) | ((q32 == 16 + p) & (l32 == 0))
        rows = xsb[p // 4, (p % 4) * 128 : (p % 4 + 1) * 128, :]
        edge = edge + nt(pick.astype(bf16), rows)
    zsend[...] = edge.astype(bf16)

    pl.semaphore_wait(barrier, partners)

    def ring(axis, step):
        n = size[axis]
        return place(axis, lax.rem(pos[axis] + step + n, n))

    halo = [
        send(zsend.at[pl.ds(0, 16)], hz.at[0], ring("gz", 1)),
        send(zsend.at[pl.ds(16, 16)], hz.at[1], ring("gz", -1)),
        send(xsb.at[CX - 1], hx.at[0], ring("gx", 1)),
        send(xsb.at[0], hx.at[1], ring("gx", -1)),
        send(xsb.at[:, pl.ds((CY - 1) * RHS, RHS)], hy.at[0], ring("gy", 1)),
        send(xsb.at[:, pl.ds(0, RHS)], hy.at[1], ring("gy", -1)),
    ]

    mine = pl.ds(pl.multiple_of(a * SEP, SEP), SEP)
    lane_group = iota((SEP, LANES), 1) // SEP
    per_tile = LANES // SEP
    gather = []
    for i in range(3):
        get_m[i].wait()
        tiles = [
            m_v[i, :, t * LANES : (t + 1) * LANES].astype(f32) for t in range(depth // LANES)
        ]
        for t in range(depth // LANES):
            out = jnp.zeros((SEP, LANES), f32)
            for g in range(per_tile):
                chunk = t * per_tile + g
                old = (chunk % na) * nb + chunk // na
                piece = tiles[old // per_tile]
                shift = ((g - old % per_tile) * SEP) % LANES
                if shift:
                    piece = pltpu.roll(piece, shift, 1)
                out = jnp.where(lane_group == g, piece, out)
            gath[i, mine, t * LANES : (t + 1) * LANES] = out.astype(bf16)
        gather.append(
            share("gx", lambda to, i=i: gath.at[i, mine], gath.at[i, mine])
        )

    get_c.wait()
    cells = jnp.broadcast_to(c_v[...], (SEP, SEP)).astype(f32)
    square = iota((SEP, SEP), 0) == iota((SEP, SEP), 1)
    column = jnp.sum(jnp.where(square, cells, 0.0), axis=1, keepdims=True)
    column = jnp.broadcast_to(column, (SEP, 2 * CZ))
    z256 = iota((SEP, 2 * CZ), 1).astype(f32)
    for p in range(PAIRS):
        oh[p] = jnp.zeros((wide, 2 * CZ), bf16)
        oh[p, mine, :] = jnp.where(column == z256 + float(p * 2 * CZ), 1.0, 0.0).astype(bf16)
    vsh[...] = jnp.zeros(vsh.shape, bf16)
    vsl[...] = jnp.zeros(vsl.shape, bf16)

    get_d.wait()
    get_v.wait()
    get_r.wait()
    arrive(halo)

    before_z = hz[0].astype(f32) * flag(z > 0)
    after_z = hz[1].astype(f32) * flag(z < nz - 1)
    ends = jnp.concatenate(
        [before_z, after_z, jnp.zeros((LANES - 32, LANES), f32)], axis=0
    ).T.astype(bf16)
    keep = {
        (0, -1): flag(a > 0), (0, 1): flag(a < na - 1),
        (1, -1): flag(b > 0), (1, 1): flag(b < nb - 1),
    }
    q128, l128 = iota((LANES, LANES), 0), iota((LANES, LANES), 1)
    lane64 = iota((RHS, LANES), 1)
    seps = jnp.zeros((RHS, wide), f32)
    for p in range(PAIRS):
        spread = ((q128 == p) & (l128 == 0)) | ((q128 == 16 + p) & (l128 == CZ - 1))
        z_ends = nn(ends, spread.astype(bf16))
        halves = []
        for h in range(2):
            s = 2 * p + h
            cx, cy = divmod(s, CY)
            x = slab(x_v, s)
            diag = 6.0 + d_v[s : s + 1, :]

            def beside(k, step):
                if k == 0 and not 0 <= cx + step < CX:
                    rows = hx[(step + 1) // 2, cy * RHS : (cy + 1) * RHS, :]
                    return rows.astype(f32), keep[0, step]
                if k == 1 and not 0 <= cy + step < CY:
                    return hy[(step + 1) // 2, cx].astype(f32), keep[1, step]
                return slab(x_v, s + step * (CY if k == 0 else 1)), None

            total = diag * x
            for k in range(2):
                for step in (-1, 1):
                    coef = 1.0 - step * v_v[k * SLABS + s : k * SLABS + s + 1, :]
                    value, mask = beside(k, step)
                    if mask is not None:
                        coef = coef * mask
                    total = total - coef * value
            end = z_ends[h * RHS : (h + 1) * RHS, :]
            v2 = v_v[2 * SLABS + s : 2 * SLABS + s + 1, :]
            before = jnp.where(lane64 == 0, end, pltpu.roll(x, 1, 1))
            after = jnp.where(lane64 == CZ - 1, end, pltpu.roll(x, CZ - 1, 1))
            total = total - (1.0 + v2) * before - (1.0 - v2) * after
            res = slab(r_v, s) - total
            r_v[pl.ds(s, RHS, stride=SLABS), :] = res
            halves.append(res.astype(bf16))
            w = res / diag
            hi, lo = split(w)
            at = slice(h * CZ, (h + 1) * CZ)
            w0[p, :, at] = w
            wh[p, :, at] = hi
            wl[p, :, at] = lo
        seps = seps + nt(jnp.concatenate(halves, axis=1), oh[p])
    put_res = pltpu.make_async_copy(r_v, res_o, loc_sem.at[9])
    put_res.start()

    sep_loc[...] = seps.astype(bf16).reshape(na, group, wide)
    hop = share("gx", lambda to: sep_loc.at[to], sep_hop.at[a])
    sep_hop[a] = sep_loc[a]
    arrive(hop)
    mixed = sep_hop[0].astype(f32)
    for i in range(1, na):
        mixed = mixed + sep_hop[i].astype(f32)
    sep_all[b] = mixed.astype(bf16)
    hop = share("gy", lambda to: sep_all.at[b], sep_all.at[b])
    arrive(hop)

    def row_of(ref):
        return jnp.concatenate([ref[i] for i in range(nb)], axis=1)

    arrive(gather[0])
    base[...] = nt(row_of(sep_all), gath[0])

    def earlier_work():
        get_e.wait()
        pacc[...] = jnp.zeros(pacc.shape, f32)

        def step(p, carry):
            s_h, s_l = carry
            rows = e_v.shape[0] // SLABS
            both = jnp.concatenate(
                [slab(e_v, 2 * p, rows), slab(e_v, 2 * p + 1, rows)], axis=1
            )
            hi, lo = split(both)
            vh[p] = hi
            vl[p] = lo
            own = oh[p, mine, :]
            first = nt(jnp.concatenate([wh[p], wl[p], own], axis=0), hi)
            second = nt(jnp.concatenate([wh[p], own], axis=0), lo)
            pacc[...] += first[:RHS] + first[RHS : 2 * RHS] + second[:RHS]
            return s_h + first[2 * RHS :], s_l + second[RHS:]

        zero = jnp.zeros((SEP, e_v.shape[0] // SLABS), f32)
        s_h, s_l = lax.fori_loop(0, PAIRS, step, (zero, zero))
        vsh[mine, :] = s_h.astype(bf16)
        vsl[mine, :] = s_l.astype(bf16)

    def sweep_push(dst, step):
        out = []
        for d in range(nb):
            to = lax.rem(b + d, nb)
            out.append(send(stateb.at[0 if step > 0 else 1], dst.at[b], (a, to, z + step), False))
        return out

    def sweep_copies(first, dst, step):
        return [
            pltpu.make_async_remote_copy(
                src_ref=stateb.at[0 if step > 0 else 1], dst_ref=dst.at[b],
                send_sem=send_sem.at[first + d], recv_sem=recv_sem.at[first + d],
                device_id=(a, lax.rem(b + d, nb), z + step),
                device_id_type=pl.DeviceIdType.MESH,
            )
            for d in range(nb)
        ]

    pl.when(z >= early)(earlier_work)

    fw_first = count[0]
    arrive(gather[1])

    @pl.when(z == 0)
    def _():
        state[...] = base[...]

    @pl.when(z > 0)
    def _():
        arrive(sweep_copies(fw_first, fw_in, 1))
        state[...] = base[...] - nt(row_of(fw_in), gath[1])

    @pl.when(z < nz - 1)
    def _():
        stateb[0] = state[...].astype(bf16)
        sweep_push(fw_in, 1)

    count[0] = fw_first + nb
    pl.when(z < early)(earlier_work)

    bw_first = count[0]
    arrive(gather[2])

    @pl.when(z < nz - 1)
    def _():
        arrive(sweep_copies(bw_first, bw_in, -1))
        state[...] = state[...] - nt(row_of(bw_in), gath[2])

    @pl.when(z > 0)
    def _():
        stateb[1] = state[...].astype(bf16)
        sweep_push(bw_in, -1)

    count[0] = bw_first + nb

    hop = share("gx", lambda to: state, ret.at[a])
    ret[a] = state[...]
    arrive(hop)
    sol_h, sol_l = split(ret[...].reshape(RHS, wide))
    corr = nn(jnp.concatenate([sol_h, sol_l], axis=0), vsh[...])
    corr = pacc[...] + corr[:RHS] + corr[RHS:] + nn(sol_h, vsl[...])
    cols = corr.shape[1]

    psend[...] = corr.reshape(na, group, cols)
    hop = share("gx", lambda to: psend.at[to], pin1.at[a])
    pin1[a] = psend[a]

    sol_hl = jnp.concatenate([sol_h, sol_l], axis=1)

    def add_sol(p, carry):
        w0[p] = w0[p] + nn(sol_hl, jnp.concatenate([oh[p], oh[p]], axis=0))
        return carry

    lax.fori_loop(0, PAIRS, add_sol, 0, unroll=2)

    def total_of(ref, n):
        out = ref[0]
        for i in range(1, n):
            out = out + ref[i]
        return out

    arrive(hop)
    part = total_of(pin1, na)
    ph = group // 8
    pw = nb // ph
    width = cols // pw
    for i in range(nb):
        r, c = divmod(i, pw)
        psum1[i] = part[r * 8 : r * 8 + 8, c * width : (c + 1) * width]
    hop = share("gy", lambda to: psum1.at[to], pin2.at[b])
    pin2[b] = psum1[b]
    arrive(hop)
    pin3[z] = total_of(pin2, nb)
    hop = share("gz", lambda to: pin3.at[z], pin3.at[z])
    arrive(hop)
    pin4[b] = total_of(pin3, nz)
    hop = share("gy", lambda to: pin4.at[b], pin4.at[b])
    arrive(hop)
    pin5[a] = jnp.concatenate(
        [jnp.concatenate([pin4[r * pw + c] for c in range(pw)], axis=1) for r in range(ph)], axis=0
    )
    hop = share("gx", lambda to: pin5.at[a], pin5.at[a])
    arrive(hop)
    full = pin5[...].reshape(RHS, cols)
    hi, lo = split(full)
    pt_hl[:RHS] = hi
    pt_hl[RHS:] = lo

    def project(p, gram):
        main = nn(pt_hl[...], vh[p])
        o = w0[p] - (main[:RHS] + main[RHS:] + nn(pt_hl[:RHS], vl[p]))
        hi, lo = split(o)
        both = jnp.concatenate([hi, lo], axis=0)
        orth[p] = both
        return gram + nt(both, both)

    gram = lax.fori_loop(0, PAIRS, project, jnp.zeros((2 * RHS, 2 * RHS), f32), unroll=2)
    gram = gram[:RHS] + gram[RHS:]
    gram = gram + pltpu.roll(gram, RHS, 1)
    piece = RHS // nz
    g_loc[...] = gram.reshape(nz, piece, LANES)
    hop = share("gz", lambda to: g_loc.at[to], gin1.at[z])
    gin1[z] = g_loc[z]

    proj_o[...] = jnp.concatenate([full, jnp.zeros((LANES - RHS, cols), f32)], axis=0).T[:, :RHS]

    arrive(hop)
    gin2[b] = total_of(gin1, nz)
    arrive(share("gy", lambda to: gin2.at[b], gin2.at[b]))
    gin3[a] = total_of(gin2, nb)
    arrive(share("gx", lambda to: gin3.at[a], gin3.at[a]))
    gin4[z] = total_of(gin3, na)
    arrive(share("gz", lambda to: gin4.at[z], gin4.at[z]))

    low, inverse = cholesky_and_inverse(gin4[...].reshape(RHS, LANES))
    scale = math.sqrt(na * nb * nz * CX * CY * CZ)
    chol_o[...] = low[:, :RHS] * (1.0 / scale)
    inverse = inverse * scale
    hi, lo = split(inverse)
    lhs = jnp.where(lane64 < RHS, pltpu.roll(hi.astype(f32), RHS, 1), lo.astype(f32)).astype(bf16)
    lhs = jnp.concatenate([lhs, lhs], axis=1)
    put_res.wait()
    for p in range(PAIRS):
        hi, lo = orth[p, :RHS], orth[p, RHS:]
        out = nn(lhs, jnp.concatenate([hi, hi, lo, lo], axis=0))
        for h in range(2):
            x_v[pl.ds(2 * p + h, RHS, stride=SLABS), :] = out[:, h * CZ : (h + 1) * CZ]
    put_new = pltpu.make_async_copy(x_v, new_o, loc_sem.at[10])
    put_new.start()

    for copy in sent:
        copy.wait_send()

    @pl.when(z < nz - 1)
    def _():
        for copy in sweep_copies(fw_first, fw_in, 1):
            copy.wait_send()

    @pl.when(z > 0)
    def _():
        for copy in sweep_copies(bw_first, bw_in, -1):
            copy.wait_send()

    put_new.wait()


def body(
    x_field, right_side, diag_shift, velocity, earlier_blocks, sep_cells, low_inv, low_off, up_off
):
    na, nb, nz = (lax.axis_size(n) for n in ("gx", "gy", "gz"))
    group, wide = RHS // na, SEP * na
    depth = nb * wide
    vecs = earlier_blocks.shape[0] * earlier_blocks.shape[1]
    pw = nb // (group // 8)
    width = vecs // pw
    piece = RHS // nz
    vmem = pltpu.VMEM
    scratch = [
        vmem((ROWS, CZ), f32),
        vmem((ROWS, CZ), f32),
        vmem((SLABS, CZ), f32),
        vmem((3 * SLABS, CZ), f32),
        vmem((vecs * SLABS, CZ), f32),
        vmem((1, SEP), jnp.int32),
        vmem((3, SEP, depth), bf16),
        vmem((CX, CY * RHS, CZ), bf16),
        vmem((2, CY * RHS, CZ), bf16),
        vmem((2, CX, RHS, CZ), bf16),
        vmem((2, 16, LANES), bf16),
        vmem((32, LANES), bf16),
        vmem((PAIRS, wide, 2 * CZ), bf16),
        vmem((3, wide, depth), bf16),
        vmem((PAIRS, RHS, 2 * CZ), f32),
        vmem((PAIRS, RHS, 2 * CZ), bf16),
        vmem((PAIRS, RHS, 2 * CZ), bf16),
        vmem((PAIRS, vecs, 2 * CZ), bf16),
        vmem((PAIRS, vecs, 2 * CZ), bf16),
        vmem((RHS, vecs), f32),
        vmem((wide, vecs), bf16),
        vmem((wide, vecs), bf16),
        vmem((na, group, wide), bf16),
        vmem((na, group, wide), bf16),
        vmem((nb, group, wide), bf16),
        vmem((group, wide), f32),
        vmem((group, wide), f32),
        vmem((2, group, wide), bf16),
        vmem((nb, group, wide), bf16),
        vmem((nb, group, wide), bf16),
        vmem((na, group, wide), f32),
        vmem((na, group, vecs), f32),
        vmem((na, group, vecs), f32),
        vmem((nb, 8, width), f32),
        vmem((nb, 8, width), f32),
        vmem((nz, 8, width), f32),
        vmem((nb, 8, width), f32),
        vmem((na, group, vecs), f32),
        vmem((2 * RHS, vecs), bf16),
        vmem((PAIRS, 2 * RHS, 2 * CZ), bf16),
        vmem((nz, piece, LANES), f32),
        vmem((nz, piece, LANES), f32),
        vmem((nb, piece, LANES), f32),
        vmem((na, piece, LANES), f32),
        vmem((nz, piece, LANES), f32),
        vmem((8, LANES), f32),
        pltpu.SemaphoreType.DMA((11,)),
        pltpu.SemaphoreType.DMA((128,)),
        pltpu.SemaphoreType.DMA((128,)),
    ]
    flat = lambda v: v.reshape(-1, CZ)
    anywhere = pl.BlockSpec(memory_space=pl.ANY)
    in_vmem = pl.BlockSpec(memory_space=pltpu.VMEM)
    res, new, projection, factor = pl.pallas_call(
        functools.partial(kernel, na, nb, nz, (nz * 5) // 8),
        out_shape=(
            jax.ShapeDtypeStruct((ROWS, CZ), f32),
            jax.ShapeDtypeStruct((ROWS, CZ), f32),
            jax.ShapeDtypeStruct((vecs, RHS), f32),
            jax.ShapeDtypeStruct((RHS, RHS), f32),
        ),
        in_specs=[anywhere] * 9,
        out_specs=(anywhere, anywhere, in_vmem, in_vmem),
        scratch_shapes=scratch,
        compiler_params=pltpu.CompilerParams(
            collective_id=0, has_side_effects=True, vmem_limit_bytes=50 * 2**20
        ),
        cost_estimate=pl.CostEstimate(
            flops=2 * 10**9, bytes_accessed=13 * 2**20, transcendentals=0
        ),
        name="step",
    )(
        flat(x_field), flat(right_side), flat(diag_shift), flat(velocity), flat(earlier_blocks),
        sep_cells, low_inv[0], low_off[0], up_off[0],
    )
    shape = right_side.shape
    return (res.reshape(shape), new.reshape(shape), projection, factor)


def solution(mesh):
    return jax.shard_map(
        body,
        mesh=mesh,
        in_specs=(
            P(None, "gx", "gy", "gz"),
            P(None, "gx", "gy", "gz"),
            P("gx", "gy", "gz"),
            P(None, "gx", "gy", "gz"),
            P(None, None, "gx", "gy", "gz"),
            P("gz", ("gx", "gy")),
            P("gz", ("gx", "gy"), None),
            P("gz", ("gx", "gy"), None),
            P("gz", ("gx", "gy"), None),
        ),
        out_specs=(P(None, "gx", "gy", "gz"), P(None, "gx", "gy", "gz"), P(), P()),
        check_vma=False,
    )
```

```python
import functools
import math

import jax
import jax.numpy as jnp
from jax import lax
from jax.experimental import pallas as pl
from jax.experimental.pallas import tpu as pltpu
from jax.sharding import PartitionSpec as P

bf16, f32 = jnp.bfloat16, jnp.float32
RHS, CX, CY, CZ, SEP = 64, 4, 8, 128, 32
SLABS = CX * CY
PAIRS = SLABS // 2
ROWS = RHS * SLABS
LANES = 128


def nt(a, b):
    return lax.dot_general(a, b, (((1,), (1,)), ((), ())), preferred_element_type=f32)


def nn(a, b):
    return jnp.dot(a, b, preferred_element_type=f32)


def split(v):
    hi = v.astype(bf16)
    return hi, (v - hi.astype(f32)).astype(bf16)


def iota(shape, dim):
    return lax.broadcasted_iota(jnp.int32, shape, dim)


def flag(cond):
    return jnp.where(cond, jnp.float32(1.0), jnp.float32(0.0))


def cholesky_rows(gram, out):
    n = RHS
    lane8, row8 = iota((8, LANES), 1), iota((8, LANES), 0)
    blocks = []
    for k in range(n // 8):
        eye = (lane8 - n == row8 + 8 * k).astype(f32)
        blocks.append(jnp.where(lane8 < n, gram[8 * k : 8 * k + 8, :], eye))

    def sublane(v, r):
        return jnp.broadcast_to(v[r : r + 1, :], (8, LANES))

    def panel(turn, blocks):
        first = blocks[0]
        columns = [jnp.broadcast_to(first[:, j : j + 1], (8, LANES)) for j in range(8)]
        entry = {(i, j): sublane(columns[j], i) for j in range(8) for i in range(j, 8)}
        rows = [sublane(first, i) for i in range(8)]
        for j in range(8):
            root = lax.rsqrt(entry[j, j])
            rows[j] = rows[j] * root
            for i in range(j + 1, 8):
                entry[i, j] = entry[i, j] * root
            for i in range(j + 1, 8):
                rows[i] = rows[i] - entry[i, j] * rows[j]
                for k in range(j + 1, i + 1):
                    entry[i, k] = entry[i, k] - entry[i, j] * entry[k, j]
        done = rows[0]
        for i in range(1, 8):
            done = jnp.where(row8 == i, rows[i], done)
        hi = done.astype(bf16).astype(f32)
        mid = (done - hi).astype(bf16).astype(f32)
        low = done - hi - mid
        left = jnp.concatenate([hi, hi, mid, hi, low, mid], axis=0).astype(bf16)
        right = jnp.concatenate([hi, mid, hi, low, hi, mid], axis=0).astype(bf16)
        change = lax.dot_general(
            left, right, (((0,), (0,)), ((), ())), preferred_element_type=f32
        )
        out[pl.ds(pl.multiple_of(turn * 8, 8), 8), :] = pltpu.roll(done, turn * 8, 1)
        rest = [
            pltpu.roll(blocks[k] - change[8 * k : 8 * k + 8], LANES - 8, 1)
            for k in range(1, n // 8)
        ]
        return tuple(rest + [jnp.zeros((8, LANES), f32)])

    lax.fori_loop(0, n // 8, panel, tuple(blocks))


def kernel(
    na, nb, nz, early,
    x_h, r_h, d_h, v_h, e_h, c_h, li_h, lo_h, up_h,
    res_o, orth_o, proj_o, gram_o,
    x_v, r_v, d_v, v_v, e_v, c_v, m_v,
    xp, xsb, hx, hy, hz, zsend, oh, gath, gath_t,
    w0, wh, wl, vh, vl, eacc, pacc, vsh, vsl,
    sep_loc, sep_hop, sep_all, base, state, stateb, fw_in, bw_in, ret,
    psend, pin1, psum1, pin2, pin3, pin4, pin5, pt_hl,
    orth, g_loc, gin1, gin2, gin3, gin4,
    loc_sem, send_sem, recv_sem,
):
    a, b, z = lax.axis_index("gx"), lax.axis_index("gy"), lax.axis_index("gz")
    size = {"gx": na, "gy": nb, "gz": nz}
    pos = {"gx": a, "gy": b, "gz": z}
    members, slots = nb // 2, na * 2
    member, core = b // 2, lax.rem(b, 2)
    slot = a * 2 + core
    group = RHS // members
    wide = SEP * members
    depth = slots * wide
    count = [0]
    sent = []

    def place(axis, index):
        if axis == "member":
            return (a, index * 2 + core, z)
        if axis == "slot":
            return (index // 2, member * 2 + lax.rem(index, 2), z)
        at = dict(pos)
        at[axis] = index
        return (at["gx"], at["gy"], at["gz"])

    size["member"], size["slot"] = members, slots
    pos_of = dict(pos, member=member, slot=slot)

    def send(src, dst, where, keep=True):
        n = count[0]
        count[0] += 1
        copy = pltpu.make_async_remote_copy(
            src_ref=src, dst_ref=dst, send_sem=send_sem.at[n], recv_sem=recv_sem.at[n],
            device_id=where, device_id_type=pl.DeviceIdType.MESH,
        )
        copy.start()
        if keep:
            sent.append(copy)
        return copy

    def share(axis, src_of, dst):
        n = size[axis]
        copies = []
        for d in range(1, n):
            to = lax.rem(pos_of[axis] + d, n)
            copies.append(send(src_of(to), dst, place(axis, to)))
        return copies

    def arrive(copies):
        for copy in copies:
            copy.wait_recv()

    barrier = pltpu.get_barrier_semaphore()
    partners = 0

    def greet(where):
        pl.semaphore_signal(
            barrier, inc=1, device_id=where, device_id_type=pl.DeviceIdType.MESH
        )

    for axis in ("gx", "gy", "gz"):
        for d in range(1, size[axis]):
            greet(place(axis, lax.rem(pos[axis] + d, size[axis])))
            partners += 1
    for d in range(1, na):
        greet((lax.rem(a + d, na), member * 2 + 1 - core, z))
        partners += 1

    def fetch(n, src, dst):
        copy = pltpu.make_async_copy(src, dst, loc_sem.at[n])
        copy.start()
        return copy

    get_x = fetch(0, x_h, x_v)
    get_m = [fetch(1 + i, h, m_v.at[i]) for i, h in enumerate((li_h, lo_h, up_h))]
    get_c = fetch(4, c_h, c_v)
    get_d = fetch(5, d_h, d_v)
    get_v = fetch(6, v_h, v_v)
    get_r = fetch(7, r_h, r_v)
    get_e = fetch(8, e_h, e_v)

    def slab(ref, s, n=RHS):
        return ref[pl.ds(s, n, stride=SLABS), :]

    def rows_at(start, n):
        return pl.ds(pl.multiple_of(start, n), n)

    get_x.wait()
    pad = CY + 2

    def spread_x(cx, carry):
        for cy in range(CY):
            v = slab(x_v, cx * CY + cy)
            xp[(cx + 1) * pad + cy + 1] = v
            xsb[cx, cy * RHS : (cy + 1) * RHS, :] = v.astype(bf16)
        return carry

    lax.fori_loop(0, CX, spread_x, 0)
    q32, l32 = iota((32, LANES), 0), iota((32, LANES), 1)

    def pick_edge(p, edge):
        pick = ((q32 == p) & (l32 == CZ - 1)) | ((q32 == 16 + p) & (l32 == 0))
        rows = xsb[p // 4, rows_at(lax.rem(p, 4) * 128, 128), :]
        return edge + nt(pick.astype(bf16), rows)

    zsend[...] = lax.fori_loop(
        0, PAIRS, pick_edge, jnp.zeros((32, LANES), f32), unroll=4
    ).astype(bf16)

    pl.semaphore_wait(barrier, partners)

    def ring(axis, step):
        n = size[axis]
        return place(axis, lax.rem(pos[axis] + step + n, n))

    halo = [
        send(xsb.at[CX - 1], hx.at[0], ring("gx", 1)),
        send(xsb.at[0], hx.at[1], ring("gx", -1)),
        send(xsb.at[:, pl.ds((CY - 1) * RHS, RHS)], hy.at[0], ring("gy", 1)),
        send(xsb.at[:, pl.ds(0, RHS)], hy.at[1], ring("gy", -1)),
        send(zsend.at[pl.ds(0, 16)], hz.at[0], ring("gz", 1)),
        send(zsend.at[pl.ds(16, 16)], hz.at[1], ring("gz", -1)),
    ]

    mine = rows_at(member * SEP, SEP)
    lane_group = iota((SEP, LANES), 1) // SEP
    per_tile = LANES // SEP
    for i in range(3):
        get_m[i].wait()

    def reorder(i, carry):
        tiles = [
            m_v[i, :, t * LANES : (t + 1) * LANES].astype(f32) for t in range(depth // LANES)
        ]
        for t in range(depth // LANES):
            out = jnp.zeros((SEP, LANES), f32)
            for g in range(per_tile):
                new = t * per_tile + g
                from_slot, from_member = new // members, new % members
                old = (from_slot // 2) * nb + from_member * 2 + from_slot % 2
                piece = tiles[old // per_tile]
                shift = ((g - old % per_tile) * SEP) % LANES
                if shift:
                    piece = pltpu.roll(piece, shift, 1)
                out = jnp.where(lane_group == g, piece, out)
            gath[i, mine, t * LANES : (t + 1) * LANES] = out.astype(bf16)
        return carry

    lax.fori_loop(0, 3, reorder, 0)

    def share_matrix(i):
        return share("member", lambda to: gath.at[i, mine], gath.at[i, mine])

    gather_base = share_matrix(0)

    get_c.wait()
    cells = jnp.broadcast_to(c_v[...], (SEP, SEP)).astype(f32)
    square = iota((SEP, SEP), 0) == iota((SEP, SEP), 1)
    column = jnp.sum(jnp.where(square, cells, 0.0), axis=1, keepdims=True)
    column = jnp.broadcast_to(column, (SEP, 2 * CZ))
    z256 = iota((SEP, 2 * CZ), 1)

    def mark(p, carry):
        oh[p] = jnp.zeros((wide, 2 * CZ), bf16)
        at = (z256 + p * 2 * CZ).astype(f32)
        oh[p, mine, :] = jnp.where(column == at, 1.0, 0.0).astype(bf16)
        return carry

    lax.fori_loop(0, PAIRS, mark, 0)

    get_d.wait()
    get_v.wait()
    get_r.wait()
    arrive(halo)

    before_z = hz[0].astype(f32) * flag(z > 0)
    after_z = hz[1].astype(f32) * flag(z < nz - 1)
    ends = jnp.concatenate(
        [before_z, after_z, jnp.zeros((LANES - 32, LANES), f32)], axis=0
    ).T.astype(bf16)
    for k, mask in enumerate((flag(a > 0), flag(a < na - 1))):
        for cy in range(CY):
            xp[k * (CX + 1) * pad + cy + 1] = (
                hx[k, cy * RHS : (cy + 1) * RHS, :].astype(f32) * mask
            )
    for k, mask in enumerate((flag(b > 0), flag(b < nb - 1))):
        for cx in range(CX):
            xp[(cx + 1) * pad + k * (CY + 1)] = hy[k, cx].astype(f32) * mask
    q128, l128 = iota((LANES, LANES), 0), iota((LANES, LANES), 1)
    lane64 = iota((RHS, LANES), 1)

    def residual_of(p, seps):
        spread = ((q128 == p) & (l128 == 0)) | ((q128 == 16 + p) & (l128 == CZ - 1))
        z_ends = nn(ends, spread.astype(bf16))
        halves = []
        for h in range(2):
            s = 2 * p + h
            i = (p // 4 + 1) * pad + lax.rem(p, 4) * 2 + h + 1
            x = xp[i]
            diag = 6.0 + d_v[pl.ds(s, 1), :]
            v0, v1, v2 = (v_v[pl.ds(k * SLABS + s, 1), :] for k in range(3))
            end = z_ends[h * RHS : (h + 1) * RHS, :]
            before = jnp.where(lane64 == 0, end, pltpu.roll(x, 1, 1))
            after = jnp.where(lane64 == CZ - 1, end, pltpu.roll(x, CZ - 1, 1))
            res = slab(r_v, s) - diag * x
            res = res + (1.0 + v0) * xp[i - pad] + (1.0 - v0) * xp[i + pad]
            res = res + (1.0 + v1) * xp[i - 1] + (1.0 - v1) * xp[i + 1]
            res = res + (1.0 + v2) * before + (1.0 - v2) * after
            r_v[pl.ds(s, RHS, stride=SLABS), :] = res
            halves.append(res.astype(bf16))
            w = res / diag
            hi, lo = split(w)
            at = slice(h * CZ, (h + 1) * CZ)
            w0[p, :, at] = w
            wh[p, :, at] = hi
            wl[p, :, at] = lo
        return seps + nt(jnp.concatenate(halves, axis=1), oh[p])

    seps = lax.fori_loop(0, PAIRS, residual_of, jnp.zeros((RHS, wide), f32))
    put_res = pltpu.make_async_copy(r_v, res_o, loc_sem.at[9])
    put_res.start()

    sep_loc[...] = seps.astype(bf16).reshape(members, group, wide)
    hop = share("member", lambda to: sep_loc.at[to], sep_hop.at[member])
    sep_hop[member] = sep_loc[member]
    gather_fw = share_matrix(1)
    arrive(hop)
    mixed = sep_hop[0].astype(f32)
    for i in range(1, members):
        mixed = mixed + sep_hop[i].astype(f32)
    sep_all[slot] = mixed.astype(bf16)
    hop = share("slot", lambda to: sep_all.at[slot], sep_all.at[slot])
    gather_bw = share_matrix(2)
    arrive(gather_base)
    arrive(hop)

    def row_of(ref):
        return jnp.concatenate([ref[i] for i in range(slots)], axis=1)

    base[...] = nt(row_of(sep_all), gath[0])

    vecs = e_v.shape[0] // SLABS

    def earlier_work():
        get_e.wait()
        eacc[...] = jnp.zeros(eacc.shape, f32)

        def step(p, carry):
            both = jnp.concatenate(
                [slab(e_v, 2 * p, vecs), slab(e_v, 2 * p + 1, vecs)], axis=1
            )
            hi, lo = split(both)
            vh[p] = hi
            vl[p] = lo
            right = jnp.concatenate([wh[p], wl[p], oh[p]], axis=0)
            eacc[:vecs] += nt(hi, right)
            eacc[vecs:] += nt(lo, right)
            return carry

        lax.fori_loop(0, PAIRS, step, 0)
        main = eacc[:vecs, :LANES] + eacc[vecs:, :LANES]
        main = main.T
        pacc[...] = main[:RHS] + main[RHS:]
        vsh[...] = eacc[:vecs, LANES:].T.astype(bf16)
        vsl[...] = eacc[vecs:, LANES:].T.astype(bf16)

    def sweep_copies(first, dst, step):
        copies = []
        for d in range(slots):
            to = lax.rem(slot + d, slots)
            copies.append(
                pltpu.make_async_remote_copy(
                    src_ref=stateb.at[0 if step > 0 else 1], dst_ref=dst.at[slot],
                    send_sem=send_sem.at[first + d], recv_sem=recv_sem.at[first + d],
                    device_id=(to // 2, member * 2 + lax.rem(to, 2), z + step),
                    device_id_type=pl.DeviceIdType.MESH,
                )
            )
        return copies

    def sweep_push(first, dst, step):
        for copy in sweep_copies(first, dst, step):
            copy.start()

    pl.when(z >= early)(earlier_work)

    fw_first = count[0]
    bw_first = fw_first + slots
    count[0] = bw_first + slots
    arrive(gather_fw)

    @pl.when(z == 0)
    def _():
        state[...] = base[...]

    @pl.when(z > 0)
    def _():
        gath_t[...] = gath[1].astype(f32).T.astype(bf16)
        arrive(sweep_copies(fw_first, fw_in, 1))
        state[...] = base[...] - nn(row_of(fw_in), gath_t[...])

    @pl.when(z < nz - 1)
    def _():
        stateb[0] = state[...].astype(bf16)
        sweep_push(fw_first, fw_in, 1)

    pl.when(z < early)(earlier_work)
    arrive(gather_bw)

    @pl.when(z < nz - 1)
    def _():
        gath_t[...] = gath[2].astype(f32).T.astype(bf16)
        arrive(sweep_copies(bw_first, bw_in, -1))
        state[...] = state[...] - nn(row_of(bw_in), gath_t[...])

    @pl.when(z > 0)
    def _():
        stateb[1] = state[...].astype(bf16)
        sweep_push(bw_first, bw_in, -1)

    hop = share("member", lambda to: state, ret.at[member])
    ret[member] = state[...]
    arrive(hop)
    sol_h, sol_l = split(ret[...].reshape(RHS, wide))
    corr = nn(jnp.concatenate([sol_h, sol_l], axis=0), vsh[...])
    corr = pacc[...] + corr[:RHS] + corr[RHS:] + nn(sol_h, vsl[...])
    cols = vecs

    part_rows = RHS // na
    psend[...] = corr.reshape(na, part_rows, cols)
    hop = share("gx", lambda to: psend.at[to], pin1.at[a])
    pin1[a] = psend[a]

    sol_hl = jnp.concatenate([sol_h, sol_l], axis=1)

    def add_sol(p, carry):
        w0[p] = w0[p] + nn(sol_hl, jnp.concatenate([oh[p], oh[p]], axis=0))
        return carry

    lax.fori_loop(0, PAIRS, add_sol, 0, unroll=2)

    def total_of(ref, n):
        out = ref[0]
        for i in range(1, n):
            out = out + ref[i]
        return out

    arrive(hop)
    part = total_of(pin1, na)
    ph = part_rows // 8
    pw = nb // ph
    width = cols // pw
    for i in range(nb):
        r, c = divmod(i, pw)
        psum1[i] = part[r * 8 : r * 8 + 8, c * width : (c + 1) * width]
    hop = share("gy", lambda to: psum1.at[to], pin2.at[b])
    pin2[b] = psum1[b]
    arrive(hop)
    pin3[z] = total_of(pin2, nb)
    arrive(share("gz", lambda to: pin3.at[z], pin3.at[z]))
    pin4[b] = total_of(pin3, nz)
    arrive(share("gy", lambda to: pin4.at[b], pin4.at[b]))
    pin5[a] = jnp.concatenate(
        [jnp.concatenate([pin4[r * pw + c] for c in range(pw)], axis=1) for r in range(ph)], axis=0
    )
    arrive(share("gx", lambda to: pin5.at[a], pin5.at[a]))
    full = pin5[...].reshape(RHS, cols)
    pin5_put = pltpu.make_async_copy(pin5, proj_o, loc_sem.at[10])
    pin5_put.start()
    hi, lo = split(full)
    pt_hl[:RHS] = hi
    pt_hl[RHS:] = lo

    def project(p, gram):
        main = nn(pt_hl[...], vh[p])
        o = w0[p] - (main[:RHS] + main[RHS:] + nn(pt_hl[:RHS], vl[p]))
        hi, lo = split(o)
        both = jnp.concatenate([hi, lo], axis=0)
        orth[p] = both
        return gram + nt(both, both)

    gram = lax.fori_loop(0, PAIRS, project, jnp.zeros((2 * RHS, 2 * RHS), f32), unroll=2)
    gram = gram[:RHS] + gram[RHS:]
    gram = gram + pltpu.roll(gram, RHS, 1)
    put_orth = pltpu.make_async_copy(orth, orth_o, loc_sem.at[11])
    put_orth.start()
    piece = RHS // nz
    g_loc[...] = gram.reshape(nz, piece, LANES)
    hop = share("gz", lambda to: g_loc.at[to], gin1.at[z])
    gin1[z] = g_loc[z]
    arrive(hop)
    gin2[b] = total_of(gin1, nz)
    arrive(share("gy", lambda to: gin2.at[b], gin2.at[b]))
    gin3[a] = total_of(gin2, nb)
    arrive(share("gx", lambda to: gin3.at[a], gin3.at[a]))
    gin4[z] = total_of(gin3, na)
    arrive(share("gz", lambda to: gin4.at[z], gin4.at[z]))

    put_gram = pltpu.make_async_copy(gin4, gram_o, loc_sem.at[12])
    put_gram.start()
    for copy in sent:
        copy.wait_send()

    @pl.when(z < nz - 1)
    def _():
        for copy in sweep_copies(fw_first, fw_in, 1):
            copy.wait_send()

    @pl.when(z > 0)
    def _():
        for copy in sweep_copies(bw_first, bw_in, -1):
            copy.wait_send()

    for put in (put_res, pin5_put, put_orth, put_gram):
        put.wait()


def finish_kernel(
    scale, gram_v, orth_h, res_h, proj_h, res_o, new_o, proj_o, chol_o,
    orth, rows_v, new_v, res_v, proj_v, sem,
):
    get = pltpu.make_async_copy(orth_h, orth, sem.at[0])
    hand_on = [
        (pltpu.make_async_copy(res_h, res_v, sem.at[1]), pltpu.make_async_copy(res_v, res_o, sem.at[2])),
        (pltpu.make_async_copy(proj_h, proj_v, sem.at[3]), pltpu.make_async_copy(proj_v, proj_o, sem.at[4])),
    ]
    get.start()
    for copy, _ in hand_on:
        copy.start()
    cholesky_rows(gram_v[...], rows_v)
    rows = rows_v[...]
    lane64, row64 = iota((RHS, LANES), 1), iota((RHS, LANES), 0)
    upper = jnp.where((lane64 >= row64) & (lane64 < RHS), rows * (1.0 / scale), 0.0)
    inverse = jnp.where(lane64 - RHS <= row64, rows * scale, 0.0)
    hi, lo = split(inverse)
    lhs = jnp.where(lane64 < RHS, pltpu.roll(hi.astype(f32), RHS, 1), lo.astype(f32)).astype(bf16)
    lhs = jnp.concatenate([lhs, lhs], axis=1)
    for copy, onward in hand_on:
        copy.wait()
        onward.start()
    get.wait()

    def finish(p, carry):
        hi, lo = orth[p, :RHS], orth[p, RHS:]
        out = nn(lhs, jnp.concatenate([hi, hi, lo, lo], axis=0))
        for h in range(2):
            new_v[pl.ds(2 * p + h, RHS, stride=SLABS), :] = out[:, h * CZ : (h + 1) * CZ]
        return carry

    lax.fori_loop(0, PAIRS, finish, 0, unroll=2)
    put_new = pltpu.make_async_copy(new_v, new_o, sem.at[5])
    put_new.start()
    upper = jnp.concatenate([upper, jnp.zeros((LANES - RHS, LANES), f32)], axis=0)
    chol_o[...] = upper.T[:RHS, :RHS]
    for _, onward in hand_on:
        onward.wait()
    put_new.wait()


def body(
    x_field, right_side, diag_shift, velocity, earlier_blocks, sep_cells, low_inv, low_off, up_off
):
    na, nb, nz = (lax.axis_size(n) for n in ("gx", "gy", "gz"))
    members, slots = nb // 2, na * 2
    group, wide = RHS // members, SEP * members
    depth = slots * wide
    part_rows = RHS // na
    vecs = earlier_blocks.shape[0] * earlier_blocks.shape[1]
    pw = nb // (part_rows // 8)
    width = vecs // pw
    piece = RHS // nz
    vmem = pltpu.VMEM
    scratch = [
        vmem((ROWS, CZ), f32),
        vmem((ROWS, CZ), f32),
        vmem((SLABS, CZ), f32),
        vmem((3 * SLABS, CZ), f32),
        vmem((vecs * SLABS, CZ), f32),
        vmem((1, SEP), jnp.int32),
        vmem((3, SEP, depth), bf16),
        vmem(((CX + 2) * (CY + 2), RHS, CZ), f32),
        vmem((CX, CY * RHS, CZ), bf16),
        vmem((2, CY * RHS, CZ), bf16),
        vmem((2, CX, RHS, CZ), bf16),
        vmem((2, 16, LANES), bf16),
        vmem((32, LANES), bf16),
        vmem((PAIRS, wide, 2 * CZ), bf16),
        vmem((3, wide, depth), bf16),
        vmem((depth, wide), bf16),
        vmem((PAIRS, RHS, 2 * CZ), f32),
        vmem((PAIRS, RHS, 2 * CZ), bf16),
        vmem((PAIRS, RHS, 2 * CZ), bf16),
        vmem((PAIRS, vecs, 2 * CZ), bf16),
        vmem((PAIRS, vecs, 2 * CZ), bf16),
        vmem((2 * vecs, 2 * LANES), f32),
        vmem((RHS, vecs), f32),
        vmem((wide, vecs), bf16),
        vmem((wide, vecs), bf16),
        vmem((members, group, wide), bf16),
        vmem((members, group, wide), bf16),
        vmem((slots, group, wide), bf16),
        vmem((group, wide), f32),
        vmem((group, wide), f32),
        vmem((2, group, wide), bf16),
        vmem((slots, group, wide), bf16),
        vmem((slots, group, wide), bf16),
        vmem((members, group, wide), f32),
        vmem((na, part_rows, vecs), f32),
        vmem((na, part_rows, vecs), f32),
        vmem((nb, 8, width), f32),
        vmem((nb, 8, width), f32),
        vmem((nz, 8, width), f32),
        vmem((nb, 8, width), f32),
        vmem((na, part_rows, vecs), f32),
        vmem((2 * RHS, vecs), bf16),
        vmem((PAIRS, 2 * RHS, 2 * CZ), bf16),
        vmem((nz, piece, LANES), f32),
        vmem((nz, piece, LANES), f32),
        vmem((nb, piece, LANES), f32),
        vmem((na, piece, LANES), f32),
        vmem((nz, piece, LANES), f32),
        pltpu.SemaphoreType.DMA((13,)),
        pltpu.SemaphoreType.DMA((128,)),
        pltpu.SemaphoreType.DMA((128,)),
    ]
    flat = lambda v: v.reshape(-1, CZ)
    anywhere = pl.BlockSpec(memory_space=pl.ANY)
    in_vmem = pl.BlockSpec(memory_space=pltpu.VMEM)
    res, orth, projection, gram = pl.pallas_call(
        functools.partial(kernel, na, nb, nz, (nz * 5) // 8),
        out_shape=(
            jax.ShapeDtypeStruct((ROWS, CZ), f32),
            jax.ShapeDtypeStruct((PAIRS, 2 * RHS, 2 * CZ), bf16),
            jax.ShapeDtypeStruct((na, part_rows, vecs), f32),
            jax.ShapeDtypeStruct((nz, piece, LANES), f32),
        ),
        in_specs=[anywhere] * 9,
        out_specs=(anywhere,) * 4,
        scratch_shapes=scratch,
        compiler_params=pltpu.CompilerParams(
            collective_id=0, has_side_effects=True, vmem_limit_bytes=60 * 2**20
        ),
        cost_estimate=pl.CostEstimate(
            flops=2 * 10**9, bytes_accessed=13 * 2**20, transcendentals=0
        ),
        name="step",
    )(
        flat(x_field), flat(right_side), flat(diag_shift), flat(velocity), flat(earlier_blocks),
        sep_cells, low_inv[0], low_off[0], up_off[0],
    )
    res, new, projection, factor = pl.pallas_call(
        functools.partial(finish_kernel, math.sqrt(na * nb * nz * CX * CY * CZ)),
        out_shape=(
            jax.ShapeDtypeStruct((ROWS, CZ), f32),
            jax.ShapeDtypeStruct((ROWS, CZ), f32),
            jax.ShapeDtypeStruct((RHS, vecs), f32),
            jax.ShapeDtypeStruct((RHS, RHS), f32),
        ),
        in_specs=[in_vmem, anywhere, anywhere, anywhere],
        out_specs=(anywhere, anywhere, anywhere, in_vmem),
        scratch_shapes=[
            vmem((PAIRS, 2 * RHS, 2 * CZ), bf16),
            vmem((RHS, LANES), f32),
            vmem((ROWS, CZ), f32),
            vmem((ROWS, CZ), f32),
            vmem((RHS, vecs), f32),
            pltpu.SemaphoreType.DMA((6,)),
        ],
        compiler_params=pltpu.CompilerParams(vmem_limit_bytes=60 * 2**20),
        cost_estimate=pl.CostEstimate(flops=2 * 10**8, bytes_accessed=5 * 2**20, transcendentals=0),
        name="finish",
    )(gram.reshape(RHS, LANES), orth, res, projection.reshape(RHS, vecs))
    shape = right_side.shape
    return (res.reshape(shape), new.reshape(shape), projection.T, factor)


def solution(mesh):
    return jax.shard_map(
        body,
        mesh=mesh,
        in_specs=(
            P(None, "gx", "gy", "gz"),
            P(None, "gx", "gy", "gz"),
            P("gx", "gy", "gz"),
            P(None, "gx", "gy", "gz"),
            P(None, None, "gx", "gy", "gz"),
            P("gz", ("gx", "gy")),
            P("gz", ("gx", "gy"), None),
            P("gz", ("gx", "gy"), None),
            P("gz", ("gx", "gy"), None),
        ),
        out_specs=(P(None, "gx", "gy", "gz"), P(None, "gx", "gy", "gz"), P(), P()),
        check_vma=False,
    )
```

```python
import functools
import math

import jax
import jax.numpy as jnp
from jax import lax
from jax.experimental import pallas as pl
from jax.experimental.pallas import tpu as pltpu
from jax.sharding import PartitionSpec as P

bf16, f32 = jnp.bfloat16, jnp.float32
RHS, CX, CY, CZ, SEP = 64, 4, 8, 128, 32
SLABS = CX * CY
PAIRS = SLABS // 2
QUADS = SLABS // 4
ROWS = RHS * SLABS
LANES = 128


def nt(a, b):
    return lax.dot_general(a, b, (((1,), (1,)), ((), ())), preferred_element_type=f32)


def nn(a, b):
    return jnp.dot(a, b, preferred_element_type=f32)


def split(v):
    hi = v.astype(bf16)
    return hi, (v - hi.astype(f32)).astype(bf16)


def iota(shape, dim):
    return lax.broadcasted_iota(jnp.int32, shape, dim)


def flag(cond):
    return jnp.where(cond, jnp.float32(1.0), jnp.float32(0.0))


def cholesky_rows(gram, out):
    n = RHS
    lane8, row8 = iota((8, LANES), 1), iota((8, LANES), 0)
    blocks = []
    for k in range(n // 8):
        eye = (lane8 - n == row8 + 8 * k).astype(f32)
        blocks.append(jnp.where(lane8 < n, gram[8 * k : 8 * k + 8, :], eye))

    def sublane(v, r):
        return jnp.broadcast_to(v[r : r + 1, :], (8, LANES))

    def panel(turn, blocks):
        first = blocks[0]
        columns = [jnp.broadcast_to(first[:, j : j + 1], (8, LANES)) for j in range(8)]
        entry = {(i, j): sublane(columns[j], i) for j in range(8) for i in range(j, 8)}
        rows = [sublane(first, i) for i in range(8)]
        for j in range(8):
            root = lax.rsqrt(entry[j, j])
            rows[j] = rows[j] * root
            for i in range(j + 1, 8):
                entry[i, j] = entry[i, j] * root
            for i in range(j + 1, 8):
                rows[i] = rows[i] - entry[i, j] * rows[j]
                for k in range(j + 1, i + 1):
                    entry[i, k] = entry[i, k] - entry[i, j] * entry[k, j]
        done = rows[0]
        for i in range(1, 8):
            done = jnp.where(row8 == i, rows[i], done)
        hi = done.astype(bf16).astype(f32)
        mid = (done - hi).astype(bf16).astype(f32)
        low = done - hi - mid
        left = jnp.concatenate([hi, hi, mid, hi, low, mid], axis=0).astype(bf16)
        right = jnp.concatenate([hi, mid, hi, low, hi, mid], axis=0).astype(bf16)
        change = lax.dot_general(
            left, right, (((0,), (0,)), ((), ())), preferred_element_type=f32
        )
        out[pl.ds(pl.multiple_of(turn * 8, 8), 8), :] = pltpu.roll(done, turn * 8, 1)
        rest = [
            pltpu.roll(blocks[k] - change[8 * k : 8 * k + 8], LANES - 8, 1)
            for k in range(1, n // 8)
        ]
        return tuple(rest + [jnp.zeros((8, LANES), f32)])

    lax.fori_loop(0, n // 8, panel, tuple(blocks))


def kernel(
    na, nb, nz,
    x_h, r_h, d_h, v_h, e_h, c_h, li_h, lo_h, up_h,
    res_o, orth_o, proj_o, gram_o,
    x_v, r_v, d_v, v_v, e_v, c_v, m_v,
    xp, xsb, hx, hy, hz, zsend, oh, gath, gath_in, gath_t,
    w0, wh, wl, vh, vl, eacc, pacc, vsh, vsl,
    sep_loc, sep_hop, sep_all, base_loc, base_in, base, state, stateb, tiles, fw_in, bw_in, ret,
    psend, pin1, psum1, pin2, pin3, pin4, pin5, pt_hl,
    orth, g_loc, gin1, gin2, gin3, gin4,
    loc_sem, send_sem, recv_sem,
):
    a, b, z = lax.axis_index("gx"), lax.axis_index("gy"), lax.axis_index("gz")
    size = {"gx": na, "gy": nb, "gz": nz}
    pos = {"gx": a, "gy": b, "gz": z}
    members, slots = nb // 2, na * 2
    member, core = b // 2, lax.rem(b, 2)
    slot = core * na + a
    group = RHS // members
    wide = SEP * members
    depth = slots * wide
    half = na * wide
    count = [0]
    sent = []

    def place(axis, index):
        if axis == "member":
            return (a, index * 2 + core, z)
        if axis == "slot":
            return (lax.rem(index, na), member * 2 + index // na, z)
        at = dict(pos)
        at[axis] = index
        return (at["gx"], at["gy"], at["gz"])

    size["member"], size["slot"] = members, slots
    pos_of = dict(pos, member=member, slot=slot)

    def remote(n, src, dst, where):
        return pltpu.make_async_remote_copy(
            src_ref=src, dst_ref=dst, send_sem=send_sem.at[n], recv_sem=recv_sem.at[n],
            device_id=where, device_id_type=pl.DeviceIdType.MESH,
        )

    def send(src, dst, where):
        copy = remote(count[0], src, dst, where)
        count[0] += 1
        copy.start()
        sent.append(copy.wait_send)
        return copy

    def exchange(pairs, dst):
        n = count[0]
        count[0] += 1
        for src, there, where in pairs:
            remote(n, src, there, where).start()
        whole = dst.at[pl.ds(0, len(pairs))]
        out = pltpu.make_async_copy(whole, whole, send_sem.at[n])
        sent.append(out.wait)
        return pltpu.make_async_copy(whole, whole, recv_sem.at[n])

    def share(axis, src_of, dst):
        n = size[axis]
        others = [lax.rem(pos_of[axis] + d, n) for d in range(1, n)]
        there = dst.at[pos_of[axis]]
        return exchange([(src_of(to), there, place(axis, to)) for to in others], dst)

    def arrive(copies):
        for copy in copies:
            copy.wait_recv()

    barrier = pltpu.get_barrier_semaphore()
    partners = 0

    def greet(where):
        pl.semaphore_signal(
            barrier, inc=1, device_id=where, device_id_type=pl.DeviceIdType.MESH
        )

    for axis in ("gy", "gz"):
        for d in range(1, size[axis]):
            greet(place(axis, lax.rem(pos[axis] + d, size[axis])))
            partners += 1
    for d in range(1, na):
        for e in range(members):
            greet((lax.rem(a + d, na), lax.rem(member + e, members) * 2 + core, z))
            partners += 1
        greet((lax.rem(a + d, na), member * 2 + 1 - core, z))
        partners += 1

    def fetch(n, src, dst):
        copy = pltpu.make_async_copy(src, dst, loc_sem.at[n])
        copy.start()
        return copy

    get_x = fetch(0, x_h, x_v)
    get_m = [fetch(1 + i, h, m_v.at[i]) for i, h in enumerate((li_h, lo_h, up_h))]
    get_c = fetch(4, c_h, c_v)
    get_d = fetch(5, d_h, d_v)
    get_v = fetch(6, v_h, v_v)
    get_r = fetch(7, r_h, r_v)
    chunk = e_v.shape[0] // 4
    get_e = [
        fetch((8, 13, 14, 15)[i], e_h.at[pl.ds(i * chunk, chunk)], e_v.at[pl.ds(i * chunk, chunk)])
        for i in range(4)
    ]

    def slab(ref, s, n=RHS):
        return ref[pl.ds(s, n, stride=SLABS), :]

    def rows_at(start, n):
        return pl.ds(pl.multiple_of(start, n), n)

    get_x.wait()
    pad = CY + 2

    def spread_x(cx, carry):
        for cy in range(CY):
            v = slab(x_v, cx * CY + cy)
            xp[(cx + 1) * pad + cy + 1] = v
            xsb[cx, cy * RHS : (cy + 1) * RHS, :] = v.astype(bf16)
        return carry

    lax.fori_loop(0, CX, spread_x, 0)
    pl.semaphore_wait(barrier, partners)

    def ring(axis, step):
        n = size[axis]
        return place(axis, lax.rem(pos_of[axis] + step + n, n))

    halo = [
        send(xsb.at[CX - 1], hx.at[0], ring("gx", 1)),
        send(xsb.at[0], hx.at[1], ring("gx", -1)),
        send(xsb.at[:, pl.ds((CY - 1) * RHS, RHS)], hy.at[0], ring("gy", 1)),
        send(xsb.at[:, pl.ds(0, RHS)], hy.at[1], ring("gy", -1)),
    ]
    q32, l32 = iota((32, LANES), 0), iota((32, LANES), 1)

    def pick_edge(p, edge):
        pick = ((q32 == p) & (l32 == CZ - 1)) | ((q32 == 16 + p) & (l32 == 0))
        rows = xsb[p // 4, rows_at(lax.rem(p, 4) * 128, 128), :]
        return edge + nt(pick.astype(bf16), rows)

    zsend[...] = lax.fori_loop(
        0, PAIRS, pick_edge, jnp.zeros((32, LANES), f32), unroll=4
    ).astype(bf16)

    halo += [
        send(zsend.at[pl.ds(0, 16)], hz.at[0], ring("gz", 1)),
        send(zsend.at[pl.ds(16, 16)], hz.at[1], ring("gz", -1)),
    ]

    mine = rows_at(member * SEP, SEP)
    lane_group = iota((SEP, LANES), 1) // SEP
    per_tile = LANES // SEP
    for i in range(3):
        get_m[i].wait()

    def reorder(i):
        pieces = [
            m_v[i, :, t * LANES : (t + 1) * LANES].astype(f32) for t in range(depth // LANES)
        ]
        for t in range(depth // LANES):
            out = jnp.zeros((SEP, LANES), f32)
            for g in range(per_tile):
                old = (t % na) * nb + g * 2 + t // na
                piece = pieces[old // per_tile]
                shift = ((g - old % per_tile) * SEP) % LANES
                if shift:
                    piece = pltpu.roll(piece, shift, 1)
                out = jnp.where(lane_group == g, piece, out)
            at = slice(t * LANES, (t + 1) * LANES)
            if i == 0:
                gath_in[mine, at] = out.astype(bf16)
            else:
                gath[i - 1, a, member, :, at] = out.astype(bf16)

    for i in range(3):
        reorder(i)

    axes = ("member", "gx")

    def own(m, c):
        return gath.at[m, a, member, :, pl.ds(c * half, half)]

    def near(m, c, axis, step, part):
        at = ring_index(axis, step)
        rows = pl.ds(part * (SEP // 2), SEP // 2)
        if axis == "member":
            return gath.at[m, a, at, rows, pl.ds(c * half, half)]
        return gath.at[m, at, member, rows, pl.ds(c * half, half)]

    def line(m, c, axis, step):
        at = ring_index(axis, step)
        if axis == "member":
            return gath.at[m, :, at, :, pl.ds(c * half, half)]
        return gath.at[m, at, :, :, pl.ds(c * half, half)]

    def near_line(m, c, axis, step, part):
        at = ring_index(axis, step)
        cut = pl.ds(part * 2, 2)
        if axis == "member":
            return gath.at[m, cut, at, :, pl.ds(c * half, half)]
        return gath.at[m, at, cut, :, pl.ds(c * half, half)]

    def ring_index(axis, step):
        return lax.rem(pos_of[axis] + step + size[axis], size[axis])

    def later(src, where):
        copy = remote(count[0], src, src, where)
        count[0] += 1
        return copy

    def ring_pair(block, axis):
        return [later(block, ring(axis, step)) for step in (1, -1)]

    def gather_stages(m):
        one, two, three, four = [], [], [], []
        for c in range(2):
            first, second = axes[c], axes[1 - c]
            one += ring_pair(own(m, c), first)
            three += ring_pair(line(m, c, second, 0), second)
            for part, step in enumerate((1, -1)):
                two.append(later(near(m, c, first, -step, part), ring(first, step)))
                four.append(later(near_line(m, c, second, -step, part), ring(second, step)))
        return one, two, three, four

    def launch(copies):
        for copy in copies:
            copy.start()

    def relay(came, onward):
        for got, copy in zip(came, onward):
            got.wait_recv()
            copy.start()

    low_stages, up_stages = gather_stages(0), gather_stages(1)
    use_low, use_up = z > 0, z < nz - 1
    up_after = z < (nz * 5) // 8
    up_before = jnp.logical_and(use_up, jnp.logical_not(up_after))
    pl.when(use_low)(lambda: launch(low_stages[0]))
    gather_base = [
        send(gath_in.at[mine], gath_in.at[mine], place("member", lax.rem(member + d, members)))
        for d in range(1, members)
    ]

    get_c.wait()
    cells = jnp.broadcast_to(c_v[...], (SEP, SEP)).astype(f32)
    square = iota((SEP, SEP), 0) == iota((SEP, SEP), 1)
    column = jnp.sum(jnp.where(square, cells, 0.0), axis=1, keepdims=True)
    column = jnp.broadcast_to(column, (SEP, 4 * CZ))
    z512 = iota((SEP, 4 * CZ), 1)

    def mark(q, carry):
        oh[q] = jnp.zeros((wide, 4 * CZ), bf16)
        at = (z512 + q * 4 * CZ).astype(f32)
        oh[q, mine, :] = jnp.where(column == at, 1.0, 0.0).astype(bf16)
        return carry

    lax.fori_loop(0, QUADS, mark, 0)

    vecs = e_v.shape[0] // SLABS
    part_vecs = vecs // 4

    def relayout(c):
        get_e[c].wait()
        at = slice(c * part_vecs, (c + 1) * part_vecs)

        def step(q, carry):
            for h in range(4):
                rows = pl.ds(c * chunk + 4 * q + h, part_vecs, stride=SLABS)
                hi, lo = split(e_v[rows, :])
                vh[q, at, h * CZ : (h + 1) * CZ] = hi
                vl[q, at, h * CZ : (h + 1) * CZ] = lo
            return carry

        lax.fori_loop(0, QUADS, step, 0)

    split_early = z >= 2
    pl.when(split_early)(lambda: relayout(0))
    get_d.wait()
    get_v.wait()
    get_r.wait()
    pl.when(use_low)(lambda: relay(low_stages[0], low_stages[1]))
    arrive(halo)

    @pl.when(use_low)
    def _():
        arrive(low_stages[1])
        launch(low_stages[2])

    before_z = hz[0].astype(f32) * flag(z > 0)
    after_z = hz[1].astype(f32) * flag(z < nz - 1)
    ends = jnp.concatenate(
        [before_z, after_z, jnp.zeros((LANES - 32, LANES), f32)], axis=0
    ).T.astype(bf16)
    for k, mask in enumerate((flag(a > 0), flag(a < na - 1))):
        for cy in range(CY):
            xp[k * (CX + 1) * pad + cy + 1] = (
                hx[k, cy * RHS : (cy + 1) * RHS, :].astype(f32) * mask
            )
    for k, mask in enumerate((flag(b > 0), flag(b < nb - 1))):
        for cx in range(CX):
            xp[(cx + 1) * pad + k * (CY + 1)] = hy[k, cx].astype(f32) * mask
    q128, l128 = iota((LANES, LANES), 0), iota((LANES, LANES), 1)
    lane64 = iota((RHS, LANES), 1)

    def residual_of(q, seps):
        slabs = []
        for h in range(4):
            s = 4 * q + h
            if h % 2 == 0:
                p = 2 * q + h // 2
                spread = ((q128 == p) & (l128 == 0)) | ((q128 == 16 + p) & (l128 == CZ - 1))
                z_ends = nn(ends, spread.astype(bf16))
            i = (q // 2 + 1) * pad + lax.rem(q, 2) * 4 + h + 1
            x = xp[i]
            diag = 6.0 + d_v[pl.ds(s, 1), :]
            v0, v1, v2 = (v_v[pl.ds(k * SLABS + s, 1), :] for k in range(3))
            end = z_ends[(h % 2) * RHS : (h % 2 + 1) * RHS, :]
            before = jnp.where(lane64 == 0, end, pltpu.roll(x, 1, 1))
            after = jnp.where(lane64 == CZ - 1, end, pltpu.roll(x, CZ - 1, 1))
            res = slab(r_v, s) - diag * x
            res = res + (1.0 + v0) * xp[i - pad] + (1.0 - v0) * xp[i + pad]
            res = res + (1.0 + v1) * xp[i - 1] + (1.0 - v1) * xp[i + 1]
            res = res + (1.0 + v2) * before + (1.0 - v2) * after
            r_v[pl.ds(s, RHS, stride=SLABS), :] = res
            slabs.append(res.astype(bf16))
            w = res / diag
            hi, lo = split(w)
            at = slice(h * CZ, (h + 1) * CZ)
            w0[q, :, at] = w
            wh[q, :, at] = hi
            wl[q, :, at] = lo
        return seps + nt(jnp.concatenate(slabs, axis=1), oh[q])

    seps = lax.fori_loop(0, QUADS, residual_of, jnp.zeros((RHS, wide), f32))
    put_res = pltpu.make_async_copy(r_v, res_o, loc_sem.at[9])
    put_res.start()

    sep_loc[...] = seps.astype(bf16).reshape(members, group, wide)
    hop = share("member", lambda to: sep_loc.at[to], sep_hop)
    sep_hop[member] = sep_loc[member]
    pl.when(split_early)(lambda: relayout(1))
    hop.wait()
    mixed = sep_hop[0].astype(f32)
    for i in range(1, members):
        mixed = mixed + sep_hop[i].astype(f32)
    sep_all[slot] = mixed.astype(bf16)
    hop = share("slot", lambda to: sep_all.at[slot], sep_all)
    pl.when(split_early)(lambda: relayout(2))
    pl.when(use_low)(lambda: relay(low_stages[2], low_stages[3]))
    arrive(gather_base)
    hop.wait()

    row8 = iota((8, LANES), 0)
    base_loc[...] = nt(jnp.concatenate([sep_all[i] for i in range(slots)], axis=1), gath_in[...])
    hop = share("gx", lambda to: base_loc, base_in)
    base_in[a] = base_loc[...]
    pl.when(split_early)(lambda: relayout(3))
    hop.wait()
    gx_here = jnp.zeros((8, LANES), jnp.int32) + a
    for j in range(na):
        both = base_in[j]
        v = jnp.where(gx_here >= 2, both[8:], both[:8])
        v = jnp.where(lax.rem(gx_here, 2) == 1, pltpu.roll(v, 4, 0), v)
        base[:, j * wide : (j + 1) * wide] = jnp.where(row8 < 4, v, pltpu.roll(v, 4, 0))

    eacc[...] = jnp.zeros(eacc.shape, f32)

    def earlier_product(q, carry):
        right = jnp.concatenate([wh[q], wl[q], oh[q]], axis=0)
        eacc[:vecs] += nt(vh[q], right)
        eacc[vecs:] += nt(vl[q], right)
        return carry

    def earlier_results():
        main = eacc[:vecs, :LANES] + eacc[vecs:, :LANES]
        main = main.T
        pacc[...] = main[:RHS] + main[RHS:]
        vsh[...] = eacc[:vecs, LANES:].T.astype(bf16)
        vsl[...] = eacc[vecs:, LANES:].T.astype(bf16)

    turns = (QUADS * z) // (2 * (nz - 1) - z)

    def sweep_copies(first, dst, step):
        return [
            remote(
                first + d, stateb.at[0 if step > 0 else 1], dst.at[core],
                (a, member * 2 + lax.rem(core + d, 2), z + step),
            )
            for d in range(2)
        ]

    def sweep_push(first, dst, step):
        v = state[...]
        t = [v[:, j * wide : (j + 1) * wide] for j in range(na)]
        packed = jnp.concatenate(
            [jnp.where(row8 < 4, t[0], t[1]), jnp.where(row8 < 4, t[2], t[3])], axis=0
        )
        stateb[0 if step > 0 else 1] = packed.astype(bf16)
        for copy in sweep_copies(first, dst, step):
            copy.start()

    row_group = iota((16, LANES), 0) // 4

    def product_of(first, dst, step):
        arrive(sweep_copies(first, dst, step))
        left = []
        for i in range(2):
            v = dst[i].astype(f32)
            left += [jnp.where(row_group == j, v, 0.0).astype(bf16) for j in range(na)]
        out = nn(jnp.concatenate(left, axis=1), gath_t[...])
        out = out[:8] + out[8:]
        return out + pltpu.roll(out, 4, 0)

    def transpose_matrix(m):
        def step(t, carry):
            at = rows_at(t * LANES, LANES)
            block = gath[m, :, :, :, at].reshape(half, LANES)
            gath_t[at, :] = block.astype(f32).T.astype(bf16)
            return carry

        lax.fori_loop(0, depth // LANES, step, 0)

    fw_first = count[0]
    bw_first = fw_first + 2
    count[0] = bw_first + 2

    @pl.when(up_before)
    def _():
        launch(up_stages[0])
        relay(up_stages[0], up_stages[1])
        arrive(up_stages[1])
        launch(up_stages[2])

    @pl.when(use_low)
    def _():
        arrive(low_stages[3])
        transpose_matrix(0)

    lax.fori_loop(0, turns, earlier_product, 0)
    pl.when(z == nz - 1)(earlier_results)
    pl.when(up_before)(lambda: relay(up_stages[2], up_stages[3]))

    @pl.when(z == 0)
    def _():
        state[...] = base[...]

    @pl.when(z > 0)
    def _():
        state[...] = base[...] - product_of(fw_first, fw_in, 1)

    @pl.when(z < nz - 1)
    def _():
        sweep_push(fw_first, fw_in, 1)

    pl.when(up_after)(lambda: launch(up_stages[0]))

    @pl.when(jnp.logical_not(split_early))
    def _():
        for c in range(4):
            relayout(c)

    half_way = (turns + QUADS) // 2
    lax.fori_loop(turns, half_way, earlier_product, 0)

    @pl.when(up_after)
    def _():
        relay(up_stages[0], up_stages[1])
        arrive(up_stages[1])
        launch(up_stages[2])

    lax.fori_loop(half_way, QUADS, earlier_product, 0)
    pl.when(z < nz - 1)(earlier_results)
    pl.when(up_after)(lambda: relay(up_stages[2], up_stages[3]))

    @pl.when(z < nz - 1)
    def _():
        arrive(up_stages[3])
        transpose_matrix(1)
        state[...] = state[...] - product_of(bw_first, bw_in, -1)

    @pl.when(z > 0)
    def _():
        sweep_push(bw_first, bw_in, -1)

    for j in range(na):
        tiles[j] = state[:, j * wide : (j + 1) * wide]
    here = member * na + a
    pairs = []
    for d in range(na):
        for e in range(members):
            if d or e:
                to, far = lax.rem(a + d, na), lax.rem(member + e, members)
                pairs.append((tiles.at[to], ret.at[here], (to, far * 2 + core, z)))
    hop = exchange(pairs, ret)
    ret[here] = tiles[a]
    hop.wait()
    sol = jnp.concatenate(
        [jnp.where(row8 < 4, ret[2 * i], ret[2 * i + 1]) for i in range(na * members // 2)], axis=0
    )
    sol_h, sol_l = split(sol)
    corr = nn(jnp.concatenate([sol_h, sol_l], axis=0), vsh[...])
    corr = pacc[...] + corr[:RHS] + corr[RHS:] + nn(sol_h, vsl[...])
    cols = vecs

    part_rows = RHS // na
    psend[...] = corr.reshape(na, part_rows, cols)
    hop = share("gx", lambda to: psend.at[to], pin1)
    pin1[a] = psend[a]

    sol_hl = jnp.concatenate([sol_h, sol_l], axis=1)

    def add_sol(q, carry):
        w0[q] = w0[q] + nn(sol_hl, jnp.concatenate([oh[q], oh[q]], axis=0))
        return carry

    lax.fori_loop(0, QUADS, add_sol, 0)

    def total_of(ref, n):
        out = ref[0]
        for i in range(1, n):
            out = out + ref[i]
        return out

    hop.wait()
    part = total_of(pin1, na)
    ph = part_rows // 8
    pw = nb // ph
    width = cols // pw
    for i in range(nb):
        r, c = divmod(i, pw)
        psum1[i] = part[r * 8 : r * 8 + 8, c * width : (c + 1) * width]
    hop = share("gy", lambda to: psum1.at[to], pin2)
    pin2[b] = psum1[b]
    hop.wait()
    pin3[z] = total_of(pin2, nb)
    share("gz", lambda to: pin3.at[z], pin3).wait()
    pin4[b] = total_of(pin3, nz)
    share("gy", lambda to: pin4.at[b], pin4).wait()
    pin5[a] = jnp.concatenate(
        [jnp.concatenate([pin4[r * pw + c] for c in range(pw)], axis=1) for r in range(ph)], axis=0
    )
    share("gx", lambda to: pin5.at[a], pin5).wait()
    full = pin5[...].reshape(RHS, cols)
    pin5_put = pltpu.make_async_copy(pin5, proj_o, loc_sem.at[10])
    pin5_put.start()
    hi, lo = split(full)
    pt_hl[:RHS] = hi
    pt_hl[RHS:] = lo

    def project(q, gram):
        main = nn(pt_hl[...], vh[q])
        o = w0[q] - (main[:RHS] + main[RHS:] + nn(pt_hl[:RHS], vl[q]))
        hi, lo = split(o)
        both = jnp.concatenate([hi, lo], axis=0)
        orth[q] = both
        return gram + nt(both, both)

    gram = lax.fori_loop(0, QUADS, project, jnp.zeros((2 * RHS, 2 * RHS), f32))
    gram = gram[:RHS] + gram[RHS:]
    gram = gram + pltpu.roll(gram, RHS, 1)
    put_orth = pltpu.make_async_copy(orth, orth_o, loc_sem.at[11])
    put_orth.start()
    piece = RHS // nz
    g_loc[...] = gram.reshape(nz, piece, LANES)
    hop = share("gz", lambda to: g_loc.at[to], gin1)
    gin1[z] = g_loc[z]
    hop.wait()
    gin2[b] = total_of(gin1, nz)
    share("gy", lambda to: gin2.at[b], gin2).wait()
    gin3[a] = total_of(gin2, nb)
    share("gx", lambda to: gin3.at[a], gin3).wait()
    gin4[z] = total_of(gin3, na)
    share("gz", lambda to: gin4.at[z], gin4).wait()

    put_gram = pltpu.make_async_copy(gin4, gram_o, loc_sem.at[12])
    put_gram.start()
    for wait in sent:
        wait()

    @pl.when(use_low)
    def _():
        for stage in low_stages:
            for copy in stage:
                copy.wait_send()

    @pl.when(use_up)
    def _():
        for stage in up_stages:
            for copy in stage:
                copy.wait_send()

    @pl.when(z < nz - 1)
    def _():
        for copy in sweep_copies(fw_first, fw_in, 1):
            copy.wait_send()

    @pl.when(z > 0)
    def _():
        for copy in sweep_copies(bw_first, bw_in, -1):
            copy.wait_send()

    for put in (put_res, pin5_put, put_orth, put_gram):
        put.wait()


def finish_kernel(
    scale, gram_v, orth_h, res_h, proj_h, res_o, new_o, proj_o, chol_o,
    orth, rows_v, new_v, res_v, proj_v, sem,
):
    get = pltpu.make_async_copy(orth_h, orth, sem.at[0])
    hand_on = [
        (pltpu.make_async_copy(res_h, res_v, sem.at[1]), pltpu.make_async_copy(res_v, res_o, sem.at[2])),
        (pltpu.make_async_copy(proj_h, proj_v, sem.at[3]), pltpu.make_async_copy(proj_v, proj_o, sem.at[4])),
    ]
    get.start()
    for copy, _ in hand_on:
        copy.start()
    cholesky_rows(gram_v[...], rows_v)
    rows = rows_v[...]
    lane64, row64 = iota((RHS, LANES), 1), iota((RHS, LANES), 0)
    upper = jnp.where((lane64 >= row64) & (lane64 < RHS), rows * (1.0 / scale), 0.0)
    inverse = jnp.where(lane64 - RHS <= row64, rows * scale, 0.0)
    hi, lo = split(inverse)
    lhs = jnp.where(lane64 < RHS, pltpu.roll(hi.astype(f32), RHS, 1), lo.astype(f32)).astype(bf16)
    lhs = jnp.concatenate([lhs, lhs], axis=1)
    for copy, onward in hand_on:
        copy.wait()
        onward.start()
    get.wait()

    def finish(q, carry):
        hi, lo = orth[q, :RHS], orth[q, RHS:]
        out = nn(lhs, jnp.concatenate([hi, hi, lo, lo], axis=0))
        for h in range(4):
            new_v[pl.ds(4 * q + h, RHS, stride=SLABS), :] = out[:, h * CZ : (h + 1) * CZ]
        return carry

    lax.fori_loop(0, QUADS, finish, 0)
    put_new = pltpu.make_async_copy(new_v, new_o, sem.at[5])
    put_new.start()
    upper = jnp.concatenate([upper, jnp.zeros((LANES - RHS, LANES), f32)], axis=0)
    chol_o[...] = upper.T[:RHS, :RHS]
    for _, onward in hand_on:
        onward.wait()
    put_new.wait()


def body(
    x_field, right_side, diag_shift, velocity, earlier_blocks, sep_cells, low_inv, low_off, up_off
):
    na, nb, nz = (lax.axis_size(n) for n in ("gx", "gy", "gz"))
    members, slots = nb // 2, na * 2
    group, wide = RHS // members, SEP * members
    depth, half = slots * wide, na * wide
    part_rows = RHS // na
    vecs = earlier_blocks.shape[0] * earlier_blocks.shape[1]
    pw = nb // (part_rows // 8)
    width = vecs // pw
    piece = RHS // nz
    vmem = pltpu.VMEM
    scratch = [
        vmem((ROWS, CZ), f32),
        vmem((ROWS, CZ), f32),
        vmem((SLABS, CZ), f32),
        vmem((3 * SLABS, CZ), f32),
        vmem((vecs * SLABS, CZ), f32),
        vmem((1, SEP), jnp.int32),
        vmem((3, SEP, depth), bf16),
        vmem(((CX + 2) * (CY + 2), RHS, CZ), f32),
        vmem((CX, CY * RHS, CZ), bf16),
        vmem((2, CY * RHS, CZ), bf16),
        vmem((2, CX, RHS, CZ), bf16),
        vmem((2, 16, LANES), bf16),
        vmem((32, LANES), bf16),
        vmem((QUADS, wide, 4 * CZ), bf16),
        vmem((2, na, members, SEP, depth), bf16),
        vmem((wide, depth), bf16),
        vmem((depth, half), bf16),
        vmem((QUADS, RHS, 4 * CZ), f32),
        vmem((QUADS, RHS, 4 * CZ), bf16),
        vmem((QUADS, RHS, 4 * CZ), bf16),
        vmem((QUADS, vecs, 4 * CZ), bf16),
        vmem((QUADS, vecs, 4 * CZ), bf16),
        vmem((2 * vecs, 2 * LANES), f32),
        vmem((RHS, vecs), f32),
        vmem((wide, vecs), bf16),
        vmem((wide, vecs), bf16),
        vmem((members, group, wide), bf16),
        vmem((members, group, wide), bf16),
        vmem((slots, group, wide), bf16),
        vmem((group, wide), f32),
        vmem((na, group, wide), f32),
        vmem((8, half), f32),
        vmem((8, half), f32),
        vmem((2, 16, wide), bf16),
        vmem((na, 8, wide), f32),
        vmem((2, 16, wide), bf16),
        vmem((2, 16, wide), bf16),
        vmem((na * members, 8, wide), f32),
        vmem((na, part_rows, vecs), f32),
        vmem((na, part_rows, vecs), f32),
        vmem((nb, 8, width), f32),
        vmem((nb, 8, width), f32),
        vmem((nz, 8, width), f32),
        vmem((nb, 8, width), f32),
        vmem((na, part_rows, vecs), f32),
        vmem((2 * RHS, vecs), bf16),
        vmem((QUADS, 2 * RHS, 4 * CZ), bf16),
        vmem((nz, piece, LANES), f32),
        vmem((nz, piece, LANES), f32),
        vmem((nb, piece, LANES), f32),
        vmem((na, piece, LANES), f32),
        vmem((nz, piece, LANES), f32),
        pltpu.SemaphoreType.DMA((16,)),
        pltpu.SemaphoreType.DMA((144,)),
        pltpu.SemaphoreType.DMA((144,)),
    ]
    flat = lambda v: v.reshape(-1, CZ)
    anywhere = pl.BlockSpec(memory_space=pl.ANY)
    in_vmem = pl.BlockSpec(memory_space=pltpu.VMEM)
    res, orth, projection, gram = pl.pallas_call(
        functools.partial(kernel, na, nb, nz),
        out_shape=(
            jax.ShapeDtypeStruct((ROWS, CZ), f32),
            jax.ShapeDtypeStruct((QUADS, 2 * RHS, 4 * CZ), bf16),
            jax.ShapeDtypeStruct((na, part_rows, vecs), f32),
            jax.ShapeDtypeStruct((nz, piece, LANES), f32),
        ),
        in_specs=[anywhere] * 9,
        out_specs=(anywhere,) * 4,
        scratch_shapes=scratch,
        compiler_params=pltpu.CompilerParams(
            collective_id=0, has_side_effects=True, vmem_limit_bytes=60 * 2**20
        ),
        cost_estimate=pl.CostEstimate(
            flops=2 * 10**9, bytes_accessed=13 * 2**20, transcendentals=0
        ),
        name="step",
    )(
        flat(x_field), flat(right_side), flat(diag_shift), flat(velocity), flat(earlier_blocks),
        sep_cells, low_inv[0], low_off[0], up_off[0],
    )
    res, new, projection, factor = pl.pallas_call(
        functools.partial(finish_kernel, math.sqrt(na * nb * nz * CX * CY * CZ)),
        out_shape=(
            jax.ShapeDtypeStruct((ROWS, CZ), f32),
            jax.ShapeDtypeStruct((ROWS, CZ), f32),
            jax.ShapeDtypeStruct((RHS, vecs), f32),
            jax.ShapeDtypeStruct((RHS, RHS), f32),
        ),
        in_specs=[in_vmem, anywhere, anywhere, anywhere],
        out_specs=(anywhere, anywhere, anywhere, in_vmem),
        scratch_shapes=[
            vmem((QUADS, 2 * RHS, 4 * CZ), bf16),
            vmem((RHS, LANES), f32),
            vmem((ROWS, CZ), f32),
            vmem((ROWS, CZ), f32),
            vmem((RHS, vecs), f32),
            pltpu.SemaphoreType.DMA((6,)),
        ],
        compiler_params=pltpu.CompilerParams(vmem_limit_bytes=60 * 2**20),
        cost_estimate=pl.CostEstimate(flops=2 * 10**8, bytes_accessed=5 * 2**20, transcendentals=0),
        name="finish",
    )(gram.reshape(RHS, LANES), orth, res, projection.reshape(RHS, vecs))
    shape = right_side.shape
    return (res.reshape(shape), new.reshape(shape), projection.T, factor)


def solution(mesh):
    return jax.shard_map(
        body,
        mesh=mesh,
        in_specs=(
            P(None, "gx", "gy", "gz"),
            P(None, "gx", "gy", "gz"),
            P("gx", "gy", "gz"),
            P(None, "gx", "gy", "gz"),
            P(None, None, "gx", "gy", "gz"),
            P("gz", ("gx", "gy")),
            P("gz", ("gx", "gy"), None),
            P("gz", ("gx", "gy"), None),
            P("gz", ("gx", "gy"), None),
        ),
        out_specs=(P(None, "gx", "gy", "gz"), P(None, "gx", "gy", "gz"), P(), P()),
        check_vma=False,
    )
```

```python
import functools
import math

import jax
import jax.numpy as jnp
from jax import lax
from jax.experimental import pallas as pl
from jax.experimental.pallas import tpu as pltpu
from jax.sharding import PartitionSpec as P

bf16, f32 = jnp.bfloat16, jnp.float32
RHS, CX, CY, CZ, SEP = 64, 4, 8, 128, 32
SLABS = CX * CY
PAIRS = SLABS // 2
QUADS = SLABS // 4
ROWS = RHS * SLABS
LANES = 128


def nt(a, b):
    return lax.dot_general(a, b, (((1,), (1,)), ((), ())), preferred_element_type=f32)


def nn(a, b):
    return jnp.dot(a, b, preferred_element_type=f32)


def split(v):
    hi = v.astype(bf16)
    return hi, (v - hi.astype(f32)).astype(bf16)


def iota(shape, dim):
    return lax.broadcasted_iota(jnp.int32, shape, dim)


def flag(cond):
    return jnp.where(cond, jnp.float32(1.0), jnp.float32(0.0))


def cholesky_rows(gram, out):
    n = RHS
    lane8, row8 = iota((8, LANES), 1), iota((8, LANES), 0)
    blocks = []
    for k in range(n // 8):
        eye = (lane8 - n == row8 + 8 * k).astype(f32)
        blocks.append(jnp.where(lane8 < n, gram[8 * k : 8 * k + 8, :], eye))

    def sublane(v, r):
        return jnp.broadcast_to(v[r : r + 1, :], (8, LANES))

    def panel(turn, blocks):
        first = blocks[0]
        columns = [jnp.broadcast_to(first[:, j : j + 1], (8, LANES)) for j in range(8)]
        entry = {(i, j): sublane(columns[j], i) for j in range(8) for i in range(j, 8)}
        rows = [sublane(first, i) for i in range(8)]
        for j in range(8):
            root = lax.rsqrt(entry[j, j])
            rows[j] = rows[j] * root
            for i in range(j + 1, 8):
                entry[i, j] = entry[i, j] * root
            for i in range(j + 1, 8):
                rows[i] = rows[i] - entry[i, j] * rows[j]
                for k in range(j + 1, i + 1):
                    entry[i, k] = entry[i, k] - entry[i, j] * entry[k, j]
        done = rows[0]
        for i in range(1, 8):
            done = jnp.where(row8 == i, rows[i], done)
        hi = done.astype(bf16).astype(f32)
        mid = (done - hi).astype(bf16).astype(f32)
        low = done - hi - mid
        left = jnp.concatenate([hi, hi, mid, hi, low, mid], axis=0).astype(bf16)
        right = jnp.concatenate([hi, mid, hi, low, hi, mid], axis=0).astype(bf16)
        change = lax.dot_general(
            left, right, (((0,), (0,)), ((), ())), preferred_element_type=f32
        )
        out[pl.ds(pl.multiple_of(turn * 8, 8), 8), :] = pltpu.roll(done, turn * 8, 1)
        rest = [
            pltpu.roll(blocks[k] - change[8 * k : 8 * k + 8], LANES - 8, 1)
            for k in range(1, n // 8)
        ]
        return tuple(rest + [jnp.zeros((8, LANES), f32)])

    lax.fori_loop(0, n // 8, panel, tuple(blocks))


def kernel(
    na, nb, nz,
    x_h, r_h, d_h, v_h, e_h, c_h, li_h, lo_h, up_h,
    res_o, orth_o, proj_o, gram_o,
    x_v, r_v, d_v, v_v, e_v, c_v, m_v,
    xp, xsb, hx, hy, hz, zsend, z_ends, res_b, oh, gath, gath_in, gath_t,
    w0, wh, wl, vh, vl, eacc, pacc, vsh, vsl,
    sep_loc, sep_hop, sep_all, base_loc, base_in, base, state, stateb, tiles, fw_in, bw_in, ret,
    psend, pin1, psum1, pin2, pin3, pin4, pin5, pt_hl,
    orth, g_loc, gin1, gin2, gin3, gin4,
    loc_sem, send_sem, recv_sem,
):
    a, b, z = lax.axis_index("gx"), lax.axis_index("gy"), lax.axis_index("gz")
    size = {"gx": na, "gy": nb, "gz": nz}
    pos = {"gx": a, "gy": b, "gz": z}
    members, slots = nb // 2, na * 2
    member, core = b // 2, lax.rem(b, 2)
    slot = core * na + a
    group = RHS // members
    wide = SEP * members
    depth = slots * wide
    half = na * wide
    count = [0]
    sent = []

    def place(axis, index):
        if axis == "member":
            return (a, index * 2 + core, z)
        if axis == "slot":
            return (lax.rem(index, na), member * 2 + index // na, z)
        at = dict(pos)
        at[axis] = index
        return (at["gx"], at["gy"], at["gz"])

    size["member"], size["slot"] = members, slots
    pos_of = dict(pos, member=member, slot=slot)

    def remote(n, src, dst, where):
        return pltpu.make_async_remote_copy(
            src_ref=src, dst_ref=dst, send_sem=send_sem.at[n], recv_sem=recv_sem.at[n],
            device_id=where, device_id_type=pl.DeviceIdType.MESH,
        )

    def send(src, dst, where):
        copy = remote(count[0], src, dst, where)
        count[0] += 1
        copy.start()
        sent.append(copy.wait_send)
        return copy

    def exchange(pairs, dst):
        n = count[0]
        count[0] += 1
        for src, there, where in pairs:
            remote(n, src, there, where).start()
        whole = dst.at[pl.ds(0, len(pairs))]
        out = pltpu.make_async_copy(whole, whole, send_sem.at[n])
        sent.append(out.wait)
        return pltpu.make_async_copy(whole, whole, recv_sem.at[n])

    def share(axis, src_of, dst):
        n = size[axis]
        others = [lax.rem(pos_of[axis] + d, n) for d in range(1, n)]
        there = dst.at[pos_of[axis]]
        return exchange([(src_of(to), there, place(axis, to)) for to in others], dst)

    def arrive(copies):
        for copy in copies:
            copy.wait_recv()

    barrier = pltpu.get_barrier_semaphore()
    partners = 0

    def greet(where):
        pl.semaphore_signal(
            barrier, inc=1, device_id=where, device_id_type=pl.DeviceIdType.MESH
        )

    for axis in ("gy", "gz"):
        for d in range(1, size[axis]):
            greet(place(axis, lax.rem(pos[axis] + d, size[axis])))
            partners += 1
    for d in range(1, na):
        for e in range(members):
            greet((lax.rem(a + d, na), lax.rem(member + e, members) * 2 + core, z))
            partners += 1
        greet((lax.rem(a + d, na), member * 2 + 1 - core, z))
        partners += 1

    def fetch(n, src, dst):
        copy = pltpu.make_async_copy(src, dst, loc_sem.at[n])
        copy.start()
        return copy

    x_order = (0, CX - 1) + tuple(range(1, CX - 1))
    get_x = {cx: fetch((0, 16, 17, 18)[cx], x_h.at[:, cx], x_v.at[cx]) for cx in x_order}
    get_m = [fetch(1 + i, h, m_v.at[i]) for i, h in enumerate((li_h, lo_h, up_h))]
    get_c = fetch(4, c_h, c_v)
    get_d = fetch(5, d_h, d_v)
    get_v = fetch(6, v_h, v_v)
    get_r = fetch(7, r_h, r_v)
    chunk = e_v.shape[0] // 4
    get_e = [
        fetch((8, 13, 14, 15)[i], e_h.at[pl.ds(i * chunk, chunk)], e_v.at[pl.ds(i * chunk, chunk)])
        for i in range(4)
    ]

    def slab(ref, s, n=RHS):
        return ref[pl.ds(s, n, stride=SLABS), :]

    def rows_at(start, n):
        return pl.ds(pl.multiple_of(start, n), n)

    pad = CY + 2
    q32, lane_all = iota((32, PAIRS * LANES), 0), iota((32, PAIRS * LANES), 1)
    turn_all, l_all = lane_all // LANES, lax.rem(lane_all, LANES)
    pick = ((q32 == turn_all) & (l_all == CZ - 1)) | ((q32 == 16 + turn_all) & (l_all == 0))
    pick = pick.astype(bf16)

    def spread_x(cx):
        get_x[cx].wait()
        rows = x_v.at[cx].reshape(RHS * CY, CZ)
        for cy in range(CY):
            v = rows[pl.ds(cy, RHS, stride=CY), :]
            xp[(cx + 1) * pad + cy + 1] = v
            xsb[cx, cy * RHS : (cy + 1) * RHS, :] = v.astype(bf16)

    def ring(axis, step):
        n = size[axis]
        return place(axis, lax.rem(pos_of[axis] + step + n, n))

    spread_x(x_order[0])
    spread_x(x_order[1])
    pl.semaphore_wait(barrier, partners)
    halo = [
        send(xsb.at[CX - 1], hx.at[0], ring("gx", 1)),
        send(xsb.at[0], hx.at[1], ring("gx", -1)),
    ]
    for cx in x_order[2:]:
        spread_x(cx)
    halo += [
        send(xsb.at[:, pl.ds((CY - 1) * RHS, RHS)], hy.at[0], ring("gy", 1)),
        send(xsb.at[:, pl.ds(0, RHS)], hy.at[1], ring("gy", -1)),
    ]
    rows = jnp.concatenate(
        [xsb[p // 4, (p % 4) * LANES : (p % 4 + 1) * LANES, :] for p in range(PAIRS)], axis=1
    )
    zsend[...] = nt(pick, rows).astype(bf16)
    halo += [
        send(zsend.at[pl.ds(0, 16)], hz.at[0], ring("gz", 1)),
        send(zsend.at[pl.ds(16, 16)], hz.at[1], ring("gz", -1)),
    ]

    mine = rows_at(member * SEP, SEP)
    lane_group = iota((SEP, LANES), 1) // SEP
    per_tile = LANES // SEP
    for i in range(3):
        get_m[i].wait()

    def reorder(i):
        pieces = [
            m_v[i, :, t * LANES : (t + 1) * LANES].astype(f32) for t in range(depth // LANES)
        ]
        for t in range(depth // LANES):
            out = jnp.zeros((SEP, LANES), f32)
            for g in range(per_tile):
                old = (t % na) * nb + g * 2 + t // na
                piece = pieces[old // per_tile]
                shift = ((g - old % per_tile) * SEP) % LANES
                if shift:
                    piece = pltpu.roll(piece, shift, 1)
                out = jnp.where(lane_group == g, piece, out)
            at = slice(t * LANES, (t + 1) * LANES)
            if i == 0:
                gath_in[mine, at] = out.astype(bf16)
            else:
                gath[i - 1, a, member, :, at] = out.astype(bf16)

    for i in range(3):
        reorder(i)

    axes = ("member", "gx")

    def own(m, c):
        return gath.at[m, a, member, :, pl.ds(c * half, half)]

    def near(m, c, axis, step, part):
        at = ring_index(axis, step)
        rows = pl.ds(part * (SEP // 2), SEP // 2)
        if axis == "member":
            return gath.at[m, a, at, rows, pl.ds(c * half, half)]
        return gath.at[m, at, member, rows, pl.ds(c * half, half)]

    def line(m, c, axis, step):
        at = ring_index(axis, step)
        if axis == "member":
            return gath.at[m, :, at, :, pl.ds(c * half, half)]
        return gath.at[m, at, :, :, pl.ds(c * half, half)]

    def near_line(m, c, axis, step, part):
        at = ring_index(axis, step)
        cut = pl.ds(part * 2, 2)
        if axis == "member":
            return gath.at[m, cut, at, :, pl.ds(c * half, half)]
        return gath.at[m, at, cut, :, pl.ds(c * half, half)]

    def ring_index(axis, step):
        return lax.rem(pos_of[axis] + step + size[axis], size[axis])

    def later(src, where):
        copy = remote(count[0], src, src, where)
        count[0] += 1
        return copy

    def ring_pair(block, axis):
        return [later(block, ring(axis, step)) for step in (1, -1)]

    def gather_stages(m):
        one, two, three, four = [], [], [], []
        for c in range(2):
            first, second = axes[c], axes[1 - c]
            one += ring_pair(own(m, c), first)
            three += ring_pair(line(m, c, second, 0), second)
            for part, step in enumerate((1, -1)):
                two.append(later(near(m, c, first, -step, part), ring(first, step)))
                four.append(later(near_line(m, c, second, -step, part), ring(second, step)))
        return one, two, three, four

    def launch(copies):
        for copy in copies:
            copy.start()

    def relay(came, onward):
        for got, copy in zip(came, onward):
            got.wait_recv()
            copy.start()

    low_stages, up_stages = gather_stages(0), gather_stages(1)
    use_low, use_up = z > 0, z < nz - 1
    up_after = z < (nz * 5) // 8
    up_before = jnp.logical_and(use_up, jnp.logical_not(up_after))
    pl.when(use_low)(lambda: launch(low_stages[0]))
    gather_base = [
        send(gath_in.at[mine], gath_in.at[mine], place("member", lax.rem(member + d, members)))
        for d in range(1, members)
    ]

    get_c.wait()
    cells = jnp.broadcast_to(c_v[...], (SEP, SEP)).astype(f32)
    square = iota((SEP, SEP), 0) == iota((SEP, SEP), 1)
    column = jnp.sum(jnp.where(square, cells, 0.0), axis=1, keepdims=True)
    column = jnp.broadcast_to(column, (SEP, 4 * CZ))
    z512 = iota((SEP, 4 * CZ), 1)

    def mark(q, carry):
        oh[q] = jnp.zeros((wide, 4 * CZ), bf16)
        at = (z512 + q * 4 * CZ).astype(f32)
        oh[q, mine, :] = jnp.where(column == at, 1.0, 0.0).astype(bf16)
        return carry

    lax.fori_loop(0, QUADS, mark, 0)

    vecs = e_v.shape[0] // SLABS
    part_vecs = vecs // 4

    def relayout(c):
        get_e[c].wait()
        at = slice(c * part_vecs, (c + 1) * part_vecs)

        def step(q, carry):
            for h in range(4):
                rows = pl.ds(c * chunk + 4 * q + h, part_vecs, stride=SLABS)
                hi, lo = split(e_v[rows, :])
                vh[q, at, h * CZ : (h + 1) * CZ] = hi
                vl[q, at, h * CZ : (h + 1) * CZ] = lo
            return carry

        lax.fori_loop(0, QUADS, step, 0)

    split_early = z >= 2
    pl.when(split_early)(lambda: relayout(0))
    get_d.wait()
    get_v.wait()
    get_r.wait()
    pl.when(use_low)(lambda: relay(low_stages[0], low_stages[1]))
    arrive(halo)

    @pl.when(use_low)
    def _():
        arrive(low_stages[1])
        launch(low_stages[2])

    before_z = hz[0].astype(f32) * flag(z > 0)
    after_z = hz[1].astype(f32) * flag(z < nz - 1)
    ends = jnp.concatenate(
        [before_z, after_z, jnp.zeros((LANES - 32, LANES), f32)], axis=0
    ).T.astype(bf16)
    for k, mask in enumerate((flag(a > 0), flag(a < na - 1))):
        for cy in range(CY):
            xp[k * (CX + 1) * pad + cy + 1] = (
                hx[k, cy * RHS : (cy + 1) * RHS, :].astype(f32) * mask
            )
    for k, mask in enumerate((flag(b > 0), flag(b < nb - 1))):
        for cx in range(CX):
            xp[(cx + 1) * pad + k * (CY + 1)] = hy[k, cx].astype(f32) * mask
    q128, lane_all = iota((LANES, PAIRS * LANES), 0), iota((LANES, PAIRS * LANES), 1)
    turn_all, l_all = lane_all // LANES, lax.rem(lane_all, LANES)
    spread = ((q128 == turn_all) & (l_all == 0)) | ((q128 == 16 + turn_all) & (l_all == CZ - 1))
    z_ends[...] = nn(ends, spread.astype(bf16))
    lane64 = iota((RHS, LANES), 1)

    def residual_of(q, carry):
        for h in range(4):
            s = 4 * q + h
            i = (q // 2 + 1) * pad + lax.rem(q, 2) * 4 + h + 1
            x = xp[i]
            diag = 6.0 + d_v[pl.ds(s, 1), :]
            v0, v1, v2 = (v_v[pl.ds(k * SLABS + s, 1), :] for k in range(3))
            end = z_ends[(h % 2) * RHS : (h % 2 + 1) * RHS, rows_at((2 * q + h // 2) * LANES, LANES)]
            before = jnp.where(lane64 == 0, end, pltpu.roll(x, 1, 1))
            after = jnp.where(lane64 == CZ - 1, end, pltpu.roll(x, CZ - 1, 1))
            res = slab(r_v, s) - diag * x
            res = res + (1.0 + v0) * xp[i - pad] + (1.0 - v0) * xp[i + pad]
            res = res + (1.0 + v1) * xp[i - 1] + (1.0 - v1) * xp[i + 1]
            res = res + (1.0 + v2) * before + (1.0 - v2) * after
            r_v[pl.ds(s, RHS, stride=SLABS), :] = res
            at = slice(h * CZ, (h + 1) * CZ)
            res_b[q, :, at] = res.astype(bf16)
            w = res * (1.0 / diag)
            hi, lo = split(w)
            w0[q, :, at] = w
            wh[q, :, at] = hi
            wl[q, :, at] = lo
        return carry

    lax.fori_loop(0, QUADS, residual_of, 0)
    seps = nt(
        jnp.concatenate([res_b[q] for q in range(QUADS)], axis=1),
        jnp.concatenate([oh[q] for q in range(QUADS)], axis=1),
    )
    put_res = pltpu.make_async_copy(r_v, res_o, loc_sem.at[9])
    put_res.start()

    sep_loc[...] = seps.astype(bf16).reshape(members, group, wide)
    hop = share("member", lambda to: sep_loc.at[to], sep_hop)
    sep_hop[member] = sep_loc[member]
    pl.when(split_early)(lambda: relayout(1))
    hop.wait()
    mixed = sep_hop[0].astype(f32)
    for i in range(1, members):
        mixed = mixed + sep_hop[i].astype(f32)
    sep_all[slot] = mixed.astype(bf16)
    hop = share("slot", lambda to: sep_all.at[slot], sep_all)
    pl.when(split_early)(lambda: relayout(2))
    pl.when(use_low)(lambda: relay(low_stages[2], low_stages[3]))
    arrive(gather_base)
    hop.wait()

    row8 = iota((8, LANES), 0)
    base_loc[...] = nt(jnp.concatenate([sep_all[i] for i in range(slots)], axis=1), gath_in[...])
    hop = share("gx", lambda to: base_loc, base_in)
    base_in[a] = base_loc[...]
    pl.when(split_early)(lambda: relayout(3))
    hop.wait()
    gx_here = jnp.zeros((8, LANES), jnp.int32) + a
    for j in range(na):
        both = base_in[j]
        v = jnp.where(gx_here >= 2, both[8:], both[:8])
        v = jnp.where(lax.rem(gx_here, 2) == 1, pltpu.roll(v, 4, 0), v)
        base[:, j * wide : (j + 1) * wide] = jnp.where(row8 < 4, v, pltpu.roll(v, 4, 0))

    eacc[...] = jnp.zeros(eacc.shape, f32)

    def earlier_product(q, carry):
        right = jnp.concatenate([wh[q], wl[q], oh[q]], axis=0)
        eacc[:vecs] += nt(vh[q], right)
        eacc[vecs:] += nt(vl[q], right)
        return carry

    def earlier_results():
        main = eacc[:vecs, :LANES] + eacc[vecs:, :LANES]
        main = main.T
        pacc[...] = main[:RHS] + main[RHS:]
        vsh[...] = eacc[:vecs, LANES:].T.astype(bf16)
        vsl[...] = eacc[vecs:, LANES:].T.astype(bf16)

    turns = (QUADS * z) // (2 * (nz - 1) - z)

    def sweep_copies(first, dst, step):
        return [
            remote(
                first + d, stateb.at[0 if step > 0 else 1], dst.at[core],
                (a, member * 2 + lax.rem(core + d, 2), z + step),
            )
            for d in range(2)
        ]

    def sweep_push(first, dst, step):
        v = state[...]
        t = [v[:, j * wide : (j + 1) * wide] for j in range(na)]
        packed = jnp.concatenate(
            [jnp.where(row8 < 4, t[0], t[1]), jnp.where(row8 < 4, t[2], t[3])], axis=0
        )
        stateb[0 if step > 0 else 1] = packed.astype(bf16)
        for copy in sweep_copies(first, dst, step):
            copy.start()

    row_group = iota((16, LANES), 0) // 4

    def product_of(first, dst, step):
        arrive(sweep_copies(first, dst, step))
        left = []
        for i in range(2):
            v = dst[i].astype(f32)
            left += [jnp.where(row_group == j, v, 0.0).astype(bf16) for j in range(na)]
        out = nn(jnp.concatenate(left, axis=1), gath_t[...])
        out = out[:8] + out[8:]
        return out + pltpu.roll(out, 4, 0)

    def transpose_matrix(m):
        def step(t, carry):
            at = rows_at(t * LANES, LANES)
            block = gath[m, :, :, :, at].reshape(half, LANES)
            gath_t[at, :] = block.astype(f32).T.astype(bf16)
            return carry

        lax.fori_loop(0, depth // LANES, step, 0)

    fw_first = count[0]
    bw_first = fw_first + 2
    count[0] = bw_first + 2

    @pl.when(up_before)
    def _():
        launch(up_stages[0])
        relay(up_stages[0], up_stages[1])
        arrive(up_stages[1])
        launch(up_stages[2])

    @pl.when(use_low)
    def _():
        arrive(low_stages[3])
        transpose_matrix(0)

    lax.fori_loop(0, turns, earlier_product, 0)
    pl.when(z == nz - 1)(earlier_results)
    pl.when(up_before)(lambda: relay(up_stages[2], up_stages[3]))

    @pl.when(z == 0)
    def _():
        state[...] = base[...]

    @pl.when(z > 0)
    def _():
        state[...] = base[...] - product_of(fw_first, fw_in, 1)

    @pl.when(z < nz - 1)
    def _():
        sweep_push(fw_first, fw_in, 1)

    pl.when(up_after)(lambda: launch(up_stages[0]))

    @pl.when(jnp.logical_not(split_early))
    def _():
        for c in range(4):
            relayout(c)

    half_way = (turns + QUADS) // 2
    lax.fori_loop(turns, half_way, earlier_product, 0)

    @pl.when(up_after)
    def _():
        relay(up_stages[0], up_stages[1])
        arrive(up_stages[1])
        launch(up_stages[2])

    lax.fori_loop(half_way, QUADS, earlier_product, 0)
    pl.when(z < nz - 1)(earlier_results)
    pl.when(up_after)(lambda: relay(up_stages[2], up_stages[3]))

    @pl.when(z < nz - 1)
    def _():
        arrive(up_stages[3])
        transpose_matrix(1)
        state[...] = state[...] - product_of(bw_first, bw_in, -1)

    @pl.when(z > 0)
    def _():
        sweep_push(bw_first, bw_in, -1)

    for j in range(na):
        tiles[j] = state[:, j * wide : (j + 1) * wide]
    here = member * na + a
    pairs = []
    for d in range(na):
        for e in range(members):
            if d or e:
                to, far = lax.rem(a + d, na), lax.rem(member + e, members)
                pairs.append((tiles.at[to], ret.at[here], (to, far * 2 + core, z)))
    hop = exchange(pairs, ret)
    ret[here] = tiles[a]
    hop.wait()
    sol = jnp.concatenate(
        [jnp.where(row8 < 4, ret[2 * i], ret[2 * i + 1]) for i in range(na * members // 2)], axis=0
    )
    sol_h, sol_l = split(sol)
    corr = nn(jnp.concatenate([sol_h, sol_l], axis=0), vsh[...])
    corr = pacc[...] + corr[:RHS] + corr[RHS:] + nn(sol_h, vsl[...])
    cols = vecs

    part_rows = RHS // na
    psend[...] = corr.reshape(na, part_rows, cols)
    hop = share("gx", lambda to: psend.at[to], pin1)
    pin1[a] = psend[a]

    sol_hl = jnp.concatenate([sol_h, sol_l], axis=1)

    def add_sol(first):
        twice = jnp.concatenate([oh[first], oh[first + 1]], axis=1)
        change = nn(sol_hl, jnp.concatenate([twice, twice], axis=0))
        w0[first] = w0[first] + change[:, : 4 * CZ]
        w0[first + 1] = w0[first + 1] + change[:, 4 * CZ :]

    add_sol(0)

    def total_of(ref, n):
        out = ref[0]
        for i in range(1, n):
            out = out + ref[i]
        return out

    hop.wait()
    part = total_of(pin1, na)
    ph = part_rows // 8
    pw = nb // ph
    width = cols // pw
    for i in range(nb):
        r, c = divmod(i, pw)
        psum1[i] = part[r * 8 : r * 8 + 8, c * width : (c + 1) * width]
    hop = share("gy", lambda to: psum1.at[to], pin2)
    pin2[b] = psum1[b]
    add_sol(2)
    hop.wait()
    pin3[z] = total_of(pin2, nb)
    share("gz", lambda to: pin3.at[z], pin3).wait()
    pin4[b] = total_of(pin3, nz)
    hop = share("gy", lambda to: pin4.at[b], pin4)
    add_sol(4)
    hop.wait()
    pin5[a] = jnp.concatenate(
        [jnp.concatenate([pin4[r * pw + c] for c in range(pw)], axis=1) for r in range(ph)], axis=0
    )
    hop = share("gx", lambda to: pin5.at[a], pin5)
    add_sol(6)
    hop.wait()
    full = pin5[...].reshape(RHS, cols)
    pin5_put = pltpu.make_async_copy(pin5, proj_o, loc_sem.at[10])
    pin5_put.start()
    hi, lo = split(full)
    pt_hl[:RHS] = hi
    pt_hl[RHS:] = lo

    def project(i, gram):
        for q in (2 * i, 2 * i + 1):
            main = nn(pt_hl[...], vh[q])
            o = w0[q] - (main[:RHS] + main[RHS:] + nn(pt_hl[:RHS], vl[q]))
            hi, lo = split(o)
            both = jnp.concatenate([hi, lo], axis=0)
            orth[q] = both
            gram = gram + nt(both, both)
        return gram

    gram = lax.fori_loop(0, QUADS // 2, project, jnp.zeros((2 * RHS, 2 * RHS), f32))
    gram = gram[:RHS] + gram[RHS:]
    gram = gram + pltpu.roll(gram, RHS, 1)
    put_orth = pltpu.make_async_copy(orth, orth_o, loc_sem.at[11])
    put_orth.start()
    piece = RHS // nz
    g_loc[...] = gram.reshape(nz, piece, LANES)
    hop = share("gz", lambda to: g_loc.at[to], gin1)
    gin1[z] = g_loc[z]
    for wait in sent[:-1]:
        wait()
    del sent[:-1]

    @pl.when(use_low)
    def _():
        for stage in low_stages:
            for copy in stage:
                copy.wait_send()

    @pl.when(use_up)
    def _():
        for stage in up_stages:
            for copy in stage:
                copy.wait_send()

    @pl.when(z < nz - 1)
    def _():
        for copy in sweep_copies(fw_first, fw_in, 1):
            copy.wait_send()

    @pl.when(z > 0)
    def _():
        for copy in sweep_copies(bw_first, bw_in, -1):
            copy.wait_send()

    hop.wait()
    gin2[b] = total_of(gin1, nz)
    share("gy", lambda to: gin2.at[b], gin2).wait()
    gin3[a] = total_of(gin2, nb)
    share("gx", lambda to: gin3.at[a], gin3).wait()
    gin4[z] = total_of(gin3, na)
    share("gz", lambda to: gin4.at[z], gin4).wait()

    put_gram = pltpu.make_async_copy(gin4, gram_o, loc_sem.at[12])
    put_gram.start()
    for wait in sent:
        wait()
    for put in (put_res, pin5_put, put_orth, put_gram):
        put.wait()


def finish_kernel(
    scale, gram_v, orth_h, res_h, proj_h, res_o, new_o, proj_o, chol_o,
    orth, rows_v, new_v, res_v, proj_v, sem,
):
    get = pltpu.make_async_copy(orth_h, orth, sem.at[0])
    hand_on = [
        (pltpu.make_async_copy(res_h, res_v, sem.at[1]), pltpu.make_async_copy(res_v, res_o, sem.at[2])),
        (pltpu.make_async_copy(proj_h, proj_v, sem.at[3]), pltpu.make_async_copy(proj_v, proj_o, sem.at[4])),
    ]
    get.start()
    for copy, _ in hand_on:
        copy.start()
    cholesky_rows(gram_v[...], rows_v)
    rows = rows_v[...]
    lane64, row64 = iota((RHS, LANES), 1), iota((RHS, LANES), 0)
    upper = jnp.where((lane64 >= row64) & (lane64 < RHS), rows * (1.0 / scale), 0.0)
    inverse = jnp.where(lane64 - RHS <= row64, rows * scale, 0.0)
    hi, lo = split(inverse)
    lhs = jnp.where(lane64 < RHS, pltpu.roll(hi.astype(f32), RHS, 1), lo.astype(f32)).astype(bf16)
    lhs = jnp.concatenate([lhs, lhs], axis=1)
    for copy, onward in hand_on:
        copy.wait()
        onward.start()
    get.wait()

    def finish(q, carry):
        hi, lo = orth[q, :RHS], orth[q, RHS:]
        out = nn(lhs, jnp.concatenate([hi, hi, lo, lo], axis=0))
        for h in range(4):
            new_v[pl.ds(4 * q + h, RHS, stride=SLABS), :] = out[:, h * CZ : (h + 1) * CZ]
        return carry

    lax.fori_loop(0, QUADS, finish, 0, unroll=4)
    put_new = pltpu.make_async_copy(new_v, new_o, sem.at[5])
    put_new.start()
    upper = jnp.concatenate([upper, jnp.zeros((LANES - RHS, LANES), f32)], axis=0)
    chol_o[...] = upper.T[:RHS, :RHS]
    for _, onward in hand_on:
        onward.wait()
    put_new.wait()


def body(
    x_field, right_side, diag_shift, velocity, earlier_blocks, sep_cells, low_inv, low_off, up_off
):
    na, nb, nz = (lax.axis_size(n) for n in ("gx", "gy", "gz"))
    members, slots = nb // 2, na * 2
    group, wide = RHS // members, SEP * members
    depth, half = slots * wide, na * wide
    part_rows = RHS // na
    vecs = earlier_blocks.shape[0] * earlier_blocks.shape[1]
    pw = nb // (part_rows // 8)
    width = vecs // pw
    piece = RHS // nz
    vmem = pltpu.VMEM
    scratch = [
        vmem((CX, RHS, CY, CZ), f32),
        vmem((ROWS, CZ), f32),
        vmem((SLABS, CZ), f32),
        vmem((3 * SLABS, CZ), f32),
        vmem((vecs * SLABS, CZ), f32),
        vmem((1, SEP), jnp.int32),
        vmem((3, SEP, depth), bf16),
        vmem(((CX + 2) * (CY + 2), RHS, CZ), f32),
        vmem((CX, CY * RHS, CZ), bf16),
        vmem((2, CY * RHS, CZ), bf16),
        vmem((2, CX, RHS, CZ), bf16),
        vmem((2, 16, LANES), bf16),
        vmem((32, LANES), bf16),
        vmem((LANES, PAIRS * LANES), f32),
        vmem((QUADS, RHS, 4 * CZ), bf16),
        vmem((QUADS, wide, 4 * CZ), bf16),
        vmem((2, na, members, SEP, depth), bf16),
        vmem((wide, depth), bf16),
        vmem((depth, half), bf16),
        vmem((QUADS, RHS, 4 * CZ), f32),
        vmem((QUADS, RHS, 4 * CZ), bf16),
        vmem((QUADS, RHS, 4 * CZ), bf16),
        vmem((QUADS, vecs, 4 * CZ), bf16),
        vmem((QUADS, vecs, 4 * CZ), bf16),
        vmem((2 * vecs, 2 * LANES), f32),
        vmem((RHS, vecs), f32),
        vmem((wide, vecs), bf16),
        vmem((wide, vecs), bf16),
        vmem((members, group, wide), bf16),
        vmem((members, group, wide), bf16),
        vmem((slots, group, wide), bf16),
        vmem((group, wide), f32),
        vmem((na, group, wide), f32),
        vmem((8, half), f32),
        vmem((8, half), f32),
        vmem((2, 16, wide), bf16),
        vmem((na, 8, wide), f32),
        vmem((2, 16, wide), bf16),
        vmem((2, 16, wide), bf16),
        vmem((na * members, 8, wide), f32),
        vmem((na, part_rows, vecs), f32),
        vmem((na, part_rows, vecs), f32),
        vmem((nb, 8, width), f32),
        vmem((nb, 8, width), f32),
        vmem((nz, 8, width), f32),
        vmem((nb, 8, width), f32),
        vmem((na, part_rows, vecs), f32),
        vmem((2 * RHS, vecs), bf16),
        vmem((QUADS, 2 * RHS, 4 * CZ), bf16),
        vmem((nz, piece, LANES), f32),
        vmem((nz, piece, LANES), f32),
        vmem((nb, piece, LANES), f32),
        vmem((na, piece, LANES), f32),
        vmem((nz, piece, LANES), f32),
        pltpu.SemaphoreType.DMA((19,)),
        pltpu.SemaphoreType.DMA((144,)),
        pltpu.SemaphoreType.DMA((144,)),
    ]
    flat = lambda v: v.reshape(-1, CZ)
    anywhere = pl.BlockSpec(memory_space=pl.ANY)
    in_vmem = pl.BlockSpec(memory_space=pltpu.VMEM)
    res, orth, projection, gram = pl.pallas_call(
        functools.partial(kernel, na, nb, nz),
        out_shape=(
            jax.ShapeDtypeStruct((ROWS, CZ), f32),
            jax.ShapeDtypeStruct((QUADS, 2 * RHS, 4 * CZ), bf16),
            jax.ShapeDtypeStruct((na, part_rows, vecs), f32),
            jax.ShapeDtypeStruct((nz, piece, LANES), f32),
        ),
        in_specs=[anywhere] * 9,
        out_specs=(anywhere,) * 4,
        scratch_shapes=scratch,
        compiler_params=pltpu.CompilerParams(
            collective_id=0, has_side_effects=True, vmem_limit_bytes=60 * 2**20
        ),
        cost_estimate=pl.CostEstimate(
            flops=2 * 10**9, bytes_accessed=13 * 2**20, transcendentals=0
        ),
        name="step",
    )(
        x_field, flat(right_side), flat(diag_shift), flat(velocity), flat(earlier_blocks),
        sep_cells, low_inv[0], low_off[0], up_off[0],
    )
    res, new, projection, factor = pl.pallas_call(
        functools.partial(finish_kernel, math.sqrt(na * nb * nz * CX * CY * CZ)),
        out_shape=(
            jax.ShapeDtypeStruct((ROWS, CZ), f32),
            jax.ShapeDtypeStruct((ROWS, CZ), f32),
            jax.ShapeDtypeStruct((RHS, vecs), f32),
            jax.ShapeDtypeStruct((RHS, RHS), f32),
        ),
        in_specs=[in_vmem, anywhere, anywhere, anywhere],
        out_specs=(anywhere, anywhere, anywhere, in_vmem),
        scratch_shapes=[
            vmem((QUADS, 2 * RHS, 4 * CZ), bf16),
            vmem((RHS, LANES), f32),
            vmem((ROWS, CZ), f32),
            vmem((ROWS, CZ), f32),
            vmem((RHS, vecs), f32),
            pltpu.SemaphoreType.DMA((6,)),
        ],
        compiler_params=pltpu.CompilerParams(vmem_limit_bytes=60 * 2**20),
        cost_estimate=pl.CostEstimate(flops=2 * 10**8, bytes_accessed=5 * 2**20, transcendentals=0),
        name="finish",
    )(gram.reshape(RHS, LANES), orth, res, projection.reshape(RHS, vecs))
    shape = right_side.shape
    return (res.reshape(shape), new.reshape(shape), projection.T, factor)


def solution(mesh):
    return jax.shard_map(
        body,
        mesh=mesh,
        in_specs=(
            P(None, "gx", "gy", "gz"),
            P(None, "gx", "gy", "gz"),
            P("gx", "gy", "gz"),
            P(None, "gx", "gy", "gz"),
            P(None, None, "gx", "gy", "gz"),
            P("gz", ("gx", "gy")),
            P("gz", ("gx", "gy"), None),
            P("gz", ("gx", "gy"), None),
            P("gz", ("gx", "gy"), None),
        ),
        out_specs=(P(None, "gx", "gy", "gz"), P(None, "gx", "gy", "gz"), P(), P()),
        check_vma=False,
    )
```

```python
import functools
import math

import jax
import jax.numpy as jnp
from jax import lax
from jax.experimental import pallas as pl
from jax.experimental.pallas import tpu as pltpu
from jax.sharding import PartitionSpec as P

bf16, f32 = jnp.bfloat16, jnp.float32
RHS, CX, CY, CZ, SEP = 64, 4, 8, 128, 32
SLABS = CX * CY
PAIRS = SLABS // 2
QUADS = SLABS // 4
ROWS = RHS * SLABS
LANES = 128


def nt(a, b):
    return lax.dot_general(a, b, (((1,), (1,)), ((), ())), preferred_element_type=f32)


def nn(a, b):
    return jnp.dot(a, b, preferred_element_type=f32)


def split(v):
    hi = v.astype(bf16)
    return hi, (v - hi.astype(f32)).astype(bf16)


def iota(shape, dim):
    return lax.broadcasted_iota(jnp.int32, shape, dim)


def flag(cond):
    return jnp.where(cond, jnp.float32(1.0), jnp.float32(0.0))


def cholesky_rows(gram, out):
    n = RHS
    lane8, row8 = iota((8, LANES), 1), iota((8, LANES), 0)
    blocks = []
    for k in range(n // 8):
        eye = (lane8 - n == row8 + 8 * k).astype(f32)
        blocks.append(jnp.where(lane8 < n, gram[8 * k : 8 * k + 8, :], eye))

    def sublane(v, r):
        return jnp.broadcast_to(v[r : r + 1, :], (8, LANES))

    def panel(turn, blocks):
        first = blocks[0]
        columns = [jnp.broadcast_to(first[:, j : j + 1], (8, LANES)) for j in range(8)]
        entry = {(i, j): sublane(columns[j], i) for j in range(8) for i in range(j, 8)}
        rows = [sublane(first, i) for i in range(8)]
        for j in range(8):
            root = lax.rsqrt(entry[j, j])
            rows[j] = rows[j] * root
            for i in range(j + 1, 8):
                entry[i, j] = entry[i, j] * root
            for i in range(j + 1, 8):
                rows[i] = rows[i] - entry[i, j] * rows[j]
                for k in range(j + 1, i + 1):
                    entry[i, k] = entry[i, k] - entry[i, j] * entry[k, j]
        done = rows[0]
        for i in range(1, 8):
            done = jnp.where(row8 == i, rows[i], done)
        hi = done.astype(bf16).astype(f32)
        mid = (done - hi).astype(bf16).astype(f32)
        low = done - hi - mid
        left = jnp.concatenate([hi, hi, mid, hi, low, mid], axis=0).astype(bf16)
        right = jnp.concatenate([hi, mid, hi, low, hi, mid], axis=0).astype(bf16)
        change = lax.dot_general(
            left, right, (((0,), (0,)), ((), ())), preferred_element_type=f32
        )
        out[pl.ds(pl.multiple_of(turn * 8, 8), 8), :] = pltpu.roll(done, turn * 8, 1)
        rest = [
            pltpu.roll(blocks[k] - change[8 * k : 8 * k + 8], LANES - 8, 1)
            for k in range(1, n // 8)
        ]
        return tuple(rest + [jnp.zeros((8, LANES), f32)])

    lax.fori_loop(0, n // 8, panel, tuple(blocks))


def kernel(
    na, nb, nz,
    x_h, r_h, d_h, v_h, e_h, c_h, li_h, lo_h, up_h,
    res_o, orth_o, proj_o, gram_o,
    x_v, r_v, d_v, v_v, e_v, c_v, m_v,
    xp, xsb, hx, hy, hz, zsend, z_ends, res_b, oh, gath, gath_t,
    w0, wh, wl, vh, vl, eacc,
    sep_loc, sep_in, base, state, stateb, tiles, fw_in, bw_in, ret,
    psend, pin, fin, full_in, pt_v, pt_hl,
    orth, g_loc, gin1, gin2, gin3,
    loc_sem, send_sem, recv_sem,
):
    a, b, z = lax.axis_index("gx"), lax.axis_index("gy"), lax.axis_index("gz")
    size = {"gx": na, "gy": nb, "gz": nz}
    pos = {"gx": a, "gy": b, "gz": z}
    members, slots = nb // 2, na * 2
    member, core = b // 2, lax.rem(b, 2)
    slot = core * na + a
    group = RHS // members
    wide = SEP * members
    depth = slots * wide
    half = na * wide
    count = [0]
    sent = []

    def place(axis, index):
        if axis == "member":
            return (a, index * 2 + core, z)
        if axis == "slot":
            return (lax.rem(index, na), member * 2 + index // na, z)
        at = dict(pos)
        at[axis] = index
        return (at["gx"], at["gy"], at["gz"])

    size["member"], size["slot"] = members, slots
    pos_of = dict(pos, member=member, slot=slot)

    def remote(n, src, dst, where):
        return pltpu.make_async_remote_copy(
            src_ref=src, dst_ref=dst, send_sem=send_sem.at[n], recv_sem=recv_sem.at[n],
            device_id=where, device_id_type=pl.DeviceIdType.MESH,
        )

    def send(src, dst, where):
        copy = remote(count[0], src, dst, where)
        count[0] += 1
        copy.start()
        sent.append(copy.wait_send)
        return copy

    def exchange_later(pairs, dst):
        n = count[0]
        count[0] += 1
        copies = [remote(n, *pair) for pair in pairs]
        whole = dst.at[pl.ds(0, len(pairs))]
        out = pltpu.make_async_copy(whole, whole, send_sem.at[n])
        sent.append(out.wait)
        return copies, pltpu.make_async_copy(whole, whole, recv_sem.at[n])

    def exchange(pairs, dst):
        copies, came = exchange_later(pairs, dst)
        for copy in copies:
            copy.start()
        return came

    def plane_pairs(src_of, there):
        pairs = []
        for d in range(na):
            for e in range(members):
                if d or e:
                    to, far = lax.rem(a + d, na), lax.rem(member + e, members)
                    pairs.append((src_of(to, far), there, (to, far * 2 + core, z)))
        return pairs

    def share(axis, src_of, dst):
        n = size[axis]
        others = [lax.rem(pos_of[axis] + d, n) for d in range(1, n)]
        there = dst.at[pos_of[axis]]
        return exchange([(src_of(to), there, place(axis, to)) for to in others], dst)

    def arrive(copies):
        for copy in copies:
            copy.wait_recv()

    barrier = pltpu.get_barrier_semaphore()
    partners = 0

    def greet(where):
        pl.semaphore_signal(
            barrier, inc=1, device_id=where, device_id_type=pl.DeviceIdType.MESH
        )

    for axis in ("gy", "gz"):
        for d in range(1, size[axis]):
            greet(place(axis, lax.rem(pos[axis] + d, size[axis])))
            partners += 1
    for d in range(1, na):
        for e in range(nb):
            greet((lax.rem(a + d, na), lax.rem(b + e, nb), z))
            partners += 1

    def fetch(n, src, dst):
        copy = pltpu.make_async_copy(src, dst, loc_sem.at[n])
        copy.start()
        return copy

    x_order = (0, CX - 1) + tuple(range(1, CX - 1))
    get_x = {cx: fetch((0, 16, 17, 18)[cx], x_h.at[:, cx], x_v.at[cx]) for cx in x_order}
    get_m = [fetch(1 + i, h, m_v.at[i]) for i, h in enumerate((li_h, lo_h, up_h))]
    get_c = fetch(4, c_h, c_v)
    get_d = fetch(5, d_h, d_v)
    get_v = fetch(6, v_h, v_v)
    get_r = fetch(7, r_h, r_v)
    chunk = e_v.shape[0] // 4
    get_e = [
        fetch((8, 13, 14, 15)[i], e_h.at[pl.ds(i * chunk, chunk)], e_v.at[pl.ds(i * chunk, chunk)])
        for i in range(4)
    ]

    def slab(ref, s, n=RHS):
        return ref[pl.ds(s, n, stride=SLABS), :]

    def rows_at(start, n):
        return pl.ds(pl.multiple_of(start, n), n)

    pad = CY + 2
    q32, lane_all = iota((32, PAIRS * LANES), 0), iota((32, PAIRS * LANES), 1)
    turn_all, l_all = lane_all // LANES, lax.rem(lane_all, LANES)
    pick = ((q32 == turn_all) & (l_all == CZ - 1)) | ((q32 == 16 + turn_all) & (l_all == 0))
    pick = pick.astype(bf16)

    def spread_x(cx):
        get_x[cx].wait()
        rows = x_v.at[cx].reshape(RHS * CY, CZ)
        for cy in range(CY):
            v = rows[pl.ds(cy, RHS, stride=CY), :]
            xp[(cx + 1) * pad + cy + 1] = v
            xsb[cx, cy * RHS : (cy + 1) * RHS, :] = v.astype(bf16)

    def ring(axis, step):
        n = size[axis]
        return place(axis, lax.rem(pos_of[axis] + step + n, n))

    spread_x(x_order[0])
    spread_x(x_order[1])
    pl.semaphore_wait(barrier, partners)
    halo = [
        send(xsb.at[CX - 1], hx.at[0], ring("gx", 1)),
        send(xsb.at[0], hx.at[1], ring("gx", -1)),
    ]
    for cx in x_order[2:]:
        spread_x(cx)
    halo += [
        send(xsb.at[:, pl.ds((CY - 1) * RHS, RHS)], hy.at[0], ring("gy", 1)),
        send(xsb.at[:, pl.ds(0, RHS)], hy.at[1], ring("gy", -1)),
    ]
    rows = jnp.concatenate(
        [xsb[p // 4, (p % 4) * LANES : (p % 4 + 1) * LANES, :] for p in range(PAIRS)], axis=1
    )
    zsend[...] = nt(pick, rows).astype(bf16)
    halo += [
        send(zsend.at[pl.ds(0, 16)], hz.at[0], ring("gz", 1)),
        send(zsend.at[pl.ds(16, 16)], hz.at[1], ring("gz", -1)),
    ]

    mine = rows_at(member * SEP, SEP)
    lane_group = iota((SEP, LANES), 1) // SEP
    per_tile = LANES // SEP
    for i in range(3):
        get_m[i].wait()

    def reorder(i):
        pieces = [
            m_v[i, :, t * LANES : (t + 1) * LANES].astype(f32) for t in range(depth // LANES)
        ]
        for t in range(depth // LANES):
            out = jnp.zeros((SEP, LANES), f32)
            for g in range(per_tile):
                old = (t % na) * nb + g * 2 + t // na
                piece = pieces[old // per_tile]
                shift = ((g - old % per_tile) * SEP) % LANES
                if shift:
                    piece = pltpu.roll(piece, shift, 1)
                out = jnp.where(lane_group == g, piece, out)
            at = slice(t * LANES, (t + 1) * LANES)
            gath[(3, 0, 1)[i], a, member, :, at] = out.astype(bf16)

    for i in range(3):
        reorder(i)

    axes = ("member", "gx")

    def own(m, c):
        return gath.at[m, a, member, :, pl.ds(c * half, half)]

    def near(m, c, axis, step, part):
        at = ring_index(axis, step)
        rows = pl.ds(part * (SEP // 2), SEP // 2)
        if axis == "member":
            return gath.at[m, a, at, rows, pl.ds(c * half, half)]
        return gath.at[m, at, member, rows, pl.ds(c * half, half)]

    def line(m, c, axis, step):
        at = ring_index(axis, step)
        if axis == "member":
            return gath.at[m, :, at, :, pl.ds(c * half, half)]
        return gath.at[m, at, :, :, pl.ds(c * half, half)]

    def near_line(m, c, axis, step, part):
        at = ring_index(axis, step)
        cut = pl.ds(part * 2, 2)
        if axis == "member":
            return gath.at[m, cut, at, :, pl.ds(c * half, half)]
        return gath.at[m, at, cut, :, pl.ds(c * half, half)]

    def ring_index(axis, step):
        return lax.rem(pos_of[axis] + step + size[axis], size[axis])

    def later(src, where):
        copy = remote(count[0], src, src, where)
        count[0] += 1
        return copy

    def ring_pair(block, axis):
        return [later(block, ring(axis, step)) for step in (1, -1)]

    def gather_stages(m):
        one, two, three, four = [], [], [], []
        for c in range(2):
            first, second = axes[c], axes[1 - c]
            one += ring_pair(own(m, c), first)
            three += ring_pair(line(m, c, second, 0), second)
            for part, step in enumerate((1, -1)):
                two.append(later(near(m, c, first, -step, part), ring(first, step)))
                four.append(later(near_line(m, c, second, -step, part), ring(second, step)))
        return one, two, three, four

    def launch(copies):
        for copy in copies:
            copy.start()

    def relay(came, onward):
        for got, copy in zip(came, onward):
            got.wait_recv()
            copy.start()

    low_stages, up_stages, cell_stages, base_stages = (gather_stages(m) for m in range(4))
    use_low, use_up = z > 0, z < nz - 1
    early = z >= nz // 2
    late = jnp.logical_not(early)
    up_after = z < (nz * 5) // 8
    up_before = jnp.logical_and(use_up, jnp.logical_not(up_after))
    launch(base_stages[0])
    pl.when(use_low)(lambda: launch(low_stages[0]))

    get_c.wait()
    cells = jnp.broadcast_to(c_v[...], (SEP, SEP)).astype(f32)
    square = iota((SEP, SEP), 0) == iota((SEP, SEP), 1)
    column = jnp.sum(jnp.where(square, cells, 0.0), axis=1, keepdims=True)
    column = jnp.broadcast_to(column, (SEP, 4 * CZ))
    z512 = iota((SEP, 4 * CZ), 1)

    def mark(q, carry):
        oh[q] = jnp.zeros((wide, 4 * CZ), bf16)
        at = (z512 + q * 4 * CZ).astype(f32)
        oh[q, mine, :] = jnp.where(column == at, 1.0, 0.0).astype(bf16)
        return carry

    lax.fori_loop(0, QUADS, mark, 0)

    vecs = e_v.shape[0] // SLABS
    part_vecs = vecs // 4

    def relayout(c):
        get_e[c].wait()
        at = slice(c * part_vecs, (c + 1) * part_vecs)

        def step(q, carry):
            for h in range(4):
                rows = pl.ds(c * chunk + 4 * q + h, part_vecs, stride=SLABS)
                hi, lo = split(e_v[rows, :])
                vh[q, at, h * CZ : (h + 1) * CZ] = hi
                vl[q, at, h * CZ : (h + 1) * CZ] = lo
            return carry

        lax.fori_loop(0, QUADS, step, 0)

    split_early = z >= 2
    pl.when(split_early)(lambda: relayout(0))
    get_d.wait()
    get_v.wait()
    get_r.wait()
    relay(base_stages[0], base_stages[1])
    pl.when(use_low)(lambda: relay(low_stages[0], low_stages[1]))
    arrive(halo)
    arrive(base_stages[1])
    launch(base_stages[2])

    @pl.when(use_low)
    def _():
        arrive(low_stages[1])
        launch(low_stages[2])

    before_z = hz[0].astype(f32) * flag(z > 0)
    after_z = hz[1].astype(f32) * flag(z < nz - 1)
    ends = jnp.concatenate(
        [before_z, after_z, jnp.zeros((LANES - 32, LANES), f32)], axis=0
    ).T.astype(bf16)
    for k, mask in enumerate((flag(a > 0), flag(a < na - 1))):
        for cy in range(CY):
            xp[k * (CX + 1) * pad + cy + 1] = (
                hx[k, cy * RHS : (cy + 1) * RHS, :].astype(f32) * mask
            )
    for k, mask in enumerate((flag(b > 0), flag(b < nb - 1))):
        for cx in range(CX):
            xp[(cx + 1) * pad + k * (CY + 1)] = hy[k, cx].astype(f32) * mask
    q128, lane_all = iota((LANES, PAIRS * LANES), 0), iota((LANES, PAIRS * LANES), 1)
    turn_all, l_all = lane_all // LANES, lax.rem(lane_all, LANES)
    spread = ((q128 == turn_all) & (l_all == 0)) | ((q128 == 16 + turn_all) & (l_all == CZ - 1))
    z_ends[...] = nn(ends, spread.astype(bf16))
    lane64 = iota((RHS, LANES), 1)

    def residual_of(q, carry):
        for h in range(4):
            s = 4 * q + h
            i = (q // 2 + 1) * pad + lax.rem(q, 2) * 4 + h + 1
            x = xp[i]
            diag = 6.0 + d_v[pl.ds(s, 1), :]
            v0, v1, v2 = (v_v[pl.ds(k * SLABS + s, 1), :] for k in range(3))
            end = z_ends[(h % 2) * RHS : (h % 2 + 1) * RHS, rows_at((2 * q + h // 2) * LANES, LANES)]
            before = jnp.where(lane64 == 0, end, pltpu.roll(x, 1, 1))
            after = jnp.where(lane64 == CZ - 1, end, pltpu.roll(x, CZ - 1, 1))
            res = slab(r_v, s) - diag * x
            res = res + (1.0 + v0) * xp[i - pad] + (1.0 - v0) * xp[i + pad]
            res = res + (1.0 + v1) * xp[i - 1] + (1.0 - v1) * xp[i + 1]
            res = res + (1.0 + v2) * before + (1.0 - v2) * after
            r_v[pl.ds(s, RHS, stride=SLABS), :] = res
            at = slice(h * CZ, (h + 1) * CZ)
            res_b[q, :, at] = res.astype(bf16)
            w = res * (1.0 / diag)
            hi, lo = split(w)
            w0[q, :, at] = w
            wh[q, :, at] = hi
            wl[q, :, at] = lo
        return carry

    lax.fori_loop(0, QUADS, residual_of, 0)
    seps = nt(
        jnp.concatenate([res_b[q] for q in range(QUADS)], axis=1),
        jnp.concatenate([oh[q] for q in range(QUADS)], axis=1),
    )
    put_res = pltpu.make_async_copy(r_v, res_o, loc_sem.at[9])
    put_res.start()

    sep_loc[...] = seps.astype(bf16).reshape(members, group, wide)
    me = slot * members + member
    pairs = []
    for d in range(na):
        for e in range(nb):
            if d or e:
                to, far = lax.rem(a + d, na), lax.rem(b + e, nb)
                pairs.append((sep_loc.at[far // 2], sep_in.at[me], (to, far, z)))
    hop = exchange(pairs, sep_in)
    sep_in[me] = sep_loc[member]
    relay(base_stages[2], base_stages[3])
    for c in (1, 2, 3):
        pl.when(split_early)(functools.partial(relayout, c))
    pl.when(use_low)(lambda: relay(low_stages[2], low_stages[3]))
    hop.wait()
    arrive(base_stages[3])

    row8 = iota((8, LANES), 0)
    left = []
    for i in range(slots):
        v = sep_in[i * members].astype(f32)
        for e in range(1, members):
            v = v + sep_in[i * members + e].astype(f32)
        left.append(v.astype(bf16))
    wide_base = nt(jnp.concatenate(left, axis=1), gath[3].reshape(half, depth))
    gx_here = jnp.zeros((8, LANES), jnp.int32) + a
    for j in range(na):
        both = wide_base[:, j * wide : (j + 1) * wide]
        v = jnp.where(gx_here >= 2, both[8:], both[:8])
        v = jnp.where(lax.rem(gx_here, 2) == 1, pltpu.roll(v, 4, 0), v)
        base[:, j * wide : (j + 1) * wide] = jnp.where(row8 < 4, v, pltpu.roll(v, 4, 0))

    eacc[...] = jnp.zeros(eacc.shape, f32)

    def earlier_product(q, carry):
        right = jnp.concatenate([wh[q], wl[q], oh[q]], axis=0)
        eacc[:vecs] += nt(vh[q], right)
        eacc[vecs:] += nt(vl[q], right)
        return carry

    here = member * na + a
    fold = vecs // 2
    rowf = iota((8, fold), 0)
    plane_sum, plane_came = exchange_later(
        plane_pairs(lambda to, far: psend.at[far * na + to], pin.at[here]), pin
    )

    def earlier_results():
        main = eacc[:vecs, :LANES] + eacc[vecs:, :LANES]
        main = main.T
        main = main[:RHS] + main[RHS:]
        for i in range(RHS // 8):
            one = main[8 * i : 8 * i + 8, :fold]
            two = main[8 * i : 8 * i + 8, fold:]
            psend[2 * i] = jnp.where(rowf < 4, one, pltpu.roll(two, 4, 0))
            psend[2 * i + 1] = jnp.where(rowf < 4, pltpu.roll(one, 4, 0), two)
        launch(plane_sum)
        for i in range(2):
            values = eacc[i * vecs : (i + 1) * vecs, LANES:].T
            v = values[:SEP]
            for e in range(1, members):
                v = v + values[e * SEP : (e + 1) * SEP]
            gath[2, a, member, :, i * vecs : (i + 1) * vecs] = v.astype(bf16)

    def gather_cells():
        launch(cell_stages[0])
        relay(cell_stages[0], cell_stages[1])
        arrive(cell_stages[1])
        launch(cell_stages[2])
        relay(cell_stages[2], cell_stages[3])

    def sweep_copies(first, dst, step):
        return [
            remote(
                first + d, stateb.at[0 if step > 0 else 1], dst.at[core],
                (a, member * 2 + lax.rem(core + d, 2), z + step),
            )
            for d in range(2)
        ]

    def sweep_push(first, dst, step):
        v = state[...]
        t = [v[:, j * wide : (j + 1) * wide] for j in range(na)]
        packed = jnp.concatenate(
            [jnp.where(row8 < 4, t[0], t[1]), jnp.where(row8 < 4, t[2], t[3])], axis=0
        )
        stateb[0 if step > 0 else 1] = packed.astype(bf16)
        for copy in sweep_copies(first, dst, step):
            copy.start()

    row_group = iota((16, LANES), 0) // 4

    def product_of(first, dst, step):
        arrive(sweep_copies(first, dst, step))
        left = []
        for i in range(2):
            v = dst[i].astype(f32)
            left += [jnp.where(row_group == j, v, 0.0).astype(bf16) for j in range(na)]
        out = nn(jnp.concatenate(left, axis=1), gath_t[...])
        out = out[:8] + out[8:]
        return out + pltpu.roll(out, 4, 0)

    def transpose_matrix(m):
        def step(t, carry):
            at = rows_at(t * LANES, LANES)
            block = gath[m, :, :, :, at].reshape(half, LANES)
            gath_t[at, :] = block.astype(f32).T.astype(bf16)
            return carry

        lax.fori_loop(0, depth // LANES, step, 0)

    fw_first = count[0]
    bw_first = fw_first + 2
    count[0] = bw_first + 2

    def products(first, last):
        lax.fori_loop(first, last, earlier_product, 0)

    pl.when(up_before)(lambda: launch(up_stages[0]))
    pl.when(early)(lambda: products(0, QUADS // 2))

    @pl.when(up_before)
    def _():
        relay(up_stages[0], up_stages[1])
        arrive(up_stages[1])
        launch(up_stages[2])

    @pl.when(early)
    def _():
        products(QUADS // 2, QUADS)
        earlier_results()

    pl.when(up_before)(lambda: relay(up_stages[2], up_stages[3]))

    @pl.when(use_low)
    def _():
        arrive(low_stages[3])
        transpose_matrix(0)

    @pl.when(z == 0)
    def _():
        state[...] = base[...]

    @pl.when(z > 0)
    def _():
        state[...] = base[...] - product_of(fw_first, fw_in, 1)

    @pl.when(z < nz - 1)
    def _():
        sweep_push(fw_first, fw_in, 1)

    @pl.when(z == nz - 1)
    def _():
        sweep_push(bw_first, bw_in, -1)

    pl.when(up_after)(lambda: launch(up_stages[0]))

    @pl.when(jnp.logical_not(split_early))
    def _():
        for c in range(4):
            relayout(c)

    pl.when(late)(lambda: products(0, QUADS // 2))

    @pl.when(up_after)
    def _():
        relay(up_stages[0], up_stages[1])
        arrive(up_stages[1])
        launch(up_stages[2])

    @pl.when(late)
    def _():
        products(QUADS // 2, QUADS)
        earlier_results()

    pl.when(up_after)(lambda: relay(up_stages[2], up_stages[3]))
    pl.when(late)(gather_cells)

    @pl.when(z < nz - 1)
    def _():
        arrive(up_stages[3])
        transpose_matrix(1)
        state[...] = state[...] - product_of(bw_first, bw_in, -1)

    @pl.when(jnp.logical_and(z > 0, z < nz - 1))
    def _():
        sweep_push(bw_first, bw_in, -1)

    for j in range(na):
        tiles[j] = state[:, j * wide : (j + 1) * wide]
    ret_came = exchange(plane_pairs(lambda to, far: tiles.at[to], ret.at[here]), ret)
    ret[here] = tiles[a]
    pl.when(early)(gather_cells)

    def total_of(ref, n):
        out = ref[0]
        for i in range(1, n):
            out = out + ref[i]
        return out

    pin[here] = psend[here]
    plane_came.wait()
    arrive(cell_stages[3])
    sol_h, sol_l = split(state[...])
    part = nn(jnp.concatenate([sol_h, sol_l], axis=0), gath[2].reshape(half, 2 * vecs))
    part = part[:8, :vecs] + part[8:, :vecs] + part[:8, vecs:]
    part = jnp.where(rowf < 4, part[:, :fold], part[:, fold:]) + total_of(pin, na * members)
    where_fin = z * 2 + core
    fin[where_fin] = part
    pairs = []
    for d in range(nz):
        for e in range(2):
            if d or e:
                to, kind = lax.rem(z + d, nz), lax.rem(core + e, 2)
                mine_there = fin.at[where_fin]
                pairs.append((mine_there, mine_there, (a, member * 2 + kind, to)))
    hop = exchange(pairs, fin)

    ret_came.wait()
    sol = jnp.concatenate(
        [jnp.where(row8 < 4, ret[2 * i], ret[2 * i + 1]) for i in range(na * members // 2)], axis=0
    )
    sol_h, sol_l = split(sol)
    sol_hl = jnp.concatenate([sol_h, sol_l], axis=1)

    def add_sol(first):
        twice = jnp.concatenate([oh[first], oh[first + 1]], axis=1)
        change = nn(sol_hl, jnp.concatenate([twice, twice], axis=0))
        w0[first] = w0[first] + change[:, : 4 * CZ]
        w0[first + 1] = w0[first + 1] + change[:, 4 * CZ :]

    add_sol(0)
    add_sol(2)
    hop.wait()
    full_in[here] = total_of(fin, nz * 2)
    hop = exchange(plane_pairs(lambda to, far: full_in.at[here], full_in.at[here]), full_in)
    add_sol(4)
    add_sol(6)
    hop.wait()
    for i in range(RHS // 8):
        p, q = full_in[2 * i], full_in[2 * i + 1]
        pt_v[8 * i : 8 * i + 8, :fold] = jnp.where(rowf < 4, p, pltpu.roll(q, 4, 0))
        pt_v[8 * i : 8 * i + 8, fold:] = jnp.where(rowf < 4, pltpu.roll(p, 4, 0), q)
    pin5_put = pltpu.make_async_copy(pt_v, proj_o, loc_sem.at[10])
    pin5_put.start()
    full = pt_v[...]
    hi, lo = split(full)
    pt_hl[:RHS] = hi
    pt_hl[RHS:] = lo

    def project(i, gram):
        for q in (2 * i, 2 * i + 1):
            main = nn(pt_hl[...], vh[q])
            o = w0[q] - (main[:RHS] + main[RHS:] + nn(pt_hl[:RHS], vl[q]))
            hi, lo = split(o)
            both = jnp.concatenate([hi, lo], axis=0)
            orth[q] = both
            gram = gram + nt(both, both)
        return gram

    gram = lax.fori_loop(0, QUADS // 2, project, jnp.zeros((2 * RHS, 2 * RHS), f32))
    gram = gram[:RHS] + gram[RHS:]
    gram = gram + pltpu.roll(gram, RHS, 1)
    put_orth = pltpu.make_async_copy(orth, orth_o, loc_sem.at[11])
    put_orth.start()
    piece = RHS // nz
    g_loc[...] = gram.reshape(nz, piece, LANES)
    hop = share("gz", lambda to: g_loc.at[to], gin1)
    gin1[z] = g_loc[z]
    for wait in sent[:-1]:
        wait()
    del sent[:-1]

    for stage in base_stages + cell_stages:
        for copy in stage:
            copy.wait_send()

    @pl.when(use_low)
    def _():
        for stage in low_stages:
            for copy in stage:
                copy.wait_send()

    @pl.when(use_up)
    def _():
        for stage in up_stages:
            for copy in stage:
                copy.wait_send()

    @pl.when(z < nz - 1)
    def _():
        for copy in sweep_copies(fw_first, fw_in, 1):
            copy.wait_send()

    @pl.when(z > 0)
    def _():
        for copy in sweep_copies(bw_first, bw_in, -1):
            copy.wait_send()

    hop.wait()
    seat = a * nb + b
    gin2[seat] = total_of(gin1, nz)
    pairs = []
    for d in range(na):
        for e in range(nb):
            if d or e:
                to, far = lax.rem(a + d, na), lax.rem(b + e, nb)
                pairs.append((gin2.at[seat], gin2.at[seat], (to, far, z)))
    exchange(pairs, gin2).wait()
    gin3[z] = total_of(gin2, na * nb)
    share("gz", lambda to: gin3.at[z], gin3).wait()
    put_gram = pltpu.make_async_copy(gin3, gram_o, loc_sem.at[12])
    put_gram.start()
    for wait in sent:
        wait()
    for put in (put_res, pin5_put, put_orth, put_gram):
        put.wait()


def finish_kernel(
    scale, gram_v, orth_h, res_h, proj_h, res_o, new_o, proj_o, chol_o,
    orth, rows_v, new_v, res_v, proj_v, sem,
):
    get = pltpu.make_async_copy(orth_h, orth, sem.at[0])
    hand_on = [
        (pltpu.make_async_copy(res_h, res_v, sem.at[1]), pltpu.make_async_copy(res_v, res_o, sem.at[2])),
        (pltpu.make_async_copy(proj_h, proj_v, sem.at[3]), pltpu.make_async_copy(proj_v, proj_o, sem.at[4])),
    ]
    get.start()
    for copy, _ in hand_on:
        copy.start()
    cholesky_rows(gram_v[...], rows_v)
    rows = rows_v[...]
    lane64, row64 = iota((RHS, LANES), 1), iota((RHS, LANES), 0)
    upper = jnp.where((lane64 >= row64) & (lane64 < RHS), rows * (1.0 / scale), 0.0)
    inverse = jnp.where(lane64 - RHS <= row64, rows * scale, 0.0)
    hi, lo = split(inverse)
    lhs = jnp.where(lane64 < RHS, pltpu.roll(hi.astype(f32), RHS, 1), lo.astype(f32)).astype(bf16)
    lhs = jnp.concatenate([lhs, lhs], axis=1)
    for copy, onward in hand_on:
        copy.wait()
        onward.start()
    get.wait()

    def finish(q, carry):
        hi, lo = orth[q, :RHS], orth[q, RHS:]
        out = nn(lhs, jnp.concatenate([hi, hi, lo, lo], axis=0))
        for h in range(4):
            new_v[pl.ds(4 * q + h, RHS, stride=SLABS), :] = out[:, h * CZ : (h + 1) * CZ]
        return carry

    lax.fori_loop(0, QUADS, finish, 0, unroll=4)
    put_new = pltpu.make_async_copy(new_v, new_o, sem.at[5])
    put_new.start()
    upper = jnp.concatenate([upper, jnp.zeros((LANES - RHS, LANES), f32)], axis=0)
    chol_o[...] = upper.T[:RHS, :RHS]
    for _, onward in hand_on:
        onward.wait()
    put_new.wait()


def body(
    x_field, right_side, diag_shift, velocity, earlier_blocks, sep_cells, low_inv, low_off, up_off
):
    na, nb, nz = (lax.axis_size(n) for n in ("gx", "gy", "gz"))
    members, slots = nb // 2, na * 2
    group, wide = RHS // members, SEP * members
    depth, half = slots * wide, na * wide
    vecs = earlier_blocks.shape[0] * earlier_blocks.shape[1]
    piece = RHS // nz
    vmem = pltpu.VMEM
    scratch = [
        vmem((CX, RHS, CY, CZ), f32),
        vmem((ROWS, CZ), f32),
        vmem((SLABS, CZ), f32),
        vmem((3 * SLABS, CZ), f32),
        vmem((vecs * SLABS, CZ), f32),
        vmem((1, SEP), jnp.int32),
        vmem((3, SEP, depth), bf16),
        vmem(((CX + 2) * (CY + 2), RHS, CZ), f32),
        vmem((CX, CY * RHS, CZ), bf16),
        vmem((2, CY * RHS, CZ), bf16),
        vmem((2, CX, RHS, CZ), bf16),
        vmem((2, 16, LANES), bf16),
        vmem((32, LANES), bf16),
        vmem((LANES, PAIRS * LANES), f32),
        vmem((QUADS, RHS, 4 * CZ), bf16),
        vmem((QUADS, wide, 4 * CZ), bf16),
        vmem((4, na, members, SEP, depth), bf16),
        vmem((depth, half), bf16),
        vmem((QUADS, RHS, 4 * CZ), f32),
        vmem((QUADS, RHS, 4 * CZ), bf16),
        vmem((QUADS, RHS, 4 * CZ), bf16),
        vmem((QUADS, vecs, 4 * CZ), bf16),
        vmem((QUADS, vecs, 4 * CZ), bf16),
        vmem((2 * vecs, 2 * LANES), f32),
        vmem((members, group, wide), bf16),
        vmem((slots * members, group, wide), bf16),
        vmem((8, half), f32),
        vmem((8, half), f32),
        vmem((2, 16, wide), bf16),
        vmem((na, 8, wide), f32),
        vmem((2, 16, wide), bf16),
        vmem((2, 16, wide), bf16),
        vmem((na * members, 8, wide), f32),
        vmem((na * members, 8, vecs // 2), f32),
        vmem((na * members, 8, vecs // 2), f32),
        vmem((2 * nz, 8, vecs // 2), f32),
        vmem((na * members, 8, vecs // 2), f32),
        vmem((RHS, vecs), f32),
        vmem((2 * RHS, vecs), bf16),
        vmem((QUADS, 2 * RHS, 4 * CZ), bf16),
        vmem((nz, piece, LANES), f32),
        vmem((nz, piece, LANES), f32),
        vmem((na * nb, piece, LANES), f32),
        vmem((nz, piece, LANES), f32),
        pltpu.SemaphoreType.DMA((19,)),
        pltpu.SemaphoreType.DMA((144,)),
        pltpu.SemaphoreType.DMA((144,)),
    ]
    flat = lambda v: v.reshape(-1, CZ)
    anywhere = pl.BlockSpec(memory_space=pl.ANY)
    in_vmem = pl.BlockSpec(memory_space=pltpu.VMEM)
    res, orth, projection, gram = pl.pallas_call(
        functools.partial(kernel, na, nb, nz),
        out_shape=(
            jax.ShapeDtypeStruct((ROWS, CZ), f32),
            jax.ShapeDtypeStruct((QUADS, 2 * RHS, 4 * CZ), bf16),
            jax.ShapeDtypeStruct((RHS, vecs), f32),
            jax.ShapeDtypeStruct((nz, piece, LANES), f32),
        ),
        in_specs=[anywhere] * 9,
        out_specs=(anywhere,) * 4,
        scratch_shapes=scratch,
        compiler_params=pltpu.CompilerParams(
            collective_id=0, has_side_effects=True, vmem_limit_bytes=60 * 2**20
        ),
        cost_estimate=pl.CostEstimate(
            flops=2 * 10**9, bytes_accessed=13 * 2**20, transcendentals=0
        ),
        name="step",
    )(
        x_field, flat(right_side), flat(diag_shift), flat(velocity), flat(earlier_blocks),
        sep_cells, low_inv[0], low_off[0], up_off[0],
    )
    res, new, projection, factor = pl.pallas_call(
        functools.partial(finish_kernel, math.sqrt(na * nb * nz * CX * CY * CZ)),
        out_shape=(
            jax.ShapeDtypeStruct((ROWS, CZ), f32),
            jax.ShapeDtypeStruct((ROWS, CZ), f32),
            jax.ShapeDtypeStruct((RHS, vecs), f32),
            jax.ShapeDtypeStruct((RHS, RHS), f32),
        ),
        in_specs=[in_vmem, anywhere, anywhere, anywhere],
        out_specs=(anywhere, anywhere, anywhere, in_vmem),
        scratch_shapes=[
            vmem((QUADS, 2 * RHS, 4 * CZ), bf16),
            vmem((RHS, LANES), f32),
            vmem((ROWS, CZ), f32),
            vmem((ROWS, CZ), f32),
            vmem((RHS, vecs), f32),
            pltpu.SemaphoreType.DMA((6,)),
        ],
        compiler_params=pltpu.CompilerParams(vmem_limit_bytes=60 * 2**20),
        cost_estimate=pl.CostEstimate(flops=2 * 10**8, bytes_accessed=5 * 2**20, transcendentals=0),
        name="finish",
    )(gram.reshape(RHS, LANES), orth, res, projection)
    shape = right_side.shape
    return (res.reshape(shape), new.reshape(shape), projection.T, factor)


def solution(mesh):
    return jax.shard_map(
        body,
        mesh=mesh,
        in_specs=(
            P(None, "gx", "gy", "gz"),
            P(None, "gx", "gy", "gz"),
            P("gx", "gy", "gz"),
            P(None, "gx", "gy", "gz"),
            P(None, None, "gx", "gy", "gz"),
            P("gz", ("gx", "gy")),
            P("gz", ("gx", "gy"), None),
            P("gz", ("gx", "gy"), None),
            P("gz", ("gx", "gy"), None),
        ),
        out_specs=(P(None, "gx", "gy", "gz"), P(None, "gx", "gy", "gz"), P(), P()),
        check_vma=False,
    )
```

```python
import functools
import math

import jax
import jax.numpy as jnp
from jax import lax
from jax.experimental import pallas as pl
from jax.experimental.pallas import tpu as pltpu
from jax.sharding import PartitionSpec as P

bf16, f32 = jnp.bfloat16, jnp.float32
RHS, CX, CY, CZ, SEP = 64, 4, 8, 128, 32
SLABS = CX * CY
PAIRS = SLABS // 2
QUADS = SLABS // 4
ROWS = RHS * SLABS
LANES = 128


def nt(a, b):
    return lax.dot_general(a, b, (((1,), (1,)), ((), ())), preferred_element_type=f32)


def nn(a, b):
    return jnp.dot(a, b, preferred_element_type=f32)


def split(v):
    hi = v.astype(bf16)
    return hi, (v - hi.astype(f32)).astype(bf16)


def iota(shape, dim):
    return lax.broadcasted_iota(jnp.int32, shape, dim)


def flag(cond):
    return jnp.where(cond, jnp.float32(1.0), jnp.float32(0.0))


def cholesky_rows(gram, out):
    n = RHS
    lane8, row8 = iota((8, LANES), 1), iota((8, LANES), 0)
    blocks = []
    for k in range(n // 8):
        eye = (lane8 - n == row8 + 8 * k).astype(f32)
        blocks.append(jnp.where(lane8 < n, gram[8 * k : 8 * k + 8, :], eye))

    def sublane(v, r):
        return jnp.broadcast_to(v[r : r + 1, :], (8, LANES))

    def panel(turn, blocks):
        first = blocks[0]
        columns = [jnp.broadcast_to(first[:, j : j + 1], (8, LANES)) for j in range(8)]
        entry = {(i, j): sublane(columns[j], i) for j in range(8) for i in range(j, 8)}
        rows = [sublane(first, i) for i in range(8)]
        for j in range(8):
            root = lax.rsqrt(entry[j, j])
            rows[j] = rows[j] * root
            for i in range(j + 1, 8):
                entry[i, j] = entry[i, j] * root
            for i in range(j + 1, 8):
                rows[i] = rows[i] - entry[i, j] * rows[j]
                for k in range(j + 1, i + 1):
                    entry[i, k] = entry[i, k] - entry[i, j] * entry[k, j]
        done = rows[0]
        for i in range(1, 8):
            done = jnp.where(row8 == i, rows[i], done)
        hi = done.astype(bf16).astype(f32)
        mid = (done - hi).astype(bf16).astype(f32)
        low = done - hi - mid
        left = jnp.concatenate([hi, hi, mid, hi, low, mid], axis=0).astype(bf16)
        right = jnp.concatenate([hi, mid, hi, low, hi, mid], axis=0).astype(bf16)
        change = lax.dot_general(
            left, right, (((0,), (0,)), ((), ())), preferred_element_type=f32
        )
        out[pl.ds(pl.multiple_of(turn * 8, 8), 8), :] = pltpu.roll(done, turn * 8, 1)
        rest = [
            pltpu.roll(blocks[k] - change[8 * k : 8 * k + 8], LANES - 8, 1)
            for k in range(1, n // 8)
        ]
        return tuple(rest + [jnp.zeros((8, LANES), f32)])

    lax.fori_loop(0, n // 8, panel, tuple(blocks))


def kernel(
    na, nb, nz,
    x_h, r_h, d_h, v_h, e_h, c_h, li_h, lo_h, up_h,
    res_o, orth_o, proj_o, gram_o,
    x_v, r_v, d_v, v_v, e_v, c_v, m_v,
    xp, xsb, hx, hy, hz, zsend, z_ends, res_b, oh, gath, gath_sib, gath_t, gath_t2,
    w0, wh, wl, vh, vl, eacc,
    sep_loc, sep_in, base, state, stateb, tiles, fw_in, bw_in, ret, kept, other,
    psend, pin, fin, full_in, pt_v, pt_hl,
    orth, g_loc, gin1, gin2, gin3,
    loc_sem, send_sem, recv_sem,
):
    a, b, z = lax.axis_index("gx"), lax.axis_index("gy"), lax.axis_index("gz")
    size = {"gx": na, "gy": nb, "gz": nz}
    pos = {"gx": a, "gy": b, "gz": z}
    members, slots = nb // 2, na * 2
    member, core = b // 2, lax.rem(b, 2)
    slot = core * na + a
    group = RHS // members
    wide = SEP * members
    depth = slots * wide
    half = na * wide
    count = [0]
    sent = []

    def place(axis, index):
        if axis == "member":
            return (a, index * 2 + core, z)
        if axis == "slot":
            return (lax.rem(index, na), member * 2 + index // na, z)
        at = dict(pos)
        at[axis] = index
        return (at["gx"], at["gy"], at["gz"])

    size["member"], size["slot"] = members, slots
    pos_of = dict(pos, member=member, slot=slot)

    def remote(n, src, dst, where):
        return pltpu.make_async_remote_copy(
            src_ref=src, dst_ref=dst, send_sem=send_sem.at[n], recv_sem=recv_sem.at[n],
            device_id=where, device_id_type=pl.DeviceIdType.MESH,
        )

    def send(src, dst, where):
        copy = remote(count[0], src, dst, where)
        count[0] += 1
        copy.start()
        sent.append(copy.wait_send)
        return copy

    def exchange_later(pairs, dst):
        n = count[0]
        count[0] += 1
        copies = [remote(n, *pair) for pair in pairs]
        whole = dst.at[pl.ds(0, len(pairs))]
        out = pltpu.make_async_copy(whole, whole, send_sem.at[n])
        sent.append(out.wait)
        return copies, pltpu.make_async_copy(whole, whole, recv_sem.at[n])

    def exchange(pairs, dst):
        copies, came = exchange_later(pairs, dst)
        for copy in copies:
            copy.start()
        return came

    def plane_pairs(src_of, there):
        pairs = []
        for d in range(na):
            for e in range(members):
                if d or e:
                    to, far = lax.rem(a + d, na), lax.rem(member + e, members)
                    pairs.append((src_of(to, far), there, (to, far * 2 + core, z)))
        return pairs

    def share(axis, src_of, dst):
        n = size[axis]
        others = [lax.rem(pos_of[axis] + d, n) for d in range(1, n)]
        there = dst.at[pos_of[axis]]
        return exchange([(src_of(to), there, place(axis, to)) for to in others], dst)

    def arrive(copies):
        for copy in copies:
            copy.wait_recv()

    barrier = pltpu.get_barrier_semaphore()
    partners = 0

    def greet(where):
        pl.semaphore_signal(
            barrier, inc=1, device_id=where, device_id_type=pl.DeviceIdType.MESH
        )

    for axis in ("gy", "gz"):
        for d in range(1, size[axis]):
            greet(place(axis, lax.rem(pos[axis] + d, size[axis])))
            partners += 1
    for d in range(1, na):
        for e in range(nb):
            greet((lax.rem(a + d, na), lax.rem(b + e, nb), z))
            partners += 1

    def fetch(n, src, dst):
        copy = pltpu.make_async_copy(src, dst, loc_sem.at[n])
        copy.start()
        return copy

    x_order = (0, CX - 1) + tuple(range(1, CX - 1))
    get_x = {cx: fetch((0, 16, 17, 18)[cx], x_h.at[:, cx], x_v.at[cx]) for cx in x_order}
    get_m = [fetch(1 + i, h, m_v.at[i]) for i, h in enumerate((li_h, lo_h, up_h))]
    get_c = fetch(4, c_h, c_v)
    get_d = fetch(5, d_h, d_v)
    get_v = fetch(6, v_h, v_v)
    get_r = fetch(7, r_h, r_v)
    chunk = e_v.shape[0] // 4
    get_e = [
        fetch((8, 13, 14, 15)[i], e_h.at[pl.ds(i * chunk, chunk)], e_v.at[pl.ds(i * chunk, chunk)])
        for i in range(4)
    ]

    def slab(ref, s, n=RHS):
        return ref[pl.ds(s, n, stride=SLABS), :]

    def rows_at(start, n):
        return pl.ds(pl.multiple_of(start, n), n)

    pad = CY + 2
    q32, lane_all = iota((32, PAIRS * LANES), 0), iota((32, PAIRS * LANES), 1)
    turn_all, l_all = lane_all // LANES, lax.rem(lane_all, LANES)
    pick = ((q32 == turn_all) & (l_all == CZ - 1)) | ((q32 == 16 + turn_all) & (l_all == 0))
    pick = pick.astype(bf16)

    def spread_x(cx):
        get_x[cx].wait()
        rows = x_v.at[cx].reshape(RHS * CY, CZ)
        for cy in range(CY):
            v = rows[pl.ds(cy, RHS, stride=CY), :]
            xp[(cx + 1) * pad + cy + 1] = v
            xsb[cx, cy * RHS : (cy + 1) * RHS, :] = v.astype(bf16)

    def ring(axis, step):
        n = size[axis]
        return place(axis, lax.rem(pos_of[axis] + step + n, n))

    spread_x(x_order[0])
    spread_x(x_order[1])
    pl.semaphore_wait(barrier, partners)
    halo = [
        send(xsb.at[CX - 1], hx.at[0], ring("gx", 1)),
        send(xsb.at[0], hx.at[1], ring("gx", -1)),
    ]
    for cx in x_order[2:]:
        spread_x(cx)
    halo += [
        send(xsb.at[:, pl.ds((CY - 1) * RHS, RHS)], hy.at[0], ring("gy", 1)),
        send(xsb.at[:, pl.ds(0, RHS)], hy.at[1], ring("gy", -1)),
    ]
    rows = jnp.concatenate(
        [xsb[p // 4, (p % 4) * LANES : (p % 4 + 1) * LANES, :] for p in range(PAIRS)], axis=1
    )
    zsend[...] = nt(pick, rows).astype(bf16)
    halo += [
        send(zsend.at[pl.ds(0, 16)], hz.at[0], ring("gz", 1)),
        send(zsend.at[pl.ds(16, 16)], hz.at[1], ring("gz", -1)),
    ]

    mine = rows_at(member * SEP, SEP)
    lane_group = iota((SEP, LANES), 1) // SEP
    per_tile = LANES // SEP
    for i in range(3):
        get_m[i].wait()

    def reorder(i):
        pieces = [
            m_v[i, :, t * LANES : (t + 1) * LANES].astype(f32) for t in range(depth // LANES)
        ]
        for t in range(depth // LANES):
            out = jnp.zeros((SEP, LANES), f32)
            for g in range(per_tile):
                old = (t % na) * nb + g * 2 + t // na
                piece = pieces[old // per_tile]
                shift = ((g - old % per_tile) * SEP) % LANES
                if shift:
                    piece = pltpu.roll(piece, shift, 1)
                out = jnp.where(lane_group == g, piece, out)
            at = slice(t * LANES, (t + 1) * LANES)
            gath[(3, 0, 1)[i], a, member, :, at] = out.astype(bf16)

    for i in range(3):
        reorder(i)

    axes = ("member", "gx")

    def own(m, c):
        return gath.at[m, a, member, :, pl.ds(c * half, half)]

    def near(m, c, axis, step, part):
        at = ring_index(axis, step)
        rows = pl.ds(part * (SEP // 2), SEP // 2)
        if axis == "member":
            return gath.at[m, a, at, rows, pl.ds(c * half, half)]
        return gath.at[m, at, member, rows, pl.ds(c * half, half)]

    def line(m, c, axis, step):
        at = ring_index(axis, step)
        if axis == "member":
            return gath.at[m, :, at, :, pl.ds(c * half, half)]
        return gath.at[m, at, :, :, pl.ds(c * half, half)]

    def near_line(m, c, axis, step, part):
        at = ring_index(axis, step)
        cut = pl.ds(part * 2, 2)
        if axis == "member":
            return gath.at[m, cut, at, :, pl.ds(c * half, half)]
        return gath.at[m, at, cut, :, pl.ds(c * half, half)]

    def ring_index(axis, step):
        return lax.rem(pos_of[axis] + step + size[axis], size[axis])

    def later(src, where):
        copy = remote(count[0], src, src, where)
        count[0] += 1
        return copy

    def ring_pair(block, axis):
        return [later(block, ring(axis, step)) for step in (1, -1)]

    def gather_stages(m):
        one, two, three, four = [], [], [], []
        for c in range(2):
            first, second = axes[c], axes[1 - c]
            one += ring_pair(own(m, c), first)
            three += ring_pair(line(m, c, second, 0), second)
            for part, step in enumerate((1, -1)):
                two.append(later(near(m, c, first, -step, part), ring(first, step)))
                four.append(later(near_line(m, c, second, -step, part), ring(second, step)))
        return one, two, three, four

    def launch(copies):
        for copy in copies:
            copy.start()

    def relay(came, onward):
        for got, copy in zip(came, onward):
            got.wait_recv()
            copy.start()

    low_stages, up_stages, cell_stages, base_stages, pair_stages = (
        gather_stages(m) for m in range(5)
    )
    use_low, use_up = z > 0, z < nz - 1
    odd = lax.rem(z, 2) == 1
    even = jnp.logical_not(odd)

    def all_of(*conditions):
        return functools.reduce(jnp.logical_and, conditions)

    pair_low = all_of(even, z >= 4)
    pair_up = all_of(odd, z <= nz - 3)
    give_low = all_of(odd, z >= 3, z <= nz - 3)
    give_up = all_of(even, z >= 2)
    up_after = z < (nz * 5) // 8
    up_before = all_of(use_up, jnp.logical_not(up_after))
    first_before = z >= 3
    second_before = all_of(odd, z >= 3)
    cells_before = z <= nz // 2

    def shift_copy(m, step):
        n = count[0]
        count[0] += 1
        return remote(n, gath.at[m, a, member], gath.at[4, a, member], (a, b, z + step))

    shift_low, shift_up = shift_copy(0, 1), shift_copy(1, -1)
    sibling = remote(count[0], gath.at[4], gath_sib, (a, member * 2 + 1 - core, z))
    count[0] += 1
    launch(base_stages[0])
    pl.when(use_low)(lambda: launch(low_stages[0]))
    pl.when(give_low)(shift_low.start)
    pl.when(give_up)(shift_up.start)

    get_c.wait()
    cells = jnp.broadcast_to(c_v[...], (SEP, SEP)).astype(f32)
    square = iota((SEP, SEP), 0) == iota((SEP, SEP), 1)
    column = jnp.sum(jnp.where(square, cells, 0.0), axis=1, keepdims=True)
    column = jnp.broadcast_to(column, (SEP, 4 * CZ))
    z512 = iota((SEP, 4 * CZ), 1)

    def mark(q, carry):
        oh[q] = jnp.zeros((wide, 4 * CZ), bf16)
        at = (z512 + q * 4 * CZ).astype(f32)
        oh[q, mine, :] = jnp.where(column == at, 1.0, 0.0).astype(bf16)
        return carry

    lax.fori_loop(0, QUADS, mark, 0)

    vecs = e_v.shape[0] // SLABS
    part_vecs = vecs // 4

    def relayout(c):
        get_e[c].wait()
        at = slice(c * part_vecs, (c + 1) * part_vecs)

        def step(q, carry):
            for h in range(4):
                rows = pl.ds(c * chunk + 4 * q + h, part_vecs, stride=SLABS)
                hi, lo = split(e_v[rows, :])
                vh[q, at, h * CZ : (h + 1) * CZ] = hi
                vl[q, at, h * CZ : (h + 1) * CZ] = lo
            return carry

        lax.fori_loop(0, QUADS, step, 0)

    split_early = z >= 2
    pl.when(split_early)(lambda: relayout(0))
    get_d.wait()
    get_v.wait()
    get_r.wait()
    relay(base_stages[0], base_stages[1])
    pl.when(use_low)(lambda: relay(low_stages[0], low_stages[1]))
    arrive(halo)
    arrive(base_stages[1])
    launch(base_stages[2])

    @pl.when(pair_low)
    def _():
        shift_low.wait_recv()
        launch(pair_stages[0])


    @pl.when(use_low)
    def _():
        arrive(low_stages[1])
        launch(low_stages[2])

    before_z = hz[0].astype(f32) * flag(z > 0)
    after_z = hz[1].astype(f32) * flag(z < nz - 1)
    ends = jnp.concatenate(
        [before_z, after_z, jnp.zeros((LANES - 32, LANES), f32)], axis=0
    ).T.astype(bf16)
    for k, mask in enumerate((flag(a > 0), flag(a < na - 1))):
        for cy in range(CY):
            xp[k * (CX + 1) * pad + cy + 1] = (
                hx[k, cy * RHS : (cy + 1) * RHS, :].astype(f32) * mask
            )
    for k, mask in enumerate((flag(b > 0), flag(b < nb - 1))):
        for cx in range(CX):
            xp[(cx + 1) * pad + k * (CY + 1)] = hy[k, cx].astype(f32) * mask
    q128, lane_all = iota((LANES, PAIRS * LANES), 0), iota((LANES, PAIRS * LANES), 1)
    turn_all, l_all = lane_all // LANES, lax.rem(lane_all, LANES)
    spread = ((q128 == turn_all) & (l_all == 0)) | ((q128 == 16 + turn_all) & (l_all == CZ - 1))
    z_ends[...] = nn(ends, spread.astype(bf16))
    lane64 = iota((RHS, LANES), 1)

    def residual_of(q, carry):
        for h in range(4):
            s = 4 * q + h
            i = (q // 2 + 1) * pad + lax.rem(q, 2) * 4 + h + 1
            x = xp[i]
            diag = 6.0 + d_v[pl.ds(s, 1), :]
            v0, v1, v2 = (v_v[pl.ds(k * SLABS + s, 1), :] for k in range(3))
            end = z_ends[(h % 2) * RHS : (h % 2 + 1) * RHS, rows_at((2 * q + h // 2) * LANES, LANES)]
            before = jnp.where(lane64 == 0, end, pltpu.roll(x, 1, 1))
            after = jnp.where(lane64 == CZ - 1, end, pltpu.roll(x, CZ - 1, 1))
            res = slab(r_v, s) - diag * x
            res = res + (1.0 + v0) * xp[i - pad] + (1.0 - v0) * xp[i + pad]
            res = res + (1.0 + v1) * xp[i - 1] + (1.0 - v1) * xp[i + 1]
            res = res + (1.0 + v2) * before + (1.0 - v2) * after
            r_v[pl.ds(s, RHS, stride=SLABS), :] = res
            at = slice(h * CZ, (h + 1) * CZ)
            res_b[q, :, at] = res.astype(bf16)
            w = res * (1.0 / diag)
            hi, lo = split(w)
            w0[q, :, at] = w
            wh[q, :, at] = hi
            wl[q, :, at] = lo
        return carry

    lax.fori_loop(0, QUADS, residual_of, 0)
    seps = nt(
        jnp.concatenate([res_b[q] for q in range(QUADS)], axis=1),
        jnp.concatenate([oh[q] for q in range(QUADS)], axis=1),
    )
    put_res = pltpu.make_async_copy(r_v, res_o, loc_sem.at[9])
    put_res.start()

    sep_loc[...] = seps.astype(bf16).reshape(members, group, wide)
    me = slot * members + member
    pairs = []
    for d in range(na):
        for e in range(nb):
            if d or e:
                to, far = lax.rem(a + d, na), lax.rem(b + e, nb)
                pairs.append((sep_loc.at[far // 2], sep_in.at[me], (to, far, z)))
    hop = exchange(pairs, sep_in)
    sep_in[me] = sep_loc[member]
    relay(base_stages[2], base_stages[3])
    for c in (1, 2, 3):
        pl.when(split_early)(functools.partial(relayout, c))
    pl.when(pair_low)(lambda: relay(pair_stages[0], pair_stages[1]))
    pl.when(use_low)(lambda: relay(low_stages[2], low_stages[3]))
    hop.wait()
    arrive(base_stages[3])

    row8 = iota((8, LANES), 0)
    left = []
    for i in range(slots):
        v = sep_in[i * members].astype(f32)
        for e in range(1, members):
            v = v + sep_in[i * members + e].astype(f32)
        left.append(v.astype(bf16))
    wide_base = nt(jnp.concatenate(left, axis=1), gath[3].reshape(half, depth))
    gx_here = jnp.zeros((8, LANES), jnp.int32) + a
    for j in range(na):
        both = wide_base[:, j * wide : (j + 1) * wide]
        v = jnp.where(gx_here >= 2, both[8:], both[:8])
        v = jnp.where(lax.rem(gx_here, 2) == 1, pltpu.roll(v, 4, 0), v)
        base[:, j * wide : (j + 1) * wide] = jnp.where(row8 < 4, v, pltpu.roll(v, 4, 0))

    def plane_copies(first, src, dst, step):
        return [
            remote(first + d, src, dst, (a, member * 2 + lax.rem(core + d, 2), z + step))
            for d in range(2)
        ]

    give_base = plane_copies(count[0], base, other.at[core], 1)
    give_state = plane_copies(count[0] + 2, kept, other.at[core], -1)
    count[0] += 4
    pl.when(give_low)(lambda: launch(give_base))

    @pl.when(pair_low)
    def _():
        arrive(pair_stages[1])
        launch(pair_stages[2])

    eacc[...] = jnp.zeros(eacc.shape, f32)

    def earlier_product(q, carry):
        right = jnp.concatenate([wh[q], wl[q], oh[q]], axis=0)
        eacc[:vecs] += nt(vh[q], right)
        eacc[vecs:] += nt(vl[q], right)
        return carry

    here = member * na + a
    fold = vecs // 2
    rowf = iota((8, fold), 0)
    plane_sum, plane_came = exchange_later(
        plane_pairs(lambda to, far: psend.at[far * na + to], pin.at[here]), pin
    )

    def earlier_results():
        main = eacc[:vecs, :LANES] + eacc[vecs:, :LANES]
        main = main.T
        main = main[:RHS] + main[RHS:]
        for i in range(RHS // 8):
            one = main[8 * i : 8 * i + 8, :fold]
            two = main[8 * i : 8 * i + 8, fold:]
            psend[2 * i] = jnp.where(rowf < 4, one, pltpu.roll(two, 4, 0))
            psend[2 * i + 1] = jnp.where(rowf < 4, pltpu.roll(one, 4, 0), two)
        launch(plane_sum)
        for i in range(2):
            values = eacc[i * vecs : (i + 1) * vecs, LANES:].T
            v = values[:SEP]
            for e in range(1, members):
                v = v + values[e * SEP : (e + 1) * SEP]
            gath[2, a, member, :, i * vecs : (i + 1) * vecs] = v.astype(bf16)

    def gather_cells():
        launch(cell_stages[0])
        relay(cell_stages[0], cell_stages[1])
        arrive(cell_stages[1])
        launch(cell_stages[2])
        relay(cell_stages[2], cell_stages[3])

    fw_1 = plane_copies(count[0], stateb.at[0], fw_in.at[core], 1)
    fw_2 = plane_copies(count[0] + 2, stateb.at[0], fw_in.at[core], 2)
    bw_1 = plane_copies(count[0] + 4, stateb.at[1], bw_in.at[core], -1)
    bw_2 = plane_copies(count[0] + 6, stateb.at[1], bw_in.at[core], -2)
    count[0] += 8
    fw_near = all_of(z < nz - 1, jnp.logical_or(even, z == 1))
    fw_far = all_of(even, z >= 2, z <= nz - 4)
    bw_near, bw_far = odd, all_of(odd, z >= 3)
    row_group = iota((16, LANES), 0) // 4

    def pack(v):
        t = [v[:, j * wide : (j + 1) * wide] for j in range(na)]
        return jnp.concatenate(
            [jnp.where(row8 < 4, t[0], t[1]), jnp.where(row8 < 4, t[2], t[3])], axis=0
        )

    def product_of(packed, matrix):
        left = []
        for v in packed:
            v = v.astype(f32)
            left += [jnp.where(row_group == j, v, 0.0).astype(bf16) for j in range(na)]
        out = nn(jnp.concatenate(left, axis=1), matrix[...])
        out = out[:8] + out[8:]
        return out + pltpu.roll(out, 4, 0)

    def two_steps(packed, start):
        between = jnp.concatenate([other[0], other[1]], axis=1) - product_of(packed, gath_t2)
        packed = [pack(between[:, k * half : (k + 1) * half]).astype(bf16) for k in range(2)]
        return start - product_of(packed, gath_t)

    def transpose_matrix(src, dst, column):
        def step(t, carry):
            at = rows_at(t * LANES, LANES)
            block = src[:, :, :, at].reshape(half, LANES)
            dst[at, pl.ds(column, half)] = block.astype(f32).T.astype(bf16)
            return carry

        lax.fori_loop(0, depth // LANES, step, 0)

    def transpose_pair():
        transpose_matrix(gath.at[4], gath_t2, pl.multiple_of(core * half, half))
        sibling.wait_recv()
        transpose_matrix(gath_sib, gath_t2, pl.multiple_of((1 - core) * half, half))

    def products(first, last):
        lax.fori_loop(first, last, earlier_product, 0)

    not_first, not_second = jnp.logical_not(first_before), jnp.logical_not(second_before)
    up_pair_before = all_of(pair_up, up_before)
    up_pair_after = all_of(pair_up, up_after)

    def up_launch(stage):
        launch(up_stages[stage])

    def up_middle():
        relay(up_stages[0], up_stages[1])
        arrive(up_stages[1])
        launch(up_stages[2])

    def pair_begin():
        shift_up.wait_recv()
        launch(pair_stages[0])

    def pair_middle():
        relay(pair_stages[0], pair_stages[1])
        arrive(pair_stages[1])
        launch(pair_stages[2])

    def pair_end():
        arrive(pair_stages[3])
        sibling.start()

    pl.when(up_before)(lambda: launch(up_stages[0]))
    pl.when(up_pair_before)(pair_begin)
    pl.when(first_before)(lambda: products(0, QUADS // 2))
    pl.when(pair_low)(lambda: relay(pair_stages[2], pair_stages[3]))
    pl.when(up_before)(up_middle)
    pl.when(up_pair_before)(pair_middle)
    pl.when(pair_low)(pair_end)

    @pl.when(second_before)
    def _():
        products(QUADS // 2, QUADS)
        earlier_results()

    pl.when(up_before)(lambda: relay(up_stages[2], up_stages[3]))
    pl.when(up_pair_before)(lambda: relay(pair_stages[2], pair_stages[3]))

    @pl.when(use_low)
    def _():
        arrive(low_stages[3])
        transpose_matrix(gath.at[0], gath_t, 0)

    pl.when(pair_low)(transpose_pair)

    @pl.when(z == 0)
    def _():
        state[...] = base[...]

    @pl.when(all_of(z > 0, jnp.logical_not(pair_low)))
    def _():
        arrive(fw_1)
        state[...] = base[...] - product_of([fw_in[0], fw_in[1]], gath_t)

    @pl.when(pair_low)
    def _():
        arrive(give_base)
        arrive(fw_2)
        state[...] = two_steps([fw_in[0], fw_in[1]], base[...])

    @pl.when(fw_near)
    def _():
        stateb[0] = pack(state[...]).astype(bf16)
        launch(fw_1)

    pl.when(fw_far)(lambda: launch(fw_2))

    @pl.when(give_up)
    def _():
        kept[...] = state[...]
        launch(give_state)

    def push_back():
        stateb[1] = pack(state[...]).astype(bf16)
        launch(bw_1)

    @pl.when(z == nz - 1)
    def _():
        push_back()
        launch(bw_2)

    pl.when(up_after)(lambda: launch(up_stages[0]))
    pl.when(up_pair_after)(pair_begin)

    @pl.when(jnp.logical_not(split_early))
    def _():
        for c in range(4):
            relayout(c)

    pl.when(not_first)(lambda: products(0, QUADS // 2))
    pl.when(up_after)(up_middle)
    pl.when(up_pair_after)(pair_middle)

    @pl.when(not_second)
    def _():
        products(QUADS // 2, QUADS)
        earlier_results()

    pl.when(up_after)(lambda: relay(up_stages[2], up_stages[3]))
    pl.when(up_pair_after)(lambda: relay(pair_stages[2], pair_stages[3]))
    pl.when(cells_before)(lambda: launch(cell_stages[0]))
    pl.when(pair_up)(pair_end)

    @pl.when(use_up)
    def _():
        arrive(up_stages[3])
        transpose_matrix(gath.at[1], gath_t, 0)

    @pl.when(cells_before)
    def _():
        relay(cell_stages[0], cell_stages[1])
        arrive(cell_stages[1])
        launch(cell_stages[2])

    pl.when(pair_up)(transpose_pair)
    pl.when(cells_before)(lambda: relay(cell_stages[2], cell_stages[3]))

    @pl.when(all_of(use_up, jnp.logical_not(pair_up)))
    def _():
        arrive(bw_1)
        state[...] = state[...] - product_of([bw_in[0], bw_in[1]], gath_t)

    @pl.when(pair_up)
    def _():
        arrive(give_state)
        arrive(bw_2)
        state[...] = two_steps([bw_in[0], bw_in[1]], state[...])

    pl.when(all_of(odd, use_up))(push_back)
    pl.when(all_of(bw_far, use_up))(lambda: launch(bw_2))

    for j in range(na):
        tiles[j] = state[:, j * wide : (j + 1) * wide]
    ret_came = exchange(plane_pairs(lambda to, far: tiles.at[to], ret.at[here]), ret)
    ret[here] = tiles[a]
    pl.when(jnp.logical_not(cells_before))(gather_cells)

    def total_of(ref, n):
        out = ref[0]
        for i in range(1, n):
            out = out + ref[i]
        return out

    pin[here] = psend[here]
    plane_came.wait()
    arrive(cell_stages[3])
    sol_h, sol_l = split(state[...])
    part = nn(jnp.concatenate([sol_h, sol_l], axis=0), gath[2].reshape(half, 2 * vecs))
    part = part[:8, :vecs] + part[8:, :vecs] + part[:8, vecs:]
    part = jnp.where(rowf < 4, part[:, :fold], part[:, fold:]) + total_of(pin, na * members)
    where_fin = z * 2 + core
    fin[where_fin] = part
    pairs = []
    for d in range(nz):
        for e in range(2):
            if d or e:
                to, kind = lax.rem(z + d, nz), lax.rem(core + e, 2)
                mine_there = fin.at[where_fin]
                pairs.append((mine_there, mine_there, (a, member * 2 + kind, to)))
    hop = exchange(pairs, fin)

    ret_came.wait()
    sol = jnp.concatenate(
        [jnp.where(row8 < 4, ret[2 * i], ret[2 * i + 1]) for i in range(na * members // 2)], axis=0
    )
    sol_h, sol_l = split(sol)
    sol_hl = jnp.concatenate([sol_h, sol_l], axis=1)

    def add_sol(first):
        twice = jnp.concatenate([oh[first], oh[first + 1]], axis=1)
        change = nn(sol_hl, jnp.concatenate([twice, twice], axis=0))
        w0[first] = w0[first] + change[:, : 4 * CZ]
        w0[first + 1] = w0[first + 1] + change[:, 4 * CZ :]

    add_sol(0)
    add_sol(2)
    hop.wait()
    full_in[here] = total_of(fin, nz * 2)
    hop = exchange(plane_pairs(lambda to, far: full_in.at[here], full_in.at[here]), full_in)
    add_sol(4)
    add_sol(6)
    hop.wait()
    for i in range(RHS // 8):
        p, q = full_in[2 * i], full_in[2 * i + 1]
        pt_v[8 * i : 8 * i + 8, :fold] = jnp.where(rowf < 4, p, pltpu.roll(q, 4, 0))
        pt_v[8 * i : 8 * i + 8, fold:] = jnp.where(rowf < 4, pltpu.roll(p, 4, 0), q)
    pin5_put = pltpu.make_async_copy(pt_v, proj_o, loc_sem.at[10])
    pin5_put.start()
    full = pt_v[...]
    hi, lo = split(full)
    pt_hl[:RHS] = hi
    pt_hl[RHS:] = lo

    def project(i, gram):
        for q in (2 * i, 2 * i + 1):
            main = nn(pt_hl[...], vh[q])
            o = w0[q] - (main[:RHS] + main[RHS:] + nn(pt_hl[:RHS], vl[q]))
            hi, lo = split(o)
            both = jnp.concatenate([hi, lo], axis=0)
            orth[q] = both
            gram = gram + nt(both, both)
        return gram

    gram = lax.fori_loop(0, QUADS // 2, project, jnp.zeros((2 * RHS, 2 * RHS), f32))
    gram = gram[:RHS] + gram[RHS:]
    gram = gram + pltpu.roll(gram, RHS, 1)
    put_orth = pltpu.make_async_copy(orth, orth_o, loc_sem.at[11])
    put_orth.start()
    piece = RHS // nz
    g_loc[...] = gram.reshape(nz, piece, LANES)
    hop = share("gz", lambda to: g_loc.at[to], gin1)
    gin1[z] = g_loc[z]
    for wait in sent[:-1]:
        wait()
    del sent[:-1]

    for stage in base_stages + cell_stages:
        for copy in stage:
            copy.wait_send()

    @pl.when(use_low)
    def _():
        for stage in low_stages:
            for copy in stage:
                copy.wait_send()

    @pl.when(use_up)
    def _():
        for stage in up_stages:
            for copy in stage:
                copy.wait_send()

    use_pair = jnp.logical_or(pair_low, pair_up)
    for condition, copies in (
        (use_pair, sum(pair_stages, [])), (use_pair, [sibling]),
        (give_low, [shift_low] + give_base), (give_up, [shift_up] + give_state),
        (fw_near, fw_1), (fw_far, fw_2), (bw_near, bw_1), (bw_far, bw_2),
    ):
        @pl.when(condition)
        def _(copies=copies):
            for copy in copies:
                copy.wait_send()

    hop.wait()
    seat = a * nb + b
    gin2[seat] = total_of(gin1, nz)
    pairs = []
    for d in range(na):
        for e in range(nb):
            if d or e:
                to, far = lax.rem(a + d, na), lax.rem(b + e, nb)
                pairs.append((gin2.at[seat], gin2.at[seat], (to, far, z)))
    exchange(pairs, gin2).wait()
    gin3[z] = total_of(gin2, na * nb)
    share("gz", lambda to: gin3.at[z], gin3).wait()
    put_gram = pltpu.make_async_copy(gin3, gram_o, loc_sem.at[12])
    put_gram.start()
    for wait in sent:
        wait()
    for put in (put_res, pin5_put, put_orth, put_gram):
        put.wait()


def finish_kernel(
    scale, gram_v, orth_h, res_h, proj_h, res_o, new_o, proj_o, chol_o,
    orth, rows_v, new_v, res_v, proj_v, sem,
):
    get = pltpu.make_async_copy(orth_h, orth, sem.at[0])
    hand_on = [
        (pltpu.make_async_copy(res_h, res_v, sem.at[1]), pltpu.make_async_copy(res_v, res_o, sem.at[2])),
        (pltpu.make_async_copy(proj_h, proj_v, sem.at[3]), pltpu.make_async_copy(proj_v, proj_o, sem.at[4])),
    ]
    get.start()
    for copy, _ in hand_on:
        copy.start()
    cholesky_rows(gram_v[...], rows_v)
    rows = rows_v[...]
    lane64, row64 = iota((RHS, LANES), 1), iota((RHS, LANES), 0)
    upper = jnp.where((lane64 >= row64) & (lane64 < RHS), rows * (1.0 / scale), 0.0)
    inverse = jnp.where(lane64 - RHS <= row64, rows * scale, 0.0)
    hi, lo = split(inverse)
    lhs = jnp.where(lane64 < RHS, pltpu.roll(hi.astype(f32), RHS, 1), lo.astype(f32)).astype(bf16)
    lhs = jnp.concatenate([lhs, lhs], axis=1)
    for copy, onward in hand_on:
        copy.wait()
        onward.start()
    get.wait()

    def finish(q, carry):
        hi, lo = orth[q, :RHS], orth[q, RHS:]
        out = nn(lhs, jnp.concatenate([hi, hi, lo, lo], axis=0))
        for h in range(4):
            new_v[pl.ds(4 * q + h, RHS, stride=SLABS), :] = out[:, h * CZ : (h + 1) * CZ]
        return carry

    lax.fori_loop(0, QUADS, finish, 0, unroll=4)
    put_new = pltpu.make_async_copy(new_v, new_o, sem.at[5])
    put_new.start()
    upper = jnp.concatenate([upper, jnp.zeros((LANES - RHS, LANES), f32)], axis=0)
    chol_o[...] = upper.T[:RHS, :RHS]
    for _, onward in hand_on:
        onward.wait()
    put_new.wait()


def body(
    x_field, right_side, diag_shift, velocity, earlier_blocks, sep_cells, low_inv, low_off, up_off
):
    na, nb, nz = (lax.axis_size(n) for n in ("gx", "gy", "gz"))
    members, slots = nb // 2, na * 2
    group, wide = RHS // members, SEP * members
    depth, half = slots * wide, na * wide
    vecs = earlier_blocks.shape[0] * earlier_blocks.shape[1]
    piece = RHS // nz
    vmem = pltpu.VMEM
    scratch = [
        vmem((CX, RHS, CY, CZ), f32),
        vmem((ROWS, CZ), f32),
        vmem((SLABS, CZ), f32),
        vmem((3 * SLABS, CZ), f32),
        vmem((vecs * SLABS, CZ), f32),
        vmem((1, SEP), jnp.int32),
        vmem((3, SEP, depth), bf16),
        vmem(((CX + 2) * (CY + 2), RHS, CZ), f32),
        vmem((CX, CY * RHS, CZ), bf16),
        vmem((2, CY * RHS, CZ), bf16),
        vmem((2, CX, RHS, CZ), bf16),
        vmem((2, 16, LANES), bf16),
        vmem((32, LANES), bf16),
        vmem((LANES, PAIRS * LANES), f32),
        vmem((QUADS, RHS, 4 * CZ), bf16),
        vmem((QUADS, wide, 4 * CZ), bf16),
        vmem((5, na, members, SEP, depth), bf16),
        vmem((na, members, SEP, depth), bf16),
        vmem((depth, half), bf16),
        vmem((depth, depth), bf16),
        vmem((QUADS, RHS, 4 * CZ), f32),
        vmem((QUADS, RHS, 4 * CZ), bf16),
        vmem((QUADS, RHS, 4 * CZ), bf16),
        vmem((QUADS, vecs, 4 * CZ), bf16),
        vmem((QUADS, vecs, 4 * CZ), bf16),
        vmem((2 * vecs, 2 * LANES), f32),
        vmem((members, group, wide), bf16),
        vmem((slots * members, group, wide), bf16),
        vmem((8, half), f32),
        vmem((8, half), f32),
        vmem((2, 16, wide), bf16),
        vmem((na, 8, wide), f32),
        vmem((2, 16, wide), bf16),
        vmem((2, 16, wide), bf16),
        vmem((na * members, 8, wide), f32),
        vmem((8, half), f32),
        vmem((2, 8, half), f32),
        vmem((na * members, 8, vecs // 2), f32),
        vmem((na * members, 8, vecs // 2), f32),
        vmem((2 * nz, 8, vecs // 2), f32),
        vmem((na * members, 8, vecs // 2), f32),
        vmem((RHS, vecs), f32),
        vmem((2 * RHS, vecs), bf16),
        vmem((QUADS, 2 * RHS, 4 * CZ), bf16),
        vmem((nz, piece, LANES), f32),
        vmem((nz, piece, LANES), f32),
        vmem((na * nb, piece, LANES), f32),
        vmem((nz, piece, LANES), f32),
        pltpu.SemaphoreType.DMA((19,)),
        pltpu.SemaphoreType.DMA((160,)),
        pltpu.SemaphoreType.DMA((160,)),
    ]
    flat = lambda v: v.reshape(-1, CZ)
    anywhere = pl.BlockSpec(memory_space=pl.ANY)
    in_vmem = pl.BlockSpec(memory_space=pltpu.VMEM)
    res, orth, projection, gram = pl.pallas_call(
        functools.partial(kernel, na, nb, nz),
        out_shape=(
            jax.ShapeDtypeStruct((ROWS, CZ), f32),
            jax.ShapeDtypeStruct((QUADS, 2 * RHS, 4 * CZ), bf16),
            jax.ShapeDtypeStruct((RHS, vecs), f32),
            jax.ShapeDtypeStruct((nz, piece, LANES), f32),
        ),
        in_specs=[anywhere] * 9,
        out_specs=(anywhere,) * 4,
        scratch_shapes=scratch,
        compiler_params=pltpu.CompilerParams(
            collective_id=0, has_side_effects=True, vmem_limit_bytes=60 * 2**20
        ),
        cost_estimate=pl.CostEstimate(
            flops=2 * 10**9, bytes_accessed=13 * 2**20, transcendentals=0
        ),
        name="step",
    )(
        x_field, flat(right_side), flat(diag_shift), flat(velocity), flat(earlier_blocks),
        sep_cells, low_inv[0], low_off[0], up_off[0],
    )
    res, new, projection, factor = pl.pallas_call(
        functools.partial(finish_kernel, math.sqrt(na * nb * nz * CX * CY * CZ)),
        out_shape=(
            jax.ShapeDtypeStruct((ROWS, CZ), f32),
            jax.ShapeDtypeStruct((ROWS, CZ), f32),
            jax.ShapeDtypeStruct((RHS, vecs), f32),
            jax.ShapeDtypeStruct((RHS, RHS), f32),
        ),
        in_specs=[in_vmem, anywhere, anywhere, anywhere],
        out_specs=(anywhere, anywhere, anywhere, in_vmem),
        scratch_shapes=[
            vmem((QUADS, 2 * RHS, 4 * CZ), bf16),
            vmem((RHS, LANES), f32),
            vmem((ROWS, CZ), f32),
            vmem((ROWS, CZ), f32),
            vmem((RHS, vecs), f32),
            pltpu.SemaphoreType.DMA((6,)),
        ],
        compiler_params=pltpu.CompilerParams(vmem_limit_bytes=60 * 2**20),
        cost_estimate=pl.CostEstimate(flops=2 * 10**8, bytes_accessed=5 * 2**20, transcendentals=0),
        name="finish",
    )(gram.reshape(RHS, LANES), orth, res, projection)
    shape = right_side.shape
    return (res.reshape(shape), new.reshape(shape), projection.T, factor)


def solution(mesh):
    return jax.shard_map(
        body,
        mesh=mesh,
        in_specs=(
            P(None, "gx", "gy", "gz"),
            P(None, "gx", "gy", "gz"),
            P("gx", "gy", "gz"),
            P(None, "gx", "gy", "gz"),
            P(None, None, "gx", "gy", "gz"),
            P("gz", ("gx", "gy")),
            P("gz", ("gx", "gy"), None),
            P("gz", ("gx", "gy"), None),
            P("gz", ("gx", "gy"), None),
        ),
        out_specs=(P(None, "gx", "gy", "gz"), P(None, "gx", "gy", "gz"), P(), P()),
        check_vma=False,
    )
```

```python
import functools
import math

import jax
import jax.numpy as jnp
from jax import lax
from jax.experimental import pallas as pl
from jax.experimental.pallas import tpu as pltpu
from jax.sharding import PartitionSpec as P

bf16, f32 = jnp.bfloat16, jnp.float32
RHS, CX, CY, CZ, SEP = 64, 4, 8, 128, 32
SLABS = CX * CY
PAIRS = SLABS // 2
QUADS = SLABS // 4
ROWS = RHS * SLABS
LANES = 128


def nt(a, b):
    return lax.dot_general(a, b, (((1,), (1,)), ((), ())), preferred_element_type=f32)


def nn(a, b):
    return jnp.dot(a, b, preferred_element_type=f32)


def split(v):
    hi = v.astype(bf16)
    return hi, (v - hi.astype(f32)).astype(bf16)


def iota(shape, dim):
    return lax.broadcasted_iota(jnp.int32, shape, dim)


def flag(cond):
    return jnp.where(cond, jnp.float32(1.0), jnp.float32(0.0))


def cholesky_rows(gram, out):
    n = RHS
    lane8, row8 = iota((8, LANES), 1), iota((8, LANES), 0)
    blocks = []
    for k in range(n // 8):
        eye = (lane8 - n == row8 + 8 * k).astype(f32)
        blocks.append(jnp.where(lane8 < n, gram[8 * k : 8 * k + 8, :], eye))

    def sublane(v, r):
        return jnp.broadcast_to(v[r : r + 1, :], (8, LANES))

    def panel(turn, blocks):
        first = blocks[0]
        columns = [jnp.broadcast_to(first[:, j : j + 1], (8, LANES)) for j in range(8)]
        entry = {(i, j): sublane(columns[j], i) for j in range(8) for i in range(j, 8)}
        rows = [sublane(first, i) for i in range(8)]
        for j in range(8):
            root = lax.rsqrt(entry[j, j])
            rows[j] = rows[j] * root
            for i in range(j + 1, 8):
                entry[i, j] = entry[i, j] * root
            for i in range(j + 1, 8):
                rows[i] = rows[i] - entry[i, j] * rows[j]
                for k in range(j + 1, i + 1):
                    entry[i, k] = entry[i, k] - entry[i, j] * entry[k, j]
        done = rows[0]
        for i in range(1, 8):
            done = jnp.where(row8 == i, rows[i], done)
        hi = done.astype(bf16).astype(f32)
        mid = (done - hi).astype(bf16).astype(f32)
        low = done - hi - mid
        left = jnp.concatenate([hi, hi, mid, hi, low, mid], axis=0).astype(bf16)
        right = jnp.concatenate([hi, mid, hi, low, hi, mid], axis=0).astype(bf16)
        change = lax.dot_general(
            left, right, (((0,), (0,)), ((), ())), preferred_element_type=f32
        )
        out[pl.ds(pl.multiple_of(turn * 8, 8), 8), :] = pltpu.roll(done, turn * 8, 1)
        rest = [
            pltpu.roll(blocks[k] - change[8 * k : 8 * k + 8], LANES - 8, 1)
            for k in range(1, n // 8)
        ]
        return tuple(rest + [jnp.zeros((8, LANES), f32)])

    lax.fori_loop(0, n // 8, panel, tuple(blocks))


def kernel(
    na, nb, nz,
    x_h, r_h, d_h, v_h, e_h, c_h, li_h, lo_h, up_h,
    res_o, orth_o, proj_o, gram_o,
    x_v, r_v, d_v, v_v, e_v, c_v, m_v,
    xp, xsb, hx, hy, hz, zsend, z_ends, res_b, oh, gath, gath_sib,
    w0, wh, wl, vh, vl, eacc,
    sep_loc, sep_in, base, state, stateb, tiles, fw_in, bw_in, ret, kept, other,
    psend, pin, fin, full_in, pt_v, pt_hl,
    orth, g_loc, gin1, gin2, gin3,
    loc_sem, send_sem, recv_sem,
):
    a, b, z = lax.axis_index("gx"), lax.axis_index("gy"), lax.axis_index("gz")
    size = {"gx": na, "gy": nb, "gz": nz}
    pos = {"gx": a, "gy": b, "gz": z}
    members, slots = nb // 2, na * 2
    member, core = b // 2, lax.rem(b, 2)
    slot = core * na + a
    group = RHS // members
    wide = SEP * members
    depth = slots * wide
    half = na * wide
    count = [0]
    sent = []

    def place(axis, index):
        if axis == "member":
            return (a, index * 2 + core, z)
        if axis == "slot":
            return (lax.rem(index, na), member * 2 + index // na, z)
        at = dict(pos)
        at[axis] = index
        return (at["gx"], at["gy"], at["gz"])

    size["member"], size["slot"] = members, slots
    pos_of = dict(pos, member=member, slot=slot)

    def remote(n, src, dst, where):
        return pltpu.make_async_remote_copy(
            src_ref=src, dst_ref=dst, send_sem=send_sem.at[n], recv_sem=recv_sem.at[n],
            device_id=where, device_id_type=pl.DeviceIdType.MESH,
        )

    def send(src, dst, where):
        copy = remote(count[0], src, dst, where)
        count[0] += 1
        copy.start()
        sent.append(copy.wait_send)
        return copy

    def exchange_later(pairs, dst):
        n = count[0]
        count[0] += 1
        copies = [remote(n, *pair) for pair in pairs]
        whole = dst.at[pl.ds(0, len(pairs))]
        out = pltpu.make_async_copy(whole, whole, send_sem.at[n])
        sent.append(out.wait)
        return copies, pltpu.make_async_copy(whole, whole, recv_sem.at[n])

    def exchange(pairs, dst):
        copies, came = exchange_later(pairs, dst)
        for copy in copies:
            copy.start()
        return came

    def plane_pairs(src_of, there):
        pairs = []
        for d in range(na):
            for e in range(members):
                if d or e:
                    to, far = lax.rem(a + d, na), lax.rem(member + e, members)
                    pairs.append((src_of(to, far), there, (to, far * 2 + core, z)))
        return pairs

    def share(axis, src_of, dst):
        n = size[axis]
        others = [lax.rem(pos_of[axis] + d, n) for d in range(1, n)]
        there = dst.at[pos_of[axis]]
        return exchange([(src_of(to), there, place(axis, to)) for to in others], dst)

    def arrive(copies):
        for copy in copies:
            copy.wait_recv()

    barrier = pltpu.get_barrier_semaphore()
    partners = 0

    def greet(where):
        pl.semaphore_signal(
            barrier, inc=1, device_id=where, device_id_type=pl.DeviceIdType.MESH
        )

    for axis in ("gy", "gz"):
        for d in range(1, size[axis]):
            greet(place(axis, lax.rem(pos[axis] + d, size[axis])))
            partners += 1
    for d in range(1, na):
        for e in range(nb):
            greet((lax.rem(a + d, na), lax.rem(b + e, nb), z))
            partners += 1

    def fetch(n, src, dst):
        copy = pltpu.make_async_copy(src, dst, loc_sem.at[n])
        copy.start()
        return copy

    x_order = (0, CX - 1) + tuple(range(1, CX - 1))
    get_x = {cx: fetch((0, 16, 17, 18)[cx], x_h.at[:, cx], x_v.at[cx]) for cx in x_order}
    get_m = [fetch(1 + i, h, m_v.at[i]) for i, h in enumerate((li_h, lo_h, up_h))]
    get_c = fetch(4, c_h, c_v)
    get_d = fetch(5, d_h, d_v)
    get_v = fetch(6, v_h, v_v)
    get_r = fetch(7, r_h, r_v)
    chunk = e_v.shape[0] // 4
    get_e = [
        fetch((8, 13, 14, 15)[i], e_h.at[pl.ds(i * chunk, chunk)], e_v.at[pl.ds(i * chunk, chunk)])
        for i in range(4)
    ]

    def slab(ref, s, n=RHS):
        return ref[pl.ds(s, n, stride=SLABS), :]

    def rows_at(start, n):
        return pl.ds(pl.multiple_of(start, n), n)

    pad = CY + 2
    q32, lane_all = iota((32, PAIRS * LANES), 0), iota((32, PAIRS * LANES), 1)
    turn_all, l_all = lane_all // LANES, lax.rem(lane_all, LANES)
    pick = ((q32 == turn_all) & (l_all == CZ - 1)) | ((q32 == 16 + turn_all) & (l_all == 0))
    pick = pick.astype(bf16)

    def spread_x(cx):
        get_x[cx].wait()
        rows = x_v.at[cx].reshape(RHS * CY, CZ)
        for cy in range(CY):
            v = rows[pl.ds(cy, RHS, stride=CY), :]
            xp[(cx + 1) * pad + cy + 1] = v
            xsb[cx, cy * RHS : (cy + 1) * RHS, :] = v.astype(bf16)

    def ring(axis, step):
        n = size[axis]
        return place(axis, lax.rem(pos_of[axis] + step + n, n))

    spread_x(x_order[0])
    spread_x(x_order[1])
    pl.semaphore_wait(barrier, partners)
    halo = [
        send(xsb.at[CX - 1], hx.at[0], ring("gx", 1)),
        send(xsb.at[0], hx.at[1], ring("gx", -1)),
    ]
    for cx in x_order[2:]:
        spread_x(cx)
    halo += [
        send(xsb.at[:, pl.ds((CY - 1) * RHS, RHS)], hy.at[0], ring("gy", 1)),
        send(xsb.at[:, pl.ds(0, RHS)], hy.at[1], ring("gy", -1)),
    ]
    rows = jnp.concatenate(
        [xsb[p // 4, (p % 4) * LANES : (p % 4 + 1) * LANES, :] for p in range(PAIRS)], axis=1
    )
    zsend[...] = nt(pick, rows).astype(bf16)
    halo += [
        send(zsend.at[pl.ds(0, 16)], hz.at[0], ring("gz", 1)),
        send(zsend.at[pl.ds(16, 16)], hz.at[1], ring("gz", -1)),
    ]

    mine = rows_at(member * SEP, SEP)
    lane_group = iota((SEP, LANES), 1) // SEP
    per_tile = LANES // SEP
    for i in range(3):
        get_m[i].wait()

    def reorder(i):
        pieces = [
            m_v[i, :, t * LANES : (t + 1) * LANES].astype(f32) for t in range(depth // LANES)
        ]
        for t in range(depth // LANES):
            out = jnp.zeros((SEP, LANES), f32)
            for g in range(per_tile):
                old = (t % na) * nb + g * 2 + t // na
                piece = pieces[old // per_tile]
                shift = ((g - old % per_tile) * SEP) % LANES
                if shift:
                    piece = pltpu.roll(piece, shift, 1)
                out = jnp.where(lane_group == g, piece, out)
            at = slice(t * LANES, (t + 1) * LANES)
            gath[(3, 0, 1)[i], a, member, :, at] = out.astype(bf16)

    for i in range(3):
        reorder(i)

    axes = ("member", "gx")

    def own(m, c):
        return gath.at[m, a, member, :, pl.ds(c * half, half)]

    def near(m, c, axis, step, part):
        at = ring_index(axis, step)
        rows = pl.ds(part * (SEP // 2), SEP // 2)
        if axis == "member":
            return gath.at[m, a, at, rows, pl.ds(c * half, half)]
        return gath.at[m, at, member, rows, pl.ds(c * half, half)]

    def line(m, c, axis, step):
        at = ring_index(axis, step)
        if axis == "member":
            return gath.at[m, :, at, :, pl.ds(c * half, half)]
        return gath.at[m, at, :, :, pl.ds(c * half, half)]

    def near_line(m, c, axis, step, part):
        at = ring_index(axis, step)
        cut = pl.ds(part * 2, 2)
        if axis == "member":
            return gath.at[m, cut, at, :, pl.ds(c * half, half)]
        return gath.at[m, at, cut, :, pl.ds(c * half, half)]

    def ring_index(axis, step):
        return lax.rem(pos_of[axis] + step + size[axis], size[axis])

    def later(src, where):
        copy = remote(count[0], src, src, where)
        count[0] += 1
        return copy

    def ring_pair(block, axis):
        return [later(block, ring(axis, step)) for step in (1, -1)]

    def gather_stages(m):
        one, two, three, four = [], [], [], []
        for c in range(2):
            first, second = axes[c], axes[1 - c]
            one += ring_pair(own(m, c), first)
            three += ring_pair(line(m, c, second, 0), second)
            for part, step in enumerate((1, -1)):
                two.append(later(near(m, c, first, -step, part), ring(first, step)))
                four.append(later(near_line(m, c, second, -step, part), ring(second, step)))
        return one, two, three, four

    def launch(copies):
        for copy in copies:
            copy.start()

    def relay(came, onward):
        for got, copy in zip(came, onward):
            got.wait_recv()
            copy.start()

    low_stages, up_stages, cell_stages, base_stages, pair_stages = (
        gather_stages(m) for m in range(5)
    )
    use_low, use_up = z > 0, z < nz - 1
    odd = lax.rem(z, 2) == 1
    even = jnp.logical_not(odd)

    def all_of(*conditions):
        return functools.reduce(jnp.logical_and, conditions)

    pair_low = all_of(even, z >= 4)
    pair_up = all_of(odd, z <= nz - 3)
    give_low = all_of(odd, z >= 3, z <= nz - 3)
    give_up = all_of(even, z >= 2)
    up_after = z < (nz * 5) // 8
    up_before = all_of(use_up, jnp.logical_not(up_after))
    first_before = z >= 3
    second_before = all_of(odd, z >= 3)
    cells_before = z <= nz // 2

    def shift_copy(m, step):
        n = count[0]
        count[0] += 1
        return remote(n, gath.at[m, a, member], gath.at[4, a, member], (a, b, z + step))

    shift_low, shift_up = shift_copy(0, 1), shift_copy(1, -1)
    sibling = remote(count[0], gath.at[4], gath_sib, (a, member * 2 + 1 - core, z))
    count[0] += 1
    launch(base_stages[0])
    pl.when(use_low)(lambda: launch(low_stages[0]))
    pl.when(give_low)(shift_low.start)
    pl.when(give_up)(shift_up.start)

    get_c.wait()
    cells = jnp.broadcast_to(c_v[...], (SEP, SEP)).astype(f32)
    square = iota((SEP, SEP), 0) == iota((SEP, SEP), 1)
    column = jnp.sum(jnp.where(square, cells, 0.0), axis=1, keepdims=True)
    column = jnp.broadcast_to(column, (SEP, 4 * CZ))
    z512 = iota((SEP, 4 * CZ), 1)

    def mark(q, carry):
        oh[q] = jnp.zeros((wide, 4 * CZ), bf16)
        at = (z512 + q * 4 * CZ).astype(f32)
        oh[q, mine, :] = jnp.where(column == at, 1.0, 0.0).astype(bf16)
        return carry

    lax.fori_loop(0, QUADS, mark, 0)

    vecs = e_v.shape[0] // SLABS
    part_vecs = vecs // 4

    def relayout(c):
        get_e[c].wait()
        at = slice(c * part_vecs, (c + 1) * part_vecs)

        def step(q, carry):
            for h in range(4):
                rows = pl.ds(c * chunk + 4 * q + h, part_vecs, stride=SLABS)
                hi, lo = split(e_v[rows, :])
                vh[q, at, h * CZ : (h + 1) * CZ] = hi
                vl[q, at, h * CZ : (h + 1) * CZ] = lo
            return carry

        lax.fori_loop(0, QUADS, step, 0)

    split_early = z >= 2
    pl.when(split_early)(lambda: relayout(0))
    get_d.wait()
    get_v.wait()
    get_r.wait()
    relay(base_stages[0], base_stages[1])
    pl.when(use_low)(lambda: relay(low_stages[0], low_stages[1]))
    arrive(halo)
    arrive(base_stages[1])
    launch(base_stages[2])

    @pl.when(pair_low)
    def _():
        shift_low.wait_recv()
        launch(pair_stages[0])


    @pl.when(use_low)
    def _():
        arrive(low_stages[1])
        launch(low_stages[2])

    before_z = hz[0].astype(f32) * flag(z > 0)
    after_z = hz[1].astype(f32) * flag(z < nz - 1)
    ends = jnp.concatenate(
        [before_z, after_z, jnp.zeros((LANES - 32, LANES), f32)], axis=0
    ).T.astype(bf16)
    for k, mask in enumerate((flag(a > 0), flag(a < na - 1))):
        for cy in range(CY):
            xp[k * (CX + 1) * pad + cy + 1] = (
                hx[k, cy * RHS : (cy + 1) * RHS, :].astype(f32) * mask
            )
    for k, mask in enumerate((flag(b > 0), flag(b < nb - 1))):
        for cx in range(CX):
            xp[(cx + 1) * pad + k * (CY + 1)] = hy[k, cx].astype(f32) * mask
    q128, lane_all = iota((LANES, PAIRS * LANES), 0), iota((LANES, PAIRS * LANES), 1)
    turn_all, l_all = lane_all // LANES, lax.rem(lane_all, LANES)
    spread = ((q128 == turn_all) & (l_all == 0)) | ((q128 == 16 + turn_all) & (l_all == CZ - 1))
    z_ends[...] = nn(ends, spread.astype(bf16))
    lane64 = iota((RHS, LANES), 1)

    def residual_of(q, carry):
        for h in range(4):
            s = 4 * q + h
            i = (q // 2 + 1) * pad + lax.rem(q, 2) * 4 + h + 1
            x = xp[i]
            diag = 6.0 + d_v[pl.ds(s, 1), :]
            v0, v1, v2 = (v_v[pl.ds(k * SLABS + s, 1), :] for k in range(3))
            end = z_ends[(h % 2) * RHS : (h % 2 + 1) * RHS, rows_at((2 * q + h // 2) * LANES, LANES)]
            before = jnp.where(lane64 == 0, end, pltpu.roll(x, 1, 1))
            after = jnp.where(lane64 == CZ - 1, end, pltpu.roll(x, CZ - 1, 1))
            res = slab(r_v, s) - diag * x
            res = res + (1.0 + v0) * xp[i - pad] + (1.0 - v0) * xp[i + pad]
            res = res + (1.0 + v1) * xp[i - 1] + (1.0 - v1) * xp[i + 1]
            res = res + (1.0 + v2) * before + (1.0 - v2) * after
            r_v[pl.ds(s, RHS, stride=SLABS), :] = res
            at = slice(h * CZ, (h + 1) * CZ)
            res_b[q, :, at] = res.astype(bf16)
            w = res * (1.0 / diag)
            hi, lo = split(w)
            w0[q, :, at] = w
            wh[q, :, at] = hi
            wl[q, :, at] = lo
        return carry

    lax.fori_loop(0, QUADS, residual_of, 0)
    seps = nt(
        jnp.concatenate([res_b[q] for q in range(QUADS)], axis=1),
        jnp.concatenate([oh[q] for q in range(QUADS)], axis=1),
    )
    put_res = pltpu.make_async_copy(r_v, res_o, loc_sem.at[9])
    put_res.start()

    sep_loc[...] = seps.astype(bf16).reshape(members, group, wide)
    me = slot * members + member
    pairs = []
    for d in range(na):
        for e in range(nb):
            if d or e:
                to, far = lax.rem(a + d, na), lax.rem(b + e, nb)
                pairs.append((sep_loc.at[far // 2], sep_in.at[me], (to, far, z)))
    hop = exchange(pairs, sep_in)
    sep_in[me] = sep_loc[member]
    relay(base_stages[2], base_stages[3])
    for c in (1, 2, 3):
        pl.when(split_early)(functools.partial(relayout, c))
    pl.when(pair_low)(lambda: relay(pair_stages[0], pair_stages[1]))
    pl.when(use_low)(lambda: relay(low_stages[2], low_stages[3]))
    hop.wait()
    arrive(base_stages[3])

    row8 = iota((8, LANES), 0)
    left = []
    for i in range(slots):
        v = sep_in[i * members].astype(f32)
        for e in range(1, members):
            v = v + sep_in[i * members + e].astype(f32)
        left.append(v.astype(bf16))
    wide_base = nt(jnp.concatenate(left, axis=1), gath[3].reshape(half, depth))
    gx_here = jnp.zeros((8, LANES), jnp.int32) + a
    for j in range(na):
        both = wide_base[:, j * wide : (j + 1) * wide]
        v = jnp.where(gx_here >= 2, both[8:], both[:8])
        v = jnp.where(lax.rem(gx_here, 2) == 1, pltpu.roll(v, 4, 0), v)
        base[:, j * wide : (j + 1) * wide] = jnp.where(row8 < 4, v, pltpu.roll(v, 4, 0))

    def plane_copies(first, src, dst, step):
        return [
            remote(first + d, src, dst, (a, member * 2 + lax.rem(core + d, 2), z + step))
            for d in range(2)
        ]

    give_base = plane_copies(count[0], base, other.at[core], 1)
    give_state = plane_copies(count[0] + 2, kept, other.at[core], -1)
    count[0] += 4
    pl.when(give_low)(lambda: launch(give_base))

    @pl.when(pair_low)
    def _():
        arrive(pair_stages[1])
        launch(pair_stages[2])

    eacc[...] = jnp.zeros(eacc.shape, f32)

    def earlier_product(q, carry):
        right = jnp.concatenate([wh[q], wl[q], oh[q]], axis=0)
        eacc[:vecs] += nt(vh[q], right)
        eacc[vecs:] += nt(vl[q], right)
        return carry

    here = member * na + a
    fold = vecs // 2
    rowf = iota((8, fold), 0)
    plane_sum, plane_came = exchange_later(
        plane_pairs(lambda to, far: psend.at[far * na + to], pin.at[here]), pin
    )

    def earlier_results():
        main = eacc[:vecs, :LANES] + eacc[vecs:, :LANES]
        main = main.T
        main = main[:RHS] + main[RHS:]
        for i in range(RHS // 8):
            one = main[8 * i : 8 * i + 8, :fold]
            two = main[8 * i : 8 * i + 8, fold:]
            psend[2 * i] = jnp.where(rowf < 4, one, pltpu.roll(two, 4, 0))
            psend[2 * i + 1] = jnp.where(rowf < 4, pltpu.roll(one, 4, 0), two)
        launch(plane_sum)
        for i in range(2):
            values = eacc[i * vecs : (i + 1) * vecs, LANES:].T
            v = values[:SEP]
            for e in range(1, members):
                v = v + values[e * SEP : (e + 1) * SEP]
            gath[2, a, member, :, i * vecs : (i + 1) * vecs] = v.astype(bf16)

    def gather_cells():
        launch(cell_stages[0])
        relay(cell_stages[0], cell_stages[1])
        arrive(cell_stages[1])
        launch(cell_stages[2])
        relay(cell_stages[2], cell_stages[3])

    fw_1 = plane_copies(count[0], stateb.at[0], fw_in.at[core], 1)
    fw_2 = plane_copies(count[0] + 2, stateb.at[0], fw_in.at[core], 2)
    bw_1 = plane_copies(count[0] + 4, stateb.at[1], bw_in.at[core], -1)
    bw_2 = plane_copies(count[0] + 6, stateb.at[1], bw_in.at[core], -2)
    count[0] += 8
    fw_near = all_of(z < nz - 1, jnp.logical_or(even, z == 1))
    fw_far = all_of(even, z >= 2, z <= nz - 4)
    bw_near, bw_far = odd, all_of(odd, z >= 3)
    row_group = iota((16, LANES), 0) // 4

    def pack(v):
        t = [v[:, j * wide : (j + 1) * wide] for j in range(na)]
        return jnp.concatenate(
            [jnp.where(row8 < 4, t[0], t[1]), jnp.where(row8 < 4, t[2], t[3])], axis=0
        )

    def left_of(packed):
        left = []
        for v in packed:
            v = v.astype(f32)
            left += [jnp.where(row_group == j, v, 0.0).astype(bf16) for j in range(na)]
        return jnp.concatenate(left, axis=1)

    def product_of(left, rows):
        out = nt(left, rows.reshape(half, depth)[...])
        out = out[:8] + out[8:]
        return out + pltpu.roll(out, 4, 0)

    first_core = jnp.zeros((8, half), jnp.int32) + core == 0

    def two_steps(left, start, m):
        own, far = product_of(left, gath.at[4]), product_of(left, gath_sib)
        between = (
            other[0] - jnp.where(first_core, own, far),
            other[1] - jnp.where(first_core, far, own),
        )
        return start - product_of(left_of([pack(v).astype(bf16) for v in between]), gath.at[m])

    def products(first, last):
        lax.fori_loop(first, last, earlier_product, 0)

    not_first, not_second = jnp.logical_not(first_before), jnp.logical_not(second_before)
    up_pair_before = all_of(pair_up, up_before)
    up_pair_after = all_of(pair_up, up_after)

    def up_launch(stage):
        launch(up_stages[stage])

    def up_middle():
        relay(up_stages[0], up_stages[1])
        arrive(up_stages[1])
        launch(up_stages[2])

    def pair_begin():
        shift_up.wait_recv()
        launch(pair_stages[0])

    def pair_middle():
        relay(pair_stages[0], pair_stages[1])
        arrive(pair_stages[1])
        launch(pair_stages[2])

    def pair_end():
        arrive(pair_stages[3])
        sibling.start()

    pl.when(up_before)(lambda: launch(up_stages[0]))
    pl.when(up_pair_before)(pair_begin)
    pl.when(first_before)(lambda: products(0, QUADS // 2))
    pl.when(pair_low)(lambda: relay(pair_stages[2], pair_stages[3]))
    pl.when(up_before)(up_middle)
    pl.when(up_pair_before)(pair_middle)
    pl.when(pair_low)(pair_end)

    @pl.when(second_before)
    def _():
        products(QUADS // 2, QUADS)
        earlier_results()

    pl.when(up_before)(lambda: relay(up_stages[2], up_stages[3]))
    pl.when(up_pair_before)(lambda: relay(pair_stages[2], pair_stages[3]))

    pl.when(use_low)(lambda: arrive(low_stages[3]))
    pl.when(pair_low)(sibling.wait_recv)

    @pl.when(z == 0)
    def _():
        state[...] = base[...]

    @pl.when(all_of(z > 0, jnp.logical_not(pair_low)))
    def _():
        arrive(fw_1)
        state[...] = base[...] - product_of(left_of([fw_in[0], fw_in[1]]), gath.at[0])

    @pl.when(pair_low)
    def _():
        arrive(give_base)
        arrive(fw_2)
        state[...] = two_steps(left_of([fw_in[0], fw_in[1]]), base[...], 0)

    @pl.when(fw_near)
    def _():
        stateb[0] = pack(state[...]).astype(bf16)
        launch(fw_1)

    pl.when(fw_far)(lambda: launch(fw_2))

    @pl.when(give_up)
    def _():
        kept[...] = state[...]
        launch(give_state)

    def push_back():
        stateb[1] = pack(state[...]).astype(bf16)
        launch(bw_1)

    @pl.when(z == nz - 1)
    def _():
        push_back()
        launch(bw_2)

    pl.when(up_after)(lambda: launch(up_stages[0]))
    pl.when(up_pair_after)(pair_begin)

    @pl.when(jnp.logical_not(split_early))
    def _():
        for c in range(4):
            relayout(c)

    pl.when(not_first)(lambda: products(0, QUADS // 2))
    pl.when(up_after)(up_middle)
    pl.when(up_pair_after)(pair_middle)

    @pl.when(not_second)
    def _():
        products(QUADS // 2, QUADS)
        earlier_results()

    pl.when(up_after)(lambda: relay(up_stages[2], up_stages[3]))
    pl.when(up_pair_after)(lambda: relay(pair_stages[2], pair_stages[3]))
    pl.when(cells_before)(lambda: launch(cell_stages[0]))
    pl.when(pair_up)(pair_end)

    pl.when(use_up)(lambda: arrive(up_stages[3]))

    @pl.when(cells_before)
    def _():
        relay(cell_stages[0], cell_stages[1])
        arrive(cell_stages[1])
        launch(cell_stages[2])

    pl.when(pair_up)(sibling.wait_recv)
    pl.when(cells_before)(lambda: relay(cell_stages[2], cell_stages[3]))

    @pl.when(all_of(use_up, jnp.logical_not(pair_up)))
    def _():
        arrive(bw_1)
        state[...] = state[...] - product_of(left_of([bw_in[0], bw_in[1]]), gath.at[1])

    @pl.when(pair_up)
    def _():
        arrive(give_state)
        arrive(bw_2)
        state[...] = two_steps(left_of([bw_in[0], bw_in[1]]), state[...], 1)

    pl.when(all_of(odd, use_up))(push_back)
    pl.when(all_of(bw_far, use_up))(lambda: launch(bw_2))

    for j in range(na):
        tiles[j] = state[:, j * wide : (j + 1) * wide]
    ret_came = exchange(plane_pairs(lambda to, far: tiles.at[to], ret.at[here]), ret)
    ret[here] = tiles[a]
    pl.when(jnp.logical_not(cells_before))(gather_cells)

    def total_of(ref, n):
        out = ref[0]
        for i in range(1, n):
            out = out + ref[i]
        return out

    pin[here] = psend[here]
    plane_came.wait()
    arrive(cell_stages[3])
    sol_h, sol_l = split(state[...])
    part = nn(jnp.concatenate([sol_h, sol_l], axis=0), gath[2].reshape(half, 2 * vecs))
    part = part[:8, :vecs] + part[8:, :vecs] + part[:8, vecs:]
    part = jnp.where(rowf < 4, part[:, :fold], part[:, fold:]) + total_of(pin, na * members)
    where_fin = z * 2 + core
    fin[where_fin] = part
    pairs = []
    for d in range(nz):
        for e in range(2):
            if d or e:
                to, kind = lax.rem(z + d, nz), lax.rem(core + e, 2)
                mine_there = fin.at[where_fin]
                pairs.append((mine_there, mine_there, (a, member * 2 + kind, to)))
    hop = exchange(pairs, fin)

    ret_came.wait()
    sol = jnp.concatenate(
        [jnp.where(row8 < 4, ret[2 * i], ret[2 * i + 1]) for i in range(na * members // 2)], axis=0
    )
    sol_h, sol_l = split(sol)
    sol_hl = jnp.concatenate([sol_h, sol_l], axis=1)

    def add_sol(first):
        twice = jnp.concatenate([oh[first], oh[first + 1]], axis=1)
        change = nn(sol_hl, jnp.concatenate([twice, twice], axis=0))
        w0[first] = w0[first] + change[:, : 4 * CZ]
        w0[first + 1] = w0[first + 1] + change[:, 4 * CZ :]

    add_sol(0)
    add_sol(2)
    hop.wait()
    full_in[here] = total_of(fin, nz * 2)
    hop = exchange(plane_pairs(lambda to, far: full_in.at[here], full_in.at[here]), full_in)
    add_sol(4)
    add_sol(6)
    hop.wait()
    for i in range(RHS // 8):
        p, q = full_in[2 * i], full_in[2 * i + 1]
        pt_v[8 * i : 8 * i + 8, :fold] = jnp.where(rowf < 4, p, pltpu.roll(q, 4, 0))
        pt_v[8 * i : 8 * i + 8, fold:] = jnp.where(rowf < 4, pltpu.roll(p, 4, 0), q)
    pin5_put = pltpu.make_async_copy(pt_v, proj_o, loc_sem.at[10])
    pin5_put.start()
    full = pt_v[...]
    hi, lo = split(full)
    pt_hl[:RHS] = hi
    pt_hl[RHS:] = lo

    def project(i, gram):
        for q in (2 * i, 2 * i + 1):
            main = nn(pt_hl[...], vh[q])
            o = w0[q] - (main[:RHS] + main[RHS:] + nn(pt_hl[:RHS], vl[q]))
            hi, lo = split(o)
            both = jnp.concatenate([hi, lo], axis=0)
            orth[q] = both
            gram = gram + nt(both, both)
        return gram

    gram = lax.fori_loop(0, QUADS // 2, project, jnp.zeros((2 * RHS, 2 * RHS), f32))
    gram = gram[:RHS] + gram[RHS:]
    gram = gram + pltpu.roll(gram, RHS, 1)
    put_orth = pltpu.make_async_copy(orth, orth_o, loc_sem.at[11])
    put_orth.start()
    piece = RHS // nz
    g_loc[...] = gram.reshape(nz, piece, LANES)
    hop = share("gz", lambda to: g_loc.at[to], gin1)
    gin1[z] = g_loc[z]
    for wait in sent[:-1]:
        wait()
    del sent[:-1]

    for stage in base_stages + cell_stages:
        for copy in stage:
            copy.wait_send()

    @pl.when(use_low)
    def _():
        for stage in low_stages:
            for copy in stage:
                copy.wait_send()

    @pl.when(use_up)
    def _():
        for stage in up_stages:
            for copy in stage:
                copy.wait_send()

    use_pair = jnp.logical_or(pair_low, pair_up)
    for condition, copies in (
        (use_pair, sum(pair_stages, [])), (use_pair, [sibling]),
        (give_low, [shift_low] + give_base), (give_up, [shift_up] + give_state),
        (fw_near, fw_1), (fw_far, fw_2), (bw_near, bw_1), (bw_far, bw_2),
    ):
        @pl.when(condition)
        def _(copies=copies):
            for copy in copies:
                copy.wait_send()

    hop.wait()
    seat = a * nb + b
    gin2[seat] = total_of(gin1, nz)
    pairs = []
    for d in range(na):
        for e in range(nb):
            if d or e:
                to, far = lax.rem(a + d, na), lax.rem(b + e, nb)
                pairs.append((gin2.at[seat], gin2.at[seat], (to, far, z)))
    exchange(pairs, gin2).wait()
    gin3[z] = total_of(gin2, na * nb)
    share("gz", lambda to: gin3.at[z], gin3).wait()
    put_gram = pltpu.make_async_copy(gin3, gram_o, loc_sem.at[12])
    put_gram.start()
    for wait in sent:
        wait()
    for put in (put_res, pin5_put, put_orth, put_gram):
        put.wait()


def finish_kernel(
    scale, gram_v, orth_h, res_h, proj_h, res_o, new_o, proj_o, chol_o,
    orth, rows_v, new_v, res_v, proj_v, sem,
):
    get = pltpu.make_async_copy(orth_h, orth, sem.at[0])
    hand_on = [
        (pltpu.make_async_copy(res_h, res_v, sem.at[1]), pltpu.make_async_copy(res_v, res_o, sem.at[2])),
        (pltpu.make_async_copy(proj_h, proj_v, sem.at[3]), pltpu.make_async_copy(proj_v, proj_o, sem.at[4])),
    ]
    get.start()
    for copy, _ in hand_on:
        copy.start()
    cholesky_rows(gram_v[...], rows_v)
    rows = rows_v[...]
    lane64, row64 = iota((RHS, LANES), 1), iota((RHS, LANES), 0)
    upper = jnp.where((lane64 >= row64) & (lane64 < RHS), rows * (1.0 / scale), 0.0)
    inverse = jnp.where(lane64 - RHS <= row64, rows * scale, 0.0)
    hi, lo = split(inverse)
    lhs = jnp.where(lane64 < RHS, pltpu.roll(hi.astype(f32), RHS, 1), lo.astype(f32)).astype(bf16)
    lhs = jnp.concatenate([lhs, lhs], axis=1)
    for copy, onward in hand_on:
        copy.wait()
        onward.start()
    get.wait()

    def finish(q, carry):
        hi, lo = orth[q, :RHS], orth[q, RHS:]
        out = nn(lhs, jnp.concatenate([hi, hi, lo, lo], axis=0))
        for h in range(4):
            new_v[pl.ds(4 * q + h, RHS, stride=SLABS), :] = out[:, h * CZ : (h + 1) * CZ]
        return carry

    lax.fori_loop(0, QUADS, finish, 0, unroll=4)
    put_new = pltpu.make_async_copy(new_v, new_o, sem.at[5])
    put_new.start()
    upper = jnp.concatenate([upper, jnp.zeros((LANES - RHS, LANES), f32)], axis=0)
    chol_o[...] = upper.T[:RHS, :RHS]
    for _, onward in hand_on:
        onward.wait()
    put_new.wait()


def body(
    x_field, right_side, diag_shift, velocity, earlier_blocks, sep_cells, low_inv, low_off, up_off
):
    na, nb, nz = (lax.axis_size(n) for n in ("gx", "gy", "gz"))
    members, slots = nb // 2, na * 2
    group, wide = RHS // members, SEP * members
    depth, half = slots * wide, na * wide
    vecs = earlier_blocks.shape[0] * earlier_blocks.shape[1]
    piece = RHS // nz
    vmem = pltpu.VMEM
    scratch = [
        vmem((CX, RHS, CY, CZ), f32),
        vmem((ROWS, CZ), f32),
        vmem((SLABS, CZ), f32),
        vmem((3 * SLABS, CZ), f32),
        vmem((vecs * SLABS, CZ), f32),
        vmem((1, SEP), jnp.int32),
        vmem((3, SEP, depth), bf16),
        vmem(((CX + 2) * (CY + 2), RHS, CZ), f32),
        vmem((CX, CY * RHS, CZ), bf16),
        vmem((2, CY * RHS, CZ), bf16),
        vmem((2, CX, RHS, CZ), bf16),
        vmem((2, 16, LANES), bf16),
        vmem((32, LANES), bf16),
        vmem((LANES, PAIRS * LANES), f32),
        vmem((QUADS, RHS, 4 * CZ), bf16),
        vmem((QUADS, wide, 4 * CZ), bf16),
        vmem((5, na, members, SEP, depth), bf16),
        vmem((na, members, SEP, depth), bf16),
        vmem((QUADS, RHS, 4 * CZ), f32),
        vmem((QUADS, RHS, 4 * CZ), bf16),
        vmem((QUADS, RHS, 4 * CZ), bf16),
        vmem((QUADS, vecs, 4 * CZ), bf16),
        vmem((QUADS, vecs, 4 * CZ), bf16),
        vmem((2 * vecs, 2 * LANES), f32),
        vmem((members, group, wide), bf16),
        vmem((slots * members, group, wide), bf16),
        vmem((8, half), f32),
        vmem((8, half), f32),
        vmem((2, 16, wide), bf16),
        vmem((na, 8, wide), f32),
        vmem((2, 16, wide), bf16),
        vmem((2, 16, wide), bf16),
        vmem((na * members, 8, wide), f32),
        vmem((8, half), f32),
        vmem((2, 8, half), f32),
        vmem((na * members, 8, vecs // 2), f32),
        vmem((na * members, 8, vecs // 2), f32),
        vmem((2 * nz, 8, vecs // 2), f32),
        vmem((na * members, 8, vecs // 2), f32),
        vmem((RHS, vecs), f32),
        vmem((2 * RHS, vecs), bf16),
        vmem((QUADS, 2 * RHS, 4 * CZ), bf16),
        vmem((nz, piece, LANES), f32),
        vmem((nz, piece, LANES), f32),
        vmem((na * nb, piece, LANES), f32),
        vmem((nz, piece, LANES), f32),
        pltpu.SemaphoreType.DMA((19,)),
        pltpu.SemaphoreType.DMA((160,)),
        pltpu.SemaphoreType.DMA((160,)),
    ]
    flat = lambda v: v.reshape(-1, CZ)
    anywhere = pl.BlockSpec(memory_space=pl.ANY)
    in_vmem = pl.BlockSpec(memory_space=pltpu.VMEM)
    res, orth, projection, gram = pl.pallas_call(
        functools.partial(kernel, na, nb, nz),
        out_shape=(
            jax.ShapeDtypeStruct((ROWS, CZ), f32),
            jax.ShapeDtypeStruct((QUADS, 2 * RHS, 4 * CZ), bf16),
            jax.ShapeDtypeStruct((RHS, vecs), f32),
            jax.ShapeDtypeStruct((nz, piece, LANES), f32),
        ),
        in_specs=[anywhere] * 9,
        out_specs=(anywhere,) * 4,
        scratch_shapes=scratch,
        compiler_params=pltpu.CompilerParams(
            collective_id=0, has_side_effects=True, vmem_limit_bytes=60 * 2**20
        ),
        cost_estimate=pl.CostEstimate(
            flops=2 * 10**9, bytes_accessed=13 * 2**20, transcendentals=0
        ),
        name="step",
    )(
        x_field, flat(right_side), flat(diag_shift), flat(velocity), flat(earlier_blocks),
        sep_cells, low_inv[0], low_off[0], up_off[0],
    )
    res, new, projection, factor = pl.pallas_call(
        functools.partial(finish_kernel, math.sqrt(na * nb * nz * CX * CY * CZ)),
        out_shape=(
            jax.ShapeDtypeStruct((ROWS, CZ), f32),
            jax.ShapeDtypeStruct((ROWS, CZ), f32),
            jax.ShapeDtypeStruct((RHS, vecs), f32),
            jax.ShapeDtypeStruct((RHS, RHS), f32),
        ),
        in_specs=[in_vmem, anywhere, anywhere, anywhere],
        out_specs=(anywhere, anywhere, anywhere, in_vmem),
        scratch_shapes=[
            vmem((QUADS, 2 * RHS, 4 * CZ), bf16),
            vmem((RHS, LANES), f32),
            vmem((ROWS, CZ), f32),
            vmem((ROWS, CZ), f32),
            vmem((RHS, vecs), f32),
            pltpu.SemaphoreType.DMA((6,)),
        ],
        compiler_params=pltpu.CompilerParams(vmem_limit_bytes=60 * 2**20),
        cost_estimate=pl.CostEstimate(flops=2 * 10**8, bytes_accessed=5 * 2**20, transcendentals=0),
        name="finish",
    )(gram.reshape(RHS, LANES), orth, res, projection)
    shape = right_side.shape
    return (res.reshape(shape), new.reshape(shape), projection.T, factor)


def solution(mesh):
    return jax.shard_map(
        body,
        mesh=mesh,
        in_specs=(
            P(None, "gx", "gy", "gz"),
            P(None, "gx", "gy", "gz"),
            P("gx", "gy", "gz"),
            P(None, "gx", "gy", "gz"),
            P(None, None, "gx", "gy", "gz"),
            P("gz", ("gx", "gy")),
            P("gz", ("gx", "gy"), None),
            P("gz", ("gx", "gy"), None),
            P("gz", ("gx", "gy"), None),
        ),
        out_specs=(P(None, "gx", "gy", "gz"), P(None, "gx", "gy", "gz"), P(), P()),
        check_vma=False,
    )
```

```python
import functools
import math

import jax
import jax.numpy as jnp
from jax import lax
from jax.experimental import pallas as pl
from jax.experimental.pallas import tpu as pltpu
from jax.sharding import PartitionSpec as P

bf16, f32 = jnp.bfloat16, jnp.float32
RHS, CX, CY, CZ, SEP = 64, 4, 8, 128, 32
SLABS = CX * CY
PAIRS = SLABS // 2
QUADS = SLABS // 4
ROWS = RHS * SLABS
LANES = 128


def nt(a, b):
    return lax.dot_general(a, b, (((1,), (1,)), ((), ())), preferred_element_type=f32)


def nn(a, b):
    return jnp.dot(a, b, preferred_element_type=f32)


def split(v):
    hi = v.astype(bf16)
    return hi, (v - hi.astype(f32)).astype(bf16)


def iota(shape, dim):
    return lax.broadcasted_iota(jnp.int32, shape, dim)


def flag(cond):
    return jnp.where(cond, jnp.float32(1.0), jnp.float32(0.0))


def cholesky_rows(gram, out):
    n = RHS
    lane8, row8 = iota((8, LANES), 1), iota((8, LANES), 0)
    blocks = []
    for k in range(n // 8):
        eye = (lane8 - n == row8 + 8 * k).astype(f32)
        blocks.append(jnp.where(lane8 < n, gram[8 * k : 8 * k + 8, :], eye))

    def sublane(v, r):
        return jnp.broadcast_to(v[r : r + 1, :], (8, LANES))

    def panel(turn, blocks):
        first = blocks[0]
        columns = [jnp.broadcast_to(first[:, j : j + 1], (8, LANES)) for j in range(8)]
        entry = {(i, j): sublane(columns[j], i) for j in range(8) for i in range(j, 8)}
        rows = [sublane(first, i) for i in range(8)]
        for j in range(8):
            root = lax.rsqrt(entry[j, j])
            rows[j] = rows[j] * root
            for i in range(j + 1, 8):
                entry[i, j] = entry[i, j] * root
            for i in range(j + 1, 8):
                rows[i] = rows[i] - entry[i, j] * rows[j]
                for k in range(j + 1, i + 1):
                    entry[i, k] = entry[i, k] - entry[i, j] * entry[k, j]
        done = rows[0]
        for i in range(1, 8):
            done = jnp.where(row8 == i, rows[i], done)
        hi = done.astype(bf16).astype(f32)
        mid = (done - hi).astype(bf16).astype(f32)
        low = done - hi - mid
        left = jnp.concatenate([hi, hi, mid, hi, low, mid], axis=0).astype(bf16)
        right = jnp.concatenate([hi, mid, hi, low, hi, mid], axis=0).astype(bf16)
        change = lax.dot_general(
            left, right, (((0,), (0,)), ((), ())), preferred_element_type=f32
        )
        out[pl.ds(pl.multiple_of(turn * 8, 8), 8), :] = pltpu.roll(done, turn * 8, 1)
        rest = [
            pltpu.roll(blocks[k] - change[8 * k : 8 * k + 8], LANES - 8, 1)
            for k in range(1, n // 8)
        ]
        return tuple(rest + [jnp.zeros((8, LANES), f32)])

    lax.fori_loop(0, n // 8, panel, tuple(blocks))


def kernel(
    na, nb, nz,
    x_h, r_h, d_h, v_h, e_h, c_h, li_h, lo_h, up_h,
    res_o, orth_o, proj_o, gram_o,
    x_v, r_v, d_v, v_v, e_v, c_v, m_v,
    xp, xsb, hx, hy, hz, zsend, z_ends, res_b, oh, gath, gath_sib,
    w0, wh, wl, vh, vl, eacc, cell_v, sol_v,
    sep_loc, sep_in, base, state, stateb, tiles, fw_in, bw_in, ret, kept, other,
    psend, pin, fin, full_in, pt_v, pt_hl,
    orth, g_loc, gin1, gin2, gin3,
    loc_sem, send_sem, recv_sem,
):
    a, b, z = lax.axis_index("gx"), lax.axis_index("gy"), lax.axis_index("gz")
    size = {"gx": na, "gy": nb, "gz": nz}
    pos = {"gx": a, "gy": b, "gz": z}
    members, slots = nb // 2, na * 2
    member, core = b // 2, lax.rem(b, 2)
    slot = core * na + a
    group = RHS // members
    wide = SEP * members
    depth = slots * wide
    half = na * wide
    count = [0]
    sent = []

    def place(axis, index):
        if axis == "member":
            return (a, index * 2 + core, z)
        if axis == "slot":
            return (lax.rem(index, na), member * 2 + index // na, z)
        at = dict(pos)
        at[axis] = index
        return (at["gx"], at["gy"], at["gz"])

    size["member"], size["slot"] = members, slots
    pos_of = dict(pos, member=member, slot=slot)

    def remote(n, src, dst, where):
        return pltpu.make_async_remote_copy(
            src_ref=src, dst_ref=dst, send_sem=send_sem.at[n], recv_sem=recv_sem.at[n],
            device_id=where, device_id_type=pl.DeviceIdType.MESH,
        )

    def send(src, dst, where):
        copy = remote(count[0], src, dst, where)
        count[0] += 1
        copy.start()
        sent.append(copy.wait_send)
        return copy

    def exchange_later(pairs, dst):
        n = count[0]
        count[0] += 1
        copies = [remote(n, *pair) for pair in pairs]
        whole = dst.at[pl.ds(0, len(pairs))]
        out = pltpu.make_async_copy(whole, whole, send_sem.at[n])
        sent.append(out.wait)
        return copies, pltpu.make_async_copy(whole, whole, recv_sem.at[n])

    def exchange(pairs, dst):
        copies, came = exchange_later(pairs, dst)
        for copy in copies:
            copy.start()
        return came

    def plane_pairs(src_of, there):
        pairs = []
        for d in range(na):
            for e in range(members):
                if d or e:
                    to, far = lax.rem(a + d, na), lax.rem(member + e, members)
                    pairs.append((src_of(to, far), there, (to, far * 2 + core, z)))
        return pairs

    def share(axis, src_of, dst):
        n = size[axis]
        others = [lax.rem(pos_of[axis] + d, n) for d in range(1, n)]
        there = dst.at[pos_of[axis]]
        return exchange([(src_of(to), there, place(axis, to)) for to in others], dst)

    def arrive(copies):
        for copy in copies:
            copy.wait_recv()

    barrier = pltpu.get_barrier_semaphore()
    partners = 0

    def greet(where):
        pl.semaphore_signal(
            barrier, inc=1, device_id=where, device_id_type=pl.DeviceIdType.MESH
        )

    for axis in ("gy", "gz"):
        for d in range(1, size[axis]):
            greet(place(axis, lax.rem(pos[axis] + d, size[axis])))
            partners += 1
    for d in range(1, na):
        for e in range(nb):
            greet((lax.rem(a + d, na), lax.rem(b + e, nb), z))
            partners += 1

    def fetch(n, src, dst):
        copy = pltpu.make_async_copy(src, dst, loc_sem.at[n])
        copy.start()
        return copy

    x_order = (0, CX - 1) + tuple(range(1, CX - 1))
    get_x = {cx: fetch((0, 16, 17, 18)[cx], x_h.at[:, cx], x_v.at[cx]) for cx in x_order}
    get_m = [fetch(1 + i, h, m_v.at[i]) for i, h in enumerate((li_h, lo_h, up_h))]
    get_c = fetch(4, c_h, c_v)
    get_d = fetch(5, d_h, d_v)
    get_v = fetch(6, v_h, v_v)
    get_r = fetch(7, r_h, r_v)
    chunk = e_v.shape[0] // 4
    get_e = [
        fetch((8, 13, 14, 15)[i], e_h.at[pl.ds(i * chunk, chunk)], e_v.at[pl.ds(i * chunk, chunk)])
        for i in range(4)
    ]

    def slab(ref, s, n=RHS):
        return ref[pl.ds(s, n, stride=SLABS), :]

    def rows_at(start, n):
        return pl.ds(pl.multiple_of(start, n), n)

    pad = CY + 2
    q32, lane_all = iota((32, PAIRS * LANES), 0), iota((32, PAIRS * LANES), 1)
    turn_all, l_all = lane_all // LANES, lax.rem(lane_all, LANES)
    pick = ((q32 == turn_all) & (l_all == CZ - 1)) | ((q32 == 16 + turn_all) & (l_all == 0))
    pick = pick.astype(bf16)

    def spread_x(cx):
        get_x[cx].wait()
        rows = x_v.at[cx].reshape(RHS * CY, CZ)
        for cy in range(CY):
            v = rows[pl.ds(cy, RHS, stride=CY), :]
            xp[(cx + 1) * pad + cy + 1] = v
            xsb[cx, cy * RHS : (cy + 1) * RHS, :] = v.astype(bf16)

    def ring(axis, step):
        n = size[axis]
        return place(axis, lax.rem(pos_of[axis] + step + n, n))

    spread_x(x_order[0])
    spread_x(x_order[1])
    pl.semaphore_wait(barrier, partners)
    halo = [
        send(xsb.at[CX - 1], hx.at[0], ring("gx", 1)),
        send(xsb.at[0], hx.at[1], ring("gx", -1)),
    ]
    for cx in x_order[2:]:
        spread_x(cx)
    halo += [
        send(xsb.at[:, pl.ds((CY - 1) * RHS, RHS)], hy.at[0], ring("gy", 1)),
        send(xsb.at[:, pl.ds(0, RHS)], hy.at[1], ring("gy", -1)),
    ]
    rows = jnp.concatenate(
        [xsb[p // 4, (p % 4) * LANES : (p % 4 + 1) * LANES, :] for p in range(PAIRS)], axis=1
    )
    zsend[...] = nt(pick, rows).astype(bf16)
    halo += [
        send(zsend.at[pl.ds(0, 16)], hz.at[0], ring("gz", 1)),
        send(zsend.at[pl.ds(16, 16)], hz.at[1], ring("gz", -1)),
    ]

    mine = rows_at(member * SEP, SEP)
    lane_group = iota((SEP, LANES), 1) // SEP
    per_tile = LANES // SEP
    for i in range(3):
        get_m[i].wait()

    def reorder(i):
        pieces = [
            m_v[i, :, t * LANES : (t + 1) * LANES].astype(f32) for t in range(depth // LANES)
        ]
        for t in range(depth // LANES):
            out = jnp.zeros((SEP, LANES), f32)
            for g in range(per_tile):
                old = (t % na) * nb + g * 2 + t // na
                piece = pieces[old // per_tile]
                shift = ((g - old % per_tile) * SEP) % LANES
                if shift:
                    piece = pltpu.roll(piece, shift, 1)
                out = jnp.where(lane_group == g, piece, out)
            at = slice(t * LANES, (t + 1) * LANES)
            gath[(3, 0, 1)[i], a, member, :, at] = out.astype(bf16)

    for i in range(3):
        reorder(i)

    axes = ("member", "gx")

    def own(m, c):
        return gath.at[m, a, member, :, pl.ds(c * half, half)]

    def near(m, c, axis, step, part):
        at = ring_index(axis, step)
        rows = pl.ds(part * (SEP // 2), SEP // 2)
        if axis == "member":
            return gath.at[m, a, at, rows, pl.ds(c * half, half)]
        return gath.at[m, at, member, rows, pl.ds(c * half, half)]

    def line(m, c, axis, step):
        at = ring_index(axis, step)
        if axis == "member":
            return gath.at[m, :, at, :, pl.ds(c * half, half)]
        return gath.at[m, at, :, :, pl.ds(c * half, half)]

    def near_line(m, c, axis, step, part):
        at = ring_index(axis, step)
        cut = pl.ds(part * 2, 2)
        if axis == "member":
            return gath.at[m, cut, at, :, pl.ds(c * half, half)]
        return gath.at[m, at, cut, :, pl.ds(c * half, half)]

    def ring_index(axis, step):
        return lax.rem(pos_of[axis] + step + size[axis], size[axis])

    def later(src, where):
        copy = remote(count[0], src, src, where)
        count[0] += 1
        return copy

    def ring_pair(block, axis):
        return [later(block, ring(axis, step)) for step in (1, -1)]

    def gather_stages(m):
        one, two, three, four = [], [], [], []
        for c in range(2):
            first, second = axes[c], axes[1 - c]
            one += ring_pair(own(m, c), first)
            three += ring_pair(line(m, c, second, 0), second)
            for part, step in enumerate((1, -1)):
                two.append(later(near(m, c, first, -step, part), ring(first, step)))
                four.append(later(near_line(m, c, second, -step, part), ring(second, step)))
        return one, two, three, four

    def launch(copies):
        for copy in copies:
            copy.start()

    def relay(came, onward):
        for got, copy in zip(came, onward):
            got.wait_recv()
            copy.start()

    low_stages, up_stages, cell_stages, base_stages, pair_stages = (
        gather_stages(m) for m in range(5)
    )
    use_low, use_up = z > 0, z < nz - 1
    odd = lax.rem(z, 2) == 1
    even = jnp.logical_not(odd)

    def all_of(*conditions):
        return functools.reduce(jnp.logical_and, conditions)

    pair_low = all_of(even, z >= 4)
    pair_up = all_of(odd, z <= nz - 3)
    give_low = all_of(odd, z >= 3, z <= nz - 3)
    give_up = all_of(even, z >= 2)
    up_after = z < (nz * 5) // 8
    up_before = all_of(use_up, jnp.logical_not(up_after))
    first_before = z >= 3
    second_before = all_of(odd, z >= 3)
    cells_here = z <= 2
    owners_add = jnp.logical_not(cells_here)

    def shift_copy(m, step):
        n = count[0]
        count[0] += 1
        return remote(n, gath.at[m, a, member], gath.at[4, a, member], (a, b, z + step))

    shift_low, shift_up = shift_copy(0, 1), shift_copy(1, -1)
    sibling = remote(count[0], gath.at[4], gath_sib, (a, member * 2 + 1 - core, z))
    count[0] += 1
    launch(base_stages[0])
    pl.when(use_low)(lambda: launch(low_stages[0]))
    pl.when(give_low)(shift_low.start)
    pl.when(give_up)(shift_up.start)

    get_c.wait()
    cells = jnp.broadcast_to(c_v[...], (SEP, SEP)).astype(f32)
    square = iota((SEP, SEP), 0) == iota((SEP, SEP), 1)
    column = jnp.sum(jnp.where(square, cells, 0.0), axis=1, keepdims=True)
    column = jnp.broadcast_to(column, (SEP, 4 * CZ))
    z512 = iota((SEP, 4 * CZ), 1)

    def mark(q, carry):
        oh[q] = jnp.zeros((wide, 4 * CZ), bf16)
        at = (z512 + q * 4 * CZ).astype(f32)
        oh[q, mine, :] = jnp.where(column == at, 1.0, 0.0).astype(bf16)
        return carry

    lax.fori_loop(0, QUADS, mark, 0)

    vecs = e_v.shape[0] // SLABS
    part_vecs = vecs // 4

    def relayout(c):
        get_e[c].wait()
        at = slice(c * part_vecs, (c + 1) * part_vecs)

        def step(q, carry):
            for h in range(4):
                rows = pl.ds(c * chunk + 4 * q + h, part_vecs, stride=SLABS)
                hi, lo = split(e_v[rows, :])
                vh[q, at, h * CZ : (h + 1) * CZ] = hi
                vl[q, at, h * CZ : (h + 1) * CZ] = lo
            return carry

        lax.fori_loop(0, QUADS, step, 0)

    split_early = z >= 2
    pl.when(split_early)(lambda: relayout(0))
    get_d.wait()
    get_v.wait()
    get_r.wait()
    relay(base_stages[0], base_stages[1])
    pl.when(use_low)(lambda: relay(low_stages[0], low_stages[1]))
    arrive(halo)
    arrive(base_stages[1])
    launch(base_stages[2])

    @pl.when(pair_low)
    def _():
        shift_low.wait_recv()
        launch(pair_stages[0])


    @pl.when(use_low)
    def _():
        arrive(low_stages[1])
        launch(low_stages[2])

    before_z = hz[0].astype(f32) * flag(z > 0)
    after_z = hz[1].astype(f32) * flag(z < nz - 1)
    ends = jnp.concatenate(
        [before_z, after_z, jnp.zeros((LANES - 32, LANES), f32)], axis=0
    ).T.astype(bf16)
    for k, mask in enumerate((flag(a > 0), flag(a < na - 1))):
        for cy in range(CY):
            xp[k * (CX + 1) * pad + cy + 1] = (
                hx[k, cy * RHS : (cy + 1) * RHS, :].astype(f32) * mask
            )
    for k, mask in enumerate((flag(b > 0), flag(b < nb - 1))):
        for cx in range(CX):
            xp[(cx + 1) * pad + k * (CY + 1)] = hy[k, cx].astype(f32) * mask
    q128, lane_all = iota((LANES, PAIRS * LANES), 0), iota((LANES, PAIRS * LANES), 1)
    turn_all, l_all = lane_all // LANES, lax.rem(lane_all, LANES)
    spread = ((q128 == turn_all) & (l_all == 0)) | ((q128 == 16 + turn_all) & (l_all == CZ - 1))
    z_ends[...] = nn(ends, spread.astype(bf16))
    lane64 = iota((RHS, LANES), 1)

    def residual_of(q, carry):
        for h in range(4):
            s = 4 * q + h
            i = (q // 2 + 1) * pad + lax.rem(q, 2) * 4 + h + 1
            x = xp[i]
            diag = 6.0 + d_v[pl.ds(s, 1), :]
            v0, v1, v2 = (v_v[pl.ds(k * SLABS + s, 1), :] for k in range(3))
            end = z_ends[(h % 2) * RHS : (h % 2 + 1) * RHS, rows_at((2 * q + h // 2) * LANES, LANES)]
            before = jnp.where(lane64 == 0, end, pltpu.roll(x, 1, 1))
            after = jnp.where(lane64 == CZ - 1, end, pltpu.roll(x, CZ - 1, 1))
            res = slab(r_v, s) - diag * x
            res = res + (1.0 + v0) * xp[i - pad] + (1.0 - v0) * xp[i + pad]
            res = res + (1.0 + v1) * xp[i - 1] + (1.0 - v1) * xp[i + 1]
            res = res + (1.0 + v2) * before + (1.0 - v2) * after
            r_v[pl.ds(s, RHS, stride=SLABS), :] = res
            at = slice(h * CZ, (h + 1) * CZ)
            res_b[q, :, at] = res.astype(bf16)
            w = res * (1.0 / diag)
            hi, lo = split(w)
            w0[q, :, at] = w
            wh[q, :, at] = hi
            wl[q, :, at] = lo
        return carry

    lax.fori_loop(0, QUADS, residual_of, 0)
    seps = nt(
        jnp.concatenate([res_b[q] for q in range(QUADS)], axis=1),
        jnp.concatenate([oh[q] for q in range(QUADS)], axis=1),
    )
    put_res = pltpu.make_async_copy(r_v, res_o, loc_sem.at[9])
    put_res.start()

    sep_loc[...] = seps.astype(bf16).reshape(members, group, wide)
    me = slot * members + member
    pairs = []
    for d in range(na):
        for e in range(nb):
            if d or e:
                to, far = lax.rem(a + d, na), lax.rem(b + e, nb)
                pairs.append((sep_loc.at[far // 2], sep_in.at[me], (to, far, z)))
    hop = exchange(pairs, sep_in)
    sep_in[me] = sep_loc[member]
    relay(base_stages[2], base_stages[3])
    for c in (1, 2, 3):
        pl.when(split_early)(functools.partial(relayout, c))
    pl.when(pair_low)(lambda: relay(pair_stages[0], pair_stages[1]))
    pl.when(use_low)(lambda: relay(low_stages[2], low_stages[3]))
    hop.wait()
    arrive(base_stages[3])

    row8 = iota((8, LANES), 0)
    left = []
    for i in range(slots):
        v = sep_in[i * members].astype(f32)
        for e in range(1, members):
            v = v + sep_in[i * members + e].astype(f32)
        left.append(v.astype(bf16))
    wide_base = nt(jnp.concatenate(left, axis=1), gath[3].reshape(half, depth))
    gx_here = jnp.zeros((8, LANES), jnp.int32) + a
    for j in range(na):
        both = wide_base[:, j * wide : (j + 1) * wide]
        v = jnp.where(gx_here >= 2, both[8:], both[:8])
        v = jnp.where(lax.rem(gx_here, 2) == 1, pltpu.roll(v, 4, 0), v)
        base[:, j * wide : (j + 1) * wide] = jnp.where(row8 < 4, v, pltpu.roll(v, 4, 0))

    def plane_copies(first, src, dst, step):
        return [
            remote(first + d, src, dst, (a, member * 2 + lax.rem(core + d, 2), z + step))
            for d in range(2)
        ]

    give_base = plane_copies(count[0], base, other.at[core], 1)
    give_state = plane_copies(count[0] + 2, kept, other.at[core], -1)
    count[0] += 4
    pl.when(give_low)(lambda: launch(give_base))

    @pl.when(pair_low)
    def _():
        arrive(pair_stages[1])
        launch(pair_stages[2])

    eacc[...] = jnp.zeros(eacc.shape, f32)

    def earlier_product(q, carry):
        right = jnp.concatenate([wh[q], wl[q], oh[q]], axis=0)
        eacc[:vecs] += nt(vh[q], right)
        eacc[vecs:] += nt(vl[q], right)
        return carry

    here = member * na + a
    fold = vecs // 2
    rowf = iota((8, fold), 0)
    plane_sum, plane_came = exchange_later(
        plane_pairs(lambda to, far: psend.at[far * na + to], pin.at[here]), pin
    )

    def send_sums(main):
        for i in range(RHS // 8):
            one = main[8 * i : 8 * i + 8, :fold]
            two = main[8 * i : 8 * i + 8, fold:]
            psend[2 * i] = jnp.where(rowf < 4, one, pltpu.roll(two, 4, 0))
            psend[2 * i + 1] = jnp.where(rowf < 4, pltpu.roll(one, 4, 0), two)
        launch(plane_sum)

    def earlier_results():
        main = eacc[:vecs, :LANES] + eacc[vecs:, :LANES]
        main = main.T
        main = main[:RHS] + main[RHS:]

        @pl.when(cells_here)
        def _():
            send_sums(main)
            for i in range(2):
                values = eacc[i * vecs : (i + 1) * vecs, LANES:].T
                v = values[:SEP]
                for e in range(1, members):
                    v = v + values[e * SEP : (e + 1) * SEP]
                gath[2, a, member, :, i * vecs : (i + 1) * vecs] = v.astype(bf16)

        @pl.when(owners_add)
        def _():
            pt_v[...] = main
            for i in range(2):
                cell_v[i] = eacc[i * vecs : (i + 1) * vecs, LANES:].T.astype(bf16)

    fw_1 = plane_copies(count[0], stateb.at[0], fw_in.at[core], 1)
    fw_2 = plane_copies(count[0] + 2, stateb.at[0], fw_in.at[core], 2)
    bw_1 = plane_copies(count[0] + 4, stateb.at[1], bw_in.at[core], -1)
    bw_2 = plane_copies(count[0] + 6, stateb.at[1], bw_in.at[core], -2)
    count[0] += 8
    fw_near = all_of(z < nz - 1, jnp.logical_or(even, z == 1))
    fw_far = all_of(even, z >= 2, z <= nz - 4)
    bw_near, bw_far = odd, all_of(odd, z >= 3)
    row_group = iota((16, LANES), 0) // 4

    def pack(v):
        t = [v[:, j * wide : (j + 1) * wide] for j in range(na)]
        return jnp.concatenate(
            [jnp.where(row8 < 4, t[0], t[1]), jnp.where(row8 < 4, t[2], t[3])], axis=0
        )

    def left_of(packed):
        left = []
        for v in packed:
            v = v.astype(f32)
            left += [jnp.where(row_group == j, v, 0.0).astype(bf16) for j in range(na)]
        return jnp.concatenate(left, axis=1)

    def product_of(left, rows):
        out = nt(left, rows.reshape(half, depth)[...])
        out = out[:8] + out[8:]
        return out + pltpu.roll(out, 4, 0)

    first_core = jnp.zeros((8, half), jnp.int32) + core == 0

    def two_steps(left, start, m):
        own, far = product_of(left, gath.at[4]), product_of(left, gath_sib)
        between = (
            other[0] - jnp.where(first_core, own, far),
            other[1] - jnp.where(first_core, far, own),
        )
        return start - product_of(left_of([pack(v).astype(bf16) for v in between]), gath.at[m])

    def products(first, last):
        lax.fori_loop(first, last, earlier_product, 0)

    not_first, not_second = jnp.logical_not(first_before), jnp.logical_not(second_before)
    up_pair_before = all_of(pair_up, up_before)
    up_pair_after = all_of(pair_up, up_after)

    def up_launch(stage):
        launch(up_stages[stage])

    def up_middle():
        relay(up_stages[0], up_stages[1])
        arrive(up_stages[1])
        launch(up_stages[2])

    def pair_begin():
        shift_up.wait_recv()
        launch(pair_stages[0])

    def pair_middle():
        relay(pair_stages[0], pair_stages[1])
        arrive(pair_stages[1])
        launch(pair_stages[2])

    def pair_end():
        arrive(pair_stages[3])
        sibling.start()

    pl.when(up_before)(lambda: launch(up_stages[0]))
    pl.when(up_pair_before)(pair_begin)
    pl.when(first_before)(lambda: products(0, QUADS // 2))
    pl.when(pair_low)(lambda: relay(pair_stages[2], pair_stages[3]))
    pl.when(up_before)(up_middle)
    pl.when(up_pair_before)(pair_middle)
    pl.when(pair_low)(pair_end)

    @pl.when(second_before)
    def _():
        products(QUADS // 2, QUADS)
        earlier_results()

    pl.when(up_before)(lambda: relay(up_stages[2], up_stages[3]))
    pl.when(up_pair_before)(lambda: relay(pair_stages[2], pair_stages[3]))

    pl.when(use_low)(lambda: arrive(low_stages[3]))
    pl.when(pair_low)(sibling.wait_recv)

    @pl.when(z == 0)
    def _():
        state[...] = base[...]

    @pl.when(all_of(z > 0, jnp.logical_not(pair_low)))
    def _():
        arrive(fw_1)
        state[...] = base[...] - product_of(left_of([fw_in[0], fw_in[1]]), gath.at[0])

    @pl.when(pair_low)
    def _():
        arrive(give_base)
        arrive(fw_2)
        state[...] = two_steps(left_of([fw_in[0], fw_in[1]]), base[...], 0)

    @pl.when(fw_near)
    def _():
        stateb[0] = pack(state[...]).astype(bf16)
        launch(fw_1)

    pl.when(fw_far)(lambda: launch(fw_2))

    @pl.when(give_up)
    def _():
        kept[...] = state[...]
        launch(give_state)

    def push_back():
        stateb[1] = pack(state[...]).astype(bf16)
        launch(bw_1)

    @pl.when(z == nz - 1)
    def _():
        push_back()
        launch(bw_2)

    pl.when(up_after)(lambda: launch(up_stages[0]))
    pl.when(up_pair_after)(pair_begin)

    @pl.when(jnp.logical_not(split_early))
    def _():
        for c in range(4):
            relayout(c)

    pl.when(not_first)(lambda: products(0, QUADS // 2))
    pl.when(up_after)(up_middle)
    pl.when(up_pair_after)(pair_middle)

    @pl.when(not_second)
    def _():
        products(QUADS // 2, QUADS)
        earlier_results()

    pl.when(up_after)(lambda: relay(up_stages[2], up_stages[3]))
    pl.when(up_pair_after)(lambda: relay(pair_stages[2], pair_stages[3]))
    pl.when(cells_here)(lambda: launch(cell_stages[0]))
    pl.when(pair_up)(pair_end)

    pl.when(use_up)(lambda: arrive(up_stages[3]))

    @pl.when(cells_here)
    def _():
        relay(cell_stages[0], cell_stages[1])
        arrive(cell_stages[1])
        launch(cell_stages[2])

    pl.when(pair_up)(sibling.wait_recv)
    pl.when(cells_here)(lambda: relay(cell_stages[2], cell_stages[3]))

    @pl.when(all_of(use_up, jnp.logical_not(pair_up)))
    def _():
        arrive(bw_1)
        state[...] = state[...] - product_of(left_of([bw_in[0], bw_in[1]]), gath.at[1])

    @pl.when(pair_up)
    def _():
        arrive(give_state)
        arrive(bw_2)
        state[...] = two_steps(left_of([bw_in[0], bw_in[1]]), state[...], 1)

    pl.when(all_of(odd, use_up))(push_back)
    pl.when(all_of(bw_far, use_up))(lambda: launch(bw_2))

    for j in range(na):
        tiles[j] = state[:, j * wide : (j + 1) * wide]
    ret_came = exchange(plane_pairs(lambda to, far: tiles.at[to], ret.at[here]), ret)
    ret[here] = tiles[a]

    def total_of(ref, n):
        out = ref[0]
        for i in range(1, n):
            out = out + ref[i]
        return out

    def take_sol():
        ret_came.wait()
        sol = jnp.concatenate(
            [jnp.where(row8 < 4, ret[2 * i], ret[2 * i + 1]) for i in range(na * members // 2)],
            axis=0,
        )
        sol_v[...] = jnp.concatenate(split(sol), axis=1)

    @pl.when(owners_add)
    def _():
        take_sol()
        sol_h, sol_l = sol_v[:, :wide], sol_v[:, wide:]
        part = nn(jnp.concatenate([sol_h, sol_l], axis=0), cell_v[0])
        send_sums(pt_v[...] + part[:RHS] + part[RHS:] + nn(sol_h, cell_v[1]))

    pin[here] = psend[here]
    plane_came.wait()
    where_fin = z * 2 + core
    fin[where_fin] = total_of(pin, na * members)

    @pl.when(cells_here)
    def _():
        arrive(cell_stages[3])
        part = nn(jnp.concatenate(split(state[...]), axis=0), gath[2].reshape(half, 2 * vecs))
        part = part[:8, :vecs] + part[8:, :vecs] + part[:8, vecs:]
        fin[where_fin] = fin[where_fin] + jnp.where(rowf < 4, part[:, :fold], part[:, fold:])

    pairs = []
    for d in range(nz):
        for e in range(2):
            if d or e:
                to, kind = lax.rem(z + d, nz), lax.rem(core + e, 2)
                mine_there = fin.at[where_fin]
                pairs.append((mine_there, mine_there, (a, member * 2 + kind, to)))
    hop = exchange(pairs, fin)

    pl.when(cells_here)(take_sol)
    sol_hl = sol_v[...]

    def add_sol(first):
        twice = jnp.concatenate([oh[first], oh[first + 1]], axis=1)
        change = nn(sol_hl, jnp.concatenate([twice, twice], axis=0))
        w0[first] = w0[first] + change[:, : 4 * CZ]
        w0[first + 1] = w0[first + 1] + change[:, 4 * CZ :]

    add_sol(0)
    add_sol(2)
    hop.wait()
    full_in[here] = total_of(fin, nz * 2)
    hop = exchange(plane_pairs(lambda to, far: full_in.at[here], full_in.at[here]), full_in)
    add_sol(4)
    add_sol(6)
    hop.wait()
    for i in range(RHS // 8):
        p, q = full_in[2 * i], full_in[2 * i + 1]
        pt_v[8 * i : 8 * i + 8, :fold] = jnp.where(rowf < 4, p, pltpu.roll(q, 4, 0))
        pt_v[8 * i : 8 * i + 8, fold:] = jnp.where(rowf < 4, pltpu.roll(p, 4, 0), q)
    pin5_put = pltpu.make_async_copy(pt_v, proj_o, loc_sem.at[10])
    pin5_put.start()
    full = pt_v[...]
    hi, lo = split(full)
    pt_hl[:RHS] = hi
    pt_hl[RHS:] = lo

    def project(i, gram):
        for q in (2 * i, 2 * i + 1):
            main = nn(pt_hl[...], vh[q])
            o = w0[q] - (main[:RHS] + main[RHS:] + nn(pt_hl[:RHS], vl[q]))
            hi, lo = split(o)
            both = jnp.concatenate([hi, lo], axis=0)
            orth[q] = both
            gram = gram + nt(both, both)
        return gram

    gram = lax.fori_loop(0, QUADS // 2, project, jnp.zeros((2 * RHS, 2 * RHS), f32))
    gram = gram[:RHS] + gram[RHS:]
    gram = gram + pltpu.roll(gram, RHS, 1)
    put_orth = pltpu.make_async_copy(orth, orth_o, loc_sem.at[11])
    put_orth.start()
    piece = RHS // nz
    g_loc[...] = gram.reshape(nz, piece, LANES)
    hop = share("gz", lambda to: g_loc.at[to], gin1)
    gin1[z] = g_loc[z]
    for wait in sent[:-1]:
        wait()
    del sent[:-1]

    for stage in base_stages:
        for copy in stage:
            copy.wait_send()

    @pl.when(use_low)
    def _():
        for stage in low_stages:
            for copy in stage:
                copy.wait_send()

    @pl.when(use_up)
    def _():
        for stage in up_stages:
            for copy in stage:
                copy.wait_send()

    use_pair = jnp.logical_or(pair_low, pair_up)
    for condition, copies in (
        (cells_here, sum(cell_stages, [])), (use_pair, sum(pair_stages, [])), (use_pair, [sibling]),
        (give_low, [shift_low] + give_base), (give_up, [shift_up] + give_state),
        (fw_near, fw_1), (fw_far, fw_2), (bw_near, bw_1), (bw_far, bw_2),
    ):
        @pl.when(condition)
        def _(copies=copies):
            for copy in copies:
                copy.wait_send()

    hop.wait()
    seat = a * nb + b
    gin2[seat] = total_of(gin1, nz)
    pairs = []
    for d in range(na):
        for e in range(nb):
            if d or e:
                to, far = lax.rem(a + d, na), lax.rem(b + e, nb)
                pairs.append((gin2.at[seat], gin2.at[seat], (to, far, z)))
    exchange(pairs, gin2).wait()
    gin3[z] = total_of(gin2, na * nb)
    share("gz", lambda to: gin3.at[z], gin3).wait()
    put_gram = pltpu.make_async_copy(gin3, gram_o, loc_sem.at[12])
    put_gram.start()
    for wait in sent:
        wait()
    for put in (put_res, pin5_put, put_orth, put_gram):
        put.wait()


def finish_kernel(
    scale, gram_v, orth_h, res_h, proj_h, res_o, new_o, proj_o, chol_o,
    orth, rows_v, new_v, res_v, proj_v, sem,
):
    get = pltpu.make_async_copy(orth_h, orth, sem.at[0])
    hand_on = [
        (pltpu.make_async_copy(res_h, res_v, sem.at[1]), pltpu.make_async_copy(res_v, res_o, sem.at[2])),
        (pltpu.make_async_copy(proj_h, proj_v, sem.at[3]), pltpu.make_async_copy(proj_v, proj_o, sem.at[4])),
    ]
    get.start()
    for copy, _ in hand_on:
        copy.start()
    cholesky_rows(gram_v[...], rows_v)
    rows = rows_v[...]
    lane64, row64 = iota((RHS, LANES), 1), iota((RHS, LANES), 0)
    upper = jnp.where((lane64 >= row64) & (lane64 < RHS), rows * (1.0 / scale), 0.0)
    inverse = jnp.where(lane64 - RHS <= row64, rows * scale, 0.0)
    hi, lo = split(inverse)
    lhs = jnp.where(lane64 < RHS, pltpu.roll(hi.astype(f32), RHS, 1), lo.astype(f32)).astype(bf16)
    lhs = jnp.concatenate([lhs, lhs], axis=1)
    for copy, onward in hand_on:
        copy.wait()
        onward.start()
    get.wait()

    def finish(q, carry):
        hi, lo = orth[q, :RHS], orth[q, RHS:]
        out = nn(lhs, jnp.concatenate([hi, hi, lo, lo], axis=0))
        for h in range(4):
            new_v[pl.ds(4 * q + h, RHS, stride=SLABS), :] = out[:, h * CZ : (h + 1) * CZ]
        return carry

    lax.fori_loop(0, QUADS, finish, 0, unroll=4)
    put_new = pltpu.make_async_copy(new_v, new_o, sem.at[5])
    put_new.start()
    upper = jnp.concatenate([upper, jnp.zeros((LANES - RHS, LANES), f32)], axis=0)
    chol_o[...] = upper.T[:RHS, :RHS]
    for _, onward in hand_on:
        onward.wait()
    put_new.wait()


def body(
    x_field, right_side, diag_shift, velocity, earlier_blocks, sep_cells, low_inv, low_off, up_off
):
    na, nb, nz = (lax.axis_size(n) for n in ("gx", "gy", "gz"))
    members, slots = nb // 2, na * 2
    group, wide = RHS // members, SEP * members
    depth, half = slots * wide, na * wide
    vecs = earlier_blocks.shape[0] * earlier_blocks.shape[1]
    piece = RHS // nz
    vmem = pltpu.VMEM
    scratch = [
        vmem((CX, RHS, CY, CZ), f32),
        vmem((ROWS, CZ), f32),
        vmem((SLABS, CZ), f32),
        vmem((3 * SLABS, CZ), f32),
        vmem((vecs * SLABS, CZ), f32),
        vmem((1, SEP), jnp.int32),
        vmem((3, SEP, depth), bf16),
        vmem(((CX + 2) * (CY + 2), RHS, CZ), f32),
        vmem((CX, CY * RHS, CZ), bf16),
        vmem((2, CY * RHS, CZ), bf16),
        vmem((2, CX, RHS, CZ), bf16),
        vmem((2, 16, LANES), bf16),
        vmem((32, LANES), bf16),
        vmem((LANES, PAIRS * LANES), f32),
        vmem((QUADS, RHS, 4 * CZ), bf16),
        vmem((QUADS, wide, 4 * CZ), bf16),
        vmem((5, na, members, SEP, depth), bf16),
        vmem((na, members, SEP, depth), bf16),
        vmem((QUADS, RHS, 4 * CZ), f32),
        vmem((QUADS, RHS, 4 * CZ), bf16),
        vmem((QUADS, RHS, 4 * CZ), bf16),
        vmem((QUADS, vecs, 4 * CZ), bf16),
        vmem((QUADS, vecs, 4 * CZ), bf16),
        vmem((2 * vecs, 2 * LANES), f32),
        vmem((2, wide, vecs), bf16),
        vmem((RHS, 2 * wide), bf16),
        vmem((members, group, wide), bf16),
        vmem((slots * members, group, wide), bf16),
        vmem((8, half), f32),
        vmem((8, half), f32),
        vmem((2, 16, wide), bf16),
        vmem((na, 8, wide), f32),
        vmem((2, 16, wide), bf16),
        vmem((2, 16, wide), bf16),
        vmem((na * members, 8, wide), f32),
        vmem((8, half), f32),
        vmem((2, 8, half), f32),
        vmem((na * members, 8, vecs // 2), f32),
        vmem((na * members, 8, vecs // 2), f32),
        vmem((2 * nz, 8, vecs // 2), f32),
        vmem((na * members, 8, vecs // 2), f32),
        vmem((RHS, vecs), f32),
        vmem((2 * RHS, vecs), bf16),
        vmem((QUADS, 2 * RHS, 4 * CZ), bf16),
        vmem((nz, piece, LANES), f32),
        vmem((nz, piece, LANES), f32),
        vmem((na * nb, piece, LANES), f32),
        vmem((nz, piece, LANES), f32),
        pltpu.SemaphoreType.DMA((19,)),
        pltpu.SemaphoreType.DMA((160,)),
        pltpu.SemaphoreType.DMA((160,)),
    ]
    flat = lambda v: v.reshape(-1, CZ)
    anywhere = pl.BlockSpec(memory_space=pl.ANY)
    in_vmem = pl.BlockSpec(memory_space=pltpu.VMEM)
    res, orth, projection, gram = pl.pallas_call(
        functools.partial(kernel, na, nb, nz),
        out_shape=(
            jax.ShapeDtypeStruct((ROWS, CZ), f32),
            jax.ShapeDtypeStruct((QUADS, 2 * RHS, 4 * CZ), bf16),
            jax.ShapeDtypeStruct((RHS, vecs), f32),
            jax.ShapeDtypeStruct((nz, piece, LANES), f32),
        ),
        in_specs=[anywhere] * 9,
        out_specs=(anywhere,) * 4,
        scratch_shapes=scratch,
        compiler_params=pltpu.CompilerParams(
            collective_id=0, has_side_effects=True, vmem_limit_bytes=60 * 2**20
        ),
        cost_estimate=pl.CostEstimate(
            flops=2 * 10**9, bytes_accessed=13 * 2**20, transcendentals=0
        ),
        name="step",
    )(
        x_field, flat(right_side), flat(diag_shift), flat(velocity), flat(earlier_blocks),
        sep_cells, low_inv[0], low_off[0], up_off[0],
    )
    res, new, projection, factor = pl.pallas_call(
        functools.partial(finish_kernel, math.sqrt(na * nb * nz * CX * CY * CZ)),
        out_shape=(
            jax.ShapeDtypeStruct((ROWS, CZ), f32),
            jax.ShapeDtypeStruct((ROWS, CZ), f32),
            jax.ShapeDtypeStruct((RHS, vecs), f32),
            jax.ShapeDtypeStruct((RHS, RHS), f32),
        ),
        in_specs=[in_vmem, anywhere, anywhere, anywhere],
        out_specs=(anywhere, anywhere, anywhere, in_vmem),
        scratch_shapes=[
            vmem((QUADS, 2 * RHS, 4 * CZ), bf16),
            vmem((RHS, LANES), f32),
            vmem((ROWS, CZ), f32),
            vmem((ROWS, CZ), f32),
            vmem((RHS, vecs), f32),
            pltpu.SemaphoreType.DMA((6,)),
        ],
        compiler_params=pltpu.CompilerParams(vmem_limit_bytes=60 * 2**20),
        cost_estimate=pl.CostEstimate(flops=2 * 10**8, bytes_accessed=5 * 2**20, transcendentals=0),
        name="finish",
    )(gram.reshape(RHS, LANES), orth, res, projection)
    shape = right_side.shape
    return (res.reshape(shape), new.reshape(shape), projection.T, factor)


def solution(mesh):
    return jax.shard_map(
        body,
        mesh=mesh,
        in_specs=(
            P(None, "gx", "gy", "gz"),
            P(None, "gx", "gy", "gz"),
            P("gx", "gy", "gz"),
            P(None, "gx", "gy", "gz"),
            P(None, None, "gx", "gy", "gz"),
            P("gz", ("gx", "gy")),
            P("gz", ("gx", "gy"), None),
            P("gz", ("gx", "gy"), None),
            P("gz", ("gx", "gy"), None),
        ),
        out_specs=(P(None, "gx", "gy", "gz"), P(None, "gx", "gy", "gz"), P(), P()),
        check_vma=False,
    )
```

```python
import functools
import math

import jax
import jax.numpy as jnp
from jax import lax
from jax.experimental import pallas as pl
from jax.experimental.pallas import tpu as pltpu
from jax.sharding import PartitionSpec as P

bf16, f32 = jnp.bfloat16, jnp.float32
RHS, CX, CY, CZ, SEP = 64, 4, 8, 128, 32
SLABS = CX * CY
PAIRS = SLABS // 2
QUADS = SLABS // 4
ROWS = RHS * SLABS
LANES = 128


def nt(a, b):
    return lax.dot_general(a, b, (((1,), (1,)), ((), ())), preferred_element_type=f32)


def nn(a, b):
    return jnp.dot(a, b, preferred_element_type=f32)


def split(v):
    hi = v.astype(bf16)
    return hi, (v - hi.astype(f32)).astype(bf16)


def iota(shape, dim):
    return lax.broadcasted_iota(jnp.int32, shape, dim)


def flag(cond):
    return jnp.where(cond, jnp.float32(1.0), jnp.float32(0.0))


def cholesky_rows(gram, out):
    n = RHS
    lane8, row8 = iota((8, LANES), 1), iota((8, LANES), 0)
    blocks = []
    for k in range(n // 8):
        eye = (lane8 - n == row8 + 8 * k).astype(f32)
        blocks.append(jnp.where(lane8 < n, gram[8 * k : 8 * k + 8, :], eye))

    def sublane(v, r):
        return jnp.broadcast_to(v[r : r + 1, :], (8, LANES))

    def panel(turn, blocks):
        first = blocks[0]
        columns = [jnp.broadcast_to(first[:, j : j + 1], (8, LANES)) for j in range(8)]
        entry = {(i, j): sublane(columns[j], i) for j in range(8) for i in range(j, 8)}
        rows = [sublane(first, i) for i in range(8)]
        for j in range(8):
            root = lax.rsqrt(entry[j, j])
            rows[j] = rows[j] * root
            for i in range(j + 1, 8):
                entry[i, j] = entry[i, j] * root
            for i in range(j + 1, 8):
                rows[i] = rows[i] - entry[i, j] * rows[j]
                for k in range(j + 1, i + 1):
                    entry[i, k] = entry[i, k] - entry[i, j] * entry[k, j]
        done = rows[0]
        for i in range(1, 8):
            done = jnp.where(row8 == i, rows[i], done)
        hi = done.astype(bf16).astype(f32)
        mid = (done - hi).astype(bf16).astype(f32)
        low = done - hi - mid
        left = jnp.concatenate([hi, hi, mid, hi, low, mid], axis=0).astype(bf16)
        right = jnp.concatenate([hi, mid, hi, low, hi, mid], axis=0).astype(bf16)
        change = lax.dot_general(
            left, right, (((0,), (0,)), ((), ())), preferred_element_type=f32
        )
        out[pl.ds(pl.multiple_of(turn * 8, 8), 8), :] = pltpu.roll(done, turn * 8, 1)
        rest = [
            pltpu.roll(blocks[k] - change[8 * k : 8 * k + 8], LANES - 8, 1)
            for k in range(1, n // 8)
        ]
        return tuple(rest + [jnp.zeros((8, LANES), f32)])

    lax.fori_loop(0, n // 8, panel, tuple(blocks))


def kernel(
    na, nb, nz,
    x_h, r_h, d_h, v_h, e_h, c_h, li_h, lo_h, up_h,
    res_o, orth_o, proj_o, gram_o,
    x_v, r_v, d_v, v_v, e_v, c_v, m_v,
    xp, xsb, hx, hy, hz, zsend, z_ends, res_b, oh, gath, gath_sib,
    w0, wh, wl, vh, vl, eacc, cell_v, sol_v,
    sep_loc, sep_in, base, state, stateb, tiles, fw_in, bw_in, ret, kept, other,
    psend, pin, fin, full_in, pt_v, pt_hl,
    orth, g_loc, gin1, gin2, gin3,
    loc_sem, send_sem, recv_sem,
):
    a, b, z = lax.axis_index("gx"), lax.axis_index("gy"), lax.axis_index("gz")
    size = {"gx": na, "gy": nb, "gz": nz}
    pos = {"gx": a, "gy": b, "gz": z}
    members, slots = nb // 2, na * 2
    member, core = b // 2, lax.rem(b, 2)
    slot = core * na + a
    group = RHS // members
    wide = SEP * members
    depth = slots * wide
    half = na * wide
    count = [0]
    sent = []

    def place(axis, index):
        if axis == "member":
            return (a, index * 2 + core, z)
        if axis == "slot":
            return (lax.rem(index, na), member * 2 + index // na, z)
        at = dict(pos)
        at[axis] = index
        return (at["gx"], at["gy"], at["gz"])

    size["member"], size["slot"] = members, slots
    pos_of = dict(pos, member=member, slot=slot)

    def remote(n, src, dst, where):
        return pltpu.make_async_remote_copy(
            src_ref=src, dst_ref=dst, send_sem=send_sem.at[n], recv_sem=recv_sem.at[n],
            device_id=where, device_id_type=pl.DeviceIdType.MESH,
        )

    def send(src, dst, where):
        copy = remote(count[0], src, dst, where)
        count[0] += 1
        copy.start()
        sent.append(copy.wait_send)
        return copy

    def exchange_later(pairs, dst):
        n = count[0]
        count[0] += 1
        copies = [remote(n, *pair) for pair in pairs]
        whole = dst.at[pl.ds(0, len(pairs))]
        out = pltpu.make_async_copy(whole, whole, send_sem.at[n])
        sent.append(out.wait)
        return copies, pltpu.make_async_copy(whole, whole, recv_sem.at[n])

    def exchange(pairs, dst):
        copies, came = exchange_later(pairs, dst)
        for copy in copies:
            copy.start()
        return came

    def plane_pairs(src_of, there):
        pairs = []
        for d in range(na):
            for e in range(members):
                if d or e:
                    to, far = lax.rem(a + d, na), lax.rem(member + e, members)
                    pairs.append((src_of(to, far), there, (to, far * 2 + core, z)))
        return pairs

    def share(axis, src_of, dst):
        n = size[axis]
        others = [lax.rem(pos_of[axis] + d, n) for d in range(1, n)]
        there = dst.at[pos_of[axis]]
        return exchange([(src_of(to), there, place(axis, to)) for to in others], dst)

    def arrive(copies):
        for copy in copies:
            copy.wait_recv()

    barrier = pltpu.get_barrier_semaphore()
    partners = 0

    def greet(where):
        pl.semaphore_signal(
            barrier, inc=1, device_id=where, device_id_type=pl.DeviceIdType.MESH
        )

    for axis in ("gy", "gz"):
        for d in range(1, size[axis]):
            greet(place(axis, lax.rem(pos[axis] + d, size[axis])))
            partners += 1
    for d in range(1, na):
        for e in range(nb):
            greet((lax.rem(a + d, na), lax.rem(b + e, nb), z))
            partners += 1

    def fetch(n, src, dst):
        copy = pltpu.make_async_copy(src, dst, loc_sem.at[n])
        copy.start()
        return copy

    x_order = (0, CX - 1) + tuple(range(1, CX - 1))
    get_x = {cx: fetch((0, 16, 17, 18)[cx], x_h.at[:, cx], x_v.at[cx]) for cx in x_order}
    get_m = [fetch(1 + i, h, m_v.at[i]) for i, h in enumerate((li_h, lo_h, up_h))]
    get_c = fetch(4, c_h, c_v)
    get_d = fetch(5, d_h, d_v)
    get_v = fetch(6, v_h, v_v)
    get_r = fetch(7, r_h, r_v)
    chunk = e_v.shape[0] // 4
    get_e = [
        fetch((8, 13, 14, 15)[i], e_h.at[pl.ds(i * chunk, chunk)], e_v.at[pl.ds(i * chunk, chunk)])
        for i in range(4)
    ]

    def slab(ref, s, n=RHS):
        return ref[pl.ds(s, n, stride=SLABS), :]

    def rows_at(start, n):
        return pl.ds(pl.multiple_of(start, n), n)

    pad = CY + 2
    q32, lane_all = iota((32, PAIRS * LANES), 0), iota((32, PAIRS * LANES), 1)
    turn_all, l_all = lane_all // LANES, lax.rem(lane_all, LANES)
    pick = ((q32 == turn_all) & (l_all == CZ - 1)) | ((q32 == 16 + turn_all) & (l_all == 0))
    pick = pick.astype(bf16)

    def spread_x(cx):
        get_x[cx].wait()
        rows = x_v.at[cx].reshape(RHS * CY, CZ)
        for cy in range(CY):
            v = rows[pl.ds(cy, RHS, stride=CY), :]
            xp[(cx + 1) * pad + cy + 1] = v
            xsb[cx, cy * RHS : (cy + 1) * RHS, :] = v.astype(bf16)

    def ring(axis, step):
        n = size[axis]
        return place(axis, lax.rem(pos_of[axis] + step + n, n))

    spread_x(x_order[0])
    spread_x(x_order[1])
    pl.semaphore_wait(barrier, partners)
    halo = [
        send(xsb.at[CX - 1], hx.at[0], ring("gx", 1)),
        send(xsb.at[0], hx.at[1], ring("gx", -1)),
    ]
    for cx in x_order[2:]:
        spread_x(cx)
    halo += [
        send(xsb.at[:, pl.ds((CY - 1) * RHS, RHS)], hy.at[0], ring("gy", 1)),
        send(xsb.at[:, pl.ds(0, RHS)], hy.at[1], ring("gy", -1)),
    ]
    rows = jnp.concatenate(
        [xsb[p // 4, (p % 4) * LANES : (p % 4 + 1) * LANES, :] for p in range(PAIRS)], axis=1
    )
    zsend[...] = nt(pick, rows).astype(bf16)
    halo += [
        send(zsend.at[pl.ds(0, 16)], hz.at[0], ring("gz", 1)),
        send(zsend.at[pl.ds(16, 16)], hz.at[1], ring("gz", -1)),
    ]

    mine = rows_at(member * SEP, SEP)
    lane_group = iota((SEP, LANES), 1) // SEP
    per_tile = LANES // SEP
    for i in range(3):
        get_m[i].wait()

    def reorder(i):
        pieces = [
            m_v[i, :, t * LANES : (t + 1) * LANES].astype(f32) for t in range(depth // LANES)
        ]
        for t in range(depth // LANES):
            out = jnp.zeros((SEP, LANES), f32)
            for g in range(per_tile):
                old = (t % na) * nb + g * 2 + t // na
                piece = pieces[old // per_tile]
                shift = ((g - old % per_tile) * SEP) % LANES
                if shift:
                    piece = pltpu.roll(piece, shift, 1)
                out = jnp.where(lane_group == g, piece, out)
            at = slice(t * LANES, (t + 1) * LANES)
            gath[(3, 0, 1)[i], a, member, :, at] = out.astype(bf16)

    for i in range(3):
        reorder(i)

    axes = ("member", "gx")

    def own(m, c):
        return gath.at[m, a, member, :, pl.ds(c * half, half)]

    def near(m, c, axis, step, part):
        at = ring_index(axis, step)
        rows = pl.ds(part * (SEP // 2), SEP // 2)
        if axis == "member":
            return gath.at[m, a, at, rows, pl.ds(c * half, half)]
        return gath.at[m, at, member, rows, pl.ds(c * half, half)]

    def line(m, c, axis, step):
        at = ring_index(axis, step)
        if axis == "member":
            return gath.at[m, :, at, :, pl.ds(c * half, half)]
        return gath.at[m, at, :, :, pl.ds(c * half, half)]

    def near_line(m, c, axis, step, part):
        at = ring_index(axis, step)
        cut = pl.ds(part * 2, 2)
        if axis == "member":
            return gath.at[m, cut, at, :, pl.ds(c * half, half)]
        return gath.at[m, at, cut, :, pl.ds(c * half, half)]

    def ring_index(axis, step):
        return lax.rem(pos_of[axis] + step + size[axis], size[axis])

    def later(src, where):
        copy = remote(count[0], src, src, where)
        count[0] += 1
        return copy

    def ring_pair(block, axis):
        return [later(block, ring(axis, step)) for step in (1, -1)]

    def gather_stages(m):
        one, two, three, four = [], [], [], []
        for c in range(2):
            first, second = axes[c], axes[1 - c]
            one += ring_pair(own(m, c), first)
            three += ring_pair(line(m, c, second, 0), second)
            for part, step in enumerate((1, -1)):
                two.append(later(near(m, c, first, -step, part), ring(first, step)))
                four.append(later(near_line(m, c, second, -step, part), ring(second, step)))
        return one, two, three, four

    def launch(copies):
        for copy in copies:
            copy.start()

    def relay(came, onward):
        for got, copy in zip(came, onward):
            got.wait_recv()
            copy.start()

    low_stages, up_stages, cell_stages, base_stages, pair_stages = (
        gather_stages(m) for m in range(5)
    )
    use_low, use_up = z > 0, z < nz - 1
    odd = lax.rem(z, 2) == 1
    even = jnp.logical_not(odd)

    def all_of(*conditions):
        return functools.reduce(jnp.logical_and, conditions)

    pair_low = all_of(even, z >= 4)
    pair_up = all_of(odd, z <= nz - 3)
    give_low = all_of(odd, z >= 3, z <= nz - 3)
    give_up = all_of(even, z >= 2)
    before, after = z >= 3, z < 3
    up_before = all_of(use_up, before)
    cells_here = jnp.logical_or(z == 0, z == 2)
    owners_add = jnp.logical_not(cells_here)

    def shift_copy(m, step):
        n = count[0]
        count[0] += 1
        return remote(n, gath.at[m, a, member], gath.at[4, a, member], (a, b, z + step))

    shift_low, shift_up = shift_copy(0, 1), shift_copy(1, -1)
    sibling = remote(count[0], gath.at[4], gath_sib, (a, member * 2 + 1 - core, z))
    count[0] += 1
    launch(base_stages[0])
    pl.when(use_low)(lambda: launch(low_stages[0]))
    pl.when(give_low)(shift_low.start)
    pl.when(give_up)(shift_up.start)

    get_c.wait()
    cells = jnp.broadcast_to(c_v[...], (SEP, SEP)).astype(f32)
    square = iota((SEP, SEP), 0) == iota((SEP, SEP), 1)
    column = jnp.sum(jnp.where(square, cells, 0.0), axis=1, keepdims=True)
    column = jnp.broadcast_to(column, (SEP, 4 * CZ))
    z512 = iota((SEP, 4 * CZ), 1)

    def mark(q, carry):
        oh[q] = jnp.zeros((wide, 4 * CZ), bf16)
        at = (z512 + q * 4 * CZ).astype(f32)
        oh[q, mine, :] = jnp.where(column == at, 1.0, 0.0).astype(bf16)
        return carry

    lax.fori_loop(0, QUADS, mark, 0)

    vecs = e_v.shape[0] // SLABS
    part_vecs = vecs // 4

    def relayout(c):
        get_e[c].wait()
        at = slice(c * part_vecs, (c + 1) * part_vecs)

        def step(q, carry):
            for h in range(4):
                rows = pl.ds(c * chunk + 4 * q + h, part_vecs, stride=SLABS)
                hi, lo = split(e_v[rows, :])
                vh[q, at, h * CZ : (h + 1) * CZ] = hi
                vl[q, at, h * CZ : (h + 1) * CZ] = lo
            return carry

        lax.fori_loop(0, QUADS, step, 0)

    split_early = z >= 2
    pl.when(split_early)(lambda: relayout(0))
    get_d.wait()
    get_v.wait()
    get_r.wait()
    relay(base_stages[0], base_stages[1])
    pl.when(use_low)(lambda: relay(low_stages[0], low_stages[1]))
    arrive(halo)
    arrive(base_stages[1])
    launch(base_stages[2])

    @pl.when(pair_low)
    def _():
        shift_low.wait_recv()
        launch(pair_stages[0])


    @pl.when(use_low)
    def _():
        arrive(low_stages[1])
        launch(low_stages[2])

    before_z = hz[0].astype(f32) * flag(z > 0)
    after_z = hz[1].astype(f32) * flag(z < nz - 1)
    ends = jnp.concatenate(
        [before_z, after_z, jnp.zeros((LANES - 32, LANES), f32)], axis=0
    ).T.astype(bf16)
    for k, mask in enumerate((flag(a > 0), flag(a < na - 1))):
        for cy in range(CY):
            xp[k * (CX + 1) * pad + cy + 1] = (
                hx[k, cy * RHS : (cy + 1) * RHS, :].astype(f32) * mask
            )
    for k, mask in enumerate((flag(b > 0), flag(b < nb - 1))):
        for cx in range(CX):
            xp[(cx + 1) * pad + k * (CY + 1)] = hy[k, cx].astype(f32) * mask
    q128, lane_all = iota((LANES, PAIRS * LANES), 0), iota((LANES, PAIRS * LANES), 1)
    turn_all, l_all = lane_all // LANES, lax.rem(lane_all, LANES)
    spread = ((q128 == turn_all) & (l_all == 0)) | ((q128 == 16 + turn_all) & (l_all == CZ - 1))
    z_ends[...] = nn(ends, spread.astype(bf16))
    lane64 = iota((RHS, LANES), 1)

    def residual_of(q, carry):
        for h in range(4):
            s = 4 * q + h
            i = (q // 2 + 1) * pad + lax.rem(q, 2) * 4 + h + 1
            x = xp[i]
            diag = 6.0 + d_v[pl.ds(s, 1), :]
            v0, v1, v2 = (v_v[pl.ds(k * SLABS + s, 1), :] for k in range(3))
            end = z_ends[(h % 2) * RHS : (h % 2 + 1) * RHS, rows_at((2 * q + h // 2) * LANES, LANES)]
            before = jnp.where(lane64 == 0, end, pltpu.roll(x, 1, 1))
            after = jnp.where(lane64 == CZ - 1, end, pltpu.roll(x, CZ - 1, 1))
            res = slab(r_v, s) - diag * x
            res = res + (1.0 + v0) * xp[i - pad] + (1.0 - v0) * xp[i + pad]
            res = res + (1.0 + v1) * xp[i - 1] + (1.0 - v1) * xp[i + 1]
            res = res + (1.0 + v2) * before + (1.0 - v2) * after
            r_v[pl.ds(s, RHS, stride=SLABS), :] = res
            at = slice(h * CZ, (h + 1) * CZ)
            res_b[q, :, at] = res.astype(bf16)
            w = res * (1.0 / diag)
            hi, lo = split(w)
            w0[q, :, at] = w
            wh[q, :, at] = hi
            wl[q, :, at] = lo
        return carry

    lax.fori_loop(0, QUADS, residual_of, 0)
    seps = nt(
        jnp.concatenate([res_b[q] for q in range(QUADS)], axis=1),
        jnp.concatenate([oh[q] for q in range(QUADS)], axis=1),
    )
    put_res = pltpu.make_async_copy(r_v, res_o, loc_sem.at[9])
    put_res.start()

    sep_loc[...] = seps.astype(bf16).reshape(members, group, wide)
    me = slot * members + member
    pairs = []
    for d in range(na):
        for e in range(nb):
            if d or e:
                to, far = lax.rem(a + d, na), lax.rem(b + e, nb)
                pairs.append((sep_loc.at[far // 2], sep_in.at[me], (to, far, z)))
    hop = exchange(pairs, sep_in)
    sep_in[me] = sep_loc[member]
    relay(base_stages[2], base_stages[3])
    for c in (1, 2, 3):
        pl.when(split_early)(functools.partial(relayout, c))
    pl.when(pair_low)(lambda: relay(pair_stages[0], pair_stages[1]))
    pl.when(use_low)(lambda: relay(low_stages[2], low_stages[3]))

    @pl.when(pair_low)
    def _():
        arrive(pair_stages[1])
        launch(pair_stages[2])

    hop.wait()
    arrive(base_stages[3])

    row8 = iota((8, LANES), 0)
    left = []
    for i in range(slots):
        v = sep_in[i * members].astype(f32)
        for e in range(1, members):
            v = v + sep_in[i * members + e].astype(f32)
        left.append(v.astype(bf16))
    wide_base = nt(jnp.concatenate(left, axis=1), gath[3].reshape(half, depth))
    gx_here = jnp.zeros((8, LANES), jnp.int32) + a
    for j in range(na):
        both = wide_base[:, j * wide : (j + 1) * wide]
        v = jnp.where(gx_here >= 2, both[8:], both[:8])
        v = jnp.where(lax.rem(gx_here, 2) == 1, pltpu.roll(v, 4, 0), v)
        base[:, j * wide : (j + 1) * wide] = jnp.where(row8 < 4, v, pltpu.roll(v, 4, 0))

    def plane_copies(first, src, dst, step):
        return [
            remote(first + d, src, dst, (a, member * 2 + lax.rem(core + d, 2), z + step))
            for d in range(2)
        ]

    give_base = plane_copies(count[0], base, other.at[core], 1)
    give_state = plane_copies(count[0] + 2, kept, other.at[core], -1)
    count[0] += 4
    pl.when(give_low)(lambda: launch(give_base))

    eacc[...] = jnp.zeros(eacc.shape, f32)

    def earlier_product(q, carry):
        right = jnp.concatenate([wh[q], wl[q], oh[q]], axis=0)
        eacc[:vecs] += nt(vh[q], right)
        eacc[vecs:] += nt(vl[q], right)
        return carry

    here = member * na + a
    fold = vecs // 2
    rowf = iota((8, fold), 0)
    plane_sum, plane_came = exchange_later(
        plane_pairs(lambda to, far: psend.at[far * na + to], pin.at[here]), pin
    )

    def send_sums(main):
        for i in range(RHS // 8):
            one = main[8 * i : 8 * i + 8, :fold]
            two = main[8 * i : 8 * i + 8, fold:]
            psend[2 * i] = jnp.where(rowf < 4, one, pltpu.roll(two, 4, 0))
            psend[2 * i + 1] = jnp.where(rowf < 4, pltpu.roll(one, 4, 0), two)
        launch(plane_sum)

    def earlier_results():
        main = eacc[:vecs, :LANES] + eacc[vecs:, :LANES]
        main = main.T
        main = main[:RHS] + main[RHS:]

        @pl.when(cells_here)
        def _():
            send_sums(main)
            for i in range(2):
                values = eacc[i * vecs : (i + 1) * vecs, LANES:].T
                v = values[:SEP]
                for e in range(1, members):
                    v = v + values[e * SEP : (e + 1) * SEP]
                gath[2, a, member, :, i * vecs : (i + 1) * vecs] = v.astype(bf16)

        @pl.when(owners_add)
        def _():
            pt_v[...] = main
            for i in range(2):
                cell_v[i] = eacc[i * vecs : (i + 1) * vecs, LANES:].T.astype(bf16)

    fw_1 = plane_copies(count[0], stateb.at[0], fw_in.at[core], 1)
    fw_2 = plane_copies(count[0] + 2, stateb.at[0], fw_in.at[core], 2)
    bw_1 = plane_copies(count[0] + 4, stateb.at[1], bw_in.at[core], -1)
    bw_2 = plane_copies(count[0] + 6, stateb.at[1], bw_in.at[core], -2)
    count[0] += 8
    fw_near = all_of(z < nz - 1, jnp.logical_or(even, z == 1))
    fw_far = all_of(even, z >= 2, z <= nz - 4)
    bw_near, bw_far = odd, all_of(odd, z >= 3)
    row_group = iota((16, LANES), 0) // 4

    def pack(v):
        t = [v[:, j * wide : (j + 1) * wide] for j in range(na)]
        return jnp.concatenate(
            [jnp.where(row8 < 4, t[0], t[1]), jnp.where(row8 < 4, t[2], t[3])], axis=0
        )

    def left_of(packed):
        left = []
        for v in packed:
            v = v.astype(f32)
            left += [jnp.where(row_group == j, v, 0.0).astype(bf16) for j in range(na)]
        return jnp.concatenate(left, axis=1)

    def product_of(left, rows):
        out = nt(left, rows.reshape(half, depth)[...])
        out = out[:8] + out[8:]
        return out + pltpu.roll(out, 4, 0)

    first_core = jnp.zeros((8, half), jnp.int32) + core == 0

    def two_steps(left, start, m):
        own, far = product_of(left, gath.at[4]), product_of(left, gath_sib)
        between = (
            other[0] - jnp.where(first_core, own, far),
            other[1] - jnp.where(first_core, far, own),
        )
        return start - product_of(left_of([pack(v).astype(bf16) for v in between]), gath.at[m])

    def products(first, last):
        lax.fori_loop(first, last, earlier_product, 0)

    def begin():
        launch(up_stages[0])

        @pl.when(pair_up)
        def _():
            shift_up.wait_recv()
            launch(pair_stages[0])

    def first_relay():
        relay(up_stages[0], up_stages[1])
        pl.when(pair_up)(lambda: relay(pair_stages[0], pair_stages[1]))

    def second_launch():
        arrive(up_stages[1])
        launch(up_stages[2])

        @pl.when(pair_up)
        def _():
            arrive(pair_stages[1])
            launch(pair_stages[2])

    def second_relay():
        relay(up_stages[2], up_stages[3])
        pl.when(pair_up)(lambda: relay(pair_stages[2], pair_stages[3]))

    def pair_end():
        arrive(pair_stages[3])
        sibling.start()

    pl.when(pair_low)(lambda: relay(pair_stages[2], pair_stages[3]))
    pl.when(up_before)(begin)
    pl.when(before)(lambda: products(0, 2))
    pl.when(up_before)(first_relay)
    pl.when(before)(lambda: products(2, 4))
    pl.when(pair_low)(pair_end)
    pl.when(up_before)(second_launch)
    pl.when(z >= 5)(lambda: products(4, 6))
    pl.when(all_of(pair_up, before))(second_relay)
    pl.when(use_low)(lambda: arrive(low_stages[3]))
    pl.when(pair_low)(sibling.wait_recv)

    @pl.when(z == 0)
    def _():
        state[...] = base[...]

    @pl.when(all_of(z > 0, jnp.logical_not(pair_low)))
    def _():
        arrive(fw_1)
        state[...] = base[...] - product_of(left_of([fw_in[0], fw_in[1]]), gath.at[0])

    @pl.when(pair_low)
    def _():
        arrive(give_base)
        arrive(fw_2)
        state[...] = two_steps(left_of([fw_in[0], fw_in[1]]), base[...], 0)

    @pl.when(fw_near)
    def _():
        stateb[0] = pack(state[...]).astype(bf16)
        launch(fw_1)

    pl.when(fw_far)(lambda: launch(fw_2))

    @pl.when(give_up)
    def _():
        kept[...] = state[...]
        launch(give_state)

    def push_back():
        stateb[1] = pack(state[...]).astype(bf16)
        launch(bw_1)

    @pl.when(z == nz - 1)
    def _():
        push_back()
        launch(bw_2)

    @pl.when(after)
    def _():
        begin()

        @pl.when(jnp.logical_not(split_early))
        def _():
            relayout(0)
            relayout(1)

        pl.when(split_early)(lambda: products(0, 2))
        first_relay()

        @pl.when(jnp.logical_not(split_early))
        def _():
            relayout(2)
            relayout(3)

        pl.when(split_early)(lambda: products(2, 4))
        second_launch()
        pl.when(jnp.logical_not(split_early))(lambda: products(0, 4))

    pl.when(all_of(up_before, even))(second_relay)
    pl.when(z < 5)(lambda: products(4, 6))
    pl.when(after)(second_relay)
    products(6, 8)
    pl.when(pair_up)(pair_end)
    earlier_results()

    @pl.when(cells_here)
    def _():
        launch(cell_stages[0])
        relay(cell_stages[0], cell_stages[1])
        arrive(cell_stages[1])
        launch(cell_stages[2])

    pl.when(use_up)(lambda: arrive(up_stages[3]))
    pl.when(pair_up)(sibling.wait_recv)
    pl.when(cells_here)(lambda: relay(cell_stages[2], cell_stages[3]))

    @pl.when(all_of(use_up, jnp.logical_not(pair_up)))
    def _():
        arrive(bw_1)
        state[...] = state[...] - product_of(left_of([bw_in[0], bw_in[1]]), gath.at[1])

    @pl.when(pair_up)
    def _():
        arrive(give_state)
        arrive(bw_2)
        state[...] = two_steps(left_of([bw_in[0], bw_in[1]]), state[...], 1)

    pl.when(all_of(odd, use_up))(push_back)
    pl.when(all_of(bw_far, use_up))(lambda: launch(bw_2))

    for j in range(na):
        tiles[j] = state[:, j * wide : (j + 1) * wide]
    ret_came = exchange(plane_pairs(lambda to, far: tiles.at[to], ret.at[here]), ret)
    ret[here] = tiles[a]

    def total_of(ref, n):
        out = ref[0]
        for i in range(1, n):
            out = out + ref[i]
        return out

    def take_sol():
        ret_came.wait()
        sol = jnp.concatenate(
            [jnp.where(row8 < 4, ret[2 * i], ret[2 * i + 1]) for i in range(na * members // 2)],
            axis=0,
        )
        sol_v[...] = jnp.concatenate(split(sol), axis=1)

    @pl.when(owners_add)
    def _():
        take_sol()
        sol_h, sol_l = sol_v[:, :wide], sol_v[:, wide:]
        part = nn(jnp.concatenate([sol_h, sol_l], axis=0), cell_v[0])
        send_sums(pt_v[...] + part[:RHS] + part[RHS:] + nn(sol_h, cell_v[1]))

    pin[here] = psend[here]
    plane_came.wait()
    where_fin = z * 2 + core
    fin[where_fin] = total_of(pin, na * members)

    @pl.when(cells_here)
    def _():
        arrive(cell_stages[3])
        part = nn(jnp.concatenate(split(state[...]), axis=0), gath[2].reshape(half, 2 * vecs))
        part = part[:8, :vecs] + part[8:, :vecs] + part[:8, vecs:]
        fin[where_fin] = fin[where_fin] + jnp.where(rowf < 4, part[:, :fold], part[:, fold:])

    pairs = []
    for d in range(nz):
        for e in range(2):
            if d or e:
                to, kind = lax.rem(z + d, nz), lax.rem(core + e, 2)
                mine_there = fin.at[where_fin]
                pairs.append((mine_there, mine_there, (a, member * 2 + kind, to)))
    hop = exchange(pairs, fin)

    pl.when(cells_here)(take_sol)
    sol_hl = sol_v[...]

    def add_sol(first):
        twice = jnp.concatenate([oh[first], oh[first + 1]], axis=1)
        change = nn(sol_hl, jnp.concatenate([twice, twice], axis=0))
        w0[first] = w0[first] + change[:, : 4 * CZ]
        w0[first + 1] = w0[first + 1] + change[:, 4 * CZ :]

    add_sol(0)
    add_sol(2)
    hop.wait()
    full_in[here] = total_of(fin, nz * 2)
    hop = exchange(plane_pairs(lambda to, far: full_in.at[here], full_in.at[here]), full_in)
    add_sol(4)
    add_sol(6)
    hop.wait()
    for i in range(RHS // 8):
        p, q = full_in[2 * i], full_in[2 * i + 1]
        pt_v[8 * i : 8 * i + 8, :fold] = jnp.where(rowf < 4, p, pltpu.roll(q, 4, 0))
        pt_v[8 * i : 8 * i + 8, fold:] = jnp.where(rowf < 4, pltpu.roll(p, 4, 0), q)
    pin5_put = pltpu.make_async_copy(pt_v, proj_o, loc_sem.at[10])
    pin5_put.start()
    full = pt_v[...]
    hi, lo = split(full)
    pt_hl[:RHS] = hi
    pt_hl[RHS:] = lo

    def project(i, gram):
        for q in (2 * i, 2 * i + 1):
            main = nn(pt_hl[...], vh[q])
            o = w0[q] - (main[:RHS] + main[RHS:] + nn(pt_hl[:RHS], vl[q]))
            hi, lo = split(o)
            both = jnp.concatenate([hi, lo], axis=0)
            orth[q] = both
            gram = gram + nt(both, both)
        return gram

    gram = lax.fori_loop(0, QUADS // 2, project, jnp.zeros((2 * RHS, 2 * RHS), f32))
    gram = gram[:RHS] + gram[RHS:]
    gram = gram + pltpu.roll(gram, RHS, 1)
    put_orth = pltpu.make_async_copy(orth, orth_o, loc_sem.at[11])
    put_orth.start()
    piece = RHS // nz
    g_loc[...] = gram.reshape(nz, piece, LANES)
    hop = share("gz", lambda to: g_loc.at[to], gin1)
    gin1[z] = g_loc[z]
    for wait in sent[:-1]:
        wait()
    del sent[:-1]

    for stage in base_stages:
        for copy in stage:
            copy.wait_send()

    @pl.when(use_low)
    def _():
        for stage in low_stages:
            for copy in stage:
                copy.wait_send()

    @pl.when(use_up)
    def _():
        for stage in up_stages:
            for copy in stage:
                copy.wait_send()

    use_pair = jnp.logical_or(pair_low, pair_up)
    for condition, copies in (
        (cells_here, sum(cell_stages, [])), (use_pair, sum(pair_stages, [])), (use_pair, [sibling]),
        (give_low, [shift_low] + give_base), (give_up, [shift_up] + give_state),
        (fw_near, fw_1), (fw_far, fw_2), (bw_near, bw_1), (bw_far, bw_2),
    ):
        @pl.when(condition)
        def _(copies=copies):
            for copy in copies:
                copy.wait_send()

    hop.wait()
    seat = a * nb + b
    gin2[seat] = total_of(gin1, nz)
    pairs = []
    for d in range(na):
        for e in range(nb):
            if d or e:
                to, far = lax.rem(a + d, na), lax.rem(b + e, nb)
                pairs.append((gin2.at[seat], gin2.at[seat], (to, far, z)))
    exchange(pairs, gin2).wait()
    gin3[z] = total_of(gin2, na * nb)
    share("gz", lambda to: gin3.at[z], gin3).wait()
    put_gram = pltpu.make_async_copy(gin3, gram_o, loc_sem.at[12])
    put_gram.start()
    for wait in sent:
        wait()
    for put in (put_res, pin5_put, put_orth, put_gram):
        put.wait()


def finish_kernel(
    scale, gram_v, orth_h, res_h, proj_h, res_o, new_o, proj_o, chol_o,
    orth, rows_v, new_v, res_v, proj_v, sem,
):
    get = pltpu.make_async_copy(orth_h, orth, sem.at[0])
    hand_on = [
        (pltpu.make_async_copy(res_h, res_v, sem.at[1]), pltpu.make_async_copy(res_v, res_o, sem.at[2])),
        (pltpu.make_async_copy(proj_h, proj_v, sem.at[3]), pltpu.make_async_copy(proj_v, proj_o, sem.at[4])),
    ]
    get.start()
    for copy, _ in hand_on:
        copy.start()
    cholesky_rows(gram_v[...], rows_v)
    rows = rows_v[...]
    lane64, row64 = iota((RHS, LANES), 1), iota((RHS, LANES), 0)
    upper = jnp.where((lane64 >= row64) & (lane64 < RHS), rows * (1.0 / scale), 0.0)
    inverse = jnp.where(lane64 - RHS <= row64, rows * scale, 0.0)
    hi, lo = split(inverse)
    lhs = jnp.where(lane64 < RHS, pltpu.roll(hi.astype(f32), RHS, 1), lo.astype(f32)).astype(bf16)
    lhs = jnp.concatenate([lhs, lhs], axis=1)
    for copy, onward in hand_on:
        copy.wait()
        onward.start()
    get.wait()

    def finish(q, carry):
        hi, lo = orth[q, :RHS], orth[q, RHS:]
        out = nn(lhs, jnp.concatenate([hi, hi, lo, lo], axis=0))
        for h in range(4):
            new_v[pl.ds(4 * q + h, RHS, stride=SLABS), :] = out[:, h * CZ : (h + 1) * CZ]
        return carry

    lax.fori_loop(0, QUADS, finish, 0, unroll=4)
    put_new = pltpu.make_async_copy(new_v, new_o, sem.at[5])
    put_new.start()
    upper = jnp.concatenate([upper, jnp.zeros((LANES - RHS, LANES), f32)], axis=0)
    chol_o[...] = upper.T[:RHS, :RHS]
    for _, onward in hand_on:
        onward.wait()
    put_new.wait()


def body(
    x_field, right_side, diag_shift, velocity, earlier_blocks, sep_cells, low_inv, low_off, up_off
):
    na, nb, nz = (lax.axis_size(n) for n in ("gx", "gy", "gz"))
    members, slots = nb // 2, na * 2
    group, wide = RHS // members, SEP * members
    depth, half = slots * wide, na * wide
    vecs = earlier_blocks.shape[0] * earlier_blocks.shape[1]
    piece = RHS // nz
    vmem = pltpu.VMEM
    scratch = [
        vmem((CX, RHS, CY, CZ), f32),
        vmem((ROWS, CZ), f32),
        vmem((SLABS, CZ), f32),
        vmem((3 * SLABS, CZ), f32),
        vmem((vecs * SLABS, CZ), f32),
        vmem((1, SEP), jnp.int32),
        vmem((3, SEP, depth), bf16),
        vmem(((CX + 2) * (CY + 2), RHS, CZ), f32),
        vmem((CX, CY * RHS, CZ), bf16),
        vmem((2, CY * RHS, CZ), bf16),
        vmem((2, CX, RHS, CZ), bf16),
        vmem((2, 16, LANES), bf16),
        vmem((32, LANES), bf16),
        vmem((LANES, PAIRS * LANES), f32),
        vmem((QUADS, RHS, 4 * CZ), bf16),
        vmem((QUADS, wide, 4 * CZ), bf16),
        vmem((5, na, members, SEP, depth), bf16),
        vmem((na, members, SEP, depth), bf16),
        vmem((QUADS, RHS, 4 * CZ), f32),
        vmem((QUADS, RHS, 4 * CZ), bf16),
        vmem((QUADS, RHS, 4 * CZ), bf16),
        vmem((QUADS, vecs, 4 * CZ), bf16),
        vmem((QUADS, vecs, 4 * CZ), bf16),
        vmem((2 * vecs, 2 * LANES), f32),
        vmem((2, wide, vecs), bf16),
        vmem((RHS, 2 * wide), bf16),
        vmem((members, group, wide), bf16),
        vmem((slots * members, group, wide), bf16),
        vmem((8, half), f32),
        vmem((8, half), f32),
        vmem((2, 16, wide), bf16),
        vmem((na, 8, wide), f32),
        vmem((2, 16, wide), bf16),
        vmem((2, 16, wide), bf16),
        vmem((na * members, 8, wide), f32),
        vmem((8, half), f32),
        vmem((2, 8, half), f32),
        vmem((na * members, 8, vecs // 2), f32),
        vmem((na * members, 8, vecs // 2), f32),
        vmem((2 * nz, 8, vecs // 2), f32),
        vmem((na * members, 8, vecs // 2), f32),
        vmem((RHS, vecs), f32),
        vmem((2 * RHS, vecs), bf16),
        vmem((QUADS, 2 * RHS, 4 * CZ), bf16),
        vmem((nz, piece, LANES), f32),
        vmem((nz, piece, LANES), f32),
        vmem((na * nb, piece, LANES), f32),
        vmem((nz, piece, LANES), f32),
        pltpu.SemaphoreType.DMA((19,)),
        pltpu.SemaphoreType.DMA((160,)),
        pltpu.SemaphoreType.DMA((160,)),
    ]
    flat = lambda v: v.reshape(-1, CZ)
    anywhere = pl.BlockSpec(memory_space=pl.ANY)
    in_vmem = pl.BlockSpec(memory_space=pltpu.VMEM)
    res, orth, projection, gram = pl.pallas_call(
        functools.partial(kernel, na, nb, nz),
        out_shape=(
            jax.ShapeDtypeStruct((ROWS, CZ), f32),
            jax.ShapeDtypeStruct((QUADS, 2 * RHS, 4 * CZ), bf16),
            jax.ShapeDtypeStruct((RHS, vecs), f32),
            jax.ShapeDtypeStruct((nz, piece, LANES), f32),
        ),
        in_specs=[anywhere] * 9,
        out_specs=(anywhere,) * 4,
        scratch_shapes=scratch,
        compiler_params=pltpu.CompilerParams(
            collective_id=0, has_side_effects=True, vmem_limit_bytes=60 * 2**20
        ),
        cost_estimate=pl.CostEstimate(
            flops=2 * 10**9, bytes_accessed=13 * 2**20, transcendentals=0
        ),
        name="step",
    )(
        x_field, flat(right_side), flat(diag_shift), flat(velocity), flat(earlier_blocks),
        sep_cells, low_inv[0], low_off[0], up_off[0],
    )
    res, new, projection, factor = pl.pallas_call(
        functools.partial(finish_kernel, math.sqrt(na * nb * nz * CX * CY * CZ)),
        out_shape=(
            jax.ShapeDtypeStruct((ROWS, CZ), f32),
            jax.ShapeDtypeStruct((ROWS, CZ), f32),
            jax.ShapeDtypeStruct((RHS, vecs), f32),
            jax.ShapeDtypeStruct((RHS, RHS), f32),
        ),
        in_specs=[in_vmem, anywhere, anywhere, anywhere],
        out_specs=(anywhere, anywhere, anywhere, in_vmem),
        scratch_shapes=[
            vmem((QUADS, 2 * RHS, 4 * CZ), bf16),
            vmem((RHS, LANES), f32),
            vmem((ROWS, CZ), f32),
            vmem((ROWS, CZ), f32),
            vmem((RHS, vecs), f32),
            pltpu.SemaphoreType.DMA((6,)),
        ],
        compiler_params=pltpu.CompilerParams(vmem_limit_bytes=60 * 2**20),
        cost_estimate=pl.CostEstimate(flops=2 * 10**8, bytes_accessed=5 * 2**20, transcendentals=0),
        name="finish",
    )(gram.reshape(RHS, LANES), orth, res, projection)
    shape = right_side.shape
    return (res.reshape(shape), new.reshape(shape), projection.T, factor)


def solution(mesh):
    return jax.shard_map(
        body,
        mesh=mesh,
        in_specs=(
            P(None, "gx", "gy", "gz"),
            P(None, "gx", "gy", "gz"),
            P("gx", "gy", "gz"),
            P(None, "gx", "gy", "gz"),
            P(None, None, "gx", "gy", "gz"),
            P("gz", ("gx", "gy")),
            P("gz", ("gx", "gy"), None),
            P("gz", ("gx", "gy"), None),
            P("gz", ("gx", "gy"), None),
        ),
        out_specs=(P(None, "gx", "gy", "gz"), P(None, "gx", "gy", "gz"), P(), P()),
        check_vma=False,
    )
```

```python
import functools
import math

import jax
import jax.numpy as jnp
from jax import lax
from jax.experimental import pallas as pl
from jax.experimental.pallas import tpu as pltpu
from jax.sharding import PartitionSpec as P

bf16, f32 = jnp.bfloat16, jnp.float32
RHS, CX, CY, CZ, SEP = 64, 4, 8, 128, 32
SLABS = CX * CY
PAIRS = SLABS // 2
QUADS = SLABS // 4
ROWS = RHS * SLABS
LANES = 128


def nt(a, b):
    return lax.dot_general(a, b, (((1,), (1,)), ((), ())), preferred_element_type=f32)


def nn(a, b):
    return jnp.dot(a, b, preferred_element_type=f32)


def split(v):
    hi = v.astype(bf16)
    return hi, (v - hi.astype(f32)).astype(bf16)


def iota(shape, dim):
    return lax.broadcasted_iota(jnp.int32, shape, dim)


def flag(cond):
    return jnp.where(cond, jnp.float32(1.0), jnp.float32(0.0))


def cholesky_rows(gram, out):
    n = RHS
    lane8, row8 = iota((8, LANES), 1), iota((8, LANES), 0)
    blocks = []
    for k in range(n // 8):
        eye = (lane8 - n == row8 + 8 * k).astype(f32)
        blocks.append(jnp.where(lane8 < n, gram[8 * k : 8 * k + 8, :], eye))

    def sublane(v, r):
        return jnp.broadcast_to(v[r : r + 1, :], (8, LANES))

    def panel(turn, blocks):
        first = blocks[0]
        columns = [jnp.broadcast_to(first[:, j : j + 1], (8, LANES)) for j in range(8)]
        entry = {(i, j): sublane(columns[j], i) for j in range(8) for i in range(j, 8)}
        rows = [sublane(first, i) for i in range(8)]
        for j in range(8):
            root = lax.rsqrt(entry[j, j])
            rows[j] = rows[j] * root
            for i in range(j + 1, 8):
                entry[i, j] = entry[i, j] * root
            for i in range(j + 1, 8):
                rows[i] = rows[i] - entry[i, j] * rows[j]
                for k in range(j + 1, i + 1):
                    entry[i, k] = entry[i, k] - entry[i, j] * entry[k, j]
        done = rows[0]
        for i in range(1, 8):
            done = jnp.where(row8 == i, rows[i], done)
        hi = done.astype(bf16).astype(f32)
        mid = (done - hi).astype(bf16).astype(f32)
        low = done - hi - mid
        left = jnp.concatenate([hi, hi, mid, hi, low, mid], axis=0).astype(bf16)
        right = jnp.concatenate([hi, mid, hi, low, hi, mid], axis=0).astype(bf16)
        change = lax.dot_general(
            left, right, (((0,), (0,)), ((), ())), preferred_element_type=f32
        )
        out[pl.ds(pl.multiple_of(turn * 8, 8), 8), :] = pltpu.roll(done, turn * 8, 1)
        rest = [
            pltpu.roll(blocks[k] - change[8 * k : 8 * k + 8], LANES - 8, 1)
            for k in range(1, n // 8)
        ]
        return tuple(rest + [jnp.zeros((8, LANES), f32)])

    lax.fori_loop(0, n // 8, panel, tuple(blocks))


def kernel(
    na, nb, nz,
    x_h, r_h, d_h, v_h, e_h, c_h, li_h, lo_h, up_h,
    res_o, orth_o, proj_o, gram_o,
    x_v, r_v, d_v, v_v, e_v, c_v, m_v,
    xp, xsb, hx, hy, hz, zsend, z_ends, res_b, oh, gath, gath_sib,
    w0, wh, wl, vh, vl, eacc, cell_v, sol_v,
    sep_loc, sep_in, base, state, stateb, tiles, fw_in, bw_in, ret, kept, other,
    psend, pin, fin, full_in, pt_v, pt_hl,
    orth, g_loc, gin1, gin2, gin3,
    loc_sem, send_sem, recv_sem,
):
    a, b, z = lax.axis_index("gx"), lax.axis_index("gy"), lax.axis_index("gz")
    size = {"gx": na, "gy": nb, "gz": nz}
    pos = {"gx": a, "gy": b, "gz": z}
    members, slots = nb // 2, na * 2
    member, core = b // 2, lax.rem(b, 2)
    slot = core * na + a
    group = RHS // members
    wide = SEP * members
    depth = slots * wide
    half = na * wide
    count = [0]
    sent = []

    def place(axis, index):
        if axis == "member":
            return (a, index * 2 + core, z)
        if axis == "slot":
            return (lax.rem(index, na), member * 2 + index // na, z)
        at = dict(pos)
        at[axis] = index
        return (at["gx"], at["gy"], at["gz"])

    size["member"], size["slot"] = members, slots
    pos_of = dict(pos, member=member, slot=slot)

    def remote(n, src, dst, where):
        return pltpu.make_async_remote_copy(
            src_ref=src, dst_ref=dst, send_sem=send_sem.at[n], recv_sem=recv_sem.at[n],
            device_id=where, device_id_type=pl.DeviceIdType.MESH,
        )

    def send(src, dst, where):
        copy = remote(count[0], src, dst, where)
        count[0] += 1
        copy.start()
        sent.append(copy.wait_send)
        return copy

    def exchange_later(pairs, dst):
        n = count[0]
        count[0] += 1
        copies = [remote(n, *pair) for pair in pairs]
        whole = dst.at[pl.ds(0, len(pairs))]
        out = pltpu.make_async_copy(whole, whole, send_sem.at[n])
        sent.append(out.wait)
        return copies, pltpu.make_async_copy(whole, whole, recv_sem.at[n])

    def exchange(pairs, dst):
        copies, came = exchange_later(pairs, dst)
        for copy in copies:
            copy.start()
        return came

    def plane_pairs(src_of, there):
        pairs = []
        for d in range(na):
            for e in range(members):
                if d or e:
                    to, far = lax.rem(a + d, na), lax.rem(member + e, members)
                    pairs.append((src_of(to, far), there, (to, far * 2 + core, z)))
        return pairs

    def share(axis, src_of, dst):
        n = size[axis]
        others = [lax.rem(pos_of[axis] + d, n) for d in range(1, n)]
        there = dst.at[pos_of[axis]]
        return exchange([(src_of(to), there, place(axis, to)) for to in others], dst)

    def arrive(copies):
        for copy in copies:
            copy.wait_recv()

    barrier = pltpu.get_barrier_semaphore()
    partners = 0

    def greet(where):
        pl.semaphore_signal(
            barrier, inc=1, device_id=where, device_id_type=pl.DeviceIdType.MESH
        )

    for axis in ("gy", "gz"):
        for d in range(1, size[axis]):
            greet(place(axis, lax.rem(pos[axis] + d, size[axis])))
            partners += 1
    for d in range(1, na):
        for e in range(nb):
            greet((lax.rem(a + d, na), lax.rem(b + e, nb), z))
            partners += 1

    def fetch(n, src, dst):
        copy = pltpu.make_async_copy(src, dst, loc_sem.at[n])
        copy.start()
        return copy

    x_order = (0, CX - 1) + tuple(range(1, CX - 1))
    get_x = {cx: fetch((0, 16, 17, 18)[cx], x_h.at[:, cx], x_v.at[cx]) for cx in x_order}
    get_m = [fetch(1 + i, h, m_v.at[i]) for i, h in enumerate((li_h, lo_h, up_h))]
    get_c = fetch(4, c_h, c_v)
    get_d = fetch(5, d_h, d_v)
    get_v = fetch(6, v_h, v_v)
    get_r = fetch(7, r_h, r_v)
    chunk = e_v.shape[0] // 4
    get_e = [
        fetch((8, 13, 14, 15)[i], e_h.at[pl.ds(i * chunk, chunk)], e_v.at[pl.ds(i * chunk, chunk)])
        for i in range(4)
    ]

    def slab(ref, s, n=RHS):
        return ref[pl.ds(s, n, stride=SLABS), :]

    def rows_at(start, n):
        return pl.ds(pl.multiple_of(start, n), n)

    pad = CY + 2
    q32, lane_all = iota((32, PAIRS * LANES), 0), iota((32, PAIRS * LANES), 1)
    turn_all, l_all = lane_all // LANES, lax.rem(lane_all, LANES)
    pick = ((q32 == turn_all) & (l_all == CZ - 1)) | ((q32 == 16 + turn_all) & (l_all == 0))
    pick = pick.astype(bf16)

    def spread_x(cx):
        get_x[cx].wait()
        rows = x_v.at[cx].reshape(RHS * CY, CZ)
        for cy in range(CY):
            v = rows[pl.ds(cy, RHS, stride=CY), :]
            xp[(cx + 1) * pad + cy + 1] = v
            xsb[cx, cy * RHS : (cy + 1) * RHS, :] = v.astype(bf16)

    def ring(axis, step):
        n = size[axis]
        return place(axis, lax.rem(pos_of[axis] + step + n, n))

    spread_x(x_order[0])
    spread_x(x_order[1])
    pl.semaphore_wait(barrier, partners)
    halo = [
        send(xsb.at[CX - 1], hx.at[0], ring("gx", 1)),
        send(xsb.at[0], hx.at[1], ring("gx", -1)),
    ]
    for cx in x_order[2:]:
        spread_x(cx)
    halo += [
        send(xsb.at[:, pl.ds((CY - 1) * RHS, RHS)], hy.at[0], ring("gy", 1)),
        send(xsb.at[:, pl.ds(0, RHS)], hy.at[1], ring("gy", -1)),
    ]
    rows = jnp.concatenate(
        [xsb[p // 4, (p % 4) * LANES : (p % 4 + 1) * LANES, :] for p in range(PAIRS)], axis=1
    )
    zsend[...] = nt(pick, rows).astype(bf16)
    halo += [
        send(zsend.at[pl.ds(0, 16)], hz.at[0], ring("gz", 1)),
        send(zsend.at[pl.ds(16, 16)], hz.at[1], ring("gz", -1)),
    ]

    mine = rows_at(member * SEP, SEP)
    lane_group = iota((SEP, LANES), 1) // SEP
    per_tile = LANES // SEP
    for i in range(3):
        get_m[i].wait()

    def reorder(i):
        pieces = [
            m_v[i, :, t * LANES : (t + 1) * LANES].astype(f32) for t in range(depth // LANES)
        ]
        for t in range(depth // LANES):
            out = jnp.zeros((SEP, LANES), f32)
            for g in range(per_tile):
                old = (t % na) * nb + g * 2 + t // na
                piece = pieces[old // per_tile]
                shift = ((g - old % per_tile) * SEP) % LANES
                if shift:
                    piece = pltpu.roll(piece, shift, 1)
                out = jnp.where(lane_group == g, piece, out)
            at = slice(t * LANES, (t + 1) * LANES)
            gath[(3, 0, 1)[i], a, member, :, at] = out.astype(bf16)

    for i in range(3):
        reorder(i)

    axes = ("member", "gx")

    def own(m, c):
        return gath.at[m, a, member, :, pl.ds(c * half, half)]

    def near(m, c, axis, step, part):
        at = ring_index(axis, step)
        rows = pl.ds(part * (SEP // 2), SEP // 2)
        if axis == "member":
            return gath.at[m, a, at, rows, pl.ds(c * half, half)]
        return gath.at[m, at, member, rows, pl.ds(c * half, half)]

    def line(m, c, axis, step):
        at = ring_index(axis, step)
        if axis == "member":
            return gath.at[m, :, at, :, pl.ds(c * half, half)]
        return gath.at[m, at, :, :, pl.ds(c * half, half)]

    def near_line(m, c, axis, step, part):
        at = ring_index(axis, step)
        cut = pl.ds(part * 2, 2)
        if axis == "member":
            return gath.at[m, cut, at, :, pl.ds(c * half, half)]
        return gath.at[m, at, cut, :, pl.ds(c * half, half)]

    def ring_index(axis, step):
        return lax.rem(pos_of[axis] + step + size[axis], size[axis])

    def later(src, where):
        copy = remote(count[0], src, src, where)
        count[0] += 1
        return copy

    def ring_pair(block, axis):
        return [later(block, ring(axis, step)) for step in (1, -1)]

    def gather_stages(m):
        one, two, three, four = [], [], [], []
        for c in range(2):
            first, second = axes[c], axes[1 - c]
            one += ring_pair(own(m, c), first)
            three += ring_pair(line(m, c, second, 0), second)
            for part, step in enumerate((1, -1)):
                two.append(later(near(m, c, first, -step, part), ring(first, step)))
                four.append(later(near_line(m, c, second, -step, part), ring(second, step)))
        return one, two, three, four

    def launch(copies):
        for copy in copies:
            copy.start()

    def relay(came, onward):
        for got, copy in zip(came, onward):
            got.wait_recv()
            copy.start()

    low_stages, up_stages, cell_stages, base_stages, pair_stages = (
        gather_stages(m) for m in range(5)
    )
    use_low, use_up = z > 0, z < nz - 1
    odd = lax.rem(z, 2) == 1
    even = jnp.logical_not(odd)

    def all_of(*conditions):
        return functools.reduce(jnp.logical_and, conditions)

    pair_up = all_of(odd, z <= nz - 3)
    give_up = all_of(even, z >= 2)
    up_before = all_of(use_up, z >= 5)
    cells_here = z <= 2
    owners_add = jnp.logical_not(cells_here)

    def shift_copy(m, step):
        n = count[0]
        count[0] += 1
        return remote(n, gath.at[m, a, member], gath.at[4, a, member], (a, b, z + step))

    shift_up = shift_copy(1, -1)
    sibling = remote(count[0], gath.at[4], gath_sib, (a, member * 2 + 1 - core, z))
    count[0] += 1
    launch(base_stages[0])
    pl.when(use_low)(lambda: launch(low_stages[0]))
    pl.when(give_up)(shift_up.start)

    get_c.wait()
    cells = jnp.broadcast_to(c_v[...], (SEP, SEP)).astype(f32)
    square = iota((SEP, SEP), 0) == iota((SEP, SEP), 1)
    column = jnp.sum(jnp.where(square, cells, 0.0), axis=1, keepdims=True)
    column = jnp.broadcast_to(column, (SEP, 4 * CZ))
    z512 = iota((SEP, 4 * CZ), 1)

    def mark(q, carry):
        oh[q] = jnp.zeros((wide, 4 * CZ), bf16)
        at = (z512 + q * 4 * CZ).astype(f32)
        oh[q, mine, :] = jnp.where(column == at, 1.0, 0.0).astype(bf16)
        return carry

    lax.fori_loop(0, QUADS, mark, 0)

    vecs = e_v.shape[0] // SLABS
    part_vecs = vecs // 4

    def relayout(c):
        get_e[c].wait()
        at = slice(c * part_vecs, (c + 1) * part_vecs)

        def step(q, carry):
            for h in range(4):
                rows = pl.ds(c * chunk + 4 * q + h, part_vecs, stride=SLABS)
                hi, lo = split(e_v[rows, :])
                vh[q, at, h * CZ : (h + 1) * CZ] = hi
                vl[q, at, h * CZ : (h + 1) * CZ] = lo
            return carry

        lax.fori_loop(0, QUADS, step, 0)

    split_early = z >= 2
    pl.when(split_early)(lambda: relayout(0))
    get_d.wait()
    get_v.wait()
    get_r.wait()
    relay(base_stages[0], base_stages[1])
    pl.when(use_low)(lambda: relay(low_stages[0], low_stages[1]))
    arrive(halo)
    arrive(base_stages[1])
    launch(base_stages[2])


    @pl.when(use_low)
    def _():
        arrive(low_stages[1])
        launch(low_stages[2])

    before_z = hz[0].astype(f32) * flag(z > 0)
    after_z = hz[1].astype(f32) * flag(z < nz - 1)
    ends = jnp.concatenate(
        [before_z, after_z, jnp.zeros((LANES - 32, LANES), f32)], axis=0
    ).T.astype(bf16)
    for k, mask in enumerate((flag(a > 0), flag(a < na - 1))):
        for cy in range(CY):
            xp[k * (CX + 1) * pad + cy + 1] = (
                hx[k, cy * RHS : (cy + 1) * RHS, :].astype(f32) * mask
            )
    for k, mask in enumerate((flag(b > 0), flag(b < nb - 1))):
        for cx in range(CX):
            xp[(cx + 1) * pad + k * (CY + 1)] = hy[k, cx].astype(f32) * mask
    q128, lane_all = iota((LANES, PAIRS * LANES), 0), iota((LANES, PAIRS * LANES), 1)
    turn_all, l_all = lane_all // LANES, lax.rem(lane_all, LANES)
    spread = ((q128 == turn_all) & (l_all == 0)) | ((q128 == 16 + turn_all) & (l_all == CZ - 1))
    z_ends[...] = nn(ends, spread.astype(bf16))
    lane64 = iota((RHS, LANES), 1)

    def residual_of(q, carry):
        for h in range(4):
            s = 4 * q + h
            i = (q // 2 + 1) * pad + lax.rem(q, 2) * 4 + h + 1
            x = xp[i]
            diag = 6.0 + d_v[pl.ds(s, 1), :]
            v0, v1, v2 = (v_v[pl.ds(k * SLABS + s, 1), :] for k in range(3))
            end = z_ends[(h % 2) * RHS : (h % 2 + 1) * RHS, rows_at((2 * q + h // 2) * LANES, LANES)]
            before = jnp.where(lane64 == 0, end, pltpu.roll(x, 1, 1))
            after = jnp.where(lane64 == CZ - 1, end, pltpu.roll(x, CZ - 1, 1))
            res = slab(r_v, s) - diag * x
            res = res + (1.0 + v0) * xp[i - pad] + (1.0 - v0) * xp[i + pad]
            res = res + (1.0 + v1) * xp[i - 1] + (1.0 - v1) * xp[i + 1]
            res = res + (1.0 + v2) * before + (1.0 - v2) * after
            r_v[pl.ds(s, RHS, stride=SLABS), :] = res
            at = slice(h * CZ, (h + 1) * CZ)
            res_b[q, :, at] = res.astype(bf16)
            w = res * (1.0 / diag)
            hi, lo = split(w)
            w0[q, :, at] = w
            wh[q, :, at] = hi
            wl[q, :, at] = lo
        return carry

    lax.fori_loop(0, QUADS, residual_of, 0)
    seps = nt(
        jnp.concatenate([res_b[q] for q in range(QUADS)], axis=1),
        jnp.concatenate([oh[q] for q in range(QUADS)], axis=1),
    )
    put_res = pltpu.make_async_copy(r_v, res_o, loc_sem.at[9])
    put_res.start()

    sep_loc[...] = seps.astype(bf16).reshape(members, group, wide)
    me = slot * members + member
    pairs = []
    for d in range(na):
        for e in range(nb):
            if d or e:
                to, far = lax.rem(a + d, na), lax.rem(b + e, nb)
                pairs.append((sep_loc.at[far // 2], sep_in.at[me], (to, far, z)))
    hop = exchange(pairs, sep_in)
    sep_in[me] = sep_loc[member]
    relay(base_stages[2], base_stages[3])
    for c in (1, 2, 3):
        pl.when(split_early)(functools.partial(relayout, c))
    pl.when(use_low)(lambda: relay(low_stages[2], low_stages[3]))
    hop.wait()
    arrive(base_stages[3])

    row8 = iota((8, LANES), 0)
    left = []
    for i in range(slots):
        v = sep_in[i * members].astype(f32)
        for e in range(1, members):
            v = v + sep_in[i * members + e].astype(f32)
        left.append(v.astype(bf16))
    wide_base = nt(jnp.concatenate(left, axis=1), gath[3].reshape(half, depth))
    gx_here = jnp.zeros((8, LANES), jnp.int32) + a
    for j in range(na):
        both = wide_base[:, j * wide : (j + 1) * wide]
        v = jnp.where(gx_here >= 2, both[8:], both[:8])
        v = jnp.where(lax.rem(gx_here, 2) == 1, pltpu.roll(v, 4, 0), v)
        base[:, j * wide : (j + 1) * wide] = jnp.where(row8 < 4, v, pltpu.roll(v, 4, 0))

    def plane_copies(first, src, dst, step):
        return [
            remote(first + d, src, dst, (a, member * 2 + lax.rem(core + d, 2), z + step))
            for d in range(2)
        ]

    give_state = plane_copies(count[0], kept, other.at[core], -1)
    count[0] += 2

    eacc[...] = jnp.zeros(eacc.shape, f32)

    def earlier_product(q, carry):
        right = jnp.concatenate([wh[q], wl[q], oh[q]], axis=0)
        eacc[:vecs] += nt(vh[q], right)
        eacc[vecs:] += nt(vl[q], right)
        return carry

    here = member * na + a
    fold = vecs // 2
    rowf = iota((8, fold), 0)
    plane_sum, plane_came = exchange_later(
        plane_pairs(lambda to, far: psend.at[far * na + to], pin.at[here]), pin
    )

    def send_sums(main):
        for i in range(RHS // 8):
            one = main[8 * i : 8 * i + 8, :fold]
            two = main[8 * i : 8 * i + 8, fold:]
            psend[2 * i] = jnp.where(rowf < 4, one, pltpu.roll(two, 4, 0))
            psend[2 * i + 1] = jnp.where(rowf < 4, pltpu.roll(one, 4, 0), two)
        launch(plane_sum)

    def earlier_results():
        main = eacc[:vecs, :LANES] + eacc[vecs:, :LANES]
        main = main.T
        main = main[:RHS] + main[RHS:]

        @pl.when(cells_here)
        def _():
            send_sums(main)
            for i in range(2):
                values = eacc[i * vecs : (i + 1) * vecs, LANES:].T
                v = values[:SEP]
                for e in range(1, members):
                    v = v + values[e * SEP : (e + 1) * SEP]
                gath[2, a, member, :, i * vecs : (i + 1) * vecs] = v.astype(bf16)

        @pl.when(owners_add)
        def _():
            pt_v[...] = main
            for i in range(2):
                cell_v[i] = eacc[i * vecs : (i + 1) * vecs, LANES:].T.astype(bf16)

    fw_1 = plane_copies(count[0], stateb.at[0], fw_in.at[core], 1)
    bw_1 = plane_copies(count[0] + 2, stateb.at[1], bw_in.at[core], -1)
    bw_2 = plane_copies(count[0] + 4, stateb.at[1], bw_in.at[core], -2)
    count[0] += 6
    fw_near = z < nz - 1
    bw_near, bw_far = odd, all_of(odd, z >= 3)
    row_group = iota((16, LANES), 0) // 4

    def pack(v):
        t = [v[:, j * wide : (j + 1) * wide] for j in range(na)]
        return jnp.concatenate(
            [jnp.where(row8 < 4, t[0], t[1]), jnp.where(row8 < 4, t[2], t[3])], axis=0
        )

    def left_of(packed):
        left = []
        for v in packed:
            v = v.astype(f32)
            left += [jnp.where(row_group == j, v, 0.0).astype(bf16) for j in range(na)]
        return jnp.concatenate(left, axis=1)

    def product_of(left, rows):
        out = nt(left, rows.reshape(half, depth)[...])
        out = out[:8] + out[8:]
        return out + pltpu.roll(out, 4, 0)

    first_core = jnp.zeros((8, half), jnp.int32) + core == 0

    def two_steps(left, start, m):
        own, far = product_of(left, gath.at[4]), product_of(left, gath_sib)
        between = (
            other[0] - jnp.where(first_core, own, far),
            other[1] - jnp.where(first_core, far, own),
        )
        return start - product_of(left_of([pack(v).astype(bf16) for v in between]), gath.at[m])

    def products(first, last):
        lax.fori_loop(first, last, earlier_product, 0)

    def begin():
        launch(up_stages[0])

        @pl.when(pair_up)
        def _():
            shift_up.wait_recv()
            launch(pair_stages[0])

    def first_relay():
        relay(up_stages[0], up_stages[1])
        pl.when(pair_up)(lambda: relay(pair_stages[0], pair_stages[1]))

    def second_launch():
        arrive(up_stages[1])
        launch(up_stages[2])

        @pl.when(pair_up)
        def _():
            arrive(pair_stages[1])
            launch(pair_stages[2])

    def second_relay():
        relay(up_stages[2], up_stages[3])
        pl.when(pair_up)(lambda: relay(pair_stages[2], pair_stages[3]))

    def pair_end():
        arrive(pair_stages[3])
        sibling.start()

    pl.when(up_before)(begin)
    pl.when(z >= 3)(lambda: products(0, 2))
    pl.when(up_before)(first_relay)
    pl.when(z >= 3)(lambda: products(2, 4))
    pl.when(up_before)(second_launch)
    pl.when(z >= 5)(lambda: products(4, 6))
    pl.when(up_before)(second_relay)
    pl.when(use_low)(lambda: arrive(low_stages[3]))

    @pl.when(z == 0)
    def _():
        state[...] = base[...]

    @pl.when(z > 0)
    def _():
        arrive(fw_1)
        state[...] = base[...] - product_of(left_of([fw_in[0], fw_in[1]]), gath.at[0])

    @pl.when(fw_near)
    def _():
        stateb[0] = pack(state[...]).astype(bf16)
        launch(fw_1)

    @pl.when(give_up)
    def _():
        kept[...] = state[...]
        launch(give_state)

    def push_back():
        stateb[1] = pack(state[...]).astype(bf16)
        launch(bw_1)

    @pl.when(z == nz - 1)
    def _():
        push_back()
        launch(bw_2)

    @pl.when(z < 5)
    def _():
        begin()

        @pl.when(z < 2)
        def _():
            relayout(0)
            relayout(1)

        pl.when(z == 2)(lambda: products(0, 2))
        pl.when(z >= 3)(lambda: products(4, 6))
        first_relay()

        @pl.when(z < 2)
        def _():
            relayout(2)
            relayout(3)

        pl.when(z == 2)(lambda: products(2, 4))
        second_launch()
        pl.when(z < 2)(lambda: products(0, 4))
        pl.when(z < 3)(lambda: products(4, 6))
        second_relay()

    products(6, 8)
    pl.when(pair_up)(pair_end)
    earlier_results()

    @pl.when(cells_here)
    def _():
        launch(cell_stages[0])
        relay(cell_stages[0], cell_stages[1])
        arrive(cell_stages[1])
        launch(cell_stages[2])

    pl.when(use_up)(lambda: arrive(up_stages[3]))
    pl.when(pair_up)(sibling.wait_recv)
    pl.when(cells_here)(lambda: relay(cell_stages[2], cell_stages[3]))

    @pl.when(all_of(use_up, jnp.logical_not(pair_up)))
    def _():
        arrive(bw_1)
        state[...] = state[...] - product_of(left_of([bw_in[0], bw_in[1]]), gath.at[1])

    @pl.when(pair_up)
    def _():
        arrive(give_state)
        arrive(bw_2)
        state[...] = two_steps(left_of([bw_in[0], bw_in[1]]), state[...], 1)

    pl.when(all_of(odd, use_up))(push_back)
    pl.when(all_of(bw_far, use_up))(lambda: launch(bw_2))

    for j in range(na):
        tiles[j] = state[:, j * wide : (j + 1) * wide]
    ret_came = exchange(plane_pairs(lambda to, far: tiles.at[to], ret.at[here]), ret)
    ret[here] = tiles[a]

    def total_of(ref, n):
        out = ref[0]
        for i in range(1, n):
            out = out + ref[i]
        return out

    def take_sol():
        ret_came.wait()
        sol = jnp.concatenate(
            [jnp.where(row8 < 4, ret[2 * i], ret[2 * i + 1]) for i in range(na * members // 2)],
            axis=0,
        )
        sol_v[...] = jnp.concatenate(split(sol), axis=1)

    @pl.when(owners_add)
    def _():
        take_sol()
        sol_h, sol_l = sol_v[:, :wide], sol_v[:, wide:]
        part = nn(jnp.concatenate([sol_h, sol_l], axis=0), cell_v[0])
        send_sums(pt_v[...] + part[:RHS] + part[RHS:] + nn(sol_h, cell_v[1]))

    pin[here] = psend[here]
    plane_came.wait()
    where_fin = z * 2 + core
    fin[where_fin] = total_of(pin, na * members)

    @pl.when(cells_here)
    def _():
        arrive(cell_stages[3])
        part = nn(jnp.concatenate(split(state[...]), axis=0), gath[2].reshape(half, 2 * vecs))
        part = part[:8, :vecs] + part[8:, :vecs] + part[:8, vecs:]
        fin[where_fin] = fin[where_fin] + jnp.where(rowf < 4, part[:, :fold], part[:, fold:])

    pairs = []
    for d in range(nz):
        for e in range(2):
            if d or e:
                to, kind = lax.rem(z + d, nz), lax.rem(core + e, 2)
                mine_there = fin.at[where_fin]
                pairs.append((mine_there, mine_there, (a, member * 2 + kind, to)))
    hop = exchange(pairs, fin)

    pl.when(cells_here)(take_sol)
    sol_hl = sol_v[...]

    def add_sol(first):
        twice = jnp.concatenate([oh[first], oh[first + 1]], axis=1)
        change = nn(sol_hl, jnp.concatenate([twice, twice], axis=0))
        w0[first] = w0[first] + change[:, : 4 * CZ]
        w0[first + 1] = w0[first + 1] + change[:, 4 * CZ :]

    add_sol(0)
    add_sol(2)
    hop.wait()
    full_in[here] = total_of(fin, nz * 2)
    hop = exchange(plane_pairs(lambda to, far: full_in.at[here], full_in.at[here]), full_in)
    add_sol(4)
    add_sol(6)
    hop.wait()
    for i in range(RHS // 8):
        p, q = full_in[2 * i], full_in[2 * i + 1]
        pt_v[8 * i : 8 * i + 8, :fold] = jnp.where(rowf < 4, p, pltpu.roll(q, 4, 0))
        pt_v[8 * i : 8 * i + 8, fold:] = jnp.where(rowf < 4, pltpu.roll(p, 4, 0), q)
    pin5_put = pltpu.make_async_copy(pt_v, proj_o, loc_sem.at[10])
    pin5_put.start()
    full = pt_v[...]
    hi, lo = split(full)
    pt_hl[:RHS] = hi
    pt_hl[RHS:] = lo

    def project(i, gram):
        for q in (2 * i, 2 * i + 1):
            main = nn(pt_hl[...], vh[q])
            o = w0[q] - (main[:RHS] + main[RHS:] + nn(pt_hl[:RHS], vl[q]))
            hi, lo = split(o)
            both = jnp.concatenate([hi, lo], axis=0)
            orth[q] = both
            gram = gram + nt(both, both)
        return gram

    gram = lax.fori_loop(0, QUADS // 2, project, jnp.zeros((2 * RHS, 2 * RHS), f32))
    gram = gram[:RHS] + gram[RHS:]
    gram = gram + pltpu.roll(gram, RHS, 1)
    put_orth = pltpu.make_async_copy(orth, orth_o, loc_sem.at[11])
    put_orth.start()
    piece = RHS // nz
    g_loc[...] = gram.reshape(nz, piece, LANES)
    hop = share("gz", lambda to: g_loc.at[to], gin1)
    gin1[z] = g_loc[z]
    for wait in sent[:-1]:
        wait()
    del sent[:-1]

    for stage in base_stages:
        for copy in stage:
            copy.wait_send()

    @pl.when(use_low)
    def _():
        for stage in low_stages:
            for copy in stage:
                copy.wait_send()

    @pl.when(use_up)
    def _():
        for stage in up_stages:
            for copy in stage:
                copy.wait_send()

    for condition, copies in (
        (cells_here, sum(cell_stages, [])), (pair_up, sum(pair_stages, [])), (pair_up, [sibling]),
        (give_up, [shift_up] + give_state), (fw_near, fw_1), (bw_near, bw_1), (bw_far, bw_2),
    ):
        @pl.when(condition)
        def _(copies=copies):
            for copy in copies:
                copy.wait_send()

    hop.wait()
    seat = a * nb + b
    gin2[seat] = total_of(gin1, nz)
    pairs = []
    for d in range(na):
        for e in range(nb):
            if d or e:
                to, far = lax.rem(a + d, na), lax.rem(b + e, nb)
                pairs.append((gin2.at[seat], gin2.at[seat], (to, far, z)))
    exchange(pairs, gin2).wait()
    gin3[z] = total_of(gin2, na * nb)
    share("gz", lambda to: gin3.at[z], gin3).wait()
    put_gram = pltpu.make_async_copy(gin3, gram_o, loc_sem.at[12])
    put_gram.start()
    for wait in sent:
        wait()
    for put in (put_res, pin5_put, put_orth, put_gram):
        put.wait()


def finish_kernel(
    scale, gram_v, orth_h, res_h, proj_h, res_o, new_o, proj_o, chol_o,
    orth, rows_v, new_v, res_v, proj_v, sem,
):
    get = pltpu.make_async_copy(orth_h, orth, sem.at[0])
    hand_on = [
        (pltpu.make_async_copy(res_h, res_v, sem.at[1]), pltpu.make_async_copy(res_v, res_o, sem.at[2])),
        (pltpu.make_async_copy(proj_h, proj_v, sem.at[3]), pltpu.make_async_copy(proj_v, proj_o, sem.at[4])),
    ]
    get.start()
    for copy, _ in hand_on:
        copy.start()
    cholesky_rows(gram_v[...], rows_v)
    rows = rows_v[...]
    lane64, row64 = iota((RHS, LANES), 1), iota((RHS, LANES), 0)
    upper = jnp.where((lane64 >= row64) & (lane64 < RHS), rows * (1.0 / scale), 0.0)
    inverse = jnp.where(lane64 - RHS <= row64, rows * scale, 0.0)
    hi, lo = split(inverse)
    lhs = jnp.where(lane64 < RHS, pltpu.roll(hi.astype(f32), RHS, 1), lo.astype(f32)).astype(bf16)
    lhs = jnp.concatenate([lhs, lhs], axis=1)
    for copy, onward in hand_on:
        copy.wait()
        onward.start()
    get.wait()

    def finish(q, carry):
        hi, lo = orth[q, :RHS], orth[q, RHS:]
        out = nn(lhs, jnp.concatenate([hi, hi, lo, lo], axis=0))
        for h in range(4):
            new_v[pl.ds(4 * q + h, RHS, stride=SLABS), :] = out[:, h * CZ : (h + 1) * CZ]
        return carry

    lax.fori_loop(0, QUADS, finish, 0, unroll=4)
    put_new = pltpu.make_async_copy(new_v, new_o, sem.at[5])
    put_new.start()
    upper = jnp.concatenate([upper, jnp.zeros((LANES - RHS, LANES), f32)], axis=0)
    chol_o[...] = upper.T[:RHS, :RHS]
    for _, onward in hand_on:
        onward.wait()
    put_new.wait()


def body(
    x_field, right_side, diag_shift, velocity, earlier_blocks, sep_cells, low_inv, low_off, up_off
):
    na, nb, nz = (lax.axis_size(n) for n in ("gx", "gy", "gz"))
    members, slots = nb // 2, na * 2
    group, wide = RHS // members, SEP * members
    depth, half = slots * wide, na * wide
    vecs = earlier_blocks.shape[0] * earlier_blocks.shape[1]
    piece = RHS // nz
    vmem = pltpu.VMEM
    scratch = [
        vmem((CX, RHS, CY, CZ), f32),
        vmem((ROWS, CZ), f32),
        vmem((SLABS, CZ), f32),
        vmem((3 * SLABS, CZ), f32),
        vmem((vecs * SLABS, CZ), f32),
        vmem((1, SEP), jnp.int32),
        vmem((3, SEP, depth), bf16),
        vmem(((CX + 2) * (CY + 2), RHS, CZ), f32),
        vmem((CX, CY * RHS, CZ), bf16),
        vmem((2, CY * RHS, CZ), bf16),
        vmem((2, CX, RHS, CZ), bf16),
        vmem((2, 16, LANES), bf16),
        vmem((32, LANES), bf16),
        vmem((LANES, PAIRS * LANES), f32),
        vmem((QUADS, RHS, 4 * CZ), bf16),
        vmem((QUADS, wide, 4 * CZ), bf16),
        vmem((5, na, members, SEP, depth), bf16),
        vmem((na, members, SEP, depth), bf16),
        vmem((QUADS, RHS, 4 * CZ), f32),
        vmem((QUADS, RHS, 4 * CZ), bf16),
        vmem((QUADS, RHS, 4 * CZ), bf16),
        vmem((QUADS, vecs, 4 * CZ), bf16),
        vmem((QUADS, vecs, 4 * CZ), bf16),
        vmem((2 * vecs, 2 * LANES), f32),
        vmem((2, wide, vecs), bf16),
        vmem((RHS, 2 * wide), bf16),
        vmem((members, group, wide), bf16),
        vmem((slots * members, group, wide), bf16),
        vmem((8, half), f32),
        vmem((8, half), f32),
        vmem((2, 16, wide), bf16),
        vmem((na, 8, wide), f32),
        vmem((2, 16, wide), bf16),
        vmem((2, 16, wide), bf16),
        vmem((na * members, 8, wide), f32),
        vmem((8, half), f32),
        vmem((2, 8, half), f32),
        vmem((na * members, 8, vecs // 2), f32),
        vmem((na * members, 8, vecs // 2), f32),
        vmem((2 * nz, 8, vecs // 2), f32),
        vmem((na * members, 8, vecs // 2), f32),
        vmem((RHS, vecs), f32),
        vmem((2 * RHS, vecs), bf16),
        vmem((QUADS, 2 * RHS, 4 * CZ), bf16),
        vmem((nz, piece, LANES), f32),
        vmem((nz, piece, LANES), f32),
        vmem((na * nb, piece, LANES), f32),
        vmem((nz, piece, LANES), f32),
        pltpu.SemaphoreType.DMA((19,)),
        pltpu.SemaphoreType.DMA((160,)),
        pltpu.SemaphoreType.DMA((160,)),
    ]
    flat = lambda v: v.reshape(-1, CZ)
    anywhere = pl.BlockSpec(memory_space=pl.ANY)
    in_vmem = pl.BlockSpec(memory_space=pltpu.VMEM)
    res, orth, projection, gram = pl.pallas_call(
        functools.partial(kernel, na, nb, nz),
        out_shape=(
            jax.ShapeDtypeStruct((ROWS, CZ), f32),
            jax.ShapeDtypeStruct((QUADS, 2 * RHS, 4 * CZ), bf16),
            jax.ShapeDtypeStruct((RHS, vecs), f32),
            jax.ShapeDtypeStruct((nz, piece, LANES), f32),
        ),
        in_specs=[anywhere] * 9,
        out_specs=(anywhere,) * 4,
        scratch_shapes=scratch,
        compiler_params=pltpu.CompilerParams(
            collective_id=0, has_side_effects=True, vmem_limit_bytes=60 * 2**20
        ),
        cost_estimate=pl.CostEstimate(
            flops=2 * 10**9, bytes_accessed=13 * 2**20, transcendentals=0
        ),
        name="step",
    )(
        x_field, flat(right_side), flat(diag_shift), flat(velocity), flat(earlier_blocks),
        sep_cells, low_inv[0], low_off[0], up_off[0],
    )
    res, new, projection, factor = pl.pallas_call(
        functools.partial(finish_kernel, math.sqrt(na * nb * nz * CX * CY * CZ)),
        out_shape=(
            jax.ShapeDtypeStruct((ROWS, CZ), f32),
            jax.ShapeDtypeStruct((ROWS, CZ), f32),
            jax.ShapeDtypeStruct((RHS, vecs), f32),
            jax.ShapeDtypeStruct((RHS, RHS), f32),
        ),
        in_specs=[in_vmem, anywhere, anywhere, anywhere],
        out_specs=(anywhere, anywhere, anywhere, in_vmem),
        scratch_shapes=[
            vmem((QUADS, 2 * RHS, 4 * CZ), bf16),
            vmem((RHS, LANES), f32),
            vmem((ROWS, CZ), f32),
            vmem((ROWS, CZ), f32),
            vmem((RHS, vecs), f32),
            pltpu.SemaphoreType.DMA((6,)),
        ],
        compiler_params=pltpu.CompilerParams(vmem_limit_bytes=60 * 2**20),
        cost_estimate=pl.CostEstimate(flops=2 * 10**8, bytes_accessed=5 * 2**20, transcendentals=0),
        name="finish",
    )(gram.reshape(RHS, LANES), orth, res, projection)
    shape = right_side.shape
    return (res.reshape(shape), new.reshape(shape), projection.T, factor)


def solution(mesh):
    return jax.shard_map(
        body,
        mesh=mesh,
        in_specs=(
            P(None, "gx", "gy", "gz"),
            P(None, "gx", "gy", "gz"),
            P("gx", "gy", "gz"),
            P(None, "gx", "gy", "gz"),
            P(None, None, "gx", "gy", "gz"),
            P("gz", ("gx", "gy")),
            P("gz", ("gx", "gy"), None),
            P("gz", ("gx", "gy"), None),
            P("gz", ("gx", "gy"), None),
        ),
        out_specs=(P(None, "gx", "gy", "gz"), P(None, "gx", "gy", "gz"), P(), P()),
        check_vma=False,
    )
```

```python
import functools
import math

import jax
import jax.numpy as jnp
from jax import lax
from jax.experimental import pallas as pl
from jax.experimental.pallas import tpu as pltpu
from jax.sharding import PartitionSpec as P

bf16, f32 = jnp.bfloat16, jnp.float32
RHS, CX, CY, CZ, SEP = 64, 4, 8, 128, 32
SLABS = CX * CY
PAIRS = SLABS // 2
QUADS = SLABS // 4
ROWS = RHS * SLABS
LANES = 128


def nt(a, b):
    return lax.dot_general(a, b, (((1,), (1,)), ((), ())), preferred_element_type=f32)


def nn(a, b):
    return jnp.dot(a, b, preferred_element_type=f32)


def split(v):
    hi = v.astype(bf16)
    return hi, (v - hi.astype(f32)).astype(bf16)


def iota(shape, dim):
    return lax.broadcasted_iota(jnp.int32, shape, dim)


def flag(cond):
    return jnp.where(cond, jnp.float32(1.0), jnp.float32(0.0))


def cholesky_rows(gram, out):
    n = RHS
    lane8, row8 = iota((8, LANES), 1), iota((8, LANES), 0)
    blocks = []
    for k in range(n // 8):
        eye = (lane8 - n == row8 + 8 * k).astype(f32)
        blocks.append(jnp.where(lane8 < n, gram[8 * k : 8 * k + 8, :], eye))

    def sublane(v, r):
        return jnp.broadcast_to(v[r : r + 1, :], (8, LANES))

    def panel(turn, blocks):
        first = blocks[0]
        columns = [jnp.broadcast_to(first[:, j : j + 1], (8, LANES)) for j in range(8)]
        entry = {(i, j): sublane(columns[j], i) for j in range(8) for i in range(j, 8)}
        rows = [sublane(first, i) for i in range(8)]
        for j in range(8):
            root = lax.rsqrt(entry[j, j])
            rows[j] = rows[j] * root
            for i in range(j + 1, 8):
                entry[i, j] = entry[i, j] * root
            for i in range(j + 1, 8):
                rows[i] = rows[i] - entry[i, j] * rows[j]
                for k in range(j + 1, i + 1):
                    entry[i, k] = entry[i, k] - entry[i, j] * entry[k, j]
        done = rows[0]
        for i in range(1, 8):
            done = jnp.where(row8 == i, rows[i], done)
        hi = done.astype(bf16).astype(f32)
        mid = (done - hi).astype(bf16).astype(f32)
        low = done - hi - mid
        left = jnp.concatenate([hi, hi, mid, hi, low, mid], axis=0).astype(bf16)
        right = jnp.concatenate([hi, mid, hi, low, hi, mid], axis=0).astype(bf16)
        change = lax.dot_general(
            left, right, (((0,), (0,)), ((), ())), preferred_element_type=f32
        )
        out[pl.ds(pl.multiple_of(turn * 8, 8), 8), :] = pltpu.roll(done, turn * 8, 1)
        rest = [
            pltpu.roll(blocks[k] - change[8 * k : 8 * k + 8], LANES - 8, 1)
            for k in range(1, n // 8)
        ]
        return tuple(rest + [jnp.zeros((8, LANES), f32)])

    lax.fori_loop(0, n // 8, panel, tuple(blocks))


def kernel(
    na, nb, nz,
    x_h, r_h, d_h, v_h, e_h, c_h, li_h, lo_h, up_h,
    res_o, orth_o, proj_o, gram_o,
    x_v, r_v, d_v, v_v, e_v, c_v, m_v,
    xp, xsb, hx, hy, hz, zsend, z_ends, res_b, oh, gath, gath_sib,
    w0, wh, wl, vh, vl, eacc, cell_v, sol_v,
    sep_loc, sep_in, base, state, stateb, tiles, fw_in, bw_in, ret, kept, other,
    psend, pin, fin, full_in, pt_v, pt_hl,
    orth, g_loc, gin1, gin2, gin3,
    loc_sem, send_sem, recv_sem,
):
    a, b, z = lax.axis_index("gx"), lax.axis_index("gy"), lax.axis_index("gz")
    size = {"gx": na, "gy": nb, "gz": nz}
    pos = {"gx": a, "gy": b, "gz": z}
    members, slots = nb // 2, na * 2
    member, core = b // 2, lax.rem(b, 2)
    slot = core * na + a
    group = RHS // members
    wide = SEP * members
    depth = slots * wide
    half = na * wide
    count = [0]
    sent = []

    def place(axis, index):
        if axis == "member":
            return (a, index * 2 + core, z)
        if axis == "slot":
            return (lax.rem(index, na), member * 2 + index // na, z)
        at = dict(pos)
        at[axis] = index
        return (at["gx"], at["gy"], at["gz"])

    size["member"], size["slot"] = members, slots
    pos_of = dict(pos, member=member, slot=slot)

    def remote(n, src, dst, where):
        return pltpu.make_async_remote_copy(
            src_ref=src, dst_ref=dst, send_sem=send_sem.at[n], recv_sem=recv_sem.at[n],
            device_id=where, device_id_type=pl.DeviceIdType.MESH,
        )

    def send(src, dst, where):
        copy = remote(count[0], src, dst, where)
        count[0] += 1
        copy.start()
        sent.append(copy.wait_send)
        return copy

    def exchange_later(pairs, dst):
        n = count[0]
        count[0] += 1
        copies = [remote(n, *pair) for pair in pairs]
        whole = dst.at[pl.ds(0, len(pairs))]
        out = pltpu.make_async_copy(whole, whole, send_sem.at[n])
        sent.append(out.wait)
        return copies, pltpu.make_async_copy(whole, whole, recv_sem.at[n])

    def exchange(pairs, dst):
        copies, came = exchange_later(pairs, dst)
        for copy in copies:
            copy.start()
        return came

    def plane_pairs(src_of, there):
        pairs = []
        for d in range(na):
            for e in range(members):
                if d or e:
                    to, far = lax.rem(a + d, na), lax.rem(member + e, members)
                    pairs.append((src_of(to, far), there, (to, far * 2 + core, z)))
        return pairs

    def share(axis, src_of, dst):
        n = size[axis]
        others = [lax.rem(pos_of[axis] + d, n) for d in range(1, n)]
        there = dst.at[pos_of[axis]]
        return exchange([(src_of(to), there, place(axis, to)) for to in others], dst)

    def arrive(copies):
        for copy in copies:
            copy.wait_recv()

    barrier = pltpu.get_barrier_semaphore()
    partners = 0

    def greet(where):
        pl.semaphore_signal(
            barrier, inc=1, device_id=where, device_id_type=pl.DeviceIdType.MESH
        )

    for axis in ("gy", "gz"):
        for d in range(1, size[axis]):
            greet(place(axis, lax.rem(pos[axis] + d, size[axis])))
            partners += 1
    for d in range(1, na):
        for e in range(nb):
            greet((lax.rem(a + d, na), lax.rem(b + e, nb), z))
            partners += 1

    def fetch(n, src, dst):
        copy = pltpu.make_async_copy(src, dst, loc_sem.at[n])
        copy.start()
        return copy

    x_order = (0, CX - 1) + tuple(range(1, CX - 1))
    get_x = {cx: fetch((0, 16, 17, 18)[cx], x_h.at[:, cx], x_v.at[cx]) for cx in x_order}
    get_m = [fetch(1 + i, h, m_v.at[i]) for i, h in enumerate((li_h, lo_h, up_h))]
    get_c = fetch(4, c_h, c_v)
    get_d = fetch(5, d_h, d_v)
    get_v = fetch(6, v_h, v_v)
    get_r = fetch(7, r_h, r_v)
    chunk = e_v.shape[0] // 4
    get_e = [
        fetch((8, 13, 14, 15)[i], e_h.at[pl.ds(i * chunk, chunk)], e_v.at[pl.ds(i * chunk, chunk)])
        for i in range(4)
    ]

    def slab(ref, s, n=RHS):
        return ref[pl.ds(s, n, stride=SLABS), :]

    def rows_at(start, n):
        return pl.ds(pl.multiple_of(start, n), n)

    pad = CY + 2
    q32, lane_all = iota((32, PAIRS * LANES), 0), iota((32, PAIRS * LANES), 1)
    turn_all, l_all = lane_all // LANES, lax.rem(lane_all, LANES)
    pick = ((q32 == turn_all) & (l_all == CZ - 1)) | ((q32 == 16 + turn_all) & (l_all == 0))
    pick = pick.astype(bf16)

    def spread_x(cx):
        get_x[cx].wait()
        rows = x_v.at[cx].reshape(RHS * CY, CZ)
        for cy in range(CY):
            v = rows[pl.ds(cy, RHS, stride=CY), :]
            xp[(cx + 1) * pad + cy + 1] = v
            xsb[cx, cy * RHS : (cy + 1) * RHS, :] = v.astype(bf16)

    def ring(axis, step):
        n = size[axis]
        return place(axis, lax.rem(pos_of[axis] + step + n, n))

    spread_x(x_order[0])
    spread_x(x_order[1])
    pl.semaphore_wait(barrier, partners)
    halo = [
        send(xsb.at[CX - 1], hx.at[0], ring("gx", 1)),
        send(xsb.at[0], hx.at[1], ring("gx", -1)),
    ]
    for cx in x_order[2:]:
        spread_x(cx)
    halo += [
        send(xsb.at[:, pl.ds((CY - 1) * RHS, RHS)], hy.at[0], ring("gy", 1)),
        send(xsb.at[:, pl.ds(0, RHS)], hy.at[1], ring("gy", -1)),
    ]
    rows = jnp.concatenate(
        [xsb[p // 4, (p % 4) * LANES : (p % 4 + 1) * LANES, :] for p in range(PAIRS)], axis=1
    )
    zsend[...] = nt(pick, rows).astype(bf16)
    halo += [
        send(zsend.at[pl.ds(0, 16)], hz.at[0], ring("gz", 1)),
        send(zsend.at[pl.ds(16, 16)], hz.at[1], ring("gz", -1)),
    ]

    mine = rows_at(member * SEP, SEP)
    lane_group = iota((SEP, LANES), 1) // SEP
    per_tile = LANES // SEP
    for i in range(3):
        get_m[i].wait()

    def reorder(i):
        pieces = [
            m_v[i, :, t * LANES : (t + 1) * LANES].astype(f32) for t in range(depth // LANES)
        ]
        for t in range(depth // LANES):
            out = jnp.zeros((SEP, LANES), f32)
            for g in range(per_tile):
                old = (t % na) * nb + g * 2 + t // na
                piece = pieces[old // per_tile]
                shift = ((g - old % per_tile) * SEP) % LANES
                if shift:
                    piece = pltpu.roll(piece, shift, 1)
                out = jnp.where(lane_group == g, piece, out)
            at = slice(t * LANES, (t + 1) * LANES)
            gath[(3, 0, 1)[i], a, member, :, at] = out.astype(bf16)

    reorder(0)

    axes = ("member", "gx")

    def own(m, c):
        return gath.at[m, a, member, :, pl.ds(c * half, half)]

    def near(m, c, axis, step, part):
        at = ring_index(axis, step)
        rows = pl.ds(part * (SEP // 2), SEP // 2)
        if axis == "member":
            return gath.at[m, a, at, rows, pl.ds(c * half, half)]
        return gath.at[m, at, member, rows, pl.ds(c * half, half)]

    def line(m, c, axis, step):
        at = ring_index(axis, step)
        if axis == "member":
            return gath.at[m, :, at, :, pl.ds(c * half, half)]
        return gath.at[m, at, :, :, pl.ds(c * half, half)]

    def near_line(m, c, axis, step, part):
        at = ring_index(axis, step)
        cut = pl.ds(part * 2, 2)
        if axis == "member":
            return gath.at[m, cut, at, :, pl.ds(c * half, half)]
        return gath.at[m, at, cut, :, pl.ds(c * half, half)]

    def ring_index(axis, step):
        return lax.rem(pos_of[axis] + step + size[axis], size[axis])

    def later(src, where):
        copy = remote(count[0], src, src, where)
        count[0] += 1
        return copy

    def ring_pair(block, axis):
        return [later(block, ring(axis, step)) for step in (1, -1)]

    def gather_stages(m):
        one, two, three, four = [], [], [], []
        for c in range(2):
            first, second = axes[c], axes[1 - c]
            one += ring_pair(own(m, c), first)
            three += ring_pair(line(m, c, second, 0), second)
            for part, step in enumerate((1, -1)):
                two.append(later(near(m, c, first, -step, part), ring(first, step)))
                four.append(later(near_line(m, c, second, -step, part), ring(second, step)))
        return one, two, three, four

    def launch(copies):
        for copy in copies:
            copy.start()

    def relay(came, onward):
        for got, copy in zip(came, onward):
            got.wait_recv()
            copy.start()

    low_stages, up_stages, cell_stages, base_stages, pair_stages = (
        gather_stages(m) for m in range(5)
    )
    use_low, use_up = z > 0, z < nz - 1
    odd = lax.rem(z, 2) == 1
    even = jnp.logical_not(odd)

    def all_of(*conditions):
        return functools.reduce(jnp.logical_and, conditions)

    pair_up = all_of(odd, z <= nz - 3)
    give_up = all_of(even, z >= 2)
    up_before = all_of(use_up, z >= 5)
    cells_here = z <= 2
    owners_add = jnp.logical_not(cells_here)

    def shift_copy(m, step):
        n = count[0]
        count[0] += 1
        return remote(n, gath.at[m, a, member], gath.at[4, a, member], (a, b, z + step))

    shift_up = shift_copy(1, -1)
    sibling = remote(count[0], gath.at[4], gath_sib, (a, member * 2 + 1 - core, z))
    count[0] += 1
    launch(base_stages[0])
    reorder(1)
    reorder(2)
    pl.when(use_low)(lambda: launch(low_stages[0]))
    pl.when(give_up)(shift_up.start)

    get_c.wait()
    cells = jnp.broadcast_to(c_v[...], (SEP, SEP)).astype(f32)
    square = iota((SEP, SEP), 0) == iota((SEP, SEP), 1)
    column = jnp.sum(jnp.where(square, cells, 0.0), axis=1, keepdims=True)
    column = jnp.broadcast_to(column, (SEP, 4 * CZ))
    z512 = iota((SEP, 4 * CZ), 1)

    def mark(q, carry):
        oh[q] = jnp.zeros((wide, 4 * CZ), bf16)
        at = (z512 + q * 4 * CZ).astype(f32)
        oh[q, mine, :] = jnp.where(column == at, 1.0, 0.0).astype(bf16)
        return carry

    lax.fori_loop(0, QUADS, mark, 0)

    vecs = e_v.shape[0] // SLABS
    part_vecs = vecs // 4

    def relayout(c):
        get_e[c].wait()
        at = slice(c * part_vecs, (c + 1) * part_vecs)

        def step(q, carry):
            for h in range(4):
                rows = pl.ds(c * chunk + 4 * q + h, part_vecs, stride=SLABS)
                hi, lo = split(e_v[rows, :])
                vh[q, at, h * CZ : (h + 1) * CZ] = hi
                vl[q, at, h * CZ : (h + 1) * CZ] = lo
            return carry

        lax.fori_loop(0, QUADS, step, 0)

    split_early = z >= 2
    pl.when(split_early)(lambda: relayout(0))
    get_d.wait()
    get_v.wait()
    get_r.wait()
    relay(base_stages[0], base_stages[1])
    pl.when(use_low)(lambda: relay(low_stages[0], low_stages[1]))
    arrive(halo)
    arrive(base_stages[1])
    launch(base_stages[2])


    @pl.when(use_low)
    def _():
        arrive(low_stages[1])
        launch(low_stages[2])

    before_z = hz[0].astype(f32) * flag(z > 0)
    after_z = hz[1].astype(f32) * flag(z < nz - 1)
    ends = jnp.concatenate(
        [before_z, after_z, jnp.zeros((LANES - 32, LANES), f32)], axis=0
    ).T.astype(bf16)
    for k, mask in enumerate((flag(a > 0), flag(a < na - 1))):
        for cy in range(CY):
            xp[k * (CX + 1) * pad + cy + 1] = (
                hx[k, cy * RHS : (cy + 1) * RHS, :].astype(f32) * mask
            )
    for k, mask in enumerate((flag(b > 0), flag(b < nb - 1))):
        for cx in range(CX):
            xp[(cx + 1) * pad + k * (CY + 1)] = hy[k, cx].astype(f32) * mask
    q128, lane_all = iota((LANES, PAIRS * LANES), 0), iota((LANES, PAIRS * LANES), 1)
    turn_all, l_all = lane_all // LANES, lax.rem(lane_all, LANES)
    spread = ((q128 == turn_all) & (l_all == 0)) | ((q128 == 16 + turn_all) & (l_all == CZ - 1))
    z_ends[...] = nn(ends, spread.astype(bf16))
    lane64 = iota((RHS, LANES), 1)

    def residual_of(q, carry):
        for h in range(4):
            s = 4 * q + h
            i = (q // 2 + 1) * pad + lax.rem(q, 2) * 4 + h + 1
            x = xp[i]
            diag = 6.0 + d_v[pl.ds(s, 1), :]
            v0, v1, v2 = (v_v[pl.ds(k * SLABS + s, 1), :] for k in range(3))
            end = z_ends[(h % 2) * RHS : (h % 2 + 1) * RHS, rows_at((2 * q + h // 2) * LANES, LANES)]
            before = jnp.where(lane64 == 0, end, pltpu.roll(x, 1, 1))
            after = jnp.where(lane64 == CZ - 1, end, pltpu.roll(x, CZ - 1, 1))
            res = slab(r_v, s) - diag * x
            res = res + (1.0 + v0) * xp[i - pad] + (1.0 - v0) * xp[i + pad]
            res = res + (1.0 + v1) * xp[i - 1] + (1.0 - v1) * xp[i + 1]
            res = res + (1.0 + v2) * before + (1.0 - v2) * after
            r_v[pl.ds(s, RHS, stride=SLABS), :] = res
            at = slice(h * CZ, (h + 1) * CZ)
            res_b[q, :, at] = res.astype(bf16)
            w = res * (1.0 / diag)
            hi, lo = split(w)
            w0[q, :, at] = w
            wh[q, :, at] = hi
            wl[q, :, at] = lo
        return carry

    lax.fori_loop(0, QUADS, residual_of, 0)
    seps = nt(
        jnp.concatenate([res_b[q] for q in range(QUADS)], axis=1),
        jnp.concatenate([oh[q] for q in range(QUADS)], axis=1),
    )
    put_res = pltpu.make_async_copy(r_v, res_o, loc_sem.at[9])
    put_res.start()

    sep_loc[...] = seps.astype(bf16).reshape(members, group, wide)
    me = slot * members + member
    pairs = []
    for d in range(na):
        for e in range(nb):
            if d or e:
                to, far = lax.rem(a + d, na), lax.rem(b + e, nb)
                pairs.append((sep_loc.at[far // 2], sep_in.at[me], (to, far, z)))
    hop = exchange(pairs, sep_in)
    sep_in[me] = sep_loc[member]
    relay(base_stages[2], base_stages[3])
    for c in (1, 2, 3):
        pl.when(split_early)(functools.partial(relayout, c))
    pl.when(use_low)(lambda: relay(low_stages[2], low_stages[3]))
    hop.wait()
    arrive(base_stages[3])

    row8 = iota((8, LANES), 0)
    left = []
    for i in range(slots):
        v = sep_in[i * members].astype(f32)
        for e in range(1, members):
            v = v + sep_in[i * members + e].astype(f32)
        left.append(v.astype(bf16))
    wide_base = nt(jnp.concatenate(left, axis=1), gath[3].reshape(half, depth))
    gx_here = jnp.zeros((8, LANES), jnp.int32) + a
    for j in range(na):
        both = wide_base[:, j * wide : (j + 1) * wide]
        v = jnp.where(gx_here >= 2, both[8:], both[:8])
        v = jnp.where(lax.rem(gx_here, 2) == 1, pltpu.roll(v, 4, 0), v)
        base[:, j * wide : (j + 1) * wide] = jnp.where(row8 < 4, v, pltpu.roll(v, 4, 0))

    def plane_copies(first, src, dst, step):
        return [
            remote(first + d, src, dst, (a, member * 2 + lax.rem(core + d, 2), z + step))
            for d in range(2)
        ]

    give_state = plane_copies(count[0], kept, other.at[core], -1)
    count[0] += 2

    eacc[...] = jnp.zeros(eacc.shape, f32)

    def earlier_product(q, carry):
        right = jnp.concatenate([wh[q], wl[q], oh[q]], axis=0)
        eacc[:vecs] += nt(vh[q], right)
        eacc[vecs:] += nt(vl[q], right)
        return carry

    here = member * na + a
    fold = vecs // 2
    rowf = iota((8, fold), 0)
    plane_sum, plane_came = exchange_later(
        plane_pairs(lambda to, far: psend.at[far * na + to], pin.at[here]), pin
    )

    def send_sums(main):
        for i in range(RHS // 8):
            one = main[8 * i : 8 * i + 8, :fold]
            two = main[8 * i : 8 * i + 8, fold:]
            psend[2 * i] = jnp.where(rowf < 4, one, pltpu.roll(two, 4, 0))
            psend[2 * i + 1] = jnp.where(rowf < 4, pltpu.roll(one, 4, 0), two)
        launch(plane_sum)

    def earlier_results():
        main = eacc[:vecs, :LANES] + eacc[vecs:, :LANES]
        main = main.T
        main = main[:RHS] + main[RHS:]

        @pl.when(cells_here)
        def _():
            send_sums(main)
            for i in range(2):
                values = eacc[i * vecs : (i + 1) * vecs, LANES:].T
                v = values[:SEP]
                for e in range(1, members):
                    v = v + values[e * SEP : (e + 1) * SEP]
                gath[2, a, member, :, i * vecs : (i + 1) * vecs] = v.astype(bf16)

        @pl.when(owners_add)
        def _():
            pt_v[...] = main
            for i in range(2):
                cell_v[i] = eacc[i * vecs : (i + 1) * vecs, LANES:].T.astype(bf16)

    fw_1 = plane_copies(count[0], stateb.at[0], fw_in.at[core], 1)
    bw_1 = plane_copies(count[0] + 2, stateb.at[1], bw_in.at[core], -1)
    bw_2 = plane_copies(count[0] + 4, stateb.at[1], bw_in.at[core], -2)
    count[0] += 6
    fw_near = z < nz - 1
    bw_near, bw_far = odd, all_of(odd, z >= 3)
    row_group = iota((16, LANES), 0) // 4

    def pack(v):
        t = [v[:, j * wide : (j + 1) * wide] for j in range(na)]
        return jnp.concatenate(
            [jnp.where(row8 < 4, t[0], t[1]), jnp.where(row8 < 4, t[2], t[3])], axis=0
        )

    def left_of(packed):
        left = []
        for v in packed:
            v = v.astype(f32)
            left += [jnp.where(row_group == j, v, 0.0).astype(bf16) for j in range(na)]
        return jnp.concatenate(left, axis=1)

    def product_of(left, rows):
        out = nt(left, rows.reshape(half, depth)[...])
        out = out[:8] + out[8:]
        return out + pltpu.roll(out, 4, 0)

    first_core = jnp.zeros((8, half), jnp.int32) + core == 0

    def two_steps(left, start, m):
        own, far = product_of(left, gath.at[4]), product_of(left, gath_sib)
        between = (
            other[0] - jnp.where(first_core, own, far),
            other[1] - jnp.where(first_core, far, own),
        )
        return start - product_of(left_of([pack(v).astype(bf16) for v in between]), gath.at[m])

    def products(first, last):
        lax.fori_loop(first, last, earlier_product, 0)

    def begin():
        launch(up_stages[0])

        @pl.when(pair_up)
        def _():
            shift_up.wait_recv()
            launch(pair_stages[0])

    def first_relay():
        relay(up_stages[0], up_stages[1])
        pl.when(pair_up)(lambda: relay(pair_stages[0], pair_stages[1]))

    def second_launch():
        arrive(up_stages[1])
        launch(up_stages[2])

        @pl.when(pair_up)
        def _():
            arrive(pair_stages[1])
            launch(pair_stages[2])

    def second_relay():
        relay(up_stages[2], up_stages[3])
        pl.when(pair_up)(lambda: relay(pair_stages[2], pair_stages[3]))

    def pair_end():
        arrive(pair_stages[3])
        sibling.start()

    pl.when(up_before)(begin)
    pl.when(z >= 3)(lambda: products(0, 2))
    pl.when(up_before)(first_relay)
    pl.when(z >= 4)(lambda: products(2, 4))
    pl.when(up_before)(second_launch)
    pl.when(z >= 6)(lambda: products(4, 6))
    pl.when(up_before)(second_relay)
    pl.when(use_low)(lambda: arrive(low_stages[3]))

    @pl.when(z == 0)
    def _():
        state[...] = base[...]

    @pl.when(z > 0)
    def _():
        arrive(fw_1)
        state[...] = base[...] - product_of(left_of([fw_in[0], fw_in[1]]), gath.at[0])

    @pl.when(fw_near)
    def _():
        stateb[0] = pack(state[...]).astype(bf16)
        launch(fw_1)

    @pl.when(give_up)
    def _():
        kept[...] = state[...]
        launch(give_state)

    def push_back():
        stateb[1] = pack(state[...]).astype(bf16)
        launch(bw_1)

    @pl.when(z == nz - 1)
    def _():
        push_back()
        launch(bw_2)

    @pl.when(z == 5)
    def _():
        pair_end()
        products(4, 6)

    @pl.when(z < 5)
    def _():
        begin()

        @pl.when(z < 2)
        def _():
            relayout(0)
            relayout(1)

        pl.when(z == 2)(lambda: products(0, 2))
        pl.when(z == 3)(lambda: products(2, 4))
        pl.when(z == 4)(lambda: products(4, 6))
        first_relay()

        @pl.when(z < 2)
        def _():
            relayout(2)
            relayout(3)

        pl.when(z == 2)(lambda: products(2, 4))
        pl.when(z == 3)(lambda: products(4, 6))
        second_launch()
        pl.when(z < 2)(lambda: products(0, 4))
        pl.when(z < 3)(lambda: products(4, 6))
        second_relay()

    products(6, 8)
    pl.when(all_of(pair_up, z < 5))(pair_end)
    earlier_results()

    @pl.when(cells_here)
    def _():
        launch(cell_stages[0])
        relay(cell_stages[0], cell_stages[1])
        arrive(cell_stages[1])
        launch(cell_stages[2])

    pl.when(use_up)(lambda: arrive(up_stages[3]))
    pl.when(pair_up)(sibling.wait_recv)
    pl.when(cells_here)(lambda: relay(cell_stages[2], cell_stages[3]))

    @pl.when(all_of(use_up, jnp.logical_not(pair_up)))
    def _():
        arrive(bw_1)
        state[...] = state[...] - product_of(left_of([bw_in[0], bw_in[1]]), gath.at[1])

    @pl.when(pair_up)
    def _():
        arrive(give_state)
        arrive(bw_2)
        state[...] = two_steps(left_of([bw_in[0], bw_in[1]]), state[...], 1)

    pl.when(all_of(odd, use_up))(push_back)
    pl.when(all_of(bw_far, use_up))(lambda: launch(bw_2))

    for j in range(na):
        tiles[j] = state[:, j * wide : (j + 1) * wide]
    ret_came = exchange(plane_pairs(lambda to, far: tiles.at[to], ret.at[here]), ret)
    ret[here] = tiles[a]

    def total_of(ref, n):
        out = ref[0]
        for i in range(1, n):
            out = out + ref[i]
        return out

    def take_sol():
        ret_came.wait()
        sol = jnp.concatenate(
            [jnp.where(row8 < 4, ret[2 * i], ret[2 * i + 1]) for i in range(na * members // 2)],
            axis=0,
        )
        sol_v[...] = jnp.concatenate(split(sol), axis=1)

    @pl.when(owners_add)
    def _():
        take_sol()
        sol_h, sol_l = sol_v[:, :wide], sol_v[:, wide:]
        part = nn(jnp.concatenate([sol_h, sol_l], axis=0), cell_v[0])
        send_sums(pt_v[...] + part[:RHS] + part[RHS:] + nn(sol_h, cell_v[1]))

    pin[here] = psend[here]
    plane_came.wait()
    where_fin = z * 2 + core
    fin[where_fin] = total_of(pin, na * members)

    @pl.when(cells_here)
    def _():
        arrive(cell_stages[3])
        part = nn(jnp.concatenate(split(state[...]), axis=0), gath[2].reshape(half, 2 * vecs))
        part = part[:8, :vecs] + part[8:, :vecs] + part[:8, vecs:]
        fin[where_fin] = fin[where_fin] + jnp.where(rowf < 4, part[:, :fold], part[:, fold:])

    pairs = []
    for d in range(nz):
        for e in range(2):
            if d or e:
                to, kind = lax.rem(z + d, nz), lax.rem(core + e, 2)
                mine_there = fin.at[where_fin]
                pairs.append((mine_there, mine_there, (a, member * 2 + kind, to)))
    hop = exchange(pairs, fin)

    pl.when(cells_here)(take_sol)
    sol_hl = sol_v[...]

    def add_sol(first):
        twice = jnp.concatenate([oh[first], oh[first + 1]], axis=1)
        change = nn(sol_hl, jnp.concatenate([twice, twice], axis=0))
        w0[first] = w0[first] + change[:, : 4 * CZ]
        w0[first + 1] = w0[first + 1] + change[:, 4 * CZ :]

    add_sol(0)
    add_sol(2)
    hop.wait()
    full_in[here] = total_of(fin, nz * 2)
    hop = exchange(plane_pairs(lambda to, far: full_in.at[here], full_in.at[here]), full_in)
    add_sol(4)
    add_sol(6)
    hop.wait()
    for i in range(RHS // 8):
        p, q = full_in[2 * i], full_in[2 * i + 1]
        pt_v[8 * i : 8 * i + 8, :fold] = jnp.where(rowf < 4, p, pltpu.roll(q, 4, 0))
        pt_v[8 * i : 8 * i + 8, fold:] = jnp.where(rowf < 4, pltpu.roll(p, 4, 0), q)
    pin5_put = pltpu.make_async_copy(pt_v, proj_o, loc_sem.at[10])
    pin5_put.start()
    full = pt_v[...]
    hi, lo = split(full)
    pt_hl[:RHS] = hi
    pt_hl[RHS:] = lo

    def project(i, gram):
        for q in (2 * i, 2 * i + 1):
            main = nn(pt_hl[...], vh[q])
            o = w0[q] - (main[:RHS] + main[RHS:] + nn(pt_hl[:RHS], vl[q]))
            hi, lo = split(o)
            both = jnp.concatenate([hi, lo], axis=0)
            orth[q] = both
            gram = gram + nt(both, both)
        return gram

    gram = lax.fori_loop(0, QUADS // 2, project, jnp.zeros((2 * RHS, 2 * RHS), f32))
    gram = gram[:RHS] + gram[RHS:]
    gram = gram + pltpu.roll(gram, RHS, 1)
    put_orth = pltpu.make_async_copy(orth, orth_o, loc_sem.at[11])
    put_orth.start()
    piece = RHS // nz
    g_loc[...] = gram.reshape(nz, piece, LANES)
    hop = share("gz", lambda to: g_loc.at[to], gin1)
    gin1[z] = g_loc[z]
    for wait in sent[:-1]:
        wait()
    del sent[:-1]

    for stage in base_stages:
        for copy in stage:
            copy.wait_send()

    @pl.when(use_low)
    def _():
        for stage in low_stages:
            for copy in stage:
                copy.wait_send()

    @pl.when(use_up)
    def _():
        for stage in up_stages:
            for copy in stage:
                copy.wait_send()

    for condition, copies in (
        (cells_here, sum(cell_stages, [])), (pair_up, sum(pair_stages, [])), (pair_up, [sibling]),
        (give_up, [shift_up] + give_state), (fw_near, fw_1), (bw_near, bw_1), (bw_far, bw_2),
    ):
        @pl.when(condition)
        def _(copies=copies):
            for copy in copies:
                copy.wait_send()

    hop.wait()
    seat = a * nb + b
    gin2[seat] = total_of(gin1, nz)
    pairs = []
    for d in range(na):
        for e in range(nb):
            if d or e:
                to, far = lax.rem(a + d, na), lax.rem(b + e, nb)
                pairs.append((gin2.at[seat], gin2.at[seat], (to, far, z)))
    exchange(pairs, gin2).wait()
    gin3[z] = total_of(gin2, na * nb)
    share("gz", lambda to: gin3.at[z], gin3).wait()
    put_gram = pltpu.make_async_copy(gin3, gram_o, loc_sem.at[12])
    put_gram.start()
    for wait in sent:
        wait()
    for put in (put_res, pin5_put, put_orth, put_gram):
        put.wait()


def finish_kernel(
    scale, gram_v, orth_h, res_h, proj_h, res_o, new_o, proj_o, chol_o,
    orth, rows_v, new_v, res_v, proj_v, sem,
):
    get = pltpu.make_async_copy(orth_h, orth, sem.at[0])
    hand_on = [
        (pltpu.make_async_copy(res_h, res_v, sem.at[1]), pltpu.make_async_copy(res_v, res_o, sem.at[2])),
        (pltpu.make_async_copy(proj_h, proj_v, sem.at[3]), pltpu.make_async_copy(proj_v, proj_o, sem.at[4])),
    ]
    get.start()
    for copy, _ in hand_on:
        copy.start()
    cholesky_rows(gram_v[...], rows_v)
    rows = rows_v[...]
    lane64, row64 = iota((RHS, LANES), 1), iota((RHS, LANES), 0)
    upper = jnp.where((lane64 >= row64) & (lane64 < RHS), rows * (1.0 / scale), 0.0)
    inverse = jnp.where(lane64 - RHS <= row64, rows * scale, 0.0)
    hi, lo = split(inverse)
    lhs = jnp.where(lane64 < RHS, pltpu.roll(hi.astype(f32), RHS, 1), lo.astype(f32)).astype(bf16)
    lhs = jnp.concatenate([lhs, lhs], axis=1)
    for copy, onward in hand_on:
        copy.wait()
        onward.start()
    get.wait()

    def finish(q, carry):
        hi, lo = orth[q, :RHS], orth[q, RHS:]
        out = nn(lhs, jnp.concatenate([hi, hi, lo, lo], axis=0))
        for h in range(4):
            new_v[pl.ds(4 * q + h, RHS, stride=SLABS), :] = out[:, h * CZ : (h + 1) * CZ]
        return carry

    lax.fori_loop(0, QUADS, finish, 0, unroll=4)
    put_new = pltpu.make_async_copy(new_v, new_o, sem.at[5])
    put_new.start()
    upper = jnp.concatenate([upper, jnp.zeros((LANES - RHS, LANES), f32)], axis=0)
    chol_o[...] = upper.T[:RHS, :RHS]
    for _, onward in hand_on:
        onward.wait()
    put_new.wait()


def body(
    x_field, right_side, diag_shift, velocity, earlier_blocks, sep_cells, low_inv, low_off, up_off
):
    na, nb, nz = (lax.axis_size(n) for n in ("gx", "gy", "gz"))
    members, slots = nb // 2, na * 2
    group, wide = RHS // members, SEP * members
    depth, half = slots * wide, na * wide
    vecs = earlier_blocks.shape[0] * earlier_blocks.shape[1]
    piece = RHS // nz
    vmem = pltpu.VMEM
    scratch = [
        vmem((CX, RHS, CY, CZ), f32),
        vmem((ROWS, CZ), f32),
        vmem((SLABS, CZ), f32),
        vmem((3 * SLABS, CZ), f32),
        vmem((vecs * SLABS, CZ), f32),
        vmem((1, SEP), jnp.int32),
        vmem((3, SEP, depth), bf16),
        vmem(((CX + 2) * (CY + 2), RHS, CZ), f32),
        vmem((CX, CY * RHS, CZ), bf16),
        vmem((2, CY * RHS, CZ), bf16),
        vmem((2, CX, RHS, CZ), bf16),
        vmem((2, 16, LANES), bf16),
        vmem((32, LANES), bf16),
        vmem((LANES, PAIRS * LANES), f32),
        vmem((QUADS, RHS, 4 * CZ), bf16),
        vmem((QUADS, wide, 4 * CZ), bf16),
        vmem((5, na, members, SEP, depth), bf16),
        vmem((na, members, SEP, depth), bf16),
        vmem((QUADS, RHS, 4 * CZ), f32),
        vmem((QUADS, RHS, 4 * CZ), bf16),
        vmem((QUADS, RHS, 4 * CZ), bf16),
        vmem((QUADS, vecs, 4 * CZ), bf16),
        vmem((QUADS, vecs, 4 * CZ), bf16),
        vmem((2 * vecs, 2 * LANES), f32),
        vmem((2, wide, vecs), bf16),
        vmem((RHS, 2 * wide), bf16),
        vmem((members, group, wide), bf16),
        vmem((slots * members, group, wide), bf16),
        vmem((8, half), f32),
        vmem((8, half), f32),
        vmem((2, 16, wide), bf16),
        vmem((na, 8, wide), f32),
        vmem((2, 16, wide), bf16),
        vmem((2, 16, wide), bf16),
        vmem((na * members, 8, wide), f32),
        vmem((8, half), f32),
        vmem((2, 8, half), f32),
        vmem((na * members, 8, vecs // 2), f32),
        vmem((na * members, 8, vecs // 2), f32),
        vmem((2 * nz, 8, vecs // 2), f32),
        vmem((na * members, 8, vecs // 2), f32),
        vmem((RHS, vecs), f32),
        vmem((2 * RHS, vecs), bf16),
        vmem((QUADS, 2 * RHS, 4 * CZ), bf16),
        vmem((nz, piece, LANES), f32),
        vmem((nz, piece, LANES), f32),
        vmem((na * nb, piece, LANES), f32),
        vmem((nz, piece, LANES), f32),
        pltpu.SemaphoreType.DMA((19,)),
        pltpu.SemaphoreType.DMA((160,)),
        pltpu.SemaphoreType.DMA((160,)),
    ]
    flat = lambda v: v.reshape(-1, CZ)
    anywhere = pl.BlockSpec(memory_space=pl.ANY)
    in_vmem = pl.BlockSpec(memory_space=pltpu.VMEM)
    res, orth, projection, gram = pl.pallas_call(
        functools.partial(kernel, na, nb, nz),
        out_shape=(
            jax.ShapeDtypeStruct((ROWS, CZ), f32),
            jax.ShapeDtypeStruct((QUADS, 2 * RHS, 4 * CZ), bf16),
            jax.ShapeDtypeStruct((RHS, vecs), f32),
            jax.ShapeDtypeStruct((nz, piece, LANES), f32),
        ),
        in_specs=[anywhere] * 9,
        out_specs=(anywhere,) * 4,
        scratch_shapes=scratch,
        compiler_params=pltpu.CompilerParams(
            collective_id=0, has_side_effects=True, vmem_limit_bytes=60 * 2**20
        ),
        cost_estimate=pl.CostEstimate(
            flops=2 * 10**9, bytes_accessed=13 * 2**20, transcendentals=0
        ),
        name="step",
    )(
        x_field, flat(right_side), flat(diag_shift), flat(velocity), flat(earlier_blocks),
        sep_cells, low_inv[0], low_off[0], up_off[0],
    )
    res, new, projection, factor = pl.pallas_call(
        functools.partial(finish_kernel, math.sqrt(na * nb * nz * CX * CY * CZ)),
        out_shape=(
            jax.ShapeDtypeStruct((ROWS, CZ), f32),
            jax.ShapeDtypeStruct((ROWS, CZ), f32),
            jax.ShapeDtypeStruct((RHS, vecs), f32),
            jax.ShapeDtypeStruct((RHS, RHS), f32),
        ),
        in_specs=[in_vmem, anywhere, anywhere, anywhere],
        out_specs=(anywhere, anywhere, anywhere, in_vmem),
        scratch_shapes=[
            vmem((QUADS, 2 * RHS, 4 * CZ), bf16),
            vmem((RHS, LANES), f32),
            vmem((ROWS, CZ), f32),
            vmem((ROWS, CZ), f32),
            vmem((RHS, vecs), f32),
            pltpu.SemaphoreType.DMA((6,)),
        ],
        compiler_params=pltpu.CompilerParams(vmem_limit_bytes=60 * 2**20),
        cost_estimate=pl.CostEstimate(flops=2 * 10**8, bytes_accessed=5 * 2**20, transcendentals=0),
        name="finish",
    )(gram.reshape(RHS, LANES), orth, res, projection)
    shape = right_side.shape
    return (res.reshape(shape), new.reshape(shape), projection.T, factor)


def solution(mesh):
    return jax.shard_map(
        body,
        mesh=mesh,
        in_specs=(
            P(None, "gx", "gy", "gz"),
            P(None, "gx", "gy", "gz"),
            P("gx", "gy", "gz"),
            P(None, "gx", "gy", "gz"),
            P(None, None, "gx", "gy", "gz"),
            P("gz", ("gx", "gy")),
            P("gz", ("gx", "gy"), None),
            P("gz", ("gx", "gy"), None),
            P("gz", ("gx", "gy"), None),
        ),
        out_specs=(P(None, "gx", "gy", "gz"), P(None, "gx", "gy", "gz"), P(), P()),
        check_vma=False,
    )
```
